32 devices in a mesh: dp: 16 (over z, y, core), tensor: 2 (over x).
Axes of the slice: x: 2, y: 2, z: 4, core: 2. Of those that a mesh axis runs over, the one named last changes fastest.
Arguments:
- tokens: bfloat16 [6144, 2048], P(('dp', 'tensor')), may hold values from -6 to 6
- attn_gain: bfloat16 [2048], P('dp'), may hold values from 0.099609375 to 1.8984375
- w_query: bfloat16 [2048, 2048], P('dp', 'tensor'), may hold values from -0.125 to 0.125
- keyvalue_weight: bfloat16 [2, 2048, 256], P(None, 'dp', 'tensor'), may hold values from -0.125 to 0.125
- w_out: bfloat16 [2048, 2048], P('tensor', 'dp'), may hold values from -0.5 to 0.5
- mlp_gain: bfloat16 [2048], P('dp'), may hold values from 0.099609375 to 1.8984375
- w_gateup: bfloat16 [2, 2048, 5632], P(None, 'dp', 'tensor'), may hold values from -0.125 to 0.125
- w_down: bfloat16 [5632, 2048], P('tensor', 'dp'), may hold values from -0.109375 to 0.109375
- segment_ids: int32 [6144], P('dp'), may hold values from 0 to 190, as said below
- positions: int32 [6144], P('dp'), may hold values from 0 to 383, as said below
- cotangent: bfloat16 [6144, 2048], P(('dp', 'tensor')), may hold values from -6 to 6
Outputs:
- output: bfloat16 [6144, 2048], P(('dp', 'tensor'))
- input_grad: bfloat16 [6144, 2048], P(('dp', 'tensor'))
- attn_gain_grad: float32 [2048], P(('dp', 'tensor'))
- w_query_grad: float32 [2048, 2048], P('dp', 'tensor')
- w_keyval_grad: float32 [2, 2048, 256], P(None, 'dp', 'tensor')
- w_out_grad: float32 [2048, 2048], P('tensor', 'dp')
- mlp_gain_grad: float32 [2048], P(('dp', 'tensor'))
- w_gateup_grad: float32 [2, 2048, 5632], P(None, 'dp', 'tensor')
- w_down_grad: float32 [5632, 2048], P('tensor', 'dp')
The draws below stay inside these ranges and needn't reach their ends.
Inputs may be any that keep to these rules, and one draw needn't show every extreme that they name: `segment_ids`: within each group of 384 consecutive rows the ids start at 0 and rise by 0 or 1 from row to row; a sequence is a run of equal ids in one group. In every group one sequence holds more than half of the rows, and in some group one sequence holds all 384 rows. The largest id is reached in some group. `positions`: A token's place in its sequence: 0 at a sequence's first row, rising by one along it.
All inputs are finite; a program needn't handle non-finite values.
Results may differ from the reference program's by a relative error of at most 0.019.
Values may be sent and summed in bfloat16 or wider, within the bound.
A program may use at most 320 MiB of HBM per device.

```python
import math
import jax
import jax.numpy as jnp
from jax import lax

MODEL_WIDTH = 2048
QUERY_HEAD_COUNT = 32
KEYVALUE_HEADS = 4
HEAD_SIZE = 64
FF = 5632
GROUP_TOK = 384
TOKENS = 6144


def packed_layout(key):
    groups = TOKENS // GROUP_TOK
    first_key, second_key, third_key, fourth_key, fifth_key = jax.random.split(key, 5)
    longest = jax.random.randint(first_key, (groups,), GROUP_TOK // 2 + 2, GROUP_TOK + 1)
    chosen = jax.random.randint(second_key, (), 0, groups)
    busy = (chosen + 1 + jax.random.randint(fifth_key, (), 0, groups - 1)) % groups
    group_index = jnp.arange(groups)
    longest = jnp.where(group_index == chosen, GROUP_TOK, longest)
    longest = jnp.where(group_index == busy, GROUP_TOK // 2 + 2, longest)
    opening = jax.random.randint(third_key, (groups,), 0, 1 << 20) % (GROUP_TOK - longest + 1)
    opening = jnp.where(group_index == busy, 0, opening)
    places = jnp.arange(GROUP_TOK)[None, :]
    inside = (places >= opening[:, None]) & (places < (opening + longest)[:, None])
    extra_cuts = jax.random.randint(fourth_key, (groups, GROUP_TOK), 0, 24) == 0
    extra_cuts = extra_cuts | (group_index == busy)[:, None]
    boundary = (places == opening[:, None]) | (places == (opening + longest)[:, None]) | extra_cuts & ~inside
    boundary = boundary & (places > 0)
    seg_ids = jnp.cumsum(boundary.astype(jnp.int32), axis=1).astype(jnp.int32)
    starts = lax.cummax(jnp.where(boundary, places, 0).astype(jnp.int32), axis=1)
    places_in = (places - starts).astype(jnp.int32)
    return (seg_ids.reshape(TOKENS), places_in.reshape(TOKENS))


def draw_segment_ids(key, part):
    seg_ids, places_in = packed_layout(key)
    return seg_ids


def draw_positions(key, part):
    seg_ids, places_in = packed_layout(key)
    return places_in


def strengthened(values, key, source, target, parts, factor):
    owner, partner = [(jnp.arange(values.shape[position]) // (values.shape[position] // parts)).reshape([-1 if axis == position else 1 for axis in range(values.ndim)]) for position in (source, target)]
    chosen = jax.random.permutation(key, parts)[partner]
    strong = (owner == chosen) | (owner == (partner + parts // 2) % parts)
    return jnp.where(strong, factor * values, values)


def levels(key, shape, pieces, smallest, largest):
    def one(axis_at, shards_of):
        steps = jax.random.uniform(jax.random.fold_in(jax.random.fold_in(key, 6), axis_at), (shards_of,), jnp.float32, smallest / len(pieces), largest / len(pieces))
        return jnp.repeat(jnp.exp(steps), shape[axis_at] // shards_of).reshape((-1,) + (1,) * (len(shape) - axis_at - 1))

    level = one(*pieces[0])
    for cut in pieces[1:]:
        level = level * one(*cut)
    return level


def scatter_about(own_key, extent, scale, most, cuts=(), kind=jnp.bfloat16):
    factor_of = levels(own_key, extent, cuts, -0.22, 0.18) if cuts else 1.0
    drawn = jax.random.normal(own_key, extent, jnp.float32) * scale * factor_of
    return jnp.minimum(jnp.maximum(drawn, -most), most).astype(kind)


def gaussian_with(own_key, dims, spread, reach, shards, heavy, held_as=jnp.bfloat16):
    entries = spread * jax.random.normal(own_key, dims, jnp.float32)
    if shards:
        entries = entries * levels(own_key, dims, shards, -0.22, 0.18)
    return jnp.clip(strengthened(entries, jax.random.fold_in(own_key, 3), *heavy), -reach, reach).astype(held_as)


def setup_inputs(seed: int = 0) -> dict:
    keys = jax.random.split(jax.random.key(seed), 12)
    tokens = gaussian_with(keys[0], (TOKENS, MODEL_WIDTH), 1.0, 6.0, ((0, 32),), (0, 1, 32, 2.75))
    attn_gain = jnp.clip(1.0 + 0.18 * jax.random.normal(keys[1], (MODEL_WIDTH,), jnp.float32), 0.099609375, 1.8984375).astype(jnp.bfloat16)
    w_query = scatter_about(keys[2], (MODEL_WIDTH, QUERY_HEAD_COUNT * HEAD_SIZE), MODEL_WIDTH ** -0.5, 0.125, ((0, 16), (1, 2)))
    keyvalue_weight = scatter_about(keys[3], (2, MODEL_WIDTH, KEYVALUE_HEADS * HEAD_SIZE), MODEL_WIDTH ** -0.5, 0.125, ((1, 16), (2, 2)))
    w_out = scatter_about(keys[4], (QUERY_HEAD_COUNT * HEAD_SIZE, MODEL_WIDTH), (QUERY_HEAD_COUNT * HEAD_SIZE // 16) ** -0.5, 0.5, ((0, 2), (1, 16)))
    mlp_gain = jnp.clip(1.0 + 0.18 * jax.random.normal(keys[5], (MODEL_WIDTH,), jnp.float32), 0.099609375, 1.8984375).astype(jnp.bfloat16)
    w_gateup = scatter_about(keys[6], (2, MODEL_WIDTH, FF), MODEL_WIDTH ** -0.5, 0.125, ((1, 16), (2, 2)))
    w_down = scatter_about(keys[7], (FF, MODEL_WIDTH), (FF // 2) ** -0.5, 0.109375, ((0, 2), (1, 16)))
    segment_ids = draw_segment_ids(jax.random.fold_in(keys[11], 71), 0)
    positions = draw_positions(jax.random.fold_in(keys[11], 71), 0)
    cotangent = gaussian_with(keys[10], (TOKENS, MODEL_WIDTH), 1.0, 6.0, ((0, 32),), (0, 1, 32, 2.75))
    return dict(tokens=tokens, attn_gain=attn_gain, w_query=w_query, keyvalue_weight=keyvalue_weight, w_out=w_out, mlp_gain=mlp_gain, w_gateup=w_gateup, w_down=w_down, segment_ids=segment_ids, positions=positions, cotangent=cotangent)


norm_eps = 1e-05

@jax.custom_vjp
def lower_bound(v):
    return lax.optimization_barrier(v.astype(jnp.bfloat16)).astype(jnp.float32)

@jax.custom_vjp
def low_back(v):
    return v

def low_keep(v):
    return (lower_bound(v), None)

def low_pass(kept, grad):
    return (grad,)

def back_keep(v):
    return (v, None)

def back_low(kept, grad):
    return (lower_bound(grad),)
lower_bound.defvjp(low_keep, low_pass)
low_back.defvjp(back_keep, back_low)

def product(left, right):
    return jnp.dot(left, right, precision=lax.Precision.HIGHEST, preferred_element_type=jnp.float32)

def rms_scale(rows, gain):
    return rows * lax.rsqrt(lax.optimization_barrier(jnp.mean(rows * rows, axis=-1, keepdims=True)) + norm_eps) * gain

def rotary_tables(places, width):
    freqs = jnp.exp(jnp.arange(0, width, 2).astype(jnp.float32) * (-math.log(10000.0) / width))
    turned = places.astype(jnp.float32)[:, None] * freqs[None, :]
    turned = jnp.concatenate([turned, turned], axis=-1)
    return (jnp.cos(turned), jnp.sin(turned))

def apply_rotary(value_rows, cosine_table, sine_table):
    segment_count = value_rows.shape[0]
    heads = value_rows.reshape(segment_count, -1, cosine_table.shape[1])
    half = cosine_table.shape[1] // 2
    swapped = jnp.concatenate([-heads[..., half:], heads[..., :half]], axis=-1)
    return (heads * cosine_table[:, None, :] + swapped * sine_table[:, None, :]).reshape(segment_count, -1)

def group_layer(rows_in, seg_group, pos_group, attn_gain, w_query, keyvalue_weight, w_out, mlp_gain, w_gateup, w_down):
    segment_count = rows_in.shape[0]
    normed = lower_bound(rms_scale(rows_in, attn_gain))
    query_unrotated = low_back(product(normed, w_query))
    key_unrotated = low_back(product(normed, keyvalue_weight[0]))
    value_rows = lower_bound(low_back(product(normed, keyvalue_weight[1])))
    cosine_table, sine_table = rotary_tables(pos_group, HEAD_SIZE)
    query_rows = lower_bound(apply_rotary(query_unrotated, cosine_table, sine_table)).reshape(segment_count, KEYVALUE_HEADS, QUERY_HEAD_COUNT // KEYVALUE_HEADS, HEAD_SIZE)
    key_rows = lower_bound(apply_rotary(key_unrotated, cosine_table, sine_table)).reshape(segment_count, KEYVALUE_HEADS, HEAD_SIZE)
    value_rows = value_rows.reshape(segment_count, KEYVALUE_HEADS, HEAD_SIZE)
    scores = jnp.einsum('qhgd,thd->hgqt', query_rows, key_rows, precision=lax.Precision.HIGHEST) / math.sqrt(HEAD_SIZE)
    scores = low_back(scores)
    order = jnp.arange(segment_count)
    allowed = (seg_group[:, None] == seg_group[None, :]) & (order[:, None] >= order[None, :])
    scores = jnp.where(allowed[None, None], scores, -1e+30)
    peak = lax.optimization_barrier(jnp.max(scores, axis=-1, keepdims=True))
    raised = jnp.exp(scores - peak)
    probs = lower_bound(raised / lax.optimization_barrier(jnp.sum(raised, axis=-1, keepdims=True)))
    attended = jnp.einsum('hgqt,thd->qhgd', probs, value_rows, precision=lax.Precision.HIGHEST).reshape(segment_count, QUERY_HEAD_COUNT * HEAD_SIZE)
    attended = low_back(lower_bound(attended))
    middle = rows_in + low_back(product(attended, w_out))
    normed_two = lower_bound(rms_scale(middle, mlp_gain))
    gate_proj = low_back(product(normed_two, w_gateup[0]))
    up_proj = low_back(product(normed_two, w_gateup[1]))
    hidden = lower_bound(gate_proj * jax.nn.sigmoid(gate_proj) * up_proj)
    return middle + low_back(product(hidden, w_down))

def reference(tokens, attn_gain, w_query, keyvalue_weight, w_out, mlp_gain, w_gateup, w_down, segment_ids, positions, cotangent):
    groups = TOKENS // GROUP_TOK
    seg_all = segment_ids.reshape(groups, GROUP_TOK)
    pos_all = positions.reshape(groups, GROUP_TOK)

    def forward(rows_all, gain_one, query_w, keyval_w, out_w, gain_two, gateup_w, down_w):

        def one_group(rows_in, seg_group, pos_group):
            return group_layer(rows_in, seg_group, pos_group, gain_one, query_w, keyval_w, out_w, gain_two, gateup_w, down_w)
        checked = jax.checkpoint(one_group)

        def scan_step(carry, operands):
            return (carry, checked(operands[0], operands[1], operands[2]))
        _, results = lax.scan(scan_step, jnp.zeros((), jnp.float32), (rows_all.reshape(groups, GROUP_TOK, MODEL_WIDTH), seg_all, pos_all))
        return results.reshape(TOKENS, MODEL_WIDTH)
    primals = (tokens.astype(jnp.float32), attn_gain.astype(jnp.float32), w_query.astype(jnp.float32), keyvalue_weight.astype(jnp.float32), w_out.astype(jnp.float32), mlp_gain.astype(jnp.float32), w_gateup.astype(jnp.float32), w_down.astype(jnp.float32))
    result, pull = jax.vjp(forward, *primals)
    grads = pull(cotangent.astype(jnp.float32))
    return (result.astype(jnp.bfloat16), grads[0].astype(jnp.bfloat16), grads[1], grads[2], grads[3], grads[4], grads[5], grads[6], grads[7])
```

```python
import math

import jax
import jax.numpy as jnp
from jax import lax
from jax.experimental import pallas as pl
from jax.experimental.pallas import tpu as pltpu
from jax.sharding import PartitionSpec as P

MESH = pl.DeviceIdType.MESH

QUERY_HEAD_COUNT = 32
KEYVALUE_HEADS = 4
HEAD_SIZE = 64
HEADS_PER_KV = QUERY_HEAD_COUNT // KEYVALUE_HEADS
norm_eps = 1e-05

CORE_BIT = 0
SHARE_BIT = 2


def rotary_tables(places, width):
    freqs = jnp.exp(jnp.arange(0, width, 2).astype(jnp.float32) * (-math.log(10000.0) / width))
    turned = places.astype(jnp.float32)[:, None] * freqs[None, :]
    turned = jnp.concatenate([turned, turned], axis=-1)
    return (jnp.cos(turned), jnp.sin(turned))


def apply_rotary(value_rows, cosine_table, sine_table):
    rows = value_rows.shape[0]
    heads = value_rows.reshape(rows, -1, HEAD_SIZE)
    half = HEAD_SIZE // 2
    swapped = jnp.concatenate([-heads[..., half:], heads[..., :half]], axis=-1)
    return (heads * cosine_table[:, None, :] + swapped * sine_table[:, None, :]).reshape(rows, -1)


def undo_rotary(value_rows, cosine_table, sine_table):
    return apply_rotary(value_rows, cosine_table, -sine_table)


def head_backward(query_head, key_head, value_head, probs, grad_out, scale):
    grad_value = jnp.einsum(
        "gqt,qgd->td", probs, grad_out, preferred_element_type=jnp.float32
    )
    grad_probs = jnp.einsum("qgd,td->gqt", grad_out, value_head, preferred_element_type=jnp.float32)
    probs = probs.astype(jnp.float32)
    centre = jnp.sum(probs * grad_probs, axis=-1, keepdims=True)
    grad_scores = (probs * (grad_probs - centre)).astype(jnp.bfloat16)
    grad_query = (
        jnp.einsum("gqt,td->qgd", grad_scores, key_head, preferred_element_type=jnp.float32) * scale
    )
    grad_key = jnp.einsum(
        "gqt,qgd->td", grad_scores, query_head, preferred_element_type=jnp.float32
    )
    return (grad_query, grad_key, grad_value)


def dot(left, right, contract):
    return lax.dot_general(left, right, (contract, ((), ())), preferred_element_type=jnp.float32)


def rms(rows):
    return lax.rsqrt(jnp.mean(rows * rows, axis=-1, keepdims=True) + norm_eps)


def rms_grad(rows, inverse, grad_scaled):
    inner = jnp.mean(grad_scaled * rows, axis=-1, keepdims=True)
    return inverse * grad_scaled - rows * (inverse * inverse * inverse) * inner


def spread(ref, lead, row_tile):
    sizes = ref.shape
    block = sizes[-2]
    kept = 0
    while block * 2**kept < row_tile and kept < lead:
        kept += 1
    out = []
    for i in range(2 ** (lead - kept)):
        index = tuple((i >> (lead - kept - 1 - j)) & 1 for j in range(lead - kept))
        out.append((index, (block * 2**kept)))
    return out


def make_forward(dp_size, high_bits):
    bit_count = dp_size.bit_length() - 1
    all_bits = tuple(range(bit_count))

    def kernel(
        tok,
        cot,
        qkv_shard,
        out_shard,
        mlp_shard,
        cosines,
        sines,
        bias,
        qkv_full,
        out_full,
        mlp_full,
        normed,
        projected,
        probs,
        attended,
        middle,
        normed_two,
        cot_all,
        qkv_held,
        out_held,
        tok_all,
        branch_away,
        branch_in,
        send_sem,
        recv_sem,
        local_sem,
    ):
        f32, bf16 = jnp.float32, jnp.bfloat16
        me = lax.axis_index("dp")
        side = lax.axis_index("tensor")
        bits = [(me // 2**k) % 2 for k in all_bits]
        share = bits[SHARE_BIT]
        own_rows, width = tok.shape
        half = width // 2
        group_rows = 2 * own_rows

        def partner(k):
            if k is None:
                return {"tensor": 1 - side}
            return {"dp": me + (1 - 2 * bits[k]) * 2**k}

        barrier = pltpu.get_barrier_semaphore()
        for k in all_bits + (None,):
            pl.semaphore_signal(barrier, inc=1, device_id=partner(k), device_id_type=MESH)
        pl.semaphore_wait(barrier, bit_count + 1)

        counter = [0]
        started = []
        local_counter = [0]

        def push(src, dst, k):
            i = counter[0]
            counter[0] += 1
            copy = pltpu.make_async_remote_copy(
                src_ref=src,
                dst_ref=dst,
                send_sem=send_sem.at[i],
                recv_sem=recv_sem.at[i],
                device_id=partner(k),
                device_id_type=MESH,
            )
            copy.start()
            started.append(copy)
            return copy

        def keep(src, dst):
            i = local_counter[0]
            local_counter[0] += 1
            copy = pltpu.make_async_copy(src, dst, local_sem.at[i])
            copy.start()
            return copy

        def held(ref, lead, gathered):
            index = tuple(
                pl.ds(0, 2) if k in gathered else bits[k] for k in reversed(all_bits)
            )
            return ref.at[lead + index]

        class Chain:
            def __init__(self, ref, lead, order, gathered):
                self.ref, self.lead, self.order = ref, lead, list(order)
                self.gathered = set(gathered)
                self.copy = None
                self.bit = None

            def first(self, src, k):
                place = held(self.ref, self.lead, ())
                self.copy = push(src, place, k)
                self.bit = k

            def step(self):
                self.copy.wait_recv()
                if self.bit is not None:
                    self.gathered.add(self.bit)
                if not self.order:
                    return
                k = self.order.pop(0)
                view = held(self.ref, self.lead, self.gathered)
                self.copy = push(view, view, k)
                self.bit = k

        tokens_copy = push(tok, tok_all.at[side], None)
        qkv_order = high_bits + (SHARE_BIT, 1, 0)
        out_order = (1,) + high_bits + (SHARE_BIT, 0)
        qkv_chain = Chain(qkv_held, (), qkv_order[1:], ())
        qkv_chain.first(qkv_shard, qkv_order[0])
        mlp_chains = []
        for m in range(3):
            chain = Chain(mlp_full, (m,), high_bits + (1, 0), ())
            chain.first(mlp_shard.at[m, 1 - share], SHARE_BIT)
            mlp_chains.append(chain)
        out_chain = Chain(out_held, (), out_order[1:], ())
        out_chain.first(out_shard, out_order[0])
        own_copies = [
            keep(qkv_shard, held(qkv_held, (), ())),
            keep(out_shard, held(out_held, (), ())),
        ] + [keep(mlp_shard.at[m, share], held(mlp_full, (m,), ())) for m in range(3)]

        tok_all[side] = tok[...]
        cot_all[share, side] = cot[...]
        for copy in own_copies:
            copy.wait()
        tokens_copy.wait_recv()

        def norm_rows(r, _):
            rows = pl.ds(r * 16, 16)
            for s in range(2):
                x = tok_all[s, rows, :].astype(f32)
                scaled = x * lax.rsqrt(jnp.mean(x * x, axis=-1, keepdims=True) + norm_eps)
                normed[pl.ds(s * own_rows + r * 16, 16), :] = scaled.astype(bf16)
            return 0

        lax.fori_loop(0, own_rows // 16, norm_rows, 0)

        qkv_chain.step()
        out_chain.step()
        mlp_chains[0].step()
        for _ in range(len(high_bits) - 1):
            qkv_chain.step()
        qkv_chain.step()
        cot_right = push(
            cot_all.at[share, side, :, pl.ds(half, half)],
            cot_all.at[share, side, :, pl.ds(half, half)],
            SHARE_BIT,
        )
        cot_left = push(
            cot_all.at[share, side, :, pl.ds(0, half)],
            cot_all.at[share, side, :, pl.ds(0, half)],
            None,
        )
        mlp_chains[1].step()
        mlp_chains[2].step()
        for _ in range(len(high_bits) - 1):
            out_chain.step()
            for m in range(3):
                mlp_chains[m].step()
        out_chain.step()
        mlp_chains[0].step()
        qkv_chain.step()
        qkv_chain.step()
        out_copies = [keep(qkv_held, qkv_full)]

        query_width = attended.shape[1]
        key_width = (projected.shape[1] - query_width) // 2
        tile = 2 * key_width
        lanes = lax.broadcasted_iota(jnp.int32, (group_rows, tile), 1)
        first_half = lanes % HEAD_SIZE < HEAD_SIZE // 2

        def rotate(a):
            cos2 = jnp.concatenate([cosines[...], cosines[...]], axis=1)
            sin2 = jnp.concatenate([sines[...], sines[...]], axis=1)
            forward = pltpu.roll(a, tile - HEAD_SIZE // 2, 1)
            back = pltpu.roll(a, HEAD_SIZE // 2, 1)
            return a * cos2 + jnp.where(first_half, forward, back) * sin2

        lead = (slice(None),) * bit_count + (slice(None),)

        def project(columns):
            weights = qkv_held[lead + (columns,)].reshape(width, tile)
            return jnp.dot(normed[...], weights, preferred_element_type=f32)

        def query_tile(i, _):
            columns = pl.ds(pl.multiple_of(i * tile, tile), tile)
            rotated = rotate(project(columns)).astype(bf16)
            projected[:, columns] = rotated * jnp.asarray(HEAD_SIZE**-0.5, bf16)
            return 0

        lax.fori_loop(0, query_width // tile, query_tile, 0)
        last = project(slice(query_width, query_width + tile))
        keys = rotate(last)[:, :key_width].astype(bf16)
        values = last[:, key_width:].astype(bf16)
        projected[:, query_width : query_width + key_width] = keys
        projected[:, query_width + key_width :] = values

        cot_right.wait_recv()
        cot_right2 = push(
            cot_all.at[:, side, :, pl.ds(half, half)],
            cot_all.at[:, side, :, pl.ds(half, half)],
            None,
        )
        cot_left.wait_recv()
        cot_left2 = push(
            cot_all.at[share, :, :, pl.ds(0, half)],
            cot_all.at[share, :, :, pl.ds(0, half)],
            SHARE_BIT,
        )
        mlp_chains[1].step()

        rows_tile = 128
        pair_lanes = lax.broadcasted_iota(jnp.int32, (group_rows, 2 * HEAD_SIZE), 1)
        keys32 = keys.astype(f32)
        values32 = values.astype(f32)

        def padded(a, head, place):
            moved = a if head == place else pltpu.roll(a, HEAD_SIZE, 1)
            inside = pair_lanes < HEAD_SIZE if place == 0 else pair_lanes >= HEAD_SIZE
            return jnp.where(inside, moved, 0.0).astype(bf16)

        for head in range(key_width // HEAD_SIZE):
            keys_at = [padded(keys32, head, p) for p in range(2)]
            values_at = [padded(values32, head, p) for p in range(2)]
            pairs = HEADS_PER_KV // 2

            def head_pair(i, _):
                columns = pl.ds(pl.multiple_of((head * pairs + i) * 128, 128), 128)
                for low in range(0, group_rows, rows_tile):
                    high = low + rows_tile
                    query = projected[low:high, columns]
                    mixed = None
                    for p in range(2):
                        scores = dot(query, keys_at[p][:high], ((1,), (1,)))
                        scores = scores + bias[low:high, :high]
                        peak = jnp.max(scores, axis=-1, keepdims=True)
                        raised = jnp.exp(scores - peak)
                        total = jnp.sum(raised, axis=-1, keepdims=True)
                        share_of = (raised * (1.0 / total)).astype(bf16)
                        probs[head * HEADS_PER_KV + 2 * i + p, low:high, :high] = share_of
                        part = jnp.dot(share_of, values_at[p][:high], preferred_element_type=f32)
                        mixed = part if mixed is None else mixed + part
                    attended[low:high, columns] = mixed.astype(bf16)
                return 0

            lax.fori_loop(0, pairs, head_pair, 0)
            if head == 0:
                out_chain.step()
                mlp_chains[0].step()
                mlp_chains[2].step()

        out_chain.step()
        out_copies.append(keep(out_held, out_full))

        away = attended[pl.ds(pl.multiple_of((1 - side) * own_rows, 64), own_rows), :]
        tiles = spread(out_held, bit_count, 512)
        for i, (index, count) in enumerate(tiles):
            weights = out_held[index].reshape(count, query_width)
            branch_away[:, i * count : (i + 1) * count] = dot(away, weights, ((1,), (1,))).astype(
                bf16
            )
        branch_copy = push(branch_away, branch_in, None)
        near = attended[pl.ds(pl.multiple_of(side * own_rows, 64), own_rows), :]
        for i, (index, count) in enumerate(tiles):
            weights = out_held[index].reshape(count, query_width)
            middle[:, i * count : (i + 1) * count] = dot(near, weights, ((1,), (1,)))
        branch_copy.wait_recv()

        def middle_rows(r, _):
            rows = pl.ds(r * 16, 16)
            x = (
                tok[rows, :].astype(f32)
                + middle[rows, :]
                + branch_in[rows, :].astype(f32)
            )
            middle[rows, :] = x
            scaled = x * lax.rsqrt(jnp.mean(x * x, axis=-1, keepdims=True) + norm_eps)
            normed_two[share, side, rows, :] = scaled.astype(bf16)
            return 0

        lax.fori_loop(0, own_rows // 16, middle_rows, 0)
        two_right = push(
            normed_two.at[share, side, :, pl.ds(half, half)],
            normed_two.at[share, side, :, pl.ds(half, half)],
            SHARE_BIT,
        )
        two_left = push(
            normed_two.at[share, side, :, pl.ds(0, half)],
            normed_two.at[share, side, :, pl.ds(0, half)],
            None,
        )
        mlp_chains[1].step()
        two_right.wait_recv()
        two_right2 = push(
            normed_two.at[:, side, :, pl.ds(half, half)],
            normed_two.at[:, side, :, pl.ds(half, half)],
            None,
        )
        two_left.wait_recv()
        two_left2 = push(
            normed_two.at[share, :, :, pl.ds(0, half)],
            normed_two.at[share, :, :, pl.ds(0, half)],
            SHARE_BIT,
        )
        mlp_chains[2].step()
        for chain in mlp_chains:
            chain.step()
        cot_right2.wait_recv()
        cot_left2.wait_recv()
        two_right2.wait_recv()
        two_left2.wait_recv()
        for copy in out_copies:
            copy.wait()
        for copy in started:
            copy.wait_send()

    def call(tok, cot, qkv_shard, out_shard, mlp_shard, cosines, sines, bias):
        bf16, f32 = jnp.bfloat16, jnp.float32
        own_rows, width = tok.shape
        block, qkv_width = qkv_shard.shape
        query_width = out_shard.shape[1]
        mlp_width = mlp_shard.shape[-1]
        rows = 2 * own_rows
        twos = (2,) * bit_count
        heads = query_width // HEAD_SIZE
        whole = pl.BlockSpec(memory_space=pltpu.VMEM)
        away = pl.BlockSpec(memory_space=pl.ANY)
        steps = 4 * (bit_count + 1) + 16
        shape = jax.ShapeDtypeStruct
        return pl.pallas_call(
            kernel,
            out_shape=[
                shape(twos + (block, qkv_width), bf16),
                shape(twos + (block, query_width), bf16),
                shape((3,) + twos + (block, mlp_width), bf16),
                shape((rows, width), bf16),
                shape((rows, qkv_width), bf16),
                shape((heads, rows, rows), bf16),
                shape((rows, query_width), bf16),
                shape((own_rows, width), f32),
                shape((2, 2, own_rows, width), bf16),
                shape((2, 2, own_rows, width), bf16),
            ],
            in_specs=[whole, whole, away, away, away, whole, whole, whole],
            out_specs=[away, away, away] + [whole] * 7,
            scratch_shapes=[
                pltpu.VMEM(twos + (block, qkv_width), bf16),
                pltpu.VMEM(twos + (block, query_width), bf16),
                pltpu.VMEM((2, own_rows, width), bf16),
                pltpu.VMEM((own_rows, width), bf16),
                pltpu.VMEM((own_rows, width), bf16),
                pltpu.SemaphoreType.DMA((steps,)),
                pltpu.SemaphoreType.DMA((steps,)),
                pltpu.SemaphoreType.DMA((8,)),
            ],
            compiler_params=pltpu.CompilerParams(
                collective_id=1, has_side_effects=True, vmem_limit_bytes=56 * 1024 * 1024
            ),
            name="forward",
        )(tok, cot, qkv_shard, out_shard, mlp_shard, cosines, sines, bias)

    return call


def make_body(dp_size):
    bit_count = dp_size.bit_length() - 1
    high_bits = tuple(range(bit_count - 1, SHARE_BIT, -1))
    low_bits = tuple(range(SHARE_BIT - 1, -1, -1))

    def body(
        tokens,
        attn_gain,
        w_query,
        keyvalue_weight,
        w_out,
        mlp_gain,
        w_gateup,
        w_down,
        segment_ids,
        positions,
        cotangent,
    ):
        f32, bf16 = jnp.float32, jnp.bfloat16
        me = lax.axis_index("dp")
        side = lax.axis_index("tensor")
        own_rows, width = tokens.shape
        group_rows = segment_ids.shape[0]
        block = width // dp_size
        scale = 1.0 / math.sqrt(HEAD_SIZE)

        def bit(k):
            return (me >> k) & 1

        def swap(a, k):
            if k is None:
                return lax.ppermute(a, "tensor", [(0, 1), (1, 0)])
            return lax.ppermute(a, "dp", [(i, i ^ (1 << k)) for i in range(dp_size)])

        def place(k):
            return side if k is None else bit(k)

        def join(a, k, axis):
            other = swap(a, k)
            first = place(k) == 0
            return jnp.stack([jnp.where(first, a, other), jnp.where(first, other, a)], axis=axis)

        def part(a, axis, at):
            return lax.dynamic_index_in_dim(a, at, axis, keepdims=False)

        def fold(a, k, axis):
            here = place(k)
            sent = part(a, axis, 1 - here).astype(bf16)
            return part(a, axis, here).astype(f32) + swap(sent, k).astype(f32)

        def gather_rows(shard, bits, held):
            a = shard
            for k in bits:
                above = sum(1 for h in held if h > k)
                columns = a.shape[-1]
                a = a.reshape((2**above, -1, columns))
                a = join(a, k, 1)
                held = held + (k,)
            return a.reshape(-1, a.shape[-1])

        def gather_attention(shard):
            return gather_rows(shard, high_bits + (SHARE_BIT,) + low_bits, ())

        def gather_mlp(shard):
            halves = shard.reshape(block, 2, -1)
            here = bit(SHARE_BIT)
            mine = part(halves, 1, here)
            other = swap(part(halves, 1, 1 - here), SHARE_BIT)
            first = here == 0
            both = jnp.stack([jnp.where(first, mine, other), jnp.where(first, other, mine)])
            return gather_rows(both.reshape(2 * block, -1), high_bits + low_bits, (SHARE_BIT,))

        def weight_grad(left, right, bits):
            rows = left.shape[0]
            halves = left.reshape(rows, -1, 2, block)
            here = bit(CORE_BIT)
            away = part(halves, 2, 1 - here).reshape(rows, -1)
            near = part(halves, 2, here).reshape(rows, -1)
            sent = dot(away, right, ((0,), (0,))).astype(bf16)
            a = dot(near, right, ((0,), (0,))) + swap(sent, CORE_BIT).astype(f32)
            left_bits = [k for k in range(bit_count) if k != CORE_BIT]
            for k in bits:
                above = sum(1 for h in left_bits if h > k)
                a = a.reshape(2**above, 2, -1, a.shape[-1])
                a = fold(a, k, 1)
                left_bits.remove(k)
            return a.reshape(-1, a.shape[-1])

        def attention_grad(left, right):
            return weight_grad(left, right, low_bits[:-1] + (SHARE_BIT,) + high_bits[::-1])

        def mlp_grad(left, right):
            a = weight_grad(left, right, low_bits[:-1] + high_bits[::-1])
            a = a.reshape(2, block, -1)
            here = bit(SHARE_BIT)
            mine = part(a, 0, here)
            other = swap(part(a, 0, 1 - here).astype(bf16), SHARE_BIT).astype(f32)
            first = here == 0
            return jnp.concatenate(
                [jnp.where(first, mine, other), jnp.where(first, other, mine)], axis=1
            )

        def quad_gather(rows):
            left, right = rows[:, : width // 2], rows[:, width // 2 :]
            left = join(join(left, None, 0), SHARE_BIT, 0)
            right = join(join(right, SHARE_BIT, 0), None, 1)
            return jnp.concatenate([left, right], axis=-1).reshape(4 * own_rows, width)

        def quad_sum(rows):
            grid = rows.reshape(2, 2, own_rows, width)
            left, right = grid[..., : width // 2], grid[..., width // 2 :]
            left = fold(fold(left, SHARE_BIT, 0), None, 0)
            right = fold(fold(right, None, 1), SHARE_BIT, 0)
            return jnp.concatenate([left, right], axis=-1)

        def pair_gather(rows):
            return join(rows, None, 0).reshape(2 * own_rows, width)

        def pair_sum(rows):
            return fold(rows.reshape(2, own_rows, width), None, 0)

        gain_one = attn_gain.astype(f32)[:, None]
        gain_two = mlp_gain.astype(f32)[:, None]
        key_value = jnp.concatenate([keyvalue_weight[0], keyvalue_weight[1]], axis=1)
        qkv_shard = jnp.concatenate([w_query, key_value], axis=1)
        query_width, key_width = w_query.shape[1], keyvalue_weight.shape[2]
        local_kv = key_width // HEAD_SIZE

        def scaled(shard, gain):
            return (shard.astype(f32) * gain).astype(bf16)

        cosine_table, sine_table = rotary_tables(positions, HEAD_SIZE)
        signed = jnp.where(jnp.arange(HEAD_SIZE) < HEAD_SIZE // 2, -sine_table, sine_table)
        order = jnp.arange(group_rows)
        allowed = (segment_ids[:, None] == segment_ids[None, :]) & (
            order[:, None] >= order[None, :]
        )
        mlp_shard = jnp.stack([w_down.T, scaled(w_gateup[0], gain_two), scaled(w_gateup[1], gain_two)])
        mlp_shard = jnp.moveaxis(mlp_shard.reshape(3, block, 2, -1), 2, 1)
        (
            qkv_full,
            out_full,
            mlp_full,
            normed,
            projected,
            probs,
            attended,
            middle,
            normed_two,
            grad_all,
        ) = make_forward(dp_size, high_bits)(
            tokens,
            cotangent,
            scaled(qkv_shard, gain_one),
            w_out.T,
            mlp_shard,
            jnp.concatenate([cosine_table, cosine_table], axis=1),
            jnp.concatenate([signed, signed], axis=1),
            jnp.where(allowed, 0.0, -1e30).astype(f32),
        )
        qkv_full = qkv_full.reshape(width, -1)
        out_full = out_full.reshape(width, -1)
        down_full, gate_full, up_full = mlp_full.reshape(3, width, -1)
        normed_two = normed_two.reshape(4 * own_rows, width)
        grad_all = grad_all.reshape(4 * own_rows, width)
        query_heads = projected[:, :query_width].reshape(
            group_rows, local_kv, HEADS_PER_KV, HEAD_SIZE
        )
        key_heads = projected[:, query_width : query_width + key_width].reshape(
            group_rows, local_kv, HEAD_SIZE
        )
        value_heads = projected[:, query_width + key_width :].reshape(
            group_rows, local_kv, HEAD_SIZE
        )
        probs = jnp.where(allowed[None], probs, 0).reshape(
            local_kv, HEADS_PER_KV, group_rows, group_rows
        )

        inverse_two = rms(middle)
        grad_hidden = dot(grad_all, down_full, ((1,), (0,)))
        gate = dot(normed_two, gate_full, ((1,), (0,)))
        up = dot(normed_two, up_full, ((1,), (0,)))
        sig = jax.nn.sigmoid(gate)
        silu = gate * sig
        hidden = (silu * up).astype(bf16)
        grad_gate = (grad_hidden * up * sig * (1.0 + gate * (1.0 - sig))).astype(bf16)
        grad_up = (grad_hidden * silu).astype(bf16)
        scaled_two = dot(grad_gate, gate_full, ((1,), (1,))) + dot(grad_up, up_full, ((1,), (1,)))
        scaled_two = quad_sum(scaled_two)
        down_sum = mlp_grad(grad_all, hidden)
        gate_sum = mlp_grad(normed_two, grad_gate)
        up_sum = mlp_grad(normed_two, grad_up)
        result = (middle + quad_sum(dot(hidden, down_full, ((1,), (1,))))).astype(bf16)

        grad_middle = cotangent.astype(f32) + rms_grad(middle, inverse_two, scaled_two)
        grad_branch = pair_gather(grad_middle.astype(bf16))
        grad_attended = dot(grad_branch, out_full, ((1,), (0,))).astype(bf16)
        out_sum = attention_grad(grad_branch, attended)
        grad_heads = grad_attended.reshape(group_rows, local_kv, HEADS_PER_KV, HEAD_SIZE)
        grad_query, grad_key, grad_value = [], [], []
        for h in range(local_kv):
            q, k, v = head_backward(
                query_heads[:, h],
                key_heads[:, h],
                value_heads[:, h],
                probs[h],
                grad_heads[:, h],
                scale,
            )
            grad_query.append(q)
            grad_key.append(k)
            grad_value.append(v)
        grad_query = undo_rotary(
            jnp.stack(grad_query, axis=1).reshape(group_rows, -1), cosine_table, sine_table
        )
        grad_key = undo_rotary(
            jnp.stack(grad_key, axis=1).reshape(group_rows, -1), cosine_table, sine_table
        )
        grad_value = jnp.stack(grad_value, axis=1).reshape(group_rows, -1)
        grad_qkv = jnp.concatenate([grad_query, grad_key, grad_value], axis=1).astype(bf16)
        qkv_sum = attention_grad(normed, grad_qkv)
        scaled_one = pair_sum(dot(grad_qkv, qkv_full, ((1,), (1,))))
        rows_in = tokens.astype(f32)
        input_grad = (grad_middle + rms_grad(rows_in, rms(rows_in), scaled_one)).astype(bf16)

        def gain_grad(weights, sums):
            rows = sum(jnp.sum(w.astype(f32) * s, axis=1) for w, s in zip(weights, sums))
            halves = rows.reshape(2, -1)
            return part(halves, 0, side) + swap(part(halves, 0, 1 - side), None)

        attn_gain_grad = gain_grad([qkv_shard], [qkv_sum])
        mlp_gain_grad = gain_grad([w_gateup[0], w_gateup[1]], [gate_sum, up_sum])
        qkv_grad = qkv_sum * gain_one
        query_grad = qkv_grad[:, :query_width]
        keyval_grad = jnp.stack(
            [
                qkv_grad[:, query_width : query_width + key_width],
                qkv_grad[:, query_width + key_width :],
            ]
        )
        gateup_grad = jnp.stack([gate_sum * gain_two, up_sum * gain_two])
        return (
            result,
            input_grad,
            attn_gain_grad,
            query_grad,
            keyval_grad,
            out_sum.T,
            mlp_gain_grad,
            gateup_grad,
            down_sum.T,
        )

    return body


def solution(mesh):
    return jax.shard_map(
        make_body(mesh.shape["dp"]),
        mesh=mesh,
        in_specs=(
            P(("dp", "tensor"), None),
            P("dp"),
            P("dp", "tensor"),
            P(None, "dp", "tensor"),
            P("tensor", "dp"),
            P("dp"),
            P(None, "dp", "tensor"),
            P("tensor", "dp"),
            P("dp"),
            P("dp"),
            P(("dp", "tensor"), None),
        ),
        out_specs=(
            P(("dp", "tensor"), None),
            P(("dp", "tensor"), None),
            P(("dp", "tensor")),
            P("dp", "tensor"),
            P(None, "dp", "tensor"),
            P("tensor", "dp"),
            P(("dp", "tensor")),
            P(None, "dp", "tensor"),
            P("tensor", "dp"),
        ),
        check_vma=False,
    )
```

```python
import math

import jax
import jax.numpy as jnp
from jax import lax
from jax.experimental import pallas as pl
from jax.experimental.pallas import tpu as pltpu
from jax.sharding import PartitionSpec as P

MESH = pl.DeviceIdType.MESH

QUERY_HEAD_COUNT = 32
KEYVALUE_HEADS = 4
HEAD_SIZE = 64
HEADS_PER_KV = QUERY_HEAD_COUNT // KEYVALUE_HEADS
norm_eps = 1e-05

CORE_BIT = 0
SHARE_BIT = 2


def rotary_tables(places, width):
    freqs = jnp.exp(jnp.arange(0, width, 2).astype(jnp.float32) * (-math.log(10000.0) / width))
    turned = places.astype(jnp.float32)[:, None] * freqs[None, :]
    turned = jnp.concatenate([turned, turned], axis=-1)
    return (jnp.cos(turned), jnp.sin(turned))


def dot(left, right, contract):
    return lax.dot_general(left, right, (contract, ((), ())), preferred_element_type=jnp.float32)


def rms(rows):
    return lax.rsqrt(jnp.mean(rows * rows, axis=-1, keepdims=True) + norm_eps)


def rms_grad(rows, inverse, grad_scaled):
    inner = jnp.mean(grad_scaled * rows, axis=-1, keepdims=True)
    return inverse * grad_scaled - rows * (inverse * inverse * inverse) * inner


def spread(ref, lead, row_tile):
    sizes = ref.shape
    block = sizes[-2]
    kept = 0
    while block * 2**kept < row_tile and kept < lead:
        kept += 1
    out = []
    for i in range(2 ** (lead - kept)):
        index = tuple((i >> (lead - kept - 1 - j)) & 1 for j in range(lead - kept))
        out.append((index, (block * 2**kept)))
    return out


def make_forward(dp_size, high_bits):
    bit_count = dp_size.bit_length() - 1
    all_bits = tuple(range(bit_count))

    def kernel(
        tok,
        cot,
        qkv_shard,
        out_shard,
        mlp_shard,
        cosines,
        sines,
        bias,
        qkv_full,
        out_full,
        mlp_full,
        normed,
        projected,
        probs,
        attended,
        middle,
        normed_two,
        cot_all,
        qkv_held,
        out_held,
        tok_all,
        branch_away,
        branch_in,
        send_sem,
        recv_sem,
        local_sem,
    ):
        f32, bf16 = jnp.float32, jnp.bfloat16
        me = lax.axis_index("dp")
        side = lax.axis_index("tensor")
        bits = [(me // 2**k) % 2 for k in all_bits]
        share = bits[SHARE_BIT]
        own_rows, width = tok.shape
        half = width // 2
        group_rows = 2 * own_rows

        def partner(k):
            if k is None:
                return {"tensor": 1 - side}
            return {"dp": me + (1 - 2 * bits[k]) * 2**k}

        barrier = pltpu.get_barrier_semaphore()
        for k in all_bits + (None,):
            pl.semaphore_signal(barrier, inc=1, device_id=partner(k), device_id_type=MESH)
        pl.semaphore_wait(barrier, bit_count + 1)

        counter = [0]
        started = []
        local_counter = [0]

        def push(src, dst, k):
            i = counter[0]
            counter[0] += 1
            copy = pltpu.make_async_remote_copy(
                src_ref=src,
                dst_ref=dst,
                send_sem=send_sem.at[i],
                recv_sem=recv_sem.at[i],
                device_id=partner(k),
                device_id_type=MESH,
            )
            copy.start()
            started.append(copy)
            return copy

        def keep(src, dst):
            i = local_counter[0]
            local_counter[0] += 1
            copy = pltpu.make_async_copy(src, dst, local_sem.at[i])
            copy.start()
            return copy

        def held(ref, lead, gathered):
            index = tuple(
                pl.ds(0, 2) if k in gathered else bits[k] for k in reversed(all_bits)
            )
            return ref.at[lead + index]

        class Chain:
            def __init__(self, ref, lead, order, gathered):
                self.ref, self.lead, self.order = ref, lead, list(order)
                self.gathered = set(gathered)
                self.copy = None
                self.bit = None

            def first(self, src, k):
                place = held(self.ref, self.lead, ())
                self.copy = push(src, place, k)
                self.bit = k

            def step(self):
                self.copy.wait_recv()
                if self.bit is not None:
                    self.gathered.add(self.bit)
                if not self.order:
                    return
                k = self.order.pop(0)
                view = held(self.ref, self.lead, self.gathered)
                self.copy = push(view, view, k)
                self.bit = k

        tokens_copy = push(tok, tok_all.at[side], None)
        qkv_order = high_bits + (SHARE_BIT, 1, 0)
        out_order = (1,) + high_bits + (SHARE_BIT, 0)
        qkv_chain = Chain(qkv_held, (), qkv_order[1:], ())
        qkv_chain.first(qkv_shard, qkv_order[0])
        mlp_chains = []
        for m in range(3):
            chain = Chain(mlp_full, (m,), high_bits + (1, 0), ())
            chain.first(mlp_shard.at[m, 1 - share], SHARE_BIT)
            mlp_chains.append(chain)
        out_chain = Chain(out_held, (), out_order[1:], ())
        out_chain.first(out_shard, out_order[0])
        own_copies = [
            keep(qkv_shard, held(qkv_held, (), ())),
            keep(out_shard, held(out_held, (), ())),
        ] + [keep(mlp_shard.at[m, share], held(mlp_full, (m,), ())) for m in range(3)]

        tok_all[side] = tok[...]
        cot_all[share, side] = cot[...]
        for copy in own_copies:
            copy.wait()
        tokens_copy.wait_recv()

        def norm_rows(r, _):
            rows = pl.ds(r * 16, 16)
            for s in range(2):
                x = tok_all[s, rows, :].astype(f32)
                scaled = x * lax.rsqrt(jnp.mean(x * x, axis=-1, keepdims=True) + norm_eps)
                normed[pl.ds(s * own_rows + r * 16, 16), :] = scaled.astype(bf16)
            return 0

        lax.fori_loop(0, own_rows // 16, norm_rows, 0)

        qkv_chain.step()
        out_chain.step()
        mlp_chains[0].step()
        for _ in range(len(high_bits) - 1):
            qkv_chain.step()
        qkv_chain.step()
        cot_right = push(
            cot_all.at[share, side, :, pl.ds(half, half)],
            cot_all.at[share, side, :, pl.ds(half, half)],
            SHARE_BIT,
        )
        cot_left = push(
            cot_all.at[share, side, :, pl.ds(0, half)],
            cot_all.at[share, side, :, pl.ds(0, half)],
            None,
        )
        mlp_chains[1].step()
        mlp_chains[2].step()
        for _ in range(len(high_bits) - 1):
            out_chain.step()
            for m in range(3):
                mlp_chains[m].step()
        out_chain.step()
        mlp_chains[0].step()
        qkv_chain.step()
        qkv_chain.step()
        out_copies = [keep(qkv_held, qkv_full)]

        query_width = attended.shape[1]
        key_width = (projected.shape[1] - query_width) // 2
        tile = 2 * key_width
        lanes = lax.broadcasted_iota(jnp.int32, (group_rows, tile), 1)
        first_half = lanes % HEAD_SIZE < HEAD_SIZE // 2

        def rotate(a):
            cos2 = jnp.concatenate([cosines[...], cosines[...]], axis=1)
            sin2 = jnp.concatenate([sines[...], sines[...]], axis=1)
            forward = pltpu.roll(a, tile - HEAD_SIZE // 2, 1)
            back = pltpu.roll(a, HEAD_SIZE // 2, 1)
            return a * cos2 + jnp.where(first_half, forward, back) * sin2

        lead = (slice(None),) * bit_count + (slice(None),)

        def project(columns):
            weights = qkv_held[lead + (columns,)].reshape(width, tile)
            return jnp.dot(normed[...], weights, preferred_element_type=f32)

        def query_tile(i, _):
            columns = pl.ds(pl.multiple_of(i * tile, tile), tile)
            rotated = rotate(project(columns)).astype(bf16)
            projected[:, columns] = rotated * jnp.asarray(HEAD_SIZE**-0.5, bf16)
            return 0

        lax.fori_loop(0, query_width // tile, query_tile, 0)
        last = project(slice(query_width, query_width + tile))
        keys = rotate(last)[:, :key_width].astype(bf16)
        values = last[:, key_width:].astype(bf16)
        projected[:, query_width : query_width + key_width] = keys
        projected[:, query_width + key_width :] = values

        cot_right.wait_recv()
        cot_right2 = push(
            cot_all.at[:, side, :, pl.ds(half, half)],
            cot_all.at[:, side, :, pl.ds(half, half)],
            None,
        )
        cot_left.wait_recv()
        cot_left2 = push(
            cot_all.at[share, :, :, pl.ds(0, half)],
            cot_all.at[share, :, :, pl.ds(0, half)],
            SHARE_BIT,
        )
        mlp_chains[1].step()

        rows_tile = 128
        pair_lanes = lax.broadcasted_iota(jnp.int32, (group_rows, 2 * HEAD_SIZE), 1)
        keys32 = keys.astype(f32)
        values32 = values.astype(f32)

        def padded(a, head, place):
            moved = a if head == place else pltpu.roll(a, HEAD_SIZE, 1)
            inside = pair_lanes < HEAD_SIZE if place == 0 else pair_lanes >= HEAD_SIZE
            return jnp.where(inside, moved, 0.0).astype(bf16)

        for head in range(key_width // HEAD_SIZE):
            keys_at = [padded(keys32, head, p) for p in range(2)]
            values_at = [padded(values32, head, p) for p in range(2)]
            pairs = HEADS_PER_KV // 2

            def head_pair(i, _):
                columns = pl.ds(pl.multiple_of((head * pairs + i) * 128, 128), 128)
                for low in range(0, group_rows, rows_tile):
                    high = low + rows_tile
                    query = projected[low:high, columns]
                    mixed = None
                    for p in range(2):
                        scores = dot(query, keys_at[p][:high], ((1,), (1,)))
                        scores = scores + bias[low:high, :high]
                        peak = jnp.max(scores, axis=-1, keepdims=True)
                        raised = jnp.exp(scores - peak)
                        total = jnp.sum(raised, axis=-1, keepdims=True)
                        share_of = (raised * (1.0 / total)).astype(bf16)
                        probs[head * HEADS_PER_KV + 2 * i + p, low:high, :high] = share_of
                        part = jnp.dot(share_of, values_at[p][:high], preferred_element_type=f32)
                        mixed = part if mixed is None else mixed + part
                    attended[low:high, columns] = mixed.astype(bf16)
                return 0

            lax.fori_loop(0, pairs, head_pair, 0)
            if head == 0:
                out_chain.step()
                mlp_chains[0].step()
                mlp_chains[2].step()

        out_chain.step()
        out_copies.append(keep(out_held, out_full))

        away = attended[pl.ds(pl.multiple_of((1 - side) * own_rows, 64), own_rows), :]
        tiles = spread(out_held, bit_count, 512)
        for i, (index, count) in enumerate(tiles):
            weights = out_held[index].reshape(count, query_width)
            branch_away[:, i * count : (i + 1) * count] = dot(away, weights, ((1,), (1,))).astype(
                bf16
            )
        branch_copy = push(branch_away, branch_in, None)
        near = attended[pl.ds(pl.multiple_of(side * own_rows, 64), own_rows), :]
        for i, (index, count) in enumerate(tiles):
            weights = out_held[index].reshape(count, query_width)
            middle[:, i * count : (i + 1) * count] = dot(near, weights, ((1,), (1,)))
        branch_copy.wait_recv()

        def middle_rows(r, _):
            rows = pl.ds(r * 16, 16)
            x = (
                tok[rows, :].astype(f32)
                + middle[rows, :]
                + branch_in[rows, :].astype(f32)
            )
            middle[rows, :] = x
            scaled = x * lax.rsqrt(jnp.mean(x * x, axis=-1, keepdims=True) + norm_eps)
            normed_two[share, side, rows, :] = scaled.astype(bf16)
            return 0

        lax.fori_loop(0, own_rows // 16, middle_rows, 0)
        two_right = push(
            normed_two.at[share, side, :, pl.ds(half, half)],
            normed_two.at[share, side, :, pl.ds(half, half)],
            SHARE_BIT,
        )
        two_left = push(
            normed_two.at[share, side, :, pl.ds(0, half)],
            normed_two.at[share, side, :, pl.ds(0, half)],
            None,
        )
        mlp_chains[1].step()
        two_right.wait_recv()
        two_right2 = push(
            normed_two.at[:, side, :, pl.ds(half, half)],
            normed_two.at[:, side, :, pl.ds(half, half)],
            None,
        )
        two_left.wait_recv()
        two_left2 = push(
            normed_two.at[share, :, :, pl.ds(0, half)],
            normed_two.at[share, :, :, pl.ds(0, half)],
            SHARE_BIT,
        )
        mlp_chains[2].step()
        for chain in mlp_chains:
            chain.step()
        cot_right2.wait_recv()
        cot_left2.wait_recv()
        two_right2.wait_recv()
        two_left2.wait_recv()
        for copy in out_copies:
            copy.wait()
        for copy in started:
            copy.wait_send()

    def call(tok, cot, qkv_shard, out_shard, mlp_shard, cosines, sines, bias):
        bf16, f32 = jnp.bfloat16, jnp.float32
        own_rows, width = tok.shape
        block, qkv_width = qkv_shard.shape
        query_width = out_shard.shape[1]
        mlp_width = mlp_shard.shape[-1]
        rows = 2 * own_rows
        twos = (2,) * bit_count
        heads = query_width // HEAD_SIZE
        whole = pl.BlockSpec(memory_space=pltpu.VMEM)
        away = pl.BlockSpec(memory_space=pl.ANY)
        steps = 4 * (bit_count + 1) + 16
        shape = jax.ShapeDtypeStruct
        return pl.pallas_call(
            kernel,
            out_shape=[
                shape(twos + (block, qkv_width), bf16),
                shape(twos + (block, query_width), bf16),
                shape((3,) + twos + (block, mlp_width), bf16),
                shape((rows, width), bf16),
                shape((rows, qkv_width), bf16),
                shape((heads, rows, rows), bf16),
                shape((rows, query_width), bf16),
                shape((own_rows, width), f32),
                shape((2, 2, own_rows, width), bf16),
                shape((2, 2, own_rows, width), bf16),
            ],
            in_specs=[whole, whole, away, away, away, whole, whole, whole],
            out_specs=[away, away, away] + [whole] * 7,
            scratch_shapes=[
                pltpu.VMEM(twos + (block, qkv_width), bf16),
                pltpu.VMEM(twos + (block, query_width), bf16),
                pltpu.VMEM((2, own_rows, width), bf16),
                pltpu.VMEM((own_rows, width), bf16),
                pltpu.VMEM((own_rows, width), bf16),
                pltpu.SemaphoreType.DMA((steps,)),
                pltpu.SemaphoreType.DMA((steps,)),
                pltpu.SemaphoreType.DMA((8,)),
            ],
            compiler_params=pltpu.CompilerParams(
                collective_id=1, has_side_effects=True, vmem_limit_bytes=56 * 1024 * 1024
            ),
            name="forward",
        )(tok, cot, qkv_shard, out_shard, mlp_shard, cosines, sines, bias)

    return call


def make_mlp(lead):
    def kernel(rows_ref, cot_ref, weights, hid, grad_out, out_part, held, load_sem):
        f32, bf16 = jnp.float32, jnp.bfloat16
        rows, width = rows_ref.shape
        hidden_width = hid.shape[-1]
        loads = []
        for m in range(3):
            copy = pltpu.make_async_copy(weights.at[m], held.at[m], load_sem.at[m])
            copy.start()
            loads.append(copy)
        for copy in loads:
            copy.wait()
        tall = rows // 2
        starts = list(range(0, hidden_width, 512))

        def first(r, _):
            at = pl.ds(pl.multiple_of(r * tall, tall), tall)
            for low in starts:
                high = min(low + 512, hidden_width)
                take = (slice(None),) * (lead + 1) + (slice(low, high),)
                parts = []
                for m in range(3):
                    block = held[(m,) + take].reshape(width, high - low)
                    left = cot_ref if m == 0 else rows_ref
                    parts.append(jnp.dot(left[at, :], block, preferred_element_type=f32))
                grad_hidden, gate, up = parts
                sig = jax.nn.sigmoid(gate)
                silu = gate * sig
                hid[0, at, low:high] = (silu * up).astype(bf16)
                hid[1, at, low:high] = (grad_hidden * up * (sig + silu * (1.0 - sig))).astype(bf16)
                hid[2, at, low:high] = (grad_hidden * silu).astype(bf16)
            return 0

        lax.fori_loop(0, 2, first, 0)
        tiles = spread(held.at[0], lead, 512)

        def second(r, _):
            at = pl.ds(pl.multiple_of(r * tall, tall), tall)
            for i, (index, count) in enumerate(tiles):
                to = slice(i * count, (i + 1) * count)
                gate_rows = held[(1,) + index].reshape(count, hidden_width)
                up_rows = held[(2,) + index].reshape(count, hidden_width)
                total = dot(hid[1, at, :], gate_rows, ((1,), (1,)))
                total = total + dot(hid[2, at, :], up_rows, ((1,), (1,)))
                grad_out[at, to] = total.astype(bf16)
                down_rows = held[(0,) + index].reshape(count, hidden_width)
                out_part[at, to] = dot(hid[0, at, :], down_rows, ((1,), (1,))).astype(bf16)
            return 0

        lax.fori_loop(0, 2, second, 0)

    def call(rows, cot, weights):
        bf16 = jnp.bfloat16
        count, width = rows.shape
        shape = jax.ShapeDtypeStruct
        whole = pl.BlockSpec(memory_space=pltpu.VMEM)
        return pl.pallas_call(
            kernel,
            out_shape=[
                shape((3, count, weights.shape[-1]), bf16),
                shape((count, width), bf16),
                shape((count, width), bf16),
            ],
            in_specs=[whole, whole, pl.BlockSpec(memory_space=pl.ANY)],
            out_specs=[whole] * 3,
            scratch_shapes=[
                pltpu.VMEM(weights.shape, bf16),
                pltpu.SemaphoreType.DMA((3,)),
            ],
            compiler_params=pltpu.CompilerParams(vmem_limit_bytes=56 * 1024 * 1024),
            cost_estimate=pl.CostEstimate(
                flops=12 * count * width * weights.shape[-1],
                bytes_accessed=2 * weights.size,
                transcendentals=0,
            ),
            name="feed_forward",
        )(rows, cot, weights)

    return call


def make_backward(dp_size, high_bits):
    bit_count = dp_size.bit_length() - 1
    all_bits = tuple(range(bit_count))
    folded = tuple(k for k in reversed(all_bits) if k != CORE_BIT)
    low_order = tuple(range(1, SHARE_BIT)) + high_bits[::-1]
    qkv_order = (1, SHARE_BIT) + high_bits[::-1]
    out_order = (SHARE_BIT,) + high_bits[::-1] + (1,)
    step_count = len(low_order)

    def kernel(
        normed_two,
        cot_all,
        hid,
        grad_part,
        out_part,
        middle_in,
        tok,
        cot,
        out_full,
        qkv_full,
        normed,
        projected_in,
        probs,
        attended_in,
        cosines,
        sines,
        result,
        input_grad,
        qkv_sum,
        out_sum,
        mlp_sum,
        *rest,
    ):
        mlp_steps = [list(rest[m * step_count : (m + 1) * step_count]) for m in range(3)]
        (
            away_slots,
            mlp_core,
            mlp_last,
            recv_stage,
            qkv_core,
            out_core,
            quad_in,
            quad_step,
            quad_near,
            middle,
            grad_middle,
            grad_branch,
            norm_away,
            norm_in,
            stage,
            send_sem,
            recv_sem,
            local_sem,
        ) = rest[3 * step_count : 3 * step_count + 18]
        steps = list(rest[3 * step_count + 18 :])
        qkv_steps, out_steps = steps[: len(qkv_order)], steps[len(qkv_order) :]
        f32, bf16 = jnp.float32, jnp.bfloat16
        me = lax.axis_index("dp")
        side = lax.axis_index("tensor")
        bits = [(me // 2**k) % 2 for k in all_bits]
        others = [1 - b for b in bits]
        core, share = bits[CORE_BIT], bits[SHARE_BIT]
        core_other, share_other, side_other = others[CORE_BIT], others[SHARE_BIT], 1 - side
        own_rows, width = tok.shape
        half = width // 2
        rows = 2 * own_rows
        query_width = attended_in.shape[1]
        key_width = (projected_in.shape[1] - query_width) // 2
        block = width // dp_size

        partners = {k: {"dp": me + (1 - 2 * bits[k]) * 2**k} for k in all_bits}
        partners[None] = {"tensor": side_other}

        barrier = pltpu.get_barrier_semaphore()
        for k in all_bits + (None,):
            pl.semaphore_signal(barrier, inc=1, device_id=partners[k], device_id_type=MESH)
        pl.semaphore_wait(barrier, bit_count + 1)

        counter, local_counter = [0], [0]
        unsent = []

        class Push:
            def __init__(self, ends, k):
                self.ends, self.k, self.i = ends, k, counter[0]
                counter[0] += 1
                self.copy().start()
                unsent.append(self)

            def copy(self):
                src, dst = self.ends()
                return pltpu.make_async_remote_copy(
                    src_ref=src,
                    dst_ref=dst,
                    send_sem=send_sem.at[self.i],
                    recv_sem=recv_sem.at[self.i],
                    device_id=partners[self.k],
                    device_id_type=MESH,
                )

            def wait_recv(self):
                self.copy().wait_recv()

        def sent(push):
            push.copy().wait_send()
            unsent[:] = [other for other in unsent if other is not push]

        def keep(src, dst):
            i = local_counter[0]
            local_counter[0] += 1
            copy = pltpu.make_async_copy(src, dst, local_sem.at[i])
            copy.start()
            return copy

        def cells(lead):
            return [tuple((i >> (lead - 1 - j)) & 1 for j in range(lead)) for i in range(2**lead)]

        def strips(count, size, work):
            def step(r, _):
                work(pl.ds(pl.multiple_of(r * size, size), size))
                return 0

            lax.fori_loop(0, count // size, step, 0)

        def half_grad(left, right, which, give):
            lead = bit_count - 1
            kept = 0
            while block * 2**kept < 256 and kept < lead:
                kept += 1
            for i in range(2 ** (lead - kept)):
                parts = []
                for j in range(2**kept):
                    pair = (i * 2**kept + j) * 2 * block
                    if block % 128 == 0:
                        at = pl.multiple_of(pair + which * block, 128)
                        parts.append(left[:, pl.ds(at, block)])
                    else:
                        low = left[:, pair : pair + block].astype(f32)
                        high = left[:, pair + block : pair + 2 * block].astype(f32)
                        parts.append(jnp.where(which == 0, low, high).astype(bf16))
                columns = jnp.concatenate(parts, axis=1)
                product = dot(columns, right[...], ((0,), (0,)))
                index = tuple((i >> (lead - kept - 1 - j)) & 1 for j in range(lead - kept))
                give(index, product.reshape((2,) * kept + (block, product.shape[-1])))

        class Fold:
            def __init__(self, ref, lead, steps, order, staged):
                self.ref, self.lead = ref, lead
                self.steps = dict(zip(order, steps))
                self.order = list(order)
                self.staged = staged
                self.settled = {}
                self.copy = self.bit = None

            def place(self, cell):
                rest = iter(cell)
                return self.lead + tuple(
                    self.settled[k] if k in self.settled else next(rest) for k in folded
                )

            def open(self):
                return len(folded) - len(self.settled)

            def away(self, left, right, slot):
                def give(index, value):
                    slot[index] = value.astype(bf16)

                half_grad(left, right, core_other, give)
                core_ref = self.ref.at[self.lead] if self.lead else self.ref
                self.copy = Push(lambda: (slot, core_ref), CORE_BIT)
                return self.copy

            def near(self, left, right):
                self.copy.wait_recv()

                def give(index, value):
                    at = self.lead + index
                    self.ref[at] = (value + self.ref[at].astype(f32)).astype(bf16)

                half_grad(left, right, core, give)
                self.send()

            def send(self):
                self.bit = self.order.pop(0)
                self.settled[self.bit] = others[self.bit]
                place = self.place((pl.ds(0, 2),) * self.open())
                target = self.steps[self.bit]
                self.copy = Push(lambda: (self.ref.at[place], target), self.bit)
                self.settled[self.bit] = bits[self.bit]

            def step(self, last=None):
                self.copy.wait_recv()
                arrived, lead = self.steps[self.bit], ()
                if self.staged:
                    lead = (0,) * (len(folded) - 1 - self.open())
                    keep(arrived, recv_stage.at[lead] if lead else recv_stage).wait()
                    arrived = recv_stage
                for cell in cells(self.open()):
                    place = self.place(cell)

                    def work(at, cell=cell, place=place):
                        total = arrived[lead + cell + (at,)].astype(f32)
                        total = total + self.ref[place + (at,)].astype(f32)
                        if last is None:
                            self.ref[place + (at,)] = total.astype(bf16)
                        else:
                            last(cell, at, total)

                    strips(block, 16, work)
                if last is None:
                    self.send()

        class Quad:
            def __init__(self, source, slot):
                self.source, self.slot = source, slot
                self.left = Push(
                    lambda: (source.at[share_other, :, :, pl.ds(0, half)], quad_in.at[slot, 0]),
                    SHARE_BIT,
                )
                self.right = Push(
                    lambda: (source.at[:, side_other, :, pl.ds(half, half)], quad_in.at[slot, 1]),
                    None,
                )

            def load(self):
                self.loads = [
                    keep(self.source.at[share, :, :, pl.ds(0, half)], quad_near.at[0]),
                    keep(self.source.at[:, side, :, pl.ds(half, half)], quad_near.at[1]),
                ]

            def step(self):
                for copy in self.loads:
                    copy.wait()
                second = []
                for p, copy, there, k in (
                    (0, self.left, side_other, None),
                    (1, self.right, share_other, SHARE_BIT),
                ):
                    copy.wait_recv()
                    for q in range(2):

                        def work(at, p=p, q=q):
                            total = quad_in[self.slot, p, q, at, :].astype(f32)
                            total = total + quad_near[p, q, at, :].astype(f32)
                            quad_in[self.slot, p, q, at, :] = total.astype(bf16)

                        strips(own_rows, 16, work)

                    def ends(p=p, there=there):
                        return quad_in.at[self.slot, p, there], quad_step.at[self.slot, p]

                    second.append(Push(ends, k))
                self.left, self.right = second

            def finish(self):
                self.left.wait_recv()
                self.right.wait_recv()

            def value(self, at):
                halves = []
                for p, here in ((0, side), (1, share)):
                    halves.append(
                        quad_in[self.slot, p, here, at, :].astype(f32)
                        + quad_step[self.slot, p, at, :].astype(f32)
                    )
                return jnp.concatenate(halves, axis=-1)

        quad = Quad(grad_part, 0)
        quad.load()
        middle_load = keep(middle_in, middle)

        mlp_folds = [Fold(mlp_core, (m,), mlp_steps[m], low_order, True) for m in range(3)]
        qkv_fold = Fold(qkv_core, (), qkv_steps, qkv_order, False)
        out_fold = Fold(out_core, (), out_steps, out_order, False)
        mlp_copies = []
        stage_copies = [None, None]
        stage_count = [0]

        def to_output(fill, dst):
            i = stage_count[0] % 2
            stage_count[0] += 1
            if stage_copies[i] is not None:
                stage_copies[i].wait()
            fill(i)
            stage_copies[i] = keep(stage.at[i], dst)

        def mlp_share(m):
            def fill(i):
                def last(index, at, total):
                    is_own = share == index[0]

                    @pl.when(is_own)
                    def _():
                        stage[i, at, :] = total

                    @pl.when(jnp.logical_not(is_own))
                    def _():
                        mlp_last[m, 0, at, :] = total.astype(bf16)

                mlp_folds[m].step(last)

            to_output(fill, mlp_sum.at[m, share])
            mlp_copies.append(Push(lambda: (mlp_last.at[m, 0], mlp_last.at[m, 1]), SHARE_BIT))

        def mlp_finish(m):
            mlp_copies[m].wait_recv()

            def fill(i):
                def work(at):
                    stage[i, at, :] = mlp_last[m, 1, at, :].astype(f32)

                strips(block, 16, work)

            to_output(fill, mlp_sum.at[m, share_other])

        def first_phase(held_rows, held_cot, held_hid):
            loads = [
                keep(cot_all, held_cot),
                keep(hid.at[0], held_hid.at[0]),
                keep(normed_two, held_rows),
                keep(hid.at[1], held_hid.at[1]),
            ]
            loads[0].wait()
            loads[1].wait()
            first = mlp_folds[0].away(held_cot, held_hid.at[0], away_slots.at[0])
            loads[2].wait()
            loads[3].wait()
            second = mlp_folds[1].away(held_rows, held_hid.at[1], away_slots.at[1])
            mlp_folds[0].near(held_cot, held_hid.at[0])
            load = keep(hid.at[2], held_hid.at[0])
            sent(first)
            load.wait()
            third = mlp_folds[2].away(held_rows, held_hid.at[0], away_slots.at[0])
            mlp_folds[1].near(held_rows, held_hid.at[1])
            quad.step()
            mlp_folds[2].near(held_rows, held_hid.at[0])
            sent(second)
            sent(third)

        pl.run_scoped(
            first_phase,
            pltpu.VMEM(normed_two.shape, bf16),
            pltpu.VMEM(cot_all.shape, bf16),
            pltpu.VMEM((2,) + hid.shape[1:], bf16),
        )

        def second_phase(
            weights, held_normed, held_probs, projected, attended, grad_att, grad_qkv, acc
        ):
            loads = [keep(out_full, weights.at[(slice(None),) * (bit_count + 1) + (pl.ds(0, query_width),)])]
            loads.append(keep(probs.at[pl.ds(0, HEADS_PER_KV)], held_probs))
            loads.append(keep(normed, held_normed))
            loads.append(keep(projected_in, projected))
            loads.append(keep(attended_in, attended))
            middle_load.wait()
            quad.finish()

            def middle_rows(at):
                x = middle[at, :]
                inverse = rms(x)
                total = cot[at, :].astype(f32) + rms_grad(x, inverse, quad.value(at))
                grad_middle[at, :] = total
                grad_branch[side, at, :] = total.astype(bf16)

            strips(own_rows, 16, middle_rows)
            branch = Push(lambda: (grad_branch.at[side], grad_branch.at[side]), None)
            out_quad = Quad(out_part, 1)
            out_quad.load()
            mlp_folds[0].step()
            for copy in loads:
                copy.wait()
            branch.wait_recv()

            branch_all = grad_branch[...].reshape(rows, width)
            lead_all = (slice(None),) * (bit_count + 1)
            for low in range(0, query_width, 256):
                block_of = weights[lead_all + (slice(low, low + 256),)].reshape(width, 256)
                grad_att[:, low : low + 256] = jnp.dot(
                    branch_all, block_of, preferred_element_type=f32
                ).astype(bf16)
            qkv_load = keep(qkv_full, weights)
            out_slot = away_slots.at[(1,) + (slice(None),) * bit_count + (pl.ds(0, query_width),)]
            branch_flat = BranchView()
            out_away = out_fold.away(branch_flat, attended, out_slot)
            mlp_folds[1].step()
            out_fold.near(branch_flat, attended)

            pair_lanes = lax.broadcasted_iota(jnp.int32, (rows, 2 * HEAD_SIZE), 1)
            keys32 = projected[:, query_width : query_width + key_width].astype(f32)
            values32 = projected[:, query_width + key_width :].astype(f32)
            lanes = lax.broadcasted_iota(jnp.int32, (rows, key_width), 1)
            first_half = lanes % HEAD_SIZE < HEAD_SIZE // 2

            def padded(a, head, place):
                moved = a if head == place else pltpu.roll(a, HEAD_SIZE, 1)
                inside = pair_lanes < HEAD_SIZE if place == 0 else pair_lanes >= HEAD_SIZE
                return jnp.where(inside, moved, 0.0).astype(bf16)

            def unrotate(a):
                forward = pltpu.roll(a, key_width - HEAD_SIZE // 2, 1)
                back = pltpu.roll(a, HEAD_SIZE // 2, 1)
                return a * cosines[...] - jnp.where(first_half, forward, back) * sines[...]

            heads = key_width // HEAD_SIZE
            pairs = HEADS_PER_KV // 2
            tile_rows = 128
            lane_tile = lax.broadcasted_iota(jnp.int32, (tile_rows, 2 * HEAD_SIZE), 1)
            totals = []
            for head in range(heads):
                keys_at = [padded(keys32, head, p) for p in range(2)]
                values_at = [padded(values32, head, p) for p in range(2)]
                acc[...] = jnp.zeros_like(acc)

                def head_pair(i, _):
                    columns = pl.ds(pl.multiple_of((head * pairs + i) * 128, 128), 128)
                    for low in range(0, rows, tile_rows):
                        high = low + tile_rows
                        query = projected[low:high, columns].astype(f32)
                        grad_out = grad_att[low:high, columns]
                        grad_out32 = grad_out.astype(f32)
                        grad_query = None
                        for p in range(2):
                            inside = (
                                lane_tile < HEAD_SIZE if p == 0 else lane_tile >= HEAD_SIZE
                            )
                            prob = held_probs[2 * i + p, low:high, :high]
                            grad_prob = dot(grad_out, values_at[p][:high], ((1,), (1,)))
                            prob32 = prob.astype(f32)
                            centre = jnp.sum(prob32 * grad_prob, axis=-1, keepdims=True)
                            grad_score = (prob32 * (grad_prob - centre)).astype(bf16)
                            part = jnp.dot(
                                grad_score, keys_at[p][:high], preferred_element_type=f32
                            )
                            grad_query = part if grad_query is None else grad_query + part
                            only_query = jnp.where(inside, query, 0.0).astype(bf16)
                            only_grad = jnp.where(inside, grad_out32, 0.0).astype(bf16)
                            acc[0, :high, :] += dot(grad_score, only_query, ((0,), (0,)))
                            acc[1, :high, :] += dot(prob, only_grad, ((0,), (0,)))
                        acc[2, low:high, :] = grad_query * HEAD_SIZE**-0.5
                    grad_qkv[:, columns] = unrotate(acc[2]).astype(bf16)
                    return 0

                lax.fori_loop(0, pairs, head_pair, 0)
                totals.append([acc[j] + pltpu.roll(acc[j], HEAD_SIZE, 1) for j in range(2)])
                if head + 1 < heads:
                    copy = keep(
                        probs.at[pl.ds((head + 1) * HEADS_PER_KV, HEADS_PER_KV)], held_probs
                    )
                    out_quad.step()
                    mlp_folds[2].step()
                    copy.wait()
            lower = pair_lanes < HEAD_SIZE
            grad_keys = unrotate(jnp.where(lower, totals[0][0], totals[1][0]))
            grad_qkv[:, query_width : query_width + key_width] = grad_keys.astype(bf16)
            grad_values = jnp.where(lower, totals[0][1], totals[1][1])
            grad_qkv[:, query_width + key_width :] = grad_values.astype(bf16)

            qkv_width = query_width + 2 * key_width
            sent(out_away)
            qkv_slot = away_slots.at[(0,) + (slice(None),) * bit_count + (pl.ds(0, qkv_width),)]
            qkv_away = qkv_fold.away(held_normed, grad_qkv, qkv_slot)
            qkv_load.wait()
            tiles = spread(weights, bit_count, 512)

            def norm_part(which, give):
                at = pl.ds(pl.multiple_of(which * own_rows, 64), own_rows)
                chosen = grad_qkv[at, :]
                for i, (index, count) in enumerate(tiles):
                    block_of = weights[index].reshape(count, qkv_width)
                    give(slice(i * count, (i + 1) * count), dot(chosen, block_of, ((1,), (1,))))

            def give_away(to, value):
                norm_away[:, to] = value.astype(bf16)

            def give_near(to, value):
                middle[:, to] = value

            norm_part(side_other, give_away)
            norm_copy = Push(lambda: (norm_away, norm_in), None)
            qkv_fold.near(held_normed, grad_qkv)
            out_fold.step()
            out_quad.finish()

            def result_rows(at):
                result[at, :] = (middle[at, :] + out_quad.value(at)).astype(bf16)

            strips(own_rows, 16, result_rows)
            norm_part(side, give_near)
            norm_copy.wait_recv()

            def input_rows(at):
                x = tok[at, :].astype(f32)
                scaled = middle[at, :] + norm_in[at, :].astype(f32)
                total = grad_middle[at, :] + rms_grad(x, rms(x), scaled)
                input_grad[at, :] = total.astype(bf16)

            strips(own_rows, 16, input_rows)
            sent(qkv_away)

        class BranchView:
            def __getitem__(self, index):
                return grad_branch[(slice(None), slice(None), index[1])].reshape(rows, -1)

        pl.run_scoped(
            second_phase,
            pltpu.VMEM(qkv_full.shape, bf16),
            pltpu.VMEM(normed.shape, bf16),
            pltpu.VMEM((HEADS_PER_KV,) + probs.shape[1:], bf16),
            pltpu.VMEM(projected_in.shape, bf16),
            pltpu.VMEM(attended_in.shape, bf16),
            pltpu.VMEM(attended_in.shape, bf16),
            pltpu.VMEM(projected_in.shape, bf16),
            pltpu.VMEM((3, rows, 2 * HEAD_SIZE), f32),
        )

        def into(ref):
            def last(index, at, total):
                ref[at, :] = total

            return last

        for fold in mlp_folds:
            while len(fold.order) > 0:
                fold.step()
        for m in range(3):
            mlp_share(m)
        for fold, ref in ((out_fold, out_sum), (qkv_fold, qkv_sum)):
            while len(fold.order) > 0:
                fold.step()
            fold.step(into(ref))
        for m in range(3):
            mlp_finish(m)
        for copy in stage_copies:
            copy.wait()
        for copy in list(unsent):
            sent(copy)

    def call(
        normed_two,
        cot_all,
        hid,
        grad_part,
        out_part,
        middle,
        tok,
        cot,
        out_full,
        qkv_full,
        normed,
        projected,
        probs,
        attended,
        cosines,
        sines,
    ):
        bf16, f32 = jnp.bfloat16, jnp.float32
        own_rows, width = tok.shape
        half = width // 2
        block, qkv_width = qkv_full.shape[-2:]
        query_width = out_full.shape[-1]
        mlp_width = hid.shape[-1]
        shape = jax.ShapeDtypeStruct
        whole = pl.BlockSpec(memory_space=pltpu.VMEM)
        away = pl.BlockSpec(memory_space=pl.ANY)

        def twos(count):
            return (2,) * count

        slots = [
            shape(twos(bit_count - 2 - i) + (block, mlp_width), bf16) for i in range(step_count)
        ] * 3

        def steps_of(order, columns):
            return [
                pltpu.VMEM(twos(bit_count - 2 - i) + (block, columns), bf16)
                for i in range(len(order))
            ]

        def at_core(columns):
            return twos(bit_count - 1) + (block, columns)

        count = 3 * (step_count + 2) + 2 * bit_count + 12
        outs = pl.pallas_call(
            kernel,
            out_shape=[
                shape((own_rows, width), bf16),
                shape((own_rows, width), bf16),
                shape((block, qkv_width), f32),
                shape((block, query_width), f32),
                shape((3, 2, block, mlp_width), f32),
            ]
            + slots,
            in_specs=[away] * 6 + [whole] * 2 + [away] * 6 + [whole] * 2,
            out_specs=[whole] * 4 + [away] * (1 + len(slots)),
            scratch_shapes=[
                pltpu.VMEM((2,) + at_core(mlp_width), bf16),
                pltpu.VMEM((3,) + at_core(mlp_width), bf16),
                pltpu.VMEM((3, 2, block, mlp_width), bf16),
                pltpu.VMEM(twos(bit_count - 2) + (block, mlp_width), bf16),
                pltpu.VMEM(at_core(qkv_width), bf16),
                pltpu.VMEM(at_core(query_width), bf16),
                pltpu.VMEM((2, 2, 2, own_rows, half), bf16),
                pltpu.VMEM((2, 2, own_rows, half), bf16),
                pltpu.VMEM((2, 2, own_rows, half), bf16),
                pltpu.VMEM((own_rows, width), f32),
                pltpu.VMEM((own_rows, width), f32),
                pltpu.VMEM((2, own_rows, width), bf16),
                pltpu.VMEM((own_rows, width), bf16),
                pltpu.VMEM((own_rows, width), bf16),
                pltpu.VMEM((2, block, mlp_width), f32),
                pltpu.SemaphoreType.DMA((count,)),
                pltpu.SemaphoreType.DMA((count,)),
                pltpu.SemaphoreType.DMA((3 * step_count + 32,)),
            ]
            + steps_of(qkv_order, qkv_width)
            + steps_of(out_order, query_width),
            compiler_params=pltpu.CompilerParams(
                collective_id=2, has_side_effects=True, vmem_limit_bytes=62 * 1024 * 1024
            ),
            name="backward",
        )(
            normed_two,
            cot_all,
            hid,
            grad_part,
            out_part,
            middle,
            tok,
            cot,
            out_full,
            qkv_full,
            normed,
            projected,
            probs,
            attended,
            cosines,
            sines,
        )
        return outs[:5]

    return call


def make_body(dp_size):
    bit_count = dp_size.bit_length() - 1
    high_bits = tuple(range(bit_count - 1, SHARE_BIT, -1))

    def body(
        tokens,
        attn_gain,
        w_query,
        keyvalue_weight,
        w_out,
        mlp_gain,
        w_gateup,
        w_down,
        segment_ids,
        positions,
        cotangent,
    ):
        f32, bf16 = jnp.float32, jnp.bfloat16
        side = lax.axis_index("tensor")
        own_rows, width = tokens.shape
        group_rows = segment_ids.shape[0]
        block = width // dp_size

        def part(a, axis, at):
            return lax.dynamic_index_in_dim(a, at, axis, keepdims=False)

        gain_one = attn_gain.astype(f32)[:, None]
        gain_two = mlp_gain.astype(f32)[:, None]
        key_value = jnp.concatenate([keyvalue_weight[0], keyvalue_weight[1]], axis=1)
        qkv_shard = jnp.concatenate([w_query, key_value], axis=1)
        query_width, key_width = w_query.shape[1], keyvalue_weight.shape[2]

        def scaled(shard, gain):
            return (shard.astype(f32) * gain).astype(bf16)

        cosine_table, sine_table = rotary_tables(positions, HEAD_SIZE)
        sine_table = jnp.where(jnp.arange(HEAD_SIZE) < HEAD_SIZE // 2, -sine_table, sine_table)
        cosine_table = jnp.concatenate([cosine_table, cosine_table], axis=1)
        sine_table = jnp.concatenate([sine_table, sine_table], axis=1)
        order = jnp.arange(group_rows)
        allowed = (segment_ids[:, None] == segment_ids[None, :]) & (
            order[:, None] >= order[None, :]
        )
        mlp_shard = jnp.stack([w_down.T, scaled(w_gateup[0], gain_two), scaled(w_gateup[1], gain_two)])
        mlp_shard = jnp.moveaxis(mlp_shard.reshape(3, block, 2, -1), 2, 1)
        (
            qkv_full,
            out_full,
            mlp_full,
            normed,
            projected,
            probs,
            attended,
            middle,
            normed_two,
            grad_all,
        ) = make_forward(dp_size, high_bits)(
            tokens,
            cotangent,
            scaled(qkv_shard, gain_one),
            w_out.T,
            mlp_shard,
            cosine_table,
            sine_table,
            jnp.where(allowed, 0.0, -1e30).astype(f32),
        )
        normed_two = normed_two.reshape(4 * own_rows, width)
        grad_all = grad_all.reshape(4 * own_rows, width)
        hid, grad_part, out_part = make_mlp(bit_count)(normed_two, grad_all, mlp_full)
        quad_shape = (2, 2, own_rows, width)
        result, input_grad, qkv_sum, out_sum, mlp_sum = make_backward(dp_size, high_bits)(
            normed_two,
            grad_all,
            hid,
            grad_part.reshape(quad_shape),
            out_part.reshape(quad_shape),
            middle,
            tokens,
            cotangent,
            out_full,
            qkv_full,
            normed,
            projected,
            probs,
            attended,
            cosine_table,
            sine_table,
        )
        down_sum, gate_sum, up_sum = jnp.moveaxis(mlp_sum, 1, 2).reshape(3, block, -1)

        def gain_grad(weights, sums):
            rows = sum(jnp.sum(w.astype(f32) * s, axis=1) for w, s in zip(weights, sums))
            halves = rows.reshape(2, -1)
            return part(halves, 0, side) + lax.ppermute(
                part(halves, 0, 1 - side), "tensor", [(0, 1), (1, 0)]
            )

        attn_gain_grad = gain_grad([qkv_shard], [qkv_sum])
        mlp_gain_grad = gain_grad([w_gateup[0], w_gateup[1]], [gate_sum, up_sum])
        qkv_grad = qkv_sum * gain_one
        query_grad = qkv_grad[:, :query_width]
        keyval_grad = jnp.stack(
            [
                qkv_grad[:, query_width : query_width + key_width],
                qkv_grad[:, query_width + key_width :],
            ]
        )
        gateup_grad = jnp.stack([gate_sum * gain_two, up_sum * gain_two])
        return (
            result,
            input_grad,
            attn_gain_grad,
            query_grad,
            keyval_grad,
            out_sum.T,
            mlp_gain_grad,
            gateup_grad,
            down_sum.T,
        )

    return body


def solution(mesh):
    return jax.shard_map(
        make_body(mesh.shape["dp"]),
        mesh=mesh,
        in_specs=(
            P(("dp", "tensor"), None),
            P("dp"),
            P("dp", "tensor"),
            P(None, "dp", "tensor"),
            P("tensor", "dp"),
            P("dp"),
            P(None, "dp", "tensor"),
            P("tensor", "dp"),
            P("dp"),
            P("dp"),
            P(("dp", "tensor"), None),
        ),
        out_specs=(
            P(("dp", "tensor"), None),
            P(("dp", "tensor"), None),
            P(("dp", "tensor")),
            P("dp", "tensor"),
            P(None, "dp", "tensor"),
            P("tensor", "dp"),
            P(("dp", "tensor")),
            P(None, "dp", "tensor"),
            P("tensor", "dp"),
        ),
        check_vma=False,
    )
```

```python
import math

import jax
import jax.numpy as jnp
from jax import lax
from jax.experimental import pallas as pl
from jax.experimental.pallas import tpu as pltpu
from jax.sharding import PartitionSpec as P

MESH = pl.DeviceIdType.MESH

QUERY_HEAD_COUNT = 32
KEYVALUE_HEADS = 4
HEAD_SIZE = 64
HEADS_PER_KV = QUERY_HEAD_COUNT // KEYVALUE_HEADS
norm_eps = 1e-05

CORE_BIT = 0
SHARE_BIT = 2


FORWARD_ORDER = (
    "q1", "u0", "W", "u2", "q0", "q1", "q0", "o", "t", "q1", "o", "u0", "q0", "u0", "u3", "c", "u3",
    "q0", "o", "u2", "c", "q1", "t", "q0", "N", "u4", "K", "q1", "u3", "u4", "Q0", "Q1", "u2", "A0",
    "A1", "u1", "A2", "Q2", "o", "u0", "A3", "Q3", "u1", "u5", "A4", "A5", "A6", "o", "u0", "u3",
    "A7", "OA", "u4", "b", "ON", "u3", "u5", "u1", "b", "M", "nl", "nr", "nl", "c", "nr", "u5",
    "u1", "u4", "u2", "u1", "u2", "u4", "DH", "nl", "u5", "nr", "G", "u5", "U", "E", "O",
)


def rotary_tables(places, width):
    freqs = jnp.exp(jnp.arange(0, width, 2).astype(jnp.float32) * (-math.log(10000.0) / width))
    turned = places.astype(jnp.float32)[:, None] * freqs[None, :]
    turned = jnp.concatenate([turned, turned], axis=-1)
    return (jnp.cos(turned), jnp.sin(turned))


def dot(left, right, contract):
    return lax.dot_general(left, right, (contract, ((), ())), preferred_element_type=jnp.float32)


def rms(rows):
    return lax.rsqrt(jnp.mean(rows * rows, axis=-1, keepdims=True) + norm_eps)


def rms_grad(rows, inverse, grad_scaled):
    inner = jnp.mean(grad_scaled * rows, axis=-1, keepdims=True)
    return inverse * grad_scaled - rows * (inverse * inverse * inverse) * inner


def spread(ref, lead, row_tile):
    sizes = ref.shape
    block = sizes[-2]
    kept = 0
    while block * 2**kept < row_tile and kept < lead:
        kept += 1
    out = []
    for i in range(2 ** (lead - kept)):
        index = tuple((i >> (lead - kept - 1 - j)) & 1 for j in range(lead - kept))
        out.append((index, (block * 2**kept)))
    return out


def make_forward(dp_size, high_bits):
    bit_count = dp_size.bit_length() - 1
    all_bits = tuple(range(bit_count))

    def kernel(
        tok,
        cot,
        qkv_shard,
        out_shard,
        mlp_shard,
        cosines,
        sines,
        bias,
        qkv_full,
        out_full,
        probs,
        normed,
        projected,
        attended,
        middle,
        normed_two,
        cot_all,
        hid,
        grad_part,
        out_part,
        qkv_held,
        out_held,
        mlp_held,
        tok_all,
        branch_away,
        branch_in,
        prob_stage,
        send_sem,
        recv_sem,
        local_sem,
    ):
        f32, bf16 = jnp.float32, jnp.bfloat16
        me = lax.axis_index("dp")
        side = lax.axis_index("tensor")
        bits = [(me // 2**k) % 2 for k in all_bits]
        share = bits[SHARE_BIT]
        own_rows, width = tok.shape
        half = width // 2
        group_rows = 2 * own_rows
        query_width = attended.shape[1]
        key_width = (projected.shape[1] - query_width) // 2
        tile = 2 * key_width
        hidden_width = hid.shape[-1]

        def partner(k):
            if k is None:
                return {"tensor": 1 - side}
            return {"dp": me + (1 - 2 * bits[k]) * 2**k}

        barrier = pltpu.get_barrier_semaphore()
        for k in all_bits + (None,):
            pl.semaphore_signal(barrier, inc=1, device_id=partner(k), device_id_type=MESH)
        pl.semaphore_wait(barrier, bit_count + 1)

        counter, local_counter = [0], [0]
        started = []

        def push(src, dst, k):
            i = counter[0]
            counter[0] += 1
            copy = pltpu.make_async_remote_copy(
                src_ref=src,
                dst_ref=dst,
                send_sem=send_sem.at[i],
                recv_sem=recv_sem.at[i],
                device_id=partner(k),
                device_id_type=MESH,
            )
            copy.start()
            started.append(copy)
            return copy

        def keep(src, dst):
            i = local_counter[0]
            local_counter[0] += 1
            copy = pltpu.make_async_copy(src, dst, local_sem.at[i])
            copy.start()
            return copy

        def held(ref, lead, gathered, columns):
            index = tuple(
                pl.ds(0, 2) if k in gathered else bits[k] for k in reversed(all_bits)
            )
            return ref.at[lead + index + (slice(None), columns)]

        class Chain:
            def __init__(self, src, ref, lead, order, columns):
                self.src, self.ref, self.lead, self.columns = src, ref, lead, columns
                self.order = list(order)
                self.gathered = set()
                self.copy = self.bit = self.own = None
                self.done = False

            def step(self):
                if self.done:
                    return
                if self.copy is None:
                    self.bit = self.order.pop(0)
                    view = self.src.at[:, self.columns]
                    place = held(self.ref, self.lead, (), self.columns)
                    self.copy = push(view, place, self.bit)
                    return
                self.copy.wait_recv()
                self.gathered.add(self.bit)
                if not self.order:
                    self.done = True
                    return
                if self.own is not None:
                    self.own.wait()
                    self.own = None
                self.bit = self.order.pop(0)
                view = held(self.ref, self.lead, self.gathered, self.columns)
                self.copy = push(view, view, self.bit)

            def finish(self):
                while not self.done:
                    self.step()

        class Shift:
            def __init__(self, *ends):
                self.ends = list(ends)
                self.copy = None
                self.done = False

            def step(self):
                if self.copy is not None:
                    self.copy.wait_recv()
                    self.copy = None
                if self.ends:
                    self.copy = push(*self.ends.pop(0)())
                else:
                    self.done = True

            def finish(self):
                while not self.done:
                    self.step()

        cut = (hidden_width // 2 + 127) // 128 * 128
        pieces = [pl.ds(0, cut), pl.ds(cut, hidden_width - cut)]
        early = tile + query_width // 2
        full_order = high_bits + (SHARE_BIT, 1, 0)
        steps = {}
        steps["q0"] = Chain(qkv_shard, qkv_held, (), full_order, pl.ds(0, early))
        steps["q1"] = Chain(
            qkv_shard, qkv_held, (), full_order, pl.ds(early, query_width + tile - early)
        )
        steps["o"] = Chain(out_shard, out_held, (), full_order, pl.ds(0, query_width))
        for m in range(3):
            for p in range(2):
                steps[f"u{2 * m + p}"] = Chain(
                    mlp_shard.at[m, 1 - share],
                    mlp_held,
                    (m,),
                    (SHARE_BIT,) + high_bits + (1, 0),
                    pieces[p],
                )
        own = pl.ds(0, half)
        far = pl.ds(half, half)
        steps["t"] = Shift(lambda: (tok, tok_all.at[side], None))
        steps["c"] = Shift(
            lambda: (cot, cot_all.at[share, side], SHARE_BIT),
            lambda: (cot_all.at[:, side], cot_all.at[:, side], None),
        )
        steps["b"] = Shift(lambda: (branch_away, branch_in, None))
        two = normed_two
        steps["nr"] = Shift(
            lambda: (two.at[share, side, :, far], two.at[share, side, :, far], SHARE_BIT),
            lambda: (two.at[:, side, :, far], two.at[:, side, :, far], None),
        )
        steps["nl"] = Shift(
            lambda: (two.at[share, side, :, own], two.at[share, side, :, own], None),
            lambda: (two.at[share, :, :, own], two.at[share, :, :, own], SHARE_BIT),
        )

        everything = slice(None)
        own_cot = keep(cot, cot_all.at[share, side])
        own_tok = keep(tok, tok_all.at[side])
        own_qkv = keep(qkv_shard, held(qkv_held, (), (), everything))
        own_out = keep(out_shard, held(out_held, (), (), everything))
        own_mlp = [
            keep(mlp_shard.at[m, share], held(mlp_held, (m,), (), everything)) for m in range(3)
        ]
        out_copies = []
        works = {}

        def start_all():
            for copy in [own_tok, own_qkv, own_out, own_cot] + own_mlp:
                copy.wait()

        works["W"] = start_all

        def norm():
            steps["t"].finish()

            def norm_rows(r, _):
                rows = pl.ds(pl.multiple_of(r * 16, 16), 16)
                for s in range(2):
                    x = tok_all[s, rows, :].astype(f32)
                    scaled = x * lax.rsqrt(jnp.mean(x * x, axis=-1, keepdims=True) + norm_eps)
                    normed[pl.ds(s * own_rows + r * 16, 16), :] = scaled.astype(bf16)
                return 0

            lax.fori_loop(0, own_rows // 16, norm_rows, 0)

        works["N"] = norm

        lanes = lax.broadcasted_iota(jnp.int32, (group_rows, tile), 1)
        first_half = lanes % HEAD_SIZE < HEAD_SIZE // 2
        lead = (slice(None),) * bit_count + (slice(None),)
        values = {}

        def rotate(a):
            cos2 = jnp.concatenate([cosines[...], cosines[...]], axis=1)
            sin2 = jnp.concatenate([sines[...], sines[...]], axis=1)
            forward = pltpu.roll(a, tile - HEAD_SIZE // 2, 1)
            back = pltpu.roll(a, HEAD_SIZE // 2, 1)
            return a * cos2 + jnp.where(first_half, forward, back) * sin2

        def project(columns):
            weights = qkv_held[lead + (columns,)].reshape(width, tile)
            return jnp.dot(normed[...], weights, preferred_element_type=f32)

        def keys_values():
            steps["q0"].finish()
            first = project(slice(0, tile))
            values["keys"] = rotate(first)[:, :key_width].astype(bf16)
            values["values"] = first[:, key_width:].astype(bf16)
            projected[:, :key_width] = values["keys"]
            projected[:, key_width:tile] = values["values"]

        def queries(i):
            def run():
                if i >= query_width // tile // 2:
                    steps["q1"].finish()
                    if not out_copies:
                        out_copies.append(keep(qkv_held, qkv_full))
                columns = slice(tile + i * tile, tile + (i + 1) * tile)
                rotated = rotate(project(columns)).astype(bf16)
                projected[:, columns] = rotated * jnp.asarray(HEAD_SIZE**-0.5, bf16)

            return run

        works["K"] = keys_values
        for i in range(query_width // tile):
            works[f"Q{i}"] = queries(i)

        rows_tile = 128
        pair_lanes = lax.broadcasted_iota(jnp.int32, (group_rows, 2 * HEAD_SIZE), 1)
        pairs = HEADS_PER_KV // 2
        prob_copies = {}

        def padded(a, head, place):
            moved = a if head == place else pltpu.roll(a, HEAD_SIZE, 1)
            inside = pair_lanes < HEAD_SIZE if place == 0 else pair_lanes >= HEAD_SIZE
            return jnp.where(inside, moved, 0.0).astype(bf16)

        def head_pair(n):
            def run():
                head = n // pairs
                if n % pairs == 0:
                    keys32 = values["keys"].astype(f32)
                    values32 = values["values"].astype(f32)
                    values["at"] = (
                        [padded(keys32, head, p) for p in range(2)],
                        [padded(values32, head, p) for p in range(2)],
                    )
                keys_at, values_at = values["at"]
                slot = n % 2
                if slot in prob_copies:
                    prob_copies[slot].wait()
                columns = slice(tile + n * 128, tile + (n + 1) * 128)
                places = [
                    (low, low + rows_tile, p)
                    for low in range(0, group_rows, rows_tile)
                    for p in range(2)
                ]
                scores = [
                    dot(projected[low:high, columns], keys_at[p][:high], ((1,), (1,)))
                    + bias[low:high, :high]
                    for low, high, p in places
                ]
                peaks = [jnp.max(a, axis=-1, keepdims=True) for a in scores]
                raised = [jnp.exp(a - b) for a, b in zip(scores, peaks)]
                inverses = [1.0 / jnp.sum(a, axis=-1, keepdims=True) for a in raised]
                shares = [(a * b).astype(bf16) for a, b in zip(raised, inverses)]
                for (low, high, p), a in zip(places, shares):
                    prob_stage[slot, p, low:high, :high] = a
                prob_copies[slot] = keep(prob_stage.at[slot], probs.at[pl.ds(2 * n, 2)])
                parts = [
                    jnp.dot(a, values_at[p][:high], preferred_element_type=f32)
                    for (low, high, p), a in zip(places, shares)
                ]
                for j in range(0, len(places), 2):
                    low, high, _ = places[j]
                    mixed = (parts[j] + parts[j + 1]).astype(bf16)
                    attended[low:high, n * 128 : (n + 1) * 128] = mixed

            return run

        for n in range(query_width // 128):
            works[f"A{n}"] = head_pair(n)

        tiles = spread(out_held, bit_count, 512)

        def branch_rows(which, give):
            rows = attended[pl.ds(pl.multiple_of(which * own_rows, 64), own_rows), :]
            for i, (index, count) in enumerate(tiles):
                weights = out_held[index].reshape(count, query_width)
                give(slice(i * count, (i + 1) * count), dot(rows, weights, ((1,), (1,))))

        def give_away(to, value):
            branch_away[:, to] = value.astype(bf16)

        def give_near(to, value):
            middle[:, to] = value

        def branch_first():
            steps["o"].finish()
            out_copies.append(keep(out_held, out_full))
            branch_rows(1 - side, give_away)

        works["OA"] = branch_first
        works["ON"] = lambda: branch_rows(side, give_near)

        def middle_all():
            steps["b"].finish()

            def middle_rows(r, _):
                rows = pl.ds(pl.multiple_of(r * 16, 16), 16)
                x = tok[rows, :].astype(f32) + middle[rows, :] + branch_in[rows, :].astype(f32)
                middle[rows, :] = x
                scaled = x * lax.rsqrt(jnp.mean(x * x, axis=-1, keepdims=True) + norm_eps)
                normed_two[share, side, rows, :] = scaled.astype(bf16)
                return 0

            lax.fori_loop(0, own_rows // 16, middle_rows, 0)

        works["M"] = middle_all

        spans = [
            (low, min(low + 512, end))
            for start, end in ((0, cut), (cut, hidden_width))
            for low in range(start, end, 512)
        ]
        blocks = [(a, b) for a in range(2) for b in range(2)]
        mlp_lead = (slice(None),) * (bit_count + 1)

        def mlp_product(m, rows_ref, quarter, low, high):
            weights = mlp_held[(m,) + mlp_lead + (slice(low, high),)].reshape(width, high - low)
            return jnp.dot(rows_ref[quarter], weights, preferred_element_type=f32)

        def rows_of(quarter):
            at = (2 * quarter[0] + quarter[1]) * own_rows
            return slice(at, at + own_rows)

        def mlp_ready(m, *others):
            for name in (f"u{2 * m}", f"u{2 * m + 1}") + others:
                steps[name].finish()

        def store_product(m, slot, rows_ref, *others):
            def run():
                mlp_ready(m, *others)
                for low, high in spans:
                    for quarter in blocks:
                        value = mlp_product(m, rows_ref, quarter, low, high)
                        hid[slot, rows_of(quarter), low:high] = value.astype(bf16)

            return run

        works["DH"] = store_product(0, 2, cot_all, "c")
        works["G"] = store_product(1, 0, normed_two, "nl", "nr")

        def up_all():
            mlp_ready(2)
            for low, high in spans:
                for quarter in blocks:
                    up = mlp_product(2, normed_two, quarter, low, high)
                    at = rows_of(quarter)
                    gate = hid[0, at, low:high].astype(f32)
                    grad_hidden = hid[2, at, low:high].astype(f32)
                    sig = jax.nn.sigmoid(gate)
                    silu = gate * sig
                    slope = sig + silu * (1.0 - sig)
                    hid[0, at, low:high] = (silu * up).astype(bf16)
                    hid[1, at, low:high] = (grad_hidden * up * slope).astype(bf16)
                    hid[2, at, low:high] = (grad_hidden * silu).astype(bf16)

        works["U"] = up_all
        mlp_tiles = spread(mlp_held.at[0], bit_count, 512)
        all_rows = 4 * own_rows
        tall = all_rows // 2

        def mlp_back(parts, target):
            def run():
                for i, (index, count) in enumerate(mlp_tiles):
                    to = slice(i * count, (i + 1) * count)
                    for r in range(2):
                        at = slice(r * tall, (r + 1) * tall)
                        total = None
                        for m, slot in parts:
                            weights = mlp_held[(m,) + index].reshape(count, hidden_width)
                            term = dot(hid[slot, at, :], weights, ((1,), (1,)))
                            total = term if total is None else total + term
                        target[at, to] = total.astype(bf16)

            return run

        works["E"] = mlp_back(((1, 1), (2, 2)), grad_part)
        works["O"] = mlp_back(((0, 0),), out_part)

        for name in FORWARD_ORDER:
            if name in works:
                works[name]()
            else:
                steps[name].step()
        for name in steps:
            steps[name].finish()
        for copy in out_copies + list(prob_copies.values()):
            copy.wait()
        for copy in started:
            copy.wait_send()

    def call(tok, cot, qkv_shard, out_shard, mlp_shard, cosines, sines, bias):
        bf16, f32 = jnp.bfloat16, jnp.float32
        own_rows, width = tok.shape
        block, qkv_width = qkv_shard.shape
        query_width = out_shard.shape[1]
        mlp_width = mlp_shard.shape[-1]
        rows = 2 * own_rows
        twos = (2,) * bit_count
        heads = query_width // HEAD_SIZE
        whole = pl.BlockSpec(memory_space=pltpu.VMEM)
        away = pl.BlockSpec(memory_space=pl.ANY)
        count = 10 * (bit_count + 1) + 16
        shape = jax.ShapeDtypeStruct
        return pl.pallas_call(
            kernel,
            out_shape=[
                shape(twos + (block, qkv_width), bf16),
                shape(twos + (block, query_width), bf16),
                shape((heads, rows, rows), bf16),
                shape((rows, width), bf16),
                shape((rows, qkv_width), bf16),
                shape((rows, query_width), bf16),
                shape((own_rows, width), f32),
                shape((2, 2, own_rows, width), bf16),
                shape((2, 2, own_rows, width), bf16),
                shape((3, 2 * rows, mlp_width), bf16),
                shape((2 * rows, width), bf16),
                shape((2 * rows, width), bf16),
            ],
            in_specs=[whole, away, away, away, away, whole, whole, whole],
            out_specs=[away] * 3 + [whole] * 9,
            scratch_shapes=[
                pltpu.VMEM(twos + (block, qkv_width), bf16),
                pltpu.VMEM(twos + (block, query_width), bf16),
                pltpu.VMEM((3,) + twos + (block, mlp_width), bf16),
                pltpu.VMEM((2, own_rows, width), bf16),
                pltpu.VMEM((own_rows, width), bf16),
                pltpu.VMEM((own_rows, width), bf16),
                pltpu.VMEM((2, 2, rows, rows), bf16),
                pltpu.SemaphoreType.DMA((count,)),
                pltpu.SemaphoreType.DMA((count,)),
                pltpu.SemaphoreType.DMA((16 + heads,)),
            ],
            compiler_params=pltpu.CompilerParams(
                collective_id=1, has_side_effects=True, vmem_limit_bytes=62 * 1024 * 1024
            ),
            name="forward",
        )(tok, cot, qkv_shard, out_shard, mlp_shard, cosines, sines, bias)

    return call


def make_backward(dp_size, high_bits):
    bit_count = dp_size.bit_length() - 1
    all_bits = tuple(range(bit_count))
    folded = tuple(k for k in reversed(all_bits) if k != CORE_BIT)
    low_order = tuple(range(1, SHARE_BIT)) + high_bits[::-1]
    qkv_order = (1, SHARE_BIT) + high_bits[::-1]
    out_order = (SHARE_BIT,) + high_bits[::-1] + (1,)
    step_count = len(low_order)

    def kernel(
        normed_two,
        cot_all,
        hid,
        grad_part,
        out_part,
        middle_in,
        tok,
        cot,
        out_full,
        qkv_full,
        normed,
        projected_in,
        probs,
        attended_in,
        cosines,
        sines,
        result,
        input_grad,
        qkv_sum,
        out_sum,
        mlp_sum,
        *rest,
    ):
        mlp_steps = [list(rest[m * step_count : (m + 1) * step_count]) for m in range(3)]
        (
            away_slots,
            mlp_core,
            mlp_last,
            recv_stage,
            qkv_core,
            out_core,
            quad_in,
            quad_step,
            quad_near,
            middle,
            grad_middle,
            grad_branch,
            norm_away,
            norm_in,
            stage,
            send_sem,
            recv_sem,
            local_sem,
        ) = rest[3 * step_count : 3 * step_count + 18]
        steps = list(rest[3 * step_count + 18 :])
        qkv_steps, out_steps = steps[: len(qkv_order)], steps[len(qkv_order) :]
        f32, bf16 = jnp.float32, jnp.bfloat16
        me = lax.axis_index("dp")
        side = lax.axis_index("tensor")
        bits = [(me // 2**k) % 2 for k in all_bits]
        others = [1 - b for b in bits]
        core, share = bits[CORE_BIT], bits[SHARE_BIT]
        core_other, share_other, side_other = others[CORE_BIT], others[SHARE_BIT], 1 - side
        own_rows, width = tok.shape
        half = width // 2
        rows = 2 * own_rows
        query_width = attended_in.shape[1]
        key_width = (projected_in.shape[1] - query_width) // 2
        tile = 2 * key_width
        block = width // dp_size

        partners = {k: {"dp": me + (1 - 2 * bits[k]) * 2**k} for k in all_bits}
        partners[None] = {"tensor": side_other}

        barrier = pltpu.get_barrier_semaphore()
        for k in all_bits + (None,):
            pl.semaphore_signal(barrier, inc=1, device_id=partners[k], device_id_type=MESH)
        pl.semaphore_wait(barrier, bit_count + 1)

        counter, local_counter = [0], [0]
        unsent = []

        class Push:
            def __init__(self, ends, k):
                self.ends, self.k, self.i = ends, k, counter[0]
                counter[0] += 1
                self.copy().start()
                unsent.append(self)

            def copy(self):
                src, dst = self.ends()
                return pltpu.make_async_remote_copy(
                    src_ref=src,
                    dst_ref=dst,
                    send_sem=send_sem.at[self.i],
                    recv_sem=recv_sem.at[self.i],
                    device_id=partners[self.k],
                    device_id_type=MESH,
                )

            def wait_recv(self):
                self.copy().wait_recv()

        def sent(push):
            push.copy().wait_send()
            unsent[:] = [other for other in unsent if other is not push]

        def keep(src, dst):
            i = local_counter[0]
            local_counter[0] += 1
            copy = pltpu.make_async_copy(src, dst, local_sem.at[i])
            copy.start()
            return copy

        def cells(lead):
            return [tuple((i >> (lead - 1 - j)) & 1 for j in range(lead)) for i in range(2**lead)]

        def strips(count, size, work):
            def step(r, _):
                work(pl.ds(pl.multiple_of(r * size, size), size))
                return 0

            lax.fori_loop(0, count // size, step, 0)

        def half_grad(left, right, which, give):
            lead = bit_count - 1
            kept = 0
            while block * 2**kept < 256 and kept < lead:
                kept += 1
            for i in range(2 ** (lead - kept)):
                parts = []
                for j in range(2**kept):
                    pair = (i * 2**kept + j) * 2 * block
                    if block % 128 == 0:
                        at = pl.multiple_of(pair + which * block, 128)
                        parts.append(left[:, pl.ds(at, block)])
                    else:
                        low = left[:, pair : pair + block].astype(f32)
                        high = left[:, pair + block : pair + 2 * block].astype(f32)
                        parts.append(jnp.where(which == 0, low, high).astype(bf16))
                columns = jnp.concatenate(parts, axis=1)
                product = dot(columns, right[...], ((0,), (0,)))
                index = tuple((i >> (lead - kept - 1 - j)) & 1 for j in range(lead - kept))
                give(index, product.reshape((2,) * kept + (block, product.shape[-1])))

        class Product:
            def __init__(self, ref, lead):
                self.ref, self.lead, self.copy = ref, lead, None

            def away(self, left, right, slot):
                def give(index, value):
                    slot[index] = value.astype(bf16)

                half_grad(left, right, core_other, give)
                core_ref = self.ref.at[self.lead] if self.lead else self.ref
                self.copy = Push(lambda: (slot, core_ref), CORE_BIT)
                return self.copy

            def near(self, left, right):
                self.copy.wait_recv()

                def give(index, value):
                    at = self.lead + index
                    self.ref[at] = (value + self.ref[at].astype(f32)).astype(bf16)

                half_grad(left, right, core, give)

        class Fold:
            def __init__(self, ref, lead, start, size, steps, order, staged):
                self.ref, self.lead = ref, lead
                self.start, self.size = start, size
                self.steps = dict(zip(order, steps))
                self.order = list(order)
                self.staged = staged
                self.settled = {}
                self.copy = self.bit = None

            def place(self, cell):
                rest = iter(cell)
                return self.lead + tuple(
                    self.settled[k] if k in self.settled else next(rest) for k in folded
                )

            def open(self):
                return len(folded) - len(self.settled)

            def rows(self):
                return (pl.ds(self.start, self.size),)

            def send(self):
                self.bit = self.order.pop(0)
                self.settled[self.bit] = others[self.bit]
                twice = (pl.ds(0, 2),) * self.open()
                place = self.place(twice) + self.rows()
                target, there = self.steps[self.bit], twice + self.rows()
                self.copy = Push(lambda: (self.ref.at[place], target.at[there]), self.bit)
                self.settled[self.bit] = bits[self.bit]

            def add(self, last=None):
                self.copy.wait_recv()
                arrived, lead = self.steps[self.bit], ()
                if self.staged:
                    there = (pl.ds(0, 2),) * self.open() + self.rows()
                    lead = (0,) * (len(folded) - 1 - self.open())
                    keep(arrived.at[there], recv_stage.at[lead + there]).wait()
                    arrived = recv_stage
                for cell in cells(self.open()):
                    place = self.place(cell)

                    def work(r, _, cell=cell, place=place):
                        at = pl.ds(pl.multiple_of(self.start + r * 16, 16), 16)
                        new, old = arrived[lead + cell + (at,)], self.ref[place + (at,)]
                        if last is None:
                            self.ref[place + (at,)] = new + old
                        else:
                            last(cell, at, new.astype(f32) + old.astype(f32))
                        return 0

                    lax.fori_loop(0, self.size // 16, work, 0)

            def step(self):
                self.add()
                self.send()

        class Quad:
            def __init__(self, source, slot):
                self.source, self.slot = source, slot
                self.left = Push(
                    lambda: (source.at[share_other, :, :, pl.ds(0, half)], quad_in.at[slot, 0]),
                    SHARE_BIT,
                )
                self.right = Push(
                    lambda: (source.at[:, side_other, :, pl.ds(half, half)], quad_in.at[slot, 1]),
                    None,
                )

            def load(self):
                self.loads = [
                    keep(self.source.at[share, :, :, pl.ds(0, half)], quad_near.at[0]),
                    keep(self.source.at[:, side, :, pl.ds(half, half)], quad_near.at[1]),
                ]

            def step(self):
                for copy in self.loads:
                    copy.wait()
                second = []
                for p, copy, there, k in (
                    (0, self.left, side_other, None),
                    (1, self.right, share_other, SHARE_BIT),
                ):
                    copy.wait_recv()
                    for q in range(2):

                        def work(at, p=p, q=q):
                            total = quad_in[self.slot, p, q, at, :].astype(f32)
                            total = total + quad_near[p, q, at, :].astype(f32)
                            quad_in[self.slot, p, q, at, :] = total.astype(bf16)

                        strips(own_rows, 16, work)

                    def ends(p=p, there=there):
                        return quad_in.at[self.slot, p, there], quad_step.at[self.slot, p]

                    second.append(Push(ends, k))
                self.left, self.right = second

            def finish(self):
                self.left.wait_recv()
                self.right.wait_recv()

            def value(self, at):
                halves = []
                for p, here in ((0, side), (1, share)):
                    halves.append(
                        quad_in[self.slot, p, here, at, :].astype(f32)
                        + quad_step[self.slot, p, at, :].astype(f32)
                    )
                return jnp.concatenate(halves, axis=-1)

        quad = Quad(grad_part, 0)
        quad.load()
        middle_load = keep(middle_in, middle)

        part = block // 2
        mlp_products = [Product(mlp_core, (m,)) for m in range(3)]
        mlp_folds = [
            Fold(mlp_core, (m,), p * part, part, mlp_steps[m], low_order, True)
            for m in range(3)
            for p in range(2)
        ]
        qkv_product = Product(qkv_core, ())
        out_product = Product(out_core, ())
        qkv_folds = [Fold(qkv_core, (), p * part, part, qkv_steps, qkv_order, False) for p in range(2)]
        out_folds = [Fold(out_core, (), 0, block, out_steps, out_order, False)]
        mlp_copies = [None] * 6
        stage_copies = [None, None]
        stage_count = [0]

        def to_output(fill, rows_of, dst):
            i = stage_count[0] % 2
            stage_count[0] += 1
            if stage_copies[i] is not None:
                stage_copies[i]().wait()
            fill(i)
            n = local_counter[0]
            local_counter[0] += 1

            def copy():
                return pltpu.make_async_copy(stage.at[i, rows_of], dst(), local_sem.at[n])

            copy().start()
            stage_copies[i] = copy

        def mlp_share(u):
            m, fold = u // 2, mlp_folds[u]
            rows_of = pl.ds(fold.start, fold.size)

            def fill(i):
                def last(cell, at, total):
                    is_own = share == cell[0]

                    @pl.when(is_own)
                    def _():
                        stage[i, at, :] = total

                    @pl.when(jnp.logical_not(is_own))
                    def _():
                        mlp_last[m, 0, at, :] = total.astype(bf16)

                fold.add(last)

            to_output(fill, rows_of, lambda: mlp_sum.at[m, share, rows_of])
            mlp_copies[u] = Push(
                lambda: (mlp_last.at[m, 0, rows_of], mlp_last.at[m, 1, rows_of]), SHARE_BIT
            )

        def mlp_finish(u):
            m, fold = u // 2, mlp_folds[u]
            rows_of = pl.ds(fold.start, fold.size)
            mlp_copies[u].wait_recv()

            def fill(i):
                def work(r, _):
                    at = pl.ds(pl.multiple_of(fold.start + r * 16, 16), 16)
                    stage[i, at, :] = mlp_last[m, 1, at, :].astype(f32)
                    return 0

                lax.fori_loop(0, fold.size // 16, work, 0)

            to_output(fill, rows_of, lambda: mlp_sum.at[m, share_other, rows_of])

        def first_phase(held_rows, held_cot, held_hid):
            loads = [
                keep(cot_all, held_cot),
                keep(hid.at[0], held_hid.at[0]),
                keep(normed_two, held_rows),
                keep(hid.at[1], held_hid.at[1]),
            ]
            loads[0].wait()
            loads[1].wait()
            first = mlp_products[0].away(held_cot, held_hid.at[0], away_slots.at[0])
            loads[2].wait()
            loads[3].wait()
            second = mlp_products[1].away(held_rows, held_hid.at[1], away_slots.at[1])
            mlp_products[0].near(held_cot, held_hid.at[0])
            mlp_folds[0].send()
            mlp_folds[1].send()
            load = keep(hid.at[2], held_hid.at[0])
            sent(first)
            load.wait()
            third = mlp_products[2].away(held_rows, held_hid.at[0], away_slots.at[0])
            mlp_products[1].near(held_rows, held_hid.at[1])
            quad.step()
            mlp_products[2].near(held_rows, held_hid.at[0])
            mlp_folds[0].step()
            mlp_folds[2].send()
            sent(second)
            sent(third)

        pl.run_scoped(
            first_phase,
            pltpu.VMEM(normed_two.shape, bf16),
            pltpu.VMEM(cot_all.shape, bf16),
            pltpu.VMEM((2,) + hid.shape[1:], bf16),
        )

        def second_phase(
            weights, held_normed, held_probs, projected, attended, grad_att, grad_qkv, acc
        ):
            loads = [keep(out_full, weights.at[(slice(None),) * (bit_count + 1) + (pl.ds(0, query_width),)])]
            loads.append(keep(probs.at[pl.ds(0, HEADS_PER_KV)], held_probs))
            loads.append(keep(normed, held_normed))
            loads.append(keep(projected_in, projected))
            loads.append(keep(attended_in, attended))
            middle_load.wait()
            quad.finish()

            def middle_rows(at):
                x = middle[at, :]
                inverse = rms(x)
                total = cot[at, :].astype(f32) + rms_grad(x, inverse, quad.value(at))
                grad_middle[at, :] = total
                grad_branch[side, at, :] = total.astype(bf16)

            strips(own_rows, 16, middle_rows)
            branch = Push(lambda: (grad_branch.at[side], grad_branch.at[side]), None)
            out_quad = Quad(out_part, 1)
            out_quad.load()
            mlp_folds[1].step()
            mlp_folds[3].send()
            for copy in loads:
                copy.wait()
            branch.wait_recv()

            branch_all = grad_branch[...].reshape(rows, width)
            lead_all = (slice(None),) * (bit_count + 1)
            for low in range(0, query_width, 256):
                block_of = weights[lead_all + (slice(low, low + 256),)].reshape(width, 256)
                grad_att[:, low : low + 256] = jnp.dot(
                    branch_all, block_of, preferred_element_type=f32
                ).astype(bf16)
            qkv_load = keep(qkv_full, weights)
            out_slot = away_slots.at[(1,) + (slice(None),) * bit_count + (pl.ds(0, query_width),)]
            branch_flat = BranchView()
            out_away = out_product.away(branch_flat, attended, out_slot)
            mlp_folds[2].step()
            mlp_folds[4].send()
            out_product.near(branch_flat, attended)
            for fold in out_folds:
                fold.send()

            pair_lanes = lax.broadcasted_iota(jnp.int32, (rows, 2 * HEAD_SIZE), 1)
            keys32 = projected[:, :key_width].astype(f32)
            values32 = projected[:, key_width:tile].astype(f32)
            lanes = lax.broadcasted_iota(jnp.int32, (rows, key_width), 1)
            first_half = lanes % HEAD_SIZE < HEAD_SIZE // 2

            def padded(a, head, place):
                moved = a if head == place else pltpu.roll(a, HEAD_SIZE, 1)
                inside = pair_lanes < HEAD_SIZE if place == 0 else pair_lanes >= HEAD_SIZE
                return jnp.where(inside, moved, 0.0).astype(bf16)

            def unrotate(a):
                forward = pltpu.roll(a, key_width - HEAD_SIZE // 2, 1)
                back = pltpu.roll(a, HEAD_SIZE // 2, 1)
                return a * cosines[...] - jnp.where(first_half, forward, back) * sines[...]

            heads = key_width // HEAD_SIZE
            pairs = HEADS_PER_KV // 2
            tile_rows = 128
            lane_tile = lax.broadcasted_iota(jnp.int32, (tile_rows, 2 * HEAD_SIZE), 1)
            totals = []

            def go(fold, also=None):
                def run():
                    if len(fold.order) > 0:
                        fold.step()
                    else:
                        mlp_share(mlp_folds.index(fold))
                    if also is not None:
                        also.send()

                return run

            between = [
                go(mlp_folds[3], mlp_folds[5]),
                go(mlp_folds[0]),
                out_quad.step,
                go(mlp_folds[1]),
                go(mlp_folds[4]),
                out_folds[0].step,
                go(mlp_folds[2]),
                go(mlp_folds[5]),
            ]
            for head in range(heads):
                keys_at = [padded(keys32, head, p) for p in range(2)]
                values_at = [padded(values32, head, p) for p in range(2)]
                acc[...] = jnp.zeros_like(acc)

                def head_pair(i):
                    n = head * pairs + i
                    columns = slice(n * 128, (n + 1) * 128)
                    query_columns = slice(tile + n * 128, tile + (n + 1) * 128)
                    places = [
                        (low, low + tile_rows, p)
                        for low in range(0, rows, tile_rows)
                        for p in range(2)
                    ]
                    insides = [lane_tile < HEAD_SIZE, lane_tile >= HEAD_SIZE]
                    prob = [
                        held_probs[2 * i + p, low:high, :high] for low, high, p in places
                    ]
                    grad_prob = [
                        dot(grad_att[low:high, columns], values_at[p][:high], ((1,), (1,)))
                        for low, high, p in places
                    ]
                    prob32 = [a.astype(f32) for a in prob]
                    weighted = [a * b for a, b in zip(prob32, grad_prob)]
                    centre = [jnp.sum(a, axis=-1, keepdims=True) for a in weighted]
                    grad_score = [
                        (a - b * c).astype(bf16) for a, b, c in zip(weighted, prob32, centre)
                    ]
                    grad_query = [
                        jnp.dot(a, keys_at[p][:high], preferred_element_type=f32)
                        for a, (low, high, p) in zip(grad_score, places)
                    ]
                    for j, (low, high, p) in enumerate(places):
                        query = projected[low:high, query_columns].astype(f32)
                        only_query = jnp.where(insides[p], query, 0.0).astype(bf16)
                        out32 = grad_att[low:high, columns].astype(f32)
                        only_grad = jnp.where(insides[p], out32, 0.0).astype(bf16)
                        acc[0, :high, :] += dot(grad_score[j], only_query, ((0,), (0,)))
                        acc[1, :high, :] += dot(prob[j], only_grad, ((0,), (0,)))
                        if p == 1:
                            total = grad_query[j - 1] + grad_query[j]
                            acc[2, low:high, :] = total * HEAD_SIZE**-0.5
                    grad_qkv[:, query_columns] = unrotate(acc[2]).astype(bf16)

                for i in range(pairs):
                    head_pair(i)
                    between[head * pairs + i]()
                totals.append([acc[j] + pltpu.roll(acc[j], HEAD_SIZE, 1) for j in range(2)])
                if head + 1 < heads:
                    copy = keep(
                        probs.at[pl.ds((head + 1) * HEADS_PER_KV, HEADS_PER_KV)], held_probs
                    )
                    copy.wait()
            lower = pair_lanes < HEAD_SIZE
            grad_keys = unrotate(jnp.where(lower, totals[0][0], totals[1][0]))
            grad_qkv[:, :key_width] = grad_keys.astype(bf16)
            grad_values = jnp.where(lower, totals[0][1], totals[1][1])
            grad_qkv[:, key_width:tile] = grad_values.astype(bf16)

            qkv_width = query_width + 2 * key_width
            sent(out_away)
            qkv_slot = away_slots.at[(0,) + (slice(None),) * bit_count + (pl.ds(0, qkv_width),)]
            qkv_away = qkv_product.away(held_normed, grad_qkv, qkv_slot)
            qkv_load.wait()
            tiles = spread(weights, bit_count, 512)

            def norm_part(which, give):
                at = pl.ds(pl.multiple_of(which * own_rows, 64), own_rows)
                chosen = grad_qkv[at, :]
                for i, (index, count) in enumerate(tiles):
                    block_of = weights[index].reshape(count, qkv_width)
                    give(slice(i * count, (i + 1) * count), dot(chosen, block_of, ((1,), (1,))))

            def give_away(to, value):
                norm_away[:, to] = value.astype(bf16)

            def give_near(to, value):
                middle[:, to] = value

            norm_part(side_other, give_away)
            norm_copy = Push(lambda: (norm_away, norm_in), None)
            qkv_product.near(held_normed, grad_qkv)
            for fold in qkv_folds:
                fold.send()
            out_quad.finish()

            def result_rows(at):
                result[at, :] = (middle[at, :] + out_quad.value(at)).astype(bf16)

            strips(own_rows, 16, result_rows)
            norm_part(side, give_near)
            norm_copy.wait_recv()

            def input_rows(at):
                x = tok[at, :].astype(f32)
                scaled = middle[at, :] + norm_in[at, :].astype(f32)
                total = grad_middle[at, :] + rms_grad(x, rms(x), scaled)
                input_grad[at, :] = total.astype(bf16)

            strips(own_rows, 16, input_rows)
            sent(qkv_away)

        class BranchView:
            def __getitem__(self, index):
                return grad_branch[(slice(None), slice(None), index[1])].reshape(rows, -1)

        pl.run_scoped(
            second_phase,
            pltpu.VMEM(qkv_full.shape, bf16),
            pltpu.VMEM(normed.shape, bf16),
            pltpu.VMEM((HEADS_PER_KV,) + probs.shape[1:], bf16),
            pltpu.VMEM(projected_in.shape, bf16),
            pltpu.VMEM(attended_in.shape, bf16),
            pltpu.VMEM(attended_in.shape, bf16),
            pltpu.VMEM(projected_in.shape, bf16),
            pltpu.VMEM((3, rows, 2 * HEAD_SIZE), f32),
        )

        def into(ref):
            def last(index, at, total):
                ref[at, :] = total

            return last

        def drain(folds):
            while any(len(fold.order) > 0 for fold in folds):
                for fold in folds:
                    if len(fold.order) > 0:
                        fold.step()

        drain(mlp_folds)
        for u in range(6):
            if mlp_copies[u] is None:
                mlp_share(u)
        drain(qkv_folds)
        drain(out_folds)
        for u in range(6):
            mlp_finish(u)
        for fold in qkv_folds:
            fold.add(into(qkv_sum))
        for fold in out_folds:
            fold.add(into(out_sum))
        for copy in stage_copies:
            copy().wait()
        for copy in list(unsent):
            sent(copy)

    def call(
        normed_two,
        cot_all,
        hid,
        grad_part,
        out_part,
        middle,
        tok,
        cot,
        out_full,
        qkv_full,
        normed,
        projected,
        probs,
        attended,
        cosines,
        sines,
    ):
        bf16, f32 = jnp.bfloat16, jnp.float32
        own_rows, width = tok.shape
        half = width // 2
        block, qkv_width = qkv_full.shape[-2:]
        query_width = out_full.shape[-1]
        mlp_width = hid.shape[-1]
        shape = jax.ShapeDtypeStruct
        whole = pl.BlockSpec(memory_space=pltpu.VMEM)
        away = pl.BlockSpec(memory_space=pl.ANY)

        def twos(count):
            return (2,) * count

        slots = [
            shape(twos(bit_count - 2 - i) + (block, mlp_width), bf16) for i in range(step_count)
        ] * 3

        def steps_of(order, columns):
            return [
                pltpu.VMEM(twos(bit_count - 2 - i) + (block, columns), bf16)
                for i in range(len(order))
            ]

        def at_core(columns):
            return twos(bit_count - 1) + (block, columns)

        count = 6 * (step_count + 2) + 4 * bit_count + 16
        outs = pl.pallas_call(
            kernel,
            out_shape=[
                shape((own_rows, width), bf16),
                shape((own_rows, width), bf16),
                shape((block, qkv_width), f32),
                shape((block, query_width), f32),
                shape((3, 2, block, mlp_width), f32),
            ]
            + slots,
            in_specs=[away] * 6 + [whole] * 2 + [away] * 6 + [whole] * 2,
            out_specs=[whole] * 4 + [away] * (1 + len(slots)),
            scratch_shapes=[
                pltpu.VMEM((2,) + at_core(mlp_width), bf16),
                pltpu.VMEM((3,) + at_core(mlp_width), bf16),
                pltpu.VMEM((3, 2, block, mlp_width), bf16),
                pltpu.VMEM(twos(bit_count - 2) + (block, mlp_width), bf16),
                pltpu.VMEM(at_core(qkv_width), bf16),
                pltpu.VMEM(at_core(query_width), bf16),
                pltpu.VMEM((2, 2, 2, own_rows, half), bf16),
                pltpu.VMEM((2, 2, own_rows, half), bf16),
                pltpu.VMEM((2, 2, own_rows, half), bf16),
                pltpu.VMEM((own_rows, width), f32),
                pltpu.VMEM((own_rows, width), f32),
                pltpu.VMEM((2, own_rows, width), bf16),
                pltpu.VMEM((own_rows, width), bf16),
                pltpu.VMEM((own_rows, width), bf16),
                pltpu.VMEM((2, block, mlp_width), f32),
                pltpu.SemaphoreType.DMA((count,)),
                pltpu.SemaphoreType.DMA((count,)),
                pltpu.SemaphoreType.DMA((6 * step_count + 48,)),
            ]
            + steps_of(qkv_order, qkv_width)
            + steps_of(out_order, query_width),
            compiler_params=pltpu.CompilerParams(
                collective_id=2, has_side_effects=True, vmem_limit_bytes=62 * 1024 * 1024
            ),
            name="backward",
        )(
            normed_two,
            cot_all,
            hid,
            grad_part,
            out_part,
            middle,
            tok,
            cot,
            out_full,
            qkv_full,
            normed,
            projected,
            probs,
            attended,
            cosines,
            sines,
        )
        return outs[:5]

    return call


def make_body(dp_size):
    bit_count = dp_size.bit_length() - 1
    high_bits = tuple(range(bit_count - 1, SHARE_BIT, -1))

    def body(
        tokens,
        attn_gain,
        w_query,
        keyvalue_weight,
        w_out,
        mlp_gain,
        w_gateup,
        w_down,
        segment_ids,
        positions,
        cotangent,
    ):
        f32, bf16 = jnp.float32, jnp.bfloat16
        side = lax.axis_index("tensor")
        own_rows, width = tokens.shape
        group_rows = segment_ids.shape[0]
        block = width // dp_size

        def part(a, axis, at):
            return lax.dynamic_index_in_dim(a, at, axis, keepdims=False)

        gain_one = attn_gain.astype(f32)[:, None]
        gain_two = mlp_gain.astype(f32)[:, None]
        key_value = jnp.concatenate([keyvalue_weight[0], keyvalue_weight[1]], axis=1)
        qkv_shard = jnp.concatenate([key_value, w_query], axis=1)
        key_width = keyvalue_weight.shape[2]

        def scaled(shard, gain):
            return (shard.astype(f32) * gain).astype(bf16)

        cosine_table, sine_table = rotary_tables(positions, HEAD_SIZE)
        sine_table = jnp.where(jnp.arange(HEAD_SIZE) < HEAD_SIZE // 2, -sine_table, sine_table)
        cosine_table = jnp.concatenate([cosine_table, cosine_table], axis=1)
        sine_table = jnp.concatenate([sine_table, sine_table], axis=1)
        order = jnp.arange(group_rows)
        allowed = (segment_ids[:, None] == segment_ids[None, :]) & (
            order[:, None] >= order[None, :]
        )
        mlp_shard = jnp.stack([w_down.T, scaled(w_gateup[0], gain_two), scaled(w_gateup[1], gain_two)])
        mlp_shard = jnp.moveaxis(mlp_shard.reshape(3, block, 2, -1), 2, 1)
        (
            qkv_full,
            out_full,
            probs,
            normed,
            projected,
            attended,
            middle,
            normed_two,
            grad_all,
            hid,
            grad_part,
            out_part,
        ) = make_forward(dp_size, high_bits)(
            tokens,
            cotangent,
            scaled(qkv_shard, gain_one),
            w_out.T,
            mlp_shard,
            cosine_table,
            sine_table,
            jnp.where(allowed, 0.0, -1e30).astype(f32),
        )
        normed_two = normed_two.reshape(4 * own_rows, width)
        grad_all = grad_all.reshape(4 * own_rows, width)

        quad_shape = (2, 2, own_rows, width)
        result, input_grad, qkv_sum, out_sum, mlp_sum = make_backward(dp_size, high_bits)(
            normed_two,
            grad_all,
            hid,
            grad_part.reshape(quad_shape),
            out_part.reshape(quad_shape),
            middle,
            tokens,
            cotangent,
            out_full,
            qkv_full,
            normed,
            projected,
            probs,
            attended,
            cosine_table,
            sine_table,
        )
        down_sum, gate_sum, up_sum = jnp.moveaxis(mlp_sum, 1, 2).reshape(3, block, -1)

        def gain_grad(weights, sums):
            rows = sum(jnp.sum(w.astype(f32) * s, axis=1) for w, s in zip(weights, sums))
            halves = rows.reshape(2, -1)
            return part(halves, 0, side) + lax.ppermute(
                part(halves, 0, 1 - side), "tensor", [(0, 1), (1, 0)]
            )

        attn_gain_grad = gain_grad([qkv_shard], [qkv_sum])
        mlp_gain_grad = gain_grad([w_gateup[0], w_gateup[1]], [gate_sum, up_sum])
        qkv_grad = qkv_sum * gain_one
        query_grad = qkv_grad[:, 2 * key_width :]
        keyval_grad = jnp.stack(
            [qkv_grad[:, :key_width], qkv_grad[:, key_width : 2 * key_width]]
        )
        gateup_grad = jnp.stack([gate_sum * gain_two, up_sum * gain_two])
        return (
            result,
            input_grad,
            attn_gain_grad,
            query_grad,
            keyval_grad,
            out_sum.T,
            mlp_gain_grad,
            gateup_grad,
            down_sum.T,
        )

    return body


def solution(mesh):
    return jax.shard_map(
        make_body(mesh.shape["dp"]),
        mesh=mesh,
        in_specs=(
            P(("dp", "tensor"), None),
            P("dp"),
            P("dp", "tensor"),
            P(None, "dp", "tensor"),
            P("tensor", "dp"),
            P("dp"),
            P(None, "dp", "tensor"),
            P("tensor", "dp"),
            P("dp"),
            P("dp"),
            P(("dp", "tensor"), None),
        ),
        out_specs=(
            P(("dp", "tensor"), None),
            P(("dp", "tensor"), None),
            P(("dp", "tensor")),
            P("dp", "tensor"),
            P(None, "dp", "tensor"),
            P("tensor", "dp"),
            P(("dp", "tensor")),
            P(None, "dp", "tensor"),
            P("tensor", "dp"),
        ),
        check_vma=False,
    )
```

```python
import functools
import math

import jax
import jax.numpy as jnp
from jax import lax
from jax.experimental import pallas as pl
from jax.experimental.pallas import tpu as pltpu
from jax.sharding import PartitionSpec as P

MESH = pl.DeviceIdType.MESH

QUERY_HEAD_COUNT = 32
KEYVALUE_HEADS = 4
HEAD_SIZE = 64
HEADS_PER_KV = QUERY_HEAD_COUNT // KEYVALUE_HEADS
norm_eps = 1e-05

CORE_BIT = 0
SHARE_BIT = 2


FORWARD_ORDER = (
    "q1", "u1", "t", "q0", "W", "o", "q1", "q0", "t", "N", "q1", "o", "c", "q0", "q0", "q1", "u2",
    "o", "q0", "u3", "q1", "u0", "u1", "c", "u2", "K", "u1", "Q0", "Q1", "o", "A0", "Q2", "u5",
    "Q3", "A1", "o", "A2", "A3", "u0", "A4", "A5", "u2", "A6", "A7", "OA", "u3", "b", "u0", "u5",
    "ON", "u4", "b", "M", "nr", "u3", "nl", "u2", "u1", "nl", "u4", "u0", "nr", "u5", "u3", "u1",
    "u3", "c", "u0", "DHb", "u4", "DHa", "u5", "u5", "nr", "u2", "nl", "Gb", "Ub", "Eb", "Ob", "u4",
    "Ga", "u4", "Ua", "Oa", "Ea",
)

BACKWARD_ORDER = (
    "ol", "er", "W1", "K1", "el", "K1", "B1", "f2", "W0", "or", "K0", "K0", "B0", "W2", "er", "K2",
    "f3", "f2", "f0", "K2", "B2", "el", "ol", "f3", "el", "f5", "or", "er", "MR", "f4", "D", "f0",
    "f2", "f1", "f3", "f5", "D", "f0", "DA", "OA", "KO", "KO", "OB", "T0", "T1", "p1", "or", "T2",
    "f4", "T3", "T4", "T5", "ol", "p0", "T6", "T7", "QA", "KQ", "f5", "KQ", "f1", "QB", "p1", "NA",
    "q0", "p0", "N", "RR", "f1", "q1", "q0", "NB", "f0", "p0", "f2", "f5", "q1", "N", "IR", "p1",
    "q0", "f4", "q1", "p0", "f1", "f3", "q0", "p1", "f4", "q1",
)


def rotary_tables(places, width):
    freqs = jnp.exp(jnp.arange(0, width, 2).astype(jnp.float32) * (-math.log(10000.0) / width))
    turned = places.astype(jnp.float32)[:, None] * freqs[None, :]
    turned = jnp.concatenate([turned, turned], axis=-1)
    return (jnp.cos(turned), jnp.sin(turned))


def dot(left, right, contract):
    return lax.dot_general(left, right, (contract, ((), ())), preferred_element_type=jnp.float32)


def rms(rows):
    return lax.rsqrt(jnp.mean(rows * rows, axis=-1, keepdims=True) + norm_eps)


def rms_grad(rows, inverse, grad_scaled):
    inner = jnp.mean(grad_scaled * rows, axis=-1, keepdims=True)
    return inverse * grad_scaled - rows * (inverse * inverse * inverse) * inner


def spread(ref, lead, row_tile):
    sizes = ref.shape
    block = sizes[-2]
    kept = 0
    while block * 2**kept < row_tile and kept < lead:
        kept += 1
    out = []
    for i in range(2 ** (lead - kept)):
        index = tuple((i >> (lead - kept - 1 - j)) & 1 for j in range(lead - kept))
        out.append((index, (block * 2**kept)))
    return out


def make_forward(dp_size, high_bits):
    bit_count = dp_size.bit_length() - 1
    all_bits = tuple(range(bit_count))

    def kernel(
        tok,
        cot,
        w_query,
        key_value,
        w_out,
        w_gateup,
        w_down,
        gain_one,
        gain_two,
        cosines,
        sines,
        ids_row,
        ids_column,
        qkv_full,
        out_full,
        probs,
        normed,
        projected,
        attended,
        middle,
        normed_two,
        cot_all,
        hid,
        grad_part,
        out_part,
        qkv_held,
        out_held,
        mlp_held,
        tok_all,
        branch_away,
        branch_in,
        prob_stage,
        mlp_other,
        bias,
        send_sem,
        recv_sem,
        local_sem,
    ):
        f32, bf16 = jnp.float32, jnp.bfloat16
        me = lax.axis_index("dp")
        side = lax.axis_index("tensor")
        bits = [(me // 2**k) % 2 for k in all_bits]
        share = bits[SHARE_BIT]
        own_rows, width = tok.shape
        half = width // 2
        group_rows = 2 * own_rows
        query_width = attended.shape[1]
        key_width = (projected.shape[1] - query_width) // 2
        tile = 2 * key_width
        hidden_width = hid.shape[-1]

        def partner(k):
            if k is None:
                return {"tensor": 1 - side}
            return {"dp": me + (1 - 2 * bits[k]) * 2**k}

        own = tuple(bits[k] for k in reversed(all_bits))
        everything = (slice(None), slice(None))
        halves = [pl.multiple_of(h * hidden_width, 128) for h in (share, 1 - share)]
        raw = {}
        for m in range(2):
            for h in range(2):
                block_at = hid.at[m, pl.ds(h * w_query.shape[0], w_query.shape[0])]
                columns = pl.ds(halves[h], hidden_width)
                raw[m, h] = pltpu.make_async_copy(
                    w_gateup.at[m, :, columns], block_at, local_sem.at[2 * m + h]
                )
                raw[m, h].start()

        def scaled(a, gain):
            return (a.astype(f32) * gain[...]).astype(bf16)

        qkv_held[own + (slice(None), slice(0, key_width))] = scaled(key_value[0], gain_one)
        qkv_held[own + (slice(None), slice(key_width, tile))] = scaled(key_value[1], gain_one)
        qkv_held[own + (slice(None), slice(tile, tile + query_width))] = scaled(
            w_query[...], gain_one
        )
        out_held[own + everything] = w_out[...].T

        barrier = pltpu.get_barrier_semaphore()
        for k in all_bits + (None,):
            pl.semaphore_signal(barrier, inc=1, device_id=partner(k), device_id_type=MESH)
        pl.semaphore_wait(barrier, bit_count + 1)

        counter, local_counter = [0], [4]
        started = []

        def push(src, dst, k):
            i = counter[0]
            counter[0] += 1
            copy = pltpu.make_async_remote_copy(
                src_ref=src,
                dst_ref=dst,
                send_sem=send_sem.at[i],
                recv_sem=recv_sem.at[i],
                device_id=partner(k),
                device_id_type=MESH,
            )
            copy.start()
            started.append(copy)
            return copy

        def keep(src, dst):
            i = local_counter[0]
            local_counter[0] += 1
            copy = pltpu.make_async_copy(src, dst, local_sem.at[i])
            copy.start()
            return copy

        def held(ref, lead, gathered, columns):
            index = tuple(
                pl.ds(0, 2) if k in gathered else bits[k] for k in reversed(all_bits)
            )
            return ref.at[lead + index + (slice(None), columns)]

        class Chain:
            def __init__(self, src, ref, lead, order, columns):
                self.src, self.ref, self.lead, self.columns = src, ref, lead, columns
                self.order = list(order)
                self.gathered = set()
                self.copy = self.bit = None
                self.done = False

            def step(self):
                if self.done:
                    return
                if self.copy is None:
                    self.bit = self.order.pop(0)
                    place = held(self.ref, self.lead, (), self.columns)
                    view = place
                    if self.src is not None:
                        self.src[0]()
                        view = self.src[1].at[:, self.columns]
                    self.copy = push(view, place, self.bit)
                    return
                self.copy.wait_recv()
                self.gathered.add(self.bit)
                if not self.order:
                    self.done = True
                    return
                self.bit = self.order.pop(0)
                view = held(self.ref, self.lead, self.gathered, self.columns)
                self.copy = push(view, view, self.bit)

            def finish(self):
                while not self.done:
                    self.step()

        class Shift:
            def __init__(self, *ends):
                self.ends = list(ends)
                self.copy = None
                self.done = False

            def step(self):
                if self.copy is not None:
                    self.copy.wait_recv()
                    self.copy = None
                if self.ends:
                    self.copy = push(*self.ends.pop(0)())
                else:
                    self.done = True

            def finish(self):
                while not self.done:
                    self.step()

        cut = (hidden_width // 2 + 127) // 128 * 128
        pieces = [pl.ds(0, cut), pl.ds(cut, hidden_width - cut)]
        early = tile + query_width // 2
        full_order = high_bits + (SHARE_BIT, 1, 0)
        steps = {}
        prepared = set()

        def prepare(m):
            if m in prepared:
                return
            prepared.add(m)
            for h in range(2):
                if m == 0:
                    value = w_down[pl.ds(pl.multiple_of(halves[h], 128), hidden_width), :].T
                else:
                    raw[m - 1, h].wait()
                    rows = slice(h * w_query.shape[0], (h + 1) * w_query.shape[0])
                    value = scaled(hid[m - 1, rows, :], gain_two)
                if h == 0:
                    mlp_held[(m,) + own + everything] = value
                else:
                    mlp_other[m] = value

        steps["q0"] = Chain(None, qkv_held, (), full_order, pl.ds(0, early))
        steps["q1"] = Chain(
            None, qkv_held, (), full_order, pl.ds(early, query_width + tile - early)
        )
        steps["o"] = Chain(None, out_held, (), full_order, pl.ds(0, query_width))
        for m in range(3):
            for p in range(2):
                steps[f"u{2 * m + p}"] = Chain(
                    (functools.partial(prepare, m), mlp_other.at[m]),
                    mlp_held,
                    (m,),
                    (SHARE_BIT,) + high_bits + (1, 0),
                    pieces[p],
                )
        first = pl.ds(0, half)
        far = pl.ds(half, half)
        steps["t"] = Shift(lambda: (tok, tok_all.at[side], None))
        steps["c"] = Shift(
            lambda: (cot, cot_all.at[share, side], SHARE_BIT),
            lambda: (cot_all.at[:, side], cot_all.at[:, side], None),
        )
        steps["b"] = Shift(lambda: (branch_away, branch_in, None))
        two = normed_two
        steps["nr"] = Shift(
            lambda: (two.at[share, side, :, far], two.at[share, side, :, far], SHARE_BIT),
            lambda: (two.at[:, side, :, far], two.at[:, side, :, far], None),
        )
        steps["nl"] = Shift(
            lambda: (two.at[share, side, :, first], two.at[share, side, :, first], None),
            lambda: (two.at[share, :, :, first], two.at[share, :, :, first], SHARE_BIT),
        )

        own_cot = keep(cot, cot_all.at[share, side])
        own_tok = keep(tok, tok_all.at[side])
        out_copies = []
        works = {}

        def start_all():
            for copy in (own_tok, own_cot):
                copy.wait()
            for m in range(3):
                prepare(m)

        works["W"] = start_all

        def norm():
            steps["t"].finish()

            def norm_rows(r, _):
                rows = pl.ds(pl.multiple_of(r * 16, 16), 16)
                for s in range(2):
                    x = tok_all[s, rows, :].astype(f32)
                    scaled = x * lax.rsqrt(jnp.mean(x * x, axis=-1, keepdims=True) + norm_eps)
                    normed[pl.ds(s * own_rows + r * 16, 16), :] = scaled.astype(bf16)
                return 0

            lax.fori_loop(0, own_rows // 16, norm_rows, 0)

        works["N"] = norm

        lanes = lax.broadcasted_iota(jnp.int32, (group_rows, tile), 1)
        first_half = lanes % HEAD_SIZE < HEAD_SIZE // 2
        lead = (slice(None),) * bit_count + (slice(None),)
        values = {}

        def rotate(a):
            cos2 = jnp.concatenate([cosines[...], cosines[...]], axis=1)
            sin2 = jnp.concatenate([sines[...], sines[...]], axis=1)
            forward = pltpu.roll(a, tile - HEAD_SIZE // 2, 1)
            back = pltpu.roll(a, HEAD_SIZE // 2, 1)
            return a * cos2 + jnp.where(first_half, forward, back) * sin2

        def project(columns):
            weights = qkv_held[lead + (columns,)].reshape(width, tile)
            return jnp.dot(normed[...], weights, preferred_element_type=f32)

        def keys_values():
            steps["q0"].finish()
            order = [lax.broadcasted_iota(jnp.int32, bias.shape, axis) for axis in range(2)]
            allowed = (ids_column[...] == ids_row[...]) & (order[0] >= order[1])
            bias[...] = jnp.where(allowed, 0.0, -1e30)
            first = project(slice(0, tile))
            values["keys"] = rotate(first)[:, :key_width].astype(bf16)
            values["values"] = first[:, key_width:].astype(bf16)
            projected[:, :key_width] = values["keys"]
            projected[:, key_width:tile] = values["values"]

        def queries(i):
            def run():
                if i >= query_width // tile // 2:
                    steps["q1"].finish()
                    if not out_copies:
                        out_copies.append(keep(qkv_held, qkv_full))
                columns = slice(tile + i * tile, tile + (i + 1) * tile)
                rotated = rotate(project(columns)).astype(bf16)
                projected[:, columns] = rotated * jnp.asarray(HEAD_SIZE**-0.5, bf16)

            return run

        works["K"] = keys_values
        for i in range(query_width // tile):
            works[f"Q{i}"] = queries(i)

        rows_tile = 128
        pair_lanes = lax.broadcasted_iota(jnp.int32, (group_rows, 2 * HEAD_SIZE), 1)
        pairs = HEADS_PER_KV // 2
        prob_copies = {}

        def padded(a, head, place):
            moved = a if head == place else pltpu.roll(a, HEAD_SIZE, 1)
            inside = pair_lanes < HEAD_SIZE if place == 0 else pair_lanes >= HEAD_SIZE
            return jnp.where(inside, moved, 0.0).astype(bf16)

        def head_pair(n):
            def run():
                head = n // pairs
                if n % pairs == 0:
                    keys32 = values["keys"].astype(f32)
                    values32 = values["values"].astype(f32)
                    values["at"] = (
                        [padded(keys32, head, p) for p in range(2)],
                        [padded(values32, head, p) for p in range(2)],
                    )
                keys_at, values_at = values["at"]
                slot = n % 2
                if slot in prob_copies:
                    prob_copies[slot].wait()
                columns = slice(tile + n * 128, tile + (n + 1) * 128)
                places = [
                    (low, low + rows_tile, p)
                    for low in range(0, group_rows, rows_tile)
                    for p in range(2)
                ]
                scores = [
                    dot(projected[low:high, columns], keys_at[p][:high], ((1,), (1,)))
                    + bias[low:high, :high]
                    for low, high, p in places
                ]
                peaks = [jnp.max(a, axis=-1, keepdims=True) for a in scores]
                raised = [jnp.exp(a - b) for a, b in zip(scores, peaks)]
                inverses = [1.0 / jnp.sum(a, axis=-1, keepdims=True) for a in raised]
                shares = [(a * b).astype(bf16) for a, b in zip(raised, inverses)]
                for (low, high, p), a in zip(places, shares):
                    prob_stage[slot, p, low:high, :high] = a
                prob_copies[slot] = keep(prob_stage.at[slot], probs.at[pl.ds(2 * n, 2)])
                parts = [
                    jnp.dot(a, values_at[p][:high], preferred_element_type=f32)
                    for (low, high, p), a in zip(places, shares)
                ]
                for j in range(0, len(places), 2):
                    low, high, _ = places[j]
                    mixed = (parts[j] + parts[j + 1]).astype(bf16)
                    attended[low:high, n * 128 : (n + 1) * 128] = mixed

            return run

        for n in range(query_width // 128):
            works[f"A{n}"] = head_pair(n)

        tiles = spread(out_held, bit_count, 512)

        def branch_rows(which, give):
            rows = attended[pl.ds(pl.multiple_of(which * own_rows, 64), own_rows), :]
            for i, (index, count) in enumerate(tiles):
                weights = out_held[index].reshape(count, query_width)
                give(slice(i * count, (i + 1) * count), dot(rows, weights, ((1,), (1,))))

        def give_away(to, value):
            branch_away[:, to] = value.astype(bf16)

        def give_near(to, value):
            middle[:, to] = value

        def branch_first():
            steps["o"].finish()
            out_copies.append(keep(out_held, out_full))
            branch_rows(1 - side, give_away)

        works["OA"] = branch_first
        works["ON"] = lambda: branch_rows(side, give_near)

        def middle_all():
            steps["b"].finish()

            def middle_rows(r, _):
                rows = pl.ds(pl.multiple_of(r * 16, 16), 16)
                x = tok[rows, :].astype(f32) + middle[rows, :] + branch_in[rows, :].astype(f32)
                middle[rows, :] = x
                scaled = x * lax.rsqrt(jnp.mean(x * x, axis=-1, keepdims=True) + norm_eps)
                normed_two[share, side, rows, :] = scaled.astype(bf16)
                return 0

            lax.fori_loop(0, own_rows // 16, middle_rows, 0)

        works["M"] = middle_all

        bounds = [(0, cut), (cut, hidden_width)]

        def spans(p):
            start, end = bounds[p]
            return [(low, min(low + 512, end)) for low in range(start, end, 512)]

        mlp_lead = (slice(None),) * (bit_count + 1)

        def mlp_product(m, rows_ref, quarter, low, high):
            weights = mlp_held[(m,) + mlp_lead + (slice(low, high),)].reshape(width, high - low)
            return jnp.dot(
                rows_ref[quarter].reshape(group_rows, width), weights, preferred_element_type=f32
            )

        def rows_of(quarter):
            return slice(quarter * group_rows, (quarter + 1) * group_rows)

        def store_product(m, p, slot, rows_ref, *needed):
            def run():
                for name in (f"u{2 * m + p}",) + needed:
                    steps[name].finish()
                for low, high in spans(p):
                    for quarter in range(2):
                        value = mlp_product(m, rows_ref, quarter, low, high)
                        hid[slot, rows_of(quarter), low:high] = value.astype(bf16)

            return run

        def up_product(p):
            def run():
                steps[f"u{4 + p}"].finish()
                for low, high in spans(p):
                    for quarter in range(2):
                        up = mlp_product(2, normed_two, quarter, low, high)
                        at = rows_of(quarter)
                        gate = hid[0, at, low:high].astype(f32)
                        grad_hidden = hid[2, at, low:high].astype(f32)
                        sig = jax.nn.sigmoid(gate)
                        silu = gate * sig
                        slope = sig + silu * (1.0 - sig)
                        hid[0, at, low:high] = (silu * up).astype(bf16)
                        hid[1, at, low:high] = (grad_hidden * up * slope).astype(bf16)
                        hid[2, at, low:high] = (grad_hidden * silu).astype(bf16)

            return run

        mlp_tiles = spread(mlp_held.at[0], bit_count, 512)
        tall = 2 * own_rows
        opened = set()

        def mlp_back(p, parts, target):
            columns = slice(*bounds[p])
            count_of = bounds[p][1] - bounds[p][0]

            def run():
                again = id(target) in opened
                opened.add(id(target))
                for i, (index, count) in enumerate(mlp_tiles):
                    to = slice(i * count, (i + 1) * count)
                    inner = (slice(None),) * (bit_count + 1 - len(index)) + (columns,)
                    for r in range(2):
                        at = slice(r * tall, (r + 1) * tall)
                        total = target[at, to].astype(f32) if again else None
                        for m, slot in parts:
                            weights = mlp_held[(m,) + index + inner].reshape(count, count_of)
                            term = dot(hid[slot, at, columns], weights, ((1,), (1,)))
                            total = term if total is None else total + term
                        target[at, to] = total.astype(bf16)

            return run

        for p, suffix in enumerate("ab"):
            works["DH" + suffix] = store_product(0, p, 2, cot_all, "c")
            works["G" + suffix] = store_product(1, p, 0, normed_two, "nl", "nr")
            works["U" + suffix] = up_product(p)
            works["E" + suffix] = mlp_back(p, ((1, 1), (2, 2)), grad_part)
            works["O" + suffix] = mlp_back(p, ((0, 0),), out_part)

        for name in FORWARD_ORDER:
            if name in works:
                works[name]()
            else:
                steps[name].step()
        for name in steps:
            steps[name].finish()
        for copy in out_copies + list(prob_copies.values()):
            copy.wait()
        for copy in started:
            copy.wait_send()

    def call(
        tok,
        cot,
        w_query,
        key_value,
        w_out,
        w_gateup,
        w_down,
        gain_one,
        gain_two,
        cosines,
        sines,
        ids_row,
        ids_column,
    ):
        bf16, f32 = jnp.bfloat16, jnp.float32
        own_rows, width = tok.shape
        block, query_width = w_query.shape
        qkv_width = query_width + 2 * key_value.shape[2]
        mlp_width = w_gateup.shape[2] // 2
        rows = 2 * own_rows
        twos = (2,) * bit_count
        heads = query_width // HEAD_SIZE
        whole = pl.BlockSpec(memory_space=pltpu.VMEM)
        away = pl.BlockSpec(memory_space=pl.ANY)
        count = 10 * (bit_count + 1) + 16
        shape = jax.ShapeDtypeStruct
        return pl.pallas_call(
            kernel,
            out_shape=[
                shape(twos + (block, qkv_width), bf16),
                shape(twos + (block, query_width), bf16),
                shape((heads, rows, rows), bf16),
                shape((rows, width), bf16),
                shape((rows, qkv_width), bf16),
                shape((rows, query_width), bf16),
                shape((own_rows, width), f32),
                shape((2, 2, own_rows, width), bf16),
                shape((2, 2, own_rows, width), bf16),
                shape((3, 2 * rows, mlp_width), bf16),
                shape((2 * rows, width), bf16),
                shape((2 * rows, width), bf16),
            ],
            in_specs=[whole, away, whole, whole, whole, away] + [whole] * 7,
            out_specs=[away] * 3 + [whole] * 9,
            scratch_shapes=[
                pltpu.VMEM(twos + (block, qkv_width), bf16),
                pltpu.VMEM(twos + (block, query_width), bf16),
                pltpu.VMEM((3,) + twos + (block, mlp_width), bf16),
                pltpu.VMEM((2, own_rows, width), bf16),
                pltpu.VMEM((own_rows, width), bf16),
                pltpu.VMEM((own_rows, width), bf16),
                pltpu.VMEM((2, 2, rows, rows), bf16),
                pltpu.VMEM((3, block, mlp_width), bf16),
                pltpu.VMEM((rows, rows), f32),
                pltpu.SemaphoreType.DMA((count,)),
                pltpu.SemaphoreType.DMA((count,)),
                pltpu.SemaphoreType.DMA((16 + heads,)),
            ],
            compiler_params=pltpu.CompilerParams(
                collective_id=1, has_side_effects=True, vmem_limit_bytes=62 * 1024 * 1024
            ),
            name="forward",
        )(
            tok,
            cot,
            w_query,
            key_value,
            w_out,
            w_gateup,
            w_down,
            gain_one,
            gain_two,
            cosines,
            sines,
            ids_row,
            ids_column,
        )

    return call


def make_backward(dp_size, high_bits):
    bit_count = dp_size.bit_length() - 1
    all_bits = tuple(range(bit_count))
    folded = tuple(k for k in reversed(all_bits) if k != CORE_BIT)
    low_order = tuple(range(1, SHARE_BIT)) + high_bits[::-1]
    qkv_order = (1, SHARE_BIT) + high_bits[::-1]
    out_orders = ((1, SHARE_BIT) + high_bits[::-1], (SHARE_BIT,) + high_bits[::-1] + (1,))
    step_count = len(low_order)

    def kernel(
        normed_two,
        cot_all,
        hid,
        grad_part,
        out_part,
        middle_in,
        tok,
        cot,
        out_full,
        qkv_full,
        normed,
        projected_in,
        probs,
        attended_in,
        cosines,
        sines,
        w_query,
        key_value,
        w_gateup,
        gain_one,
        gain_two,
        result,
        input_grad,
        query_grad,
        keyval_grad,
        out_grad,
        gateup_grad,
        down_grad,
        gain_grads,
        *rest,
    ):
        mlp_steps = [list(rest[m * step_count : (m + 1) * step_count]) for m in range(3)]
        (
            away_slots,
            mlp_core,
            mlp_last,
            recv_stage,
            qkv_core,
            out_core,
            quad_in,
            quad_step,
            quad_near,
            middle,
            grad_middle,
            grad_branch,
            norm_away,
            norm_in,
            stage,
            down_held,
            out_sum,
            weight_stage,
            gain_sums,
            gain_in,
            send_sem,
            recv_sem,
            local_sem,
        ) = rest[3 * step_count : 3 * step_count + 23]
        steps = list(rest[3 * step_count + 23 :])
        qkv_steps, others_of = steps[: len(qkv_order)], steps[len(qkv_order) :]
        out_steps = (others_of, others_of)
        f32, bf16 = jnp.float32, jnp.bfloat16
        me = lax.axis_index("dp")
        side = lax.axis_index("tensor")
        bits = [(me // 2**k) % 2 for k in all_bits]
        others = [1 - b for b in bits]
        core, share = bits[CORE_BIT], bits[SHARE_BIT]
        core_other, share_other, side_other = others[CORE_BIT], others[SHARE_BIT], 1 - side
        own_rows, width = tok.shape
        half = width // 2
        rows = 2 * own_rows
        query_width = attended_in.shape[1]
        key_width = (projected_in.shape[1] - query_width) // 2
        tile = 2 * key_width
        block = width // dp_size

        partners = {k: {"dp": me + (1 - 2 * bits[k]) * 2**k} for k in all_bits}
        partners[None] = {"tensor": side_other}

        barrier = pltpu.get_barrier_semaphore()
        for k in all_bits + (None,):
            pl.semaphore_signal(barrier, inc=1, device_id=partners[k], device_id_type=MESH)
        pl.semaphore_wait(barrier, bit_count + 1)

        counter, local_counter = [0], [0]
        unsent = []

        class Push:
            def __init__(self, ends, k):
                self.ends, self.k, self.i = ends, k, counter[0]
                counter[0] += 1
                self.copy().start()
                unsent.append(self)

            def copy(self):
                src, dst = self.ends()
                return pltpu.make_async_remote_copy(
                    src_ref=src,
                    dst_ref=dst,
                    send_sem=send_sem.at[self.i],
                    recv_sem=recv_sem.at[self.i],
                    device_id=partners[self.k],
                    device_id_type=MESH,
                )

            def wait_recv(self):
                self.copy().wait_recv()

        def sent(push):
            push.copy().wait_send()
            unsent[:] = [other for other in unsent if other is not push]

        def keep(src, dst):
            i = local_counter[0]
            local_counter[0] += 1
            copy = pltpu.make_async_copy(src, dst, local_sem.at[i])
            copy.start()
            return copy

        def cells(lead):
            return [tuple((i >> (lead - 1 - j)) & 1 for j in range(lead)) for i in range(2**lead)]

        def strips(count, size, work):
            def step(r, _):
                work(pl.ds(pl.multiple_of(r * size, size), size))
                return 0

            lax.fori_loop(0, count // size, step, 0)

        def half_grad(left, right, which, give):
            lead = bit_count - 1
            kept = 0
            while block * 2**kept < 256 and kept < lead:
                kept += 1
            for i in range(2 ** (lead - kept)):
                parts = []
                for j in range(2**kept):
                    pair = (i * 2**kept + j) * 2 * block
                    if block % 128 == 0:
                        at = pl.multiple_of(pair + which * block, 128)
                        parts.append(left[:, pl.ds(at, block)])
                    else:
                        low = left[:, pair : pair + block].astype(f32)
                        high = left[:, pair + block : pair + 2 * block].astype(f32)
                        parts.append(jnp.where(which == 0, low, high).astype(bf16))
                columns = jnp.concatenate(parts, axis=1)
                product = dot(columns, right[...], ((0,), (0,)))
                index = tuple((i >> (lead - kept - 1 - j)) & 1 for j in range(lead - kept))
                give(index, product.reshape((2,) * kept + (block, product.shape[-1])))

        class Product:
            def __init__(self, ref, lead):
                self.ref, self.lead, self.copy = ref, lead, None

            def away(self, left, right, slot):
                def give(index, value):
                    slot[index] = value.astype(bf16)

                half_grad(left, right, core_other, give)
                self.slot = slot

            def start(self):
                slot, ref, lead = self.slot, self.ref, self.lead
                self.copy = Push(lambda: (slot, ref.at[lead] if lead else ref), CORE_BIT)

            def near(self, left, right):

                def give(index, value):
                    at = self.lead + index
                    self.ref[at] = (value + self.ref[at].astype(f32)).astype(bf16)

                half_grad(left, right, core, give)

        class Fold:
            def __init__(self, ref, lead, start, size, steps, order, staged):
                self.ref, self.lead = ref, lead
                self.start, self.size = start, size
                self.steps = dict(zip(order, steps))
                self.order = list(order)
                self.staged = staged
                self.settled = {}
                self.copy = self.bit = None

            def place(self, cell):
                rest = iter(cell)
                return self.lead + tuple(
                    self.settled[k] if k in self.settled else next(rest) for k in folded
                )

            def open(self):
                return len(folded) - len(self.settled)

            def rows(self):
                return (pl.ds(self.start, self.size),)

            def send(self):
                self.bit = self.order.pop(0)
                self.settled[self.bit] = others[self.bit]
                twice = (pl.ds(0, 2),) * self.open()
                place = self.place(twice) + self.rows()
                target, there = self.steps[self.bit], twice + self.rows()
                self.copy = Push(lambda: (self.ref.at[place], target.at[there]), self.bit)
                self.settled[self.bit] = bits[self.bit]

            def add(self, last=None):
                self.copy.wait_recv()
                arrived, lead = self.steps[self.bit], ()
                if self.staged:
                    there = (pl.ds(0, 2),) * self.open() + self.rows()
                    lead = (0,) * (len(folded) - 1 - self.open())
                    keep(arrived.at[there], recv_stage.at[lead + there]).wait()
                    arrived = recv_stage
                for cell in cells(self.open()):
                    place = self.place(cell)

                    def work(r, _, cell=cell, place=place):
                        at = pl.ds(pl.multiple_of(self.start + r * 16, 16), 16)
                        new, old = arrived[lead + cell + (at,)], self.ref[place + (at,)]
                        if last is None:
                            self.ref[place + (at,)] = new + old
                        else:
                            last(cell, at, new.astype(f32) + old.astype(f32))
                        return 0

                    lax.fori_loop(0, self.size // 16, work, 0)

            def step(self):
                self.add()
                self.send()

        class Walk:
            def __init__(self, *actions):
                self.actions = list(actions)
                self.taken = 0

            def step(self):
                if self.actions:
                    self.taken += 1
                    self.actions.pop(0)()

            def finish(self):
                while self.actions:
                    self.step()

        steps, works, done, pushes = {}, {}, set(), {}

        def do(name):
            if name not in done:
                done.add(name)
                works[name]()

        def once(name, ends, k, after):
            def start():
                do(after)
                pushes[name] = Push(ends, k)

            steps[name] = Walk(start, lambda: pushes[name].wait_recv())

        near_loads = {}

        def load_near(slot, p):
            source = (grad_part, out_part)[slot]
            n = local_counter[0]
            local_counter[0] += 1

            def copy():
                if p == 0:
                    view = source.at[share, :, :, pl.ds(0, half)]
                else:
                    view = source.at[:, side, :, pl.ds(half, half)]
                return pltpu.make_async_copy(view, quad_near.at[p], local_sem.at[n])

            copy().start()
            near_loads[slot, p] = copy

        def quad_half(name, slot, p):
            source = (grad_part, out_part)[slot]
            first_bit, second_bit = ((SHARE_BIT, None), (None, SHARE_BIT))[p]
            there = (side_other, share_other)[p]

            def first():
                def ends():
                    if p == 0:
                        view = source.at[share_other, :, :, pl.ds(0, half)]
                    else:
                        view = source.at[:, side_other, :, pl.ds(half, half)]
                    return view, quad_in.at[slot, p]

                pushes[name] = Push(ends, first_bit)

            def second():
                if slot == 1:
                    while steps["el" if p == 0 else "er"].taken < 2:
                        steps["el" if p == 0 else "er"].step()
                pushes[name].wait_recv()
                near_loads[slot, p]().wait()
                for q in range(2):

                    def work(at, q=q):
                        quad_in[slot, p, q, at, :] = (
                            quad_in[slot, p, q, at, :] + quad_near[p, q, at, :]
                        )

                    strips(own_rows, 16, work)
                pushes[name] = Push(
                    lambda: (quad_in.at[slot, p, there], quad_step.at[slot, p]), second_bit
                )
                if slot == 0:
                    load_near(1, p)

            steps[name] = Walk(first, second, lambda: pushes[name].wait_recv())

        def quad_value(slot, at):
            halves = []
            for p, here in ((0, side), (1, share)):
                halves.append(
                    quad_in[slot, p, here, at, :].astype(f32) + quad_step[slot, p, at, :].astype(f32)
                )
            return jnp.concatenate(halves, axis=-1)

        quad_half("el", 0, 0)
        quad_half("er", 0, 1)
        quad_half("ol", 1, 0)
        quad_half("or", 1, 1)
        load_near(0, 0)
        load_near(0, 1)
        middle_load = keep(middle_in, middle)

        part = block // 2
        mlp_products = [Product(mlp_core, (m,)) for m in range(3)]
        mlp_folds = [
            Fold(mlp_core, (m,), p * part, part, mlp_steps[m], low_order, True)
            for m in range(3)
            for p in range(2)
        ]
        qkv_product = Product(qkv_core, ())
        out_product = Product(out_core, ())
        qkv_folds = [Fold(qkv_core, (), p * part, part, qkv_steps, qkv_order, False) for p in range(2)]
        out_folds = [Fold(out_core, (), p * part, part, out_steps[p], out_orders[p], False) for p in range(2)]
        mlp_copies = [None] * 6
        stage_copies = [None, None]
        stage_count = [0]

        def to_output(fill, rows_of, dst):
            i = stage_count[0] % 2
            stage_count[0] += 1
            if stage_copies[i] is not None:
                stage_copies[i]().wait()
            fill(i)
            n = local_counter[0]
            local_counter[0] += 1

            def copy():
                return pltpu.make_async_copy(stage.at[i, rows_of], dst(), local_sem.at[n])

            copy().start()
            stage_copies[i] = copy

        hidden_width = hid.shape[-1]
        own_half = pl.multiple_of(share * hidden_width, 128)
        other_half = pl.multiple_of(share_other * hidden_width, 128)
        gain_sums[1] = jnp.zeros_like(gain_sums[1])

        def weight_rows(m, rows_of, start):
            columns = pl.ds(start, hidden_width)
            keep(w_gateup.at[m - 1, rows_of, columns], weight_stage.at[rows_of]).wait()

        def give_rows(m, i, at, total):
            if m == 0:
                down_held[i, at, :] = total
                return
            stage[i, at, :] = total * gain_two[at, :]
            weighted = total * weight_stage[at, :].astype(f32)
            gain_sums[1, at, :] += jnp.sum(weighted, axis=-1, keepdims=True)

        def mlp_share(u):
            m, fold = u // 2, mlp_folds[u]
            rows_of = pl.ds(fold.start, fold.size)

            def fill(i):
                def last(cell, at, total):
                    is_own = share == cell[0]

                    @pl.when(is_own)
                    def _():
                        give_rows(m, i, at, total)

                    @pl.when(jnp.logical_not(is_own))
                    def _():
                        mlp_last[m, 0, at, :] = total.astype(bf16)

                fold.add(last)

            if m == 0:
                fill(0)
            else:
                weight_rows(m, rows_of, own_half)
                columns = pl.ds(own_half, hidden_width)
                to_output(fill, rows_of, lambda: gateup_grad.at[m - 1, rows_of, columns])
            mlp_copies[u] = Push(
                lambda: (mlp_last.at[m, 0, rows_of], mlp_last.at[m, 1, rows_of]), SHARE_BIT
            )

        def mlp_finish(u):
            m, fold = u // 2, mlp_folds[u]
            rows_of = pl.ds(fold.start, fold.size)
            mlp_copies[u].wait_recv()

            def fill(i):
                def work(r, _):
                    at = pl.ds(pl.multiple_of(fold.start + r * 16, 16), 16)
                    give_rows(m, i, at, mlp_last[m, 1, at, :].astype(f32))
                    return 0

                lax.fori_loop(0, fold.size // 16, work, 0)

            if m == 0:
                fill(1)
            else:
                weight_rows(m, rows_of, other_half)
                columns = pl.ds(other_half, hidden_width)
                to_output(fill, rows_of, lambda: gateup_grad.at[m - 1, rows_of, columns])

        def out_rows(cell, at, total):
            out_sum[at, :] = total

        def qkv_rows(cell, at, total):
            gain = gain_one[at, :]
            parts = [total[:, :key_width], total[:, key_width:tile], total[:, tile:]]
            weights = [key_value[0, at, :], key_value[1, at, :], w_query[at, :]]
            row_sum = sum(
                jnp.sum(p * w.astype(f32), axis=-1, keepdims=True) for p, w in zip(parts, weights)
            )
            gain_sums[0, at, :] = jnp.broadcast_to(row_sum, (16, 128))
            keyval_grad[0, at, :] = parts[0] * gain
            keyval_grad[1, at, :] = parts[1] * gain
            query_grad[at, :] = parts[2] * gain

        def walk_fold(name, fold, after, *ends):
            def start():
                do(after)
                fold.send()

            steps[name] = Walk(start, *([fold.step] * (len(fold.order) - 1)), *ends)

        for u in range(6):
            walk_fold(
                f"f{u}",
                mlp_folds[u],
                f"B{u // 2}",
                functools.partial(mlp_share, u),
                functools.partial(mlp_finish, u),
            )
        for p in range(2):
            for name, fold, after, last in (
                (f"p{p}", out_folds[p], "OB", out_rows),
                (f"q{p}", qkv_folds[p], "QB", qkv_rows),
            ):
                walk_fold(name, fold, after, functools.partial(fold.add, last))

        def walk_core(name, product, after):
            def start():
                do(after)
                product.start()

            steps[name] = Walk(start, lambda: product.copy.wait_recv())

        for m in range(3):
            walk_core(f"K{m}", mlp_products[m], f"W{m}")
        walk_core("KO", out_product, "OA")
        walk_core("KQ", qkv_product, "QA")
        once("D", lambda: (grad_branch.at[side], grad_branch.at[side]), None, "MR")
        once("N", lambda: (norm_away, norm_in), None, "NA")

        def follow(order):
            for name in order:
                if name in works:
                    do(name)
                else:
                    steps[name].step()

        def first_phase(held_rows, held_cot, held_hid):
            loads = [
                keep(cot_all, held_cot),
                keep(hid.at[0], held_hid.at[0]),
                keep(normed_two, held_rows),
                keep(hid.at[1], held_hid.at[1]),
            ]
            waited = set()

            def ready(*numbers):
                for n in numbers:
                    if n not in waited:
                        waited.add(n)
                        loads[n].wait()

            sources = [
                (held_cot, held_hid.at[0], away_slots.at[0], (0, 1)),
                (held_rows, held_hid.at[1], away_slots.at[1], (2, 3)),
                (held_rows, held_hid.at[0], away_slots.at[0], (2, 4)),
            ]

            def away_work(m):
                def run():
                    left, right, slot, numbers = sources[m]
                    if m == 2:
                        do("B0")
                        loads.append(keep(hid.at[2], held_hid.at[0]))
                        sent(mlp_products[0].copy)
                    ready(*numbers)
                    mlp_products[m].away(left, right, slot)

                return run

            def near_work(m):
                def run():
                    steps[f"K{m}"].finish()
                    mlp_products[m].near(*sources[m][:2])

                return run

            for m in range(3):
                works[f"W{m}"] = away_work(m)
                works[f"B{m}"] = near_work(m)
            follow(BACKWARD_ORDER[:phase_at])
            for m in range(3):
                do(f"B{m}")
            for m in (1, 2):
                sent(mlp_products[m].copy)

        phase_at = BACKWARD_ORDER.index("MR")
        pl.run_scoped(
            first_phase,
            pltpu.VMEM(normed_two.shape, bf16),
            pltpu.VMEM(cot_all.shape, bf16),
            pltpu.VMEM((2,) + hid.shape[1:], bf16),
        )

        def second_phase(
            weights, held_normed, held_probs, projected, attended, grad_att, grad_qkv, acc
        ):
            qkv_width = query_width + tile
            lead_all = (slice(None),) * (bit_count + 1)
            loads = {
                "out": keep(out_full, weights.at[lead_all + (pl.ds(0, query_width),)]),
                "probs": keep(probs.at[pl.ds(0, HEADS_PER_KV)], held_probs),
                "projected": keep(projected_in, projected),
                "attended": keep(attended_in, attended),
                "normed": keep(normed, held_normed),
            }

            def ready(*names):
                for name in names:
                    if name in loads:
                        loads.pop(name).wait()

            def middle_work():
                middle_load.wait()
                steps["el"].finish()
                steps["er"].finish()

                def middle_rows(at):
                    x = middle[at, :]
                    total = cot[at, :].astype(f32) + rms_grad(x, rms(x), quad_value(0, at))
                    grad_middle[at, :] = total
                    grad_branch[side, at, :] = total.astype(bf16)

                strips(own_rows, 16, middle_rows)

            works["MR"] = middle_work
            branch_flat = BranchView()
            slots = [
                away_slots.at[(i,) + (slice(None),) * bit_count + (pl.ds(0, columns),)]
                for i, columns in ((0, qkv_width), (1, query_width))
            ]

            def attended_grad():
                steps["D"].finish()
                ready("out")
                branch_all = grad_branch[...].reshape(rows, width)
                for low in range(0, query_width, 256):
                    block_of = weights[lead_all + (slice(low, low + 256),)].reshape(width, 256)
                    grad_att[:, low : low + 256] = jnp.dot(
                        branch_all, block_of, preferred_element_type=f32
                    ).astype(bf16)
                loads["qkv"] = keep(qkv_full, weights)

            works["DA"] = attended_grad

            def out_away():
                steps["D"].finish()
                ready("attended")
                out_product.away(branch_flat, attended, slots[1])

            def out_near():
                steps["KO"].finish()
                out_product.near(branch_flat, attended)

            works["OA"] = out_away
            works["OB"] = out_near

            pair_lanes = lax.broadcasted_iota(jnp.int32, (rows, 2 * HEAD_SIZE), 1)
            lanes = lax.broadcasted_iota(jnp.int32, (rows, key_width), 1)
            first_half = lanes % HEAD_SIZE < HEAD_SIZE // 2

            def padded(a, head, place):
                moved = a if head == place else pltpu.roll(a, HEAD_SIZE, 1)
                inside = pair_lanes < HEAD_SIZE if place == 0 else pair_lanes >= HEAD_SIZE
                return jnp.where(inside, moved, 0.0).astype(bf16)

            def unrotate(a):
                forward = pltpu.roll(a, key_width - HEAD_SIZE // 2, 1)
                back = pltpu.roll(a, HEAD_SIZE // 2, 1)
                return a * cosines[...] - jnp.where(first_half, forward, back) * sines[...]

            heads = key_width // HEAD_SIZE
            pairs = HEADS_PER_KV // 2
            tile_rows = 128
            lane_tile = lax.broadcasted_iota(jnp.int32, (tile_rows, 2 * HEAD_SIZE), 1)
            totals = []
            heads_at = {}

            def head_pair(n):
                def run():
                    head, i = n // pairs, n % pairs
                    if i == 0:
                        do("DA")
                        ready("probs", "projected")
                        if head > 0:
                            first = head * HEADS_PER_KV
                            keep(probs.at[pl.ds(first, HEADS_PER_KV)], held_probs).wait()
                        keys32 = projected[:, :key_width].astype(f32)
                        values32 = projected[:, key_width:tile].astype(f32)
                        heads_at["keys"] = [padded(keys32, head, p) for p in range(2)]
                        heads_at["values"] = [padded(values32, head, p) for p in range(2)]
                        acc[...] = jnp.zeros_like(acc)
                    keys_at, values_at = heads_at["keys"], heads_at["values"]
                    columns = slice(n * 128, (n + 1) * 128)
                    query_columns = slice(tile + n * 128, tile + (n + 1) * 128)
                    places = [
                        (low, low + tile_rows, p)
                        for low in range(0, rows, tile_rows)
                        for p in range(2)
                    ]
                    insides = [lane_tile < HEAD_SIZE, lane_tile >= HEAD_SIZE]
                    prob = [
                        held_probs[2 * i + p, low:high, :high] for low, high, p in places
                    ]
                    grad_prob = [
                        dot(grad_att[low:high, columns], values_at[p][:high], ((1,), (1,)))
                        for low, high, p in places
                    ]
                    prob32 = [a.astype(f32) for a in prob]
                    weighted = [a * b for a, b in zip(prob32, grad_prob)]
                    centre = [jnp.sum(a, axis=-1, keepdims=True) for a in weighted]
                    grad_score = [
                        (a - b * c).astype(bf16) for a, b, c in zip(weighted, prob32, centre)
                    ]
                    grad_query = [
                        jnp.dot(a, keys_at[p][:high], preferred_element_type=f32)
                        for a, (low, high, p) in zip(grad_score, places)
                    ]
                    for j, (low, high, p) in enumerate(places):
                        query = projected[low:high, query_columns].astype(f32)
                        only_query = jnp.where(insides[p], query, 0.0).astype(bf16)
                        out32 = grad_att[low:high, columns].astype(f32)
                        only_grad = jnp.where(insides[p], out32, 0.0).astype(bf16)
                        acc[0, :high, :] += dot(grad_score[j], only_query, ((0,), (0,)))
                        acc[1, :high, :] += dot(prob[j], only_grad, ((0,), (0,)))
                        if p == 1:
                            total = grad_query[j - 1] + grad_query[j]
                            acc[2, low:high, :] = total * HEAD_SIZE**-0.5
                    grad_qkv[:, query_columns] = unrotate(acc[2]).astype(bf16)
                    if i == pairs - 1:
                        totals.append([acc[j] + pltpu.roll(acc[j], HEAD_SIZE, 1) for j in range(2)])

                return run

            for n in range(query_width // 128):
                works[f"T{n}"] = head_pair(n)

            def qkv_away():
                lower = pair_lanes < HEAD_SIZE
                grad_keys = unrotate(jnp.where(lower, totals[0][0], totals[1][0]))
                grad_qkv[:, :key_width] = grad_keys.astype(bf16)
                grad_values = jnp.where(lower, totals[0][1], totals[1][1])
                grad_qkv[:, key_width:tile] = grad_values.astype(bf16)
                ready("normed")
                qkv_product.away(held_normed, grad_qkv, slots[0])

            def qkv_near():
                steps["KQ"].finish()
                qkv_product.near(held_normed, grad_qkv)

            works["QA"] = qkv_away
            works["QB"] = qkv_near
            tiles = spread(weights, bit_count, 512)

            def norm_part(which, give):
                ready("qkv")
                at = pl.ds(pl.multiple_of(which * own_rows, 64), own_rows)
                chosen = grad_qkv[at, :]
                for i, (index, count) in enumerate(tiles):
                    block_of = weights[index].reshape(count, qkv_width)
                    give(slice(i * count, (i + 1) * count), dot(chosen, block_of, ((1,), (1,))))

            def give_away(to, value):
                norm_away[:, to] = value.astype(bf16)

            def give_near(to, value):
                middle[:, to] = value

            works["NA"] = lambda: norm_part(side_other, give_away)

            def result_work():
                steps["ol"].finish()
                steps["or"].finish()

                def result_rows(at):
                    result[at, :] = (middle[at, :] + quad_value(1, at)).astype(bf16)

                strips(own_rows, 16, result_rows)

            works["RR"] = result_work

            def near_rows():
                do("RR")
                norm_part(side, give_near)

            works["NB"] = near_rows

            def input_work():
                do("NB")
                steps["N"].finish()

                def input_rows(at):
                    x = tok[at, :].astype(f32)
                    scaled = middle[at, :] + norm_in[at, :].astype(f32)
                    total = grad_middle[at, :] + rms_grad(x, rms(x), scaled)
                    input_grad[at, :] = total.astype(bf16)

                strips(own_rows, 16, input_rows)

            works["IR"] = input_work
            follow(BACKWARD_ORDER[phase_at:])
            for name in works:
                do(name)
            for product in (out_product, qkv_product):
                sent(product.copy)

        class BranchView:
            def __getitem__(self, index):
                return grad_branch[(slice(None), slice(None), index[1])].reshape(rows, -1)

        pl.run_scoped(
            second_phase,
            pltpu.VMEM(qkv_full.shape, bf16),
            pltpu.VMEM(normed.shape, bf16),
            pltpu.VMEM((HEADS_PER_KV,) + probs.shape[1:], bf16),
            pltpu.VMEM(projected_in.shape, bf16),
            pltpu.VMEM(attended_in.shape, bf16),
            pltpu.VMEM(attended_in.shape, bf16),
            pltpu.VMEM(projected_in.shape, bf16),
            pltpu.VMEM((3, rows, 2 * HEAD_SIZE), f32),
        )

        def last_phase(turned):
            copies = []
            for name in ("f0", "f1"):
                steps[name].finish()
            for h, start in ((0, own_half), (1, other_half)):
                turned[h] = down_held[h].T
                copies.append(keep(turned.at[h], down_grad.at[pl.ds(start, hidden_width)]))
            for name in steps:
                steps[name].finish()
            quarter = block // 2
            there = pl.ds(pl.multiple_of(side_other * quarter, 16), quarter)
            here = pl.ds(pl.multiple_of(side * quarter, 16), quarter)
            exchange = Push(lambda: (gain_sums.at[:, there], gain_in), None)
            out_grad[...] = out_sum[...].T
            exchange.wait_recv()
            gain_grads[...] = gain_sums[:, here, :] + gain_in[...]
            sent(exchange)
            for copy in copies:
                copy.wait()

        pl.run_scoped(last_phase, pltpu.VMEM((2, hid.shape[-1], block), f32))
        for copy in stage_copies:
            copy().wait()
        for copy in list(unsent):
            sent(copy)

    def call(
        normed_two,
        cot_all,
        hid,
        grad_part,
        out_part,
        middle,
        tok,
        cot,
        out_full,
        qkv_full,
        normed,
        projected,
        probs,
        attended,
        cosines,
        sines,
        w_query,
        key_value,
        w_gateup,
        gain_one,
        gain_two,
    ):
        bf16, f32 = jnp.bfloat16, jnp.float32
        own_rows, width = tok.shape
        half = width // 2
        block, qkv_width = qkv_full.shape[-2:]
        query_width = out_full.shape[-1]
        mlp_width = hid.shape[-1]
        shape = jax.ShapeDtypeStruct
        whole = pl.BlockSpec(memory_space=pltpu.VMEM)
        away = pl.BlockSpec(memory_space=pl.ANY)

        def twos(count):
            return (2,) * count

        slots = [
            shape(twos(bit_count - 2 - i) + (block, mlp_width), bf16) for i in range(step_count)
        ] * 3

        def steps_of(order, columns):
            return [
                pltpu.VMEM(twos(bit_count - 2 - i) + (block, columns), bf16)
                for i in range(len(order))
            ]

        def at_core(columns):
            return twos(bit_count - 1) + (block, columns)

        count = 6 * (step_count + 2) + 6 * bit_count + 24
        outs = pl.pallas_call(
            kernel,
            out_shape=[
                shape((own_rows, width), bf16),
                shape((own_rows, width), bf16),
                shape((block, query_width), f32),
                shape(key_value.shape, f32),
                shape((query_width, block), f32),
                shape(w_gateup.shape, f32),
                shape((2 * mlp_width, block), f32),
                shape((2, block // 2, 128), f32),
            ]
            + slots,
            in_specs=[away] * 6 + [whole] * 2 + [away] * 6 + [whole] * 4 + [away] + [whole] * 2,
            out_specs=[whole] * 5 + [away] * 2 + [whole] + [away] * len(slots),
            scratch_shapes=[
                pltpu.VMEM((2,) + at_core(mlp_width), bf16),
                pltpu.VMEM((3,) + at_core(mlp_width), bf16),
                pltpu.VMEM((3, 2, block, mlp_width), bf16),
                pltpu.VMEM(twos(bit_count - 2) + (block, mlp_width), bf16),
                pltpu.VMEM(at_core(qkv_width), bf16),
                pltpu.VMEM(at_core(query_width), bf16),
                pltpu.VMEM((2, 2, 2, own_rows, half), bf16),
                pltpu.VMEM((2, 2, own_rows, half), bf16),
                pltpu.VMEM((2, 2, own_rows, half), bf16),
                pltpu.VMEM((own_rows, width), f32),
                pltpu.VMEM((own_rows, width), f32),
                pltpu.VMEM((2, own_rows, width), bf16),
                pltpu.VMEM((own_rows, width), bf16),
                pltpu.VMEM((own_rows, width), bf16),
                pltpu.VMEM((2, block, mlp_width), f32),
                pltpu.VMEM((2, block, mlp_width), f32),
                pltpu.VMEM((block, query_width), f32),
                pltpu.VMEM((block, mlp_width), bf16),
                pltpu.VMEM((2, block, 128), f32),
                pltpu.VMEM((2, block // 2, 128), f32),
                pltpu.SemaphoreType.DMA((count,)),
                pltpu.SemaphoreType.DMA((count,)),
                pltpu.SemaphoreType.DMA((6 * step_count + 64,)),
            ]
            + steps_of(qkv_order, qkv_width)
            + steps_of(qkv_order, query_width),
            compiler_params=pltpu.CompilerParams(
                collective_id=2, has_side_effects=True, vmem_limit_bytes=62 * 1024 * 1024
            ),
            name="backward",
        )(
            normed_two,
            cot_all,
            hid,
            grad_part,
            out_part,
            middle,
            tok,
            cot,
            out_full,
            qkv_full,
            normed,
            projected,
            probs,
            attended,
            cosines,
            sines,
            w_query,
            key_value,
            w_gateup,
            gain_one,
            gain_two,
        )
        return outs[:8]

    return call


def make_body(dp_size):
    bit_count = dp_size.bit_length() - 1
    high_bits = tuple(range(bit_count - 1, SHARE_BIT, -1))

    def body(
        tokens,
        attn_gain,
        w_query,
        keyvalue_weight,
        w_out,
        mlp_gain,
        w_gateup,
        w_down,
        segment_ids,
        positions,
        cotangent,
    ):
        f32 = jnp.float32
        own_rows, width = tokens.shape

        gain_one = attn_gain.astype(f32)[:, None]
        gain_two = mlp_gain.astype(f32)[:, None]

        cosine_table, sine_table = rotary_tables(positions, HEAD_SIZE)
        sine_table = jnp.where(jnp.arange(HEAD_SIZE) < HEAD_SIZE // 2, -sine_table, sine_table)
        cosine_table = jnp.concatenate([cosine_table, cosine_table], axis=1)
        sine_table = jnp.concatenate([sine_table, sine_table], axis=1)
        (
            qkv_full,
            out_full,
            probs,
            normed,
            projected,
            attended,
            middle,
            normed_two,
            grad_all,
            hid,
            grad_part,
            out_part,
        ) = make_forward(dp_size, high_bits)(
            tokens,
            cotangent,
            w_query,
            keyvalue_weight,
            w_out,
            w_gateup,
            w_down,
            gain_one,
            gain_two,
            cosine_table,
            sine_table,
            segment_ids[None, :],
            segment_ids[:, None],
        )
        normed_two = normed_two.reshape(4 * own_rows, width)
        grad_all = grad_all.reshape(4 * own_rows, width)

        quad_shape = (2, 2, own_rows, width)
        (
            result,
            input_grad,
            query_grad,
            keyval_grad,
            out_grad,
            gateup_grad,
            down_grad,
            gain_grads,
        ) = make_backward(dp_size, high_bits)(
            normed_two,
            grad_all,
            hid,
            grad_part.reshape(quad_shape),
            out_part.reshape(quad_shape),
            middle,
            tokens,
            cotangent,
            out_full,
            qkv_full,
            normed,
            projected,
            probs,
            attended,
            cosine_table,
            sine_table,
            w_query,
            keyvalue_weight,
            w_gateup,
            gain_one,
            gain_two,
        )
        return (
            result,
            input_grad,
            gain_grads[0, :, 0],
            query_grad,
            keyval_grad,
            out_grad,
            gain_grads[1, :, 0],
            gateup_grad,
            down_grad,
        )

    return body


def solution(mesh):
    return jax.shard_map(
        make_body(mesh.shape["dp"]),
        mesh=mesh,
        in_specs=(
            P(("dp", "tensor"), None),
            P("dp"),
            P("dp", "tensor"),
            P(None, "dp", "tensor"),
            P("tensor", "dp"),
            P("dp"),
            P(None, "dp", "tensor"),
            P("tensor", "dp"),
            P("dp"),
            P("dp"),
            P(("dp", "tensor"), None),
        ),
        out_specs=(
            P(("dp", "tensor"), None),
            P(("dp", "tensor"), None),
            P(("dp", "tensor")),
            P("dp", "tensor"),
            P(None, "dp", "tensor"),
            P("tensor", "dp"),
            P(("dp", "tensor")),
            P(None, "dp", "tensor"),
            P("tensor", "dp"),
        ),
        check_vma=False,
    )
```

```python
import functools
import math

import jax
import jax.numpy as jnp
from jax import lax
from jax.experimental import pallas as pl
from jax.experimental.pallas import tpu as pltpu
from jax.sharding import PartitionSpec as P

MESH = pl.DeviceIdType.MESH

QUERY_HEAD_COUNT = 32
KEYVALUE_HEADS = 4
HEAD_SIZE = 64
HEADS_PER_KV = QUERY_HEAD_COUNT // KEYVALUE_HEADS
norm_eps = 1e-05

CORE_BIT = 0
SHARE_BIT = 2


FORWARD_ORDER = (
    "q1", "u1", "t", "q0", "W", "o", "q1", "q0", "t", "N", "q1", "o", "c", "q0", "q0", "q1", "u2",
    "o", "q0", "u3", "q1", "u0", "u1", "c", "u2", "K", "u1", "Q0", "Q1", "o", "A0", "Q2", "u5",
    "Q3", "A1", "o", "A2", "A3", "u0", "A4", "A5", "u2", "A6", "A7", "OA", "u3", "b", "u0", "u5",
    "ON", "u4", "b", "M", "nr", "u3", "nl", "u2", "u1", "nl", "u4", "u0", "nr", "u5", "u3", "u1",
    "u3", "c", "u0", "DHb", "u4", "DHa", "u5", "u5", "nr", "u2", "nl", "Gb", "Ub", "Eb", "u4", "Ga",
    "u4", "Ua", "Ea",
)

BACKWARD_ORDER = (
    "er", "el", "W0", "K0", "W1", "K1", "K1", "B1", "f2", "er", "K0", "el", "f3", "O", "ol", "or",
    "W2", "K2", "er", "f2", "el", "B0", "K2", "f1", "B2", "MR", "D", "f3", "f0", "f2", "ol", "or",
    "D", "DA", "f1", "f3", "OA", "KO", "KO", "OB", "T0", "T1", "f4", "T2", "T3", "p0", "T4", "f0",
    "p1", "f4", "T5", "f5", "T6", "T7", "ol", "QA", "f1", "p1", "NA", "p0", "KQ", "KQ", "QB", "N",
    "q0", "q1", "f1", "f5", "f4", "or", "p0", "f0", "f3", "f4", "N", "RR", "q0", "p0", "q1", "f5",
    "NB", "IR", "q0", "p1", "f0", "q1", "q0", "p1", "TD", "f2", "TO", "f5", "q1",
)


def rotary_tables(places, width):
    freqs = jnp.exp(jnp.arange(0, width, 2).astype(jnp.float32) * (-math.log(10000.0) / width))
    turned = places.astype(jnp.float32)[:, None] * freqs[None, :]
    turned = jnp.concatenate([turned, turned], axis=-1)
    return (jnp.cos(turned), jnp.sin(turned))


def dot(left, right, contract):
    return lax.dot_general(left, right, (contract, ((), ())), preferred_element_type=jnp.float32)


def rms(rows):
    return lax.rsqrt(jnp.mean(rows * rows, axis=-1, keepdims=True) + norm_eps)


def rms_grad(rows, inverse, grad_scaled):
    inner = jnp.mean(grad_scaled * rows, axis=-1, keepdims=True)
    return inverse * grad_scaled - rows * (inverse * inverse * inverse) * inner


def spread(ref, lead, row_tile):
    sizes = ref.shape
    block = sizes[-2]
    kept = 0
    while block * 2**kept < row_tile and kept < lead:
        kept += 1
    out = []
    for i in range(2 ** (lead - kept)):
        index = tuple((i >> (lead - kept - 1 - j)) & 1 for j in range(lead - kept))
        out.append((index, (block * 2**kept)))
    return out


def spread_gains(gains, columns):
    block = gains.shape[1]
    order = [lax.broadcasted_iota(jnp.int32, (block, block), axis) for axis in range(2)]
    for i in range(gains.shape[0]):
        only = jnp.where(order[0] == order[1], gains[i : i + 1, :], 0.0)
        columns[i] = jnp.broadcast_to(jnp.sum(only, axis=1, keepdims=True), columns.shape[1:])


def make_forward(dp_size, high_bits):
    bit_count = dp_size.bit_length() - 1
    all_bits = tuple(range(bit_count))

    def kernel(
        tok,
        cot,
        w_query,
        key_value,
        w_out,
        w_gateup,
        w_down,
        gains,
        cosines,
        sines,
        bias,
        qkv_full,
        out_full,
        probs,
        normed_to,
        projected_to,
        attended_to,
        middle_to,
        normed_two_to,
        cot_all_to,
        hid_to,
        grad_part_to,
        down_full,
        normed,
        projected,
        attended,
        middle,
        normed_two,
        cot_all,
        hid,
        grad_part,
        qkv_held,
        out_held,
        mlp_held,
        tok_all,
        branch_away,
        branch_in,
        prob_stage,
        mlp_other,
        gain_columns,
        send_sem,
        recv_sem,
        local_sem,
    ):
        f32, bf16 = jnp.float32, jnp.bfloat16
        me = lax.axis_index("dp")
        side = lax.axis_index("tensor")
        bits = [(me // 2**k) % 2 for k in all_bits]
        share = bits[SHARE_BIT]
        own_rows, width = tok.shape
        half = width // 2
        group_rows = 2 * own_rows
        query_width = attended.shape[1]
        key_width = (projected.shape[1] - query_width) // 2
        tile = 2 * key_width
        hidden_width = hid.shape[-1]

        def partner(k):
            if k is None:
                return {"tensor": 1 - side}
            return {"dp": me + (1 - 2 * bits[k]) * 2**k}

        own = tuple(bits[k] for k in reversed(all_bits))
        everything = (slice(None), slice(None))
        halves = [pl.multiple_of(h * hidden_width, 128) for h in (share, 1 - share)]
        raw = {}
        for m in range(2):
            for h in range(2):
                block_at = hid.at[m, pl.ds(h * w_query.shape[0], w_query.shape[0])]
                columns = pl.ds(halves[h], hidden_width)
                raw[m, h] = pltpu.make_async_copy(
                    w_gateup.at[m, :, columns], block_at, local_sem.at[2 * m + h]
                )
                raw[m, h].start()

        spread_gains(gains, gain_columns)

        def scaled(a, gain):
            return (a.astype(f32) * gain_columns[gain][:, :1]).astype(bf16)

        qkv_held[own + (slice(None), slice(0, key_width))] = scaled(key_value[0], 0)
        qkv_held[own + (slice(None), slice(key_width, tile))] = scaled(key_value[1], 0)
        qkv_held[own + (slice(None), slice(tile, tile + query_width))] = scaled(
            w_query[...], 0
        )
        out_held[own + everything] = w_out[...].T

        barrier = pltpu.get_barrier_semaphore()
        for k in all_bits + (None,):
            pl.semaphore_signal(barrier, inc=1, device_id=partner(k), device_id_type=MESH)
        pl.semaphore_wait(barrier, bit_count + 1)

        counter, local_counter = [0], [4]
        started = []

        def push(src, dst, k):
            i = counter[0]
            counter[0] += 1
            copy = pltpu.make_async_remote_copy(
                src_ref=src,
                dst_ref=dst,
                send_sem=send_sem.at[i],
                recv_sem=recv_sem.at[i],
                device_id=partner(k),
                device_id_type=MESH,
            )
            copy.start()
            started.append(copy)
            return copy

        def keep(src, dst):
            i = local_counter[0]
            local_counter[0] += 1
            copy = pltpu.make_async_copy(src, dst, local_sem.at[i])
            copy.start()
            return copy

        def held(ref, lead, gathered, columns):
            index = tuple(
                pl.ds(0, 2) if k in gathered else bits[k] for k in reversed(all_bits)
            )
            return ref.at[lead + index + (slice(None), columns)]

        class Chain:
            def __init__(self, src, ref, lead, order, columns):
                self.src, self.ref, self.lead, self.columns = src, ref, lead, columns
                self.order = list(order)
                self.gathered = set()
                self.copy = self.bit = None
                self.done = False

            def step(self):
                if self.done:
                    return
                if self.copy is None:
                    self.bit = self.order.pop(0)
                    place = held(self.ref, self.lead, (), self.columns)
                    view = place
                    if self.src is not None:
                        self.src[0]()
                        view = self.src[1].at[:, self.columns]
                    self.copy = push(view, place, self.bit)
                    return
                self.copy.wait_recv()
                self.gathered.add(self.bit)
                if not self.order:
                    self.done = True
                    return
                self.bit = self.order.pop(0)
                view = held(self.ref, self.lead, self.gathered, self.columns)
                self.copy = push(view, view, self.bit)

            def finish(self):
                while not self.done:
                    self.step()

        class Shift:
            def __init__(self, *ends):
                self.ends = list(ends)
                self.copy = None
                self.done = False

            def step(self):
                if self.copy is not None:
                    self.copy.wait_recv()
                    self.copy = None
                if self.ends:
                    self.copy = push(*self.ends.pop(0)())
                else:
                    self.done = True

            def finish(self):
                while not self.done:
                    self.step()

        cut = (hidden_width // 2 + 127) // 128 * 128
        pieces = [pl.ds(0, cut), pl.ds(cut, hidden_width - cut)]
        early = tile + query_width // 2
        full_order = high_bits + (SHARE_BIT, 1, 0)
        steps = {}
        prepared = set()

        def prepare(m):
            if m in prepared:
                return
            prepared.add(m)
            for h in range(2):
                if m == 0:
                    value = w_down[pl.ds(pl.multiple_of(halves[h], 128), hidden_width), :].T
                else:
                    raw[m - 1, h].wait()
                    rows = slice(h * w_query.shape[0], (h + 1) * w_query.shape[0])
                    value = scaled(hid[m - 1, rows, :], 1)
                if h == 0:
                    mlp_held[(m,) + own + everything] = value
                else:
                    mlp_other[m] = value

        steps["q0"] = Chain(None, qkv_held, (), full_order, pl.ds(0, early))
        steps["q1"] = Chain(
            None, qkv_held, (), full_order, pl.ds(early, query_width + tile - early)
        )
        steps["o"] = Chain(None, out_held, (), full_order, pl.ds(0, query_width))
        for m in range(3):
            for p in range(2):
                steps[f"u{2 * m + p}"] = Chain(
                    (functools.partial(prepare, m), mlp_other.at[m]),
                    mlp_held,
                    (m,),
                    (SHARE_BIT,) + high_bits + (1, 0),
                    pieces[p],
                )
        first = pl.ds(0, half)
        far = pl.ds(half, half)
        steps["t"] = Shift(lambda: (tok, tok_all.at[side], None))
        steps["c"] = Shift(
            lambda: (cot, cot_all.at[share, side], SHARE_BIT),
            lambda: (cot_all.at[:, side], cot_all.at[:, side], None),
        )
        steps["b"] = Shift(lambda: (branch_away, branch_in, None))
        two = normed_two
        steps["nr"] = Shift(
            lambda: (two.at[share, side, :, far], two.at[share, side, :, far], SHARE_BIT),
            lambda: (two.at[:, side, :, far], two.at[:, side, :, far], None),
        )
        steps["nl"] = Shift(
            lambda: (two.at[share, side, :, first], two.at[share, side, :, first], None),
            lambda: (two.at[share, :, :, first], two.at[share, :, :, first], SHARE_BIT),
        )

        own_cot = keep(cot, cot_all.at[share, side])
        own_tok = keep(tok, tok_all.at[side])
        out_copies = []
        works = {}

        def start_all():
            for copy in (own_tok, own_cot):
                copy.wait()
            for m in range(3):
                prepare(m)

        works["W"] = start_all

        def norm():
            steps["t"].finish()

            def norm_rows(r, _):
                rows = pl.ds(pl.multiple_of(r * 16, 16), 16)
                for s in range(2):
                    x = tok_all[s, rows, :].astype(f32)
                    scaled = x * lax.rsqrt(jnp.mean(x * x, axis=-1, keepdims=True) + norm_eps)
                    normed[pl.ds(s * own_rows + r * 16, 16), :] = scaled.astype(bf16)
                return 0

            lax.fori_loop(0, own_rows // 16, norm_rows, 0)

        works["N"] = norm

        lanes = lax.broadcasted_iota(jnp.int32, (group_rows, tile), 1)
        first_half = lanes % HEAD_SIZE < HEAD_SIZE // 2
        lead = (slice(None),) * bit_count + (slice(None),)
        values = {}

        def rotate(a):
            cos2 = jnp.concatenate([cosines[...], cosines[...]], axis=1)
            sin2 = jnp.concatenate([sines[...], sines[...]], axis=1)
            forward = pltpu.roll(a, tile - HEAD_SIZE // 2, 1)
            back = pltpu.roll(a, HEAD_SIZE // 2, 1)
            return a * cos2 + jnp.where(first_half, forward, back) * sin2

        def project(columns):
            weights = qkv_held[lead + (columns,)].reshape(width, tile)
            return jnp.dot(normed[...], weights, preferred_element_type=f32)

        def keys_values():
            steps["q0"].finish()
            first = project(slice(0, tile))
            values["keys"] = rotate(first)[:, :key_width].astype(bf16)
            values["values"] = first[:, key_width:].astype(bf16)
            projected[:, :key_width] = values["keys"]
            projected[:, key_width:tile] = values["values"]

        def queries(i):
            def run():
                if i >= query_width // tile // 2:
                    steps["q1"].finish()
                    if not out_copies:
                        out_copies.append(keep(qkv_held, qkv_full))
                columns = slice(tile + i * tile, tile + (i + 1) * tile)
                rotated = rotate(project(columns)).astype(bf16)
                projected[:, columns] = rotated * jnp.asarray(HEAD_SIZE**-0.5, bf16)

            return run

        works["K"] = keys_values
        for i in range(query_width // tile):
            works[f"Q{i}"] = queries(i)

        rows_tile = 128
        pair_lanes = lax.broadcasted_iota(jnp.int32, (group_rows, 2 * HEAD_SIZE), 1)
        pairs = HEADS_PER_KV // 2
        prob_copies = {}

        def padded(a, head, place):
            moved = a if head == place else pltpu.roll(a, HEAD_SIZE, 1)
            inside = pair_lanes < HEAD_SIZE if place == 0 else pair_lanes >= HEAD_SIZE
            return jnp.where(inside, moved, 0.0).astype(bf16)

        def head_pair(n):
            def run():
                head = n // pairs
                if n % pairs == 0:
                    keys32 = values["keys"].astype(f32)
                    values32 = values["values"].astype(f32)
                    values["at"] = (
                        [padded(keys32, head, p) for p in range(2)],
                        [padded(values32, head, p) for p in range(2)],
                    )
                keys_at, values_at = values["at"]
                slot = n % 2
                if slot in prob_copies:
                    prob_copies[slot].wait()
                columns = slice(tile + n * 128, tile + (n + 1) * 128)
                places = [
                    (low, low + rows_tile, p)
                    for low in range(0, group_rows, rows_tile)
                    for p in range(2)
                ]
                scores = [
                    dot(projected[low:high, columns], keys_at[p][:high], ((1,), (1,)))
                    + bias[low:high, :high]
                    for low, high, p in places
                ]
                peaks = [jnp.max(a, axis=-1, keepdims=True) for a in scores]
                raised = [jnp.exp(a - b) for a, b in zip(scores, peaks)]
                inverses = [1.0 / jnp.sum(a, axis=-1, keepdims=True) for a in raised]
                shares = [(a * b).astype(bf16) for a, b in zip(raised, inverses)]
                for (low, high, p), a in zip(places, shares):
                    prob_stage[slot, p, low:high, :high] = a
                prob_copies[slot] = keep(prob_stage.at[slot], probs.at[pl.ds(2 * n, 2)])
                parts = [
                    jnp.dot(a, values_at[p][:high], preferred_element_type=f32)
                    for (low, high, p), a in zip(places, shares)
                ]
                for j in range(0, len(places), 2):
                    low, high, _ = places[j]
                    mixed = (parts[j] + parts[j + 1]).astype(bf16)
                    attended[low:high, n * 128 : (n + 1) * 128] = mixed

            return run

        for n in range(query_width // 128):
            works[f"A{n}"] = head_pair(n)

        tiles = spread(out_held, bit_count, 512)

        def branch_rows(which, give):
            rows = attended[pl.ds(pl.multiple_of(which * own_rows, 64), own_rows), :]
            for i, (index, count) in enumerate(tiles):
                weights = out_held[index].reshape(count, query_width)
                give(slice(i * count, (i + 1) * count), dot(rows, weights, ((1,), (1,))))

        def give_away(to, value):
            branch_away[:, to] = value.astype(bf16)

        def give_near(to, value):
            middle[:, to] = value

        def branch_first():
            steps["o"].finish()
            out_copies.extend(
                [
                    keep(normed, normed_to),
                    keep(projected, projected_to),
                    keep(attended, attended_to),
                ]
            )
            out_copies.append(keep(out_held, out_full))
            branch_rows(1 - side, give_away)

        works["OA"] = branch_first
        works["ON"] = lambda: branch_rows(side, give_near)

        def middle_all():
            steps["b"].finish()

            def middle_rows(r, _):
                rows = pl.ds(pl.multiple_of(r * 16, 16), 16)
                x = tok[rows, :].astype(f32) + middle[rows, :] + branch_in[rows, :].astype(f32)
                middle[rows, :] = x
                scaled = x * lax.rsqrt(jnp.mean(x * x, axis=-1, keepdims=True) + norm_eps)
                normed_two[share, side, rows, :] = scaled.astype(bf16)
                return 0

            lax.fori_loop(0, own_rows // 16, middle_rows, 0)
            out_copies.append(keep(middle, middle_to))

        works["M"] = middle_all

        bounds = [(0, cut), (cut, hidden_width)]

        def spans(p):
            start, end = bounds[p]
            return [(low, min(low + 512, end)) for low in range(start, end, 512)]

        mlp_lead = (slice(None),) * (bit_count + 1)

        def mlp_product(m, rows_ref, quarter, low, high):
            weights = mlp_held[(m,) + mlp_lead + (slice(low, high),)].reshape(width, high - low)
            return jnp.dot(
                rows_ref[quarter].reshape(group_rows, width), weights, preferred_element_type=f32
            )

        def rows_of(quarter):
            return slice(quarter * group_rows, (quarter + 1) * group_rows)

        prepared_out = set()

        def store_product(m, p, slot, rows_ref, *needed):
            def run():
                for name in (f"u{2 * m + p}",) + needed:
                    steps[name].finish()
                if m == 0:
                    columns = (slice(None),) * (bit_count + 1) + (pieces[p],)
                    out_copies.append(keep(mlp_held.at[(0,) + columns], down_full.at[columns]))
                if slot not in prepared_out:
                    prepared_out.add(slot)
                    target = cot_all_to if m == 0 else normed_two_to
                    out_copies.append(keep(rows_ref, target))
                for low, high in spans(p):
                    for quarter in range(2):
                        value = mlp_product(m, rows_ref, quarter, low, high)
                        hid[slot, rows_of(quarter), low:high] = value.astype(bf16)

            return run

        def up_product(p):
            def run():
                steps[f"u{4 + p}"].finish()
                for low, high in spans(p):
                    for quarter in range(2):
                        up = mlp_product(2, normed_two, quarter, low, high)
                        at = rows_of(quarter)
                        gate = hid[0, at, low:high].astype(f32)
                        grad_hidden = hid[2, at, low:high].astype(f32)
                        sig = jax.nn.sigmoid(gate)
                        silu = gate * sig
                        slope = sig + silu * (1.0 - sig)
                        hid[0, at, low:high] = (silu * up).astype(bf16)
                        hid[1, at, low:high] = (grad_hidden * up * slope).astype(bf16)
                        hid[2, at, low:high] = (grad_hidden * silu).astype(bf16)
                columns = (slice(None), slice(None), pieces[p])
                out_copies.append(keep(hid.at[columns], hid_to.at[columns]))

            return run

        mlp_tiles = spread(mlp_held.at[0], bit_count, 512)
        tall = 2 * own_rows
        opened = set()

        def mlp_back(p, parts, target):
            columns = slice(*bounds[p])
            count_of = bounds[p][1] - bounds[p][0]

            def run():
                again = id(target) in opened
                opened.add(id(target))
                for i, (index, count) in enumerate(mlp_tiles):
                    to = slice(i * count, (i + 1) * count)
                    inner = (slice(None),) * (bit_count + 1 - len(index)) + (columns,)
                    for r in range(2):
                        at = slice(r * tall, (r + 1) * tall)
                        total = target[at, to].astype(f32) if again else None
                        for m, slot in parts:
                            weights = mlp_held[(m,) + index + inner].reshape(count, count_of)
                            term = dot(hid[slot, at, columns], weights, ((1,), (1,)))
                            total = term if total is None else total + term
                        target[at, to] = total.astype(bf16)
                    if again:
                        full = (slice(None), pl.ds(i * count, count))
                        out_copies.append(keep(target.at[full], grad_part_to.at[full]))

            return run

        for p, suffix in enumerate("ab"):
            works["DH" + suffix] = store_product(0, p, 2, cot_all, "c")
            works["G" + suffix] = store_product(1, p, 0, normed_two, "nl", "nr")
            works["U" + suffix] = up_product(p)
            works["E" + suffix] = mlp_back(p, ((1, 1), (2, 2)), grad_part)

        for name in FORWARD_ORDER:
            if name in works:
                works[name]()
            else:
                steps[name].step()
        for name in steps:
            steps[name].finish()
        for copy in out_copies + list(prob_copies.values()):
            copy.wait()
        for copy in started:
            copy.wait_send()

    def call(
        tok,
        cot,
        w_query,
        key_value,
        w_out,
        w_gateup,
        w_down,
        gains,
        cosines,
        sines,
        bias,
    ):
        bf16, f32 = jnp.bfloat16, jnp.float32
        own_rows, width = tok.shape
        block, query_width = w_query.shape
        qkv_width = query_width + 2 * key_value.shape[2]
        mlp_width = w_gateup.shape[2] // 2
        rows = 2 * own_rows
        twos = (2,) * bit_count
        heads = query_width // HEAD_SIZE
        whole = pl.BlockSpec(memory_space=pltpu.VMEM)
        away = pl.BlockSpec(memory_space=pl.ANY)
        count = 10 * (bit_count + 1) + 16
        shape = jax.ShapeDtypeStruct
        return pl.pallas_call(
            kernel,
            out_shape=[
                shape(twos + (block, qkv_width), bf16),
                shape(twos + (block, query_width), bf16),
                shape((heads, rows, rows), bf16),
                shape((rows, width), bf16),
                shape((rows, qkv_width), bf16),
                shape((rows, query_width), bf16),
                shape((own_rows, width), f32),
                shape((2, 2, own_rows, width), bf16),
                shape((2, 2, own_rows, width), bf16),
                shape((3, 2 * rows, mlp_width), bf16),
                shape((2 * rows, width), bf16),
                shape(twos + (block, mlp_width), bf16),
            ],
            in_specs=[whole, away, whole, whole, whole, away] + [whole] * 5,
            out_specs=[away] * 12,
            scratch_shapes=[
                pltpu.VMEM((rows, width), bf16),
                pltpu.VMEM((rows, qkv_width), bf16),
                pltpu.VMEM((rows, query_width), bf16),
                pltpu.VMEM((own_rows, width), f32),
                pltpu.VMEM((2, 2, own_rows, width), bf16),
                pltpu.VMEM((2, 2, own_rows, width), bf16),
                pltpu.VMEM((3, 2 * rows, mlp_width), bf16),
                pltpu.VMEM((2 * rows, width), bf16),
                pltpu.VMEM(twos + (block, qkv_width), bf16),
                pltpu.VMEM(twos + (block, query_width), bf16),
                pltpu.VMEM((3,) + twos + (block, mlp_width), bf16),
                pltpu.VMEM((2, own_rows, width), bf16),
                pltpu.VMEM((own_rows, width), bf16),
                pltpu.VMEM((own_rows, width), bf16),
                pltpu.VMEM((2, 2, rows, rows), bf16),
                pltpu.VMEM((3, block, mlp_width), bf16),
                pltpu.VMEM((2, block, 128), f32),
                pltpu.SemaphoreType.DMA((count,)),
                pltpu.SemaphoreType.DMA((count,)),
                pltpu.SemaphoreType.DMA((40 + heads,)),
            ],
            compiler_params=pltpu.CompilerParams(
                collective_id=1, has_side_effects=True, vmem_limit_bytes=63 * 1024 * 1024
            ),
            name="forward",
        )(
            tok,
            cot,
            w_query,
            key_value,
            w_out,
            w_gateup,
            w_down,
            gains,
            cosines,
            sines,
            bias,
        )

    return call


def make_backward(dp_size, high_bits):
    bit_count = dp_size.bit_length() - 1
    all_bits = tuple(range(bit_count))
    folded = tuple(k for k in reversed(all_bits) if k != CORE_BIT)
    low_order = tuple(range(1, SHARE_BIT)) + high_bits[::-1]
    qkv_order = (1, SHARE_BIT) + high_bits[::-1]
    out_orders = ((1, SHARE_BIT) + high_bits[::-1], (SHARE_BIT,) + high_bits[::-1] + (1,))
    step_count = len(low_order)

    def kernel(
        normed_two,
        cot_all,
        hid,
        grad_part,
        down_full,
        middle_in,
        tok,
        cot,
        out_full,
        qkv_full,
        normed,
        projected_in,
        probs,
        attended_in,
        cosines,
        sines,
        w_query,
        key_value,
        w_gateup,
        gains,
        result,
        input_grad,
        query_grad,
        keyval_grad,
        out_grad,
        gateup_grad,
        down_grad,
        gain_grads,
        *rest,
    ):
        mlp_steps = [list(rest[m * step_count : (m + 1) * step_count]) for m in range(3)]
        (
            recv_stage,
            out_part,
            away_slots,
            mlp_core,
            mlp_last,
            qkv_core,
            out_core,
            quad_in,
            quad_step,
            quad_near,
            middle,
            grad_middle,
            grad_branch,
            norm_away,
            norm_in,
            stage,
            down_held,
            out_sum,
            weight_stage,
            gain_sums,
            gain_in,
            gain_columns,
            send_sem,
            recv_sem,
            local_sem,
        ) = rest[3 * step_count : 3 * step_count + 25]
        steps = list(rest[3 * step_count + 25 :])
        qkv_steps, others_of = steps[: len(qkv_order)], steps[len(qkv_order) :]
        out_steps = (others_of, others_of)
        f32, bf16 = jnp.float32, jnp.bfloat16
        me = lax.axis_index("dp")
        side = lax.axis_index("tensor")
        bits = [(me // 2**k) % 2 for k in all_bits]
        others = [1 - b for b in bits]
        core, share = bits[CORE_BIT], bits[SHARE_BIT]
        core_other, share_other, side_other = others[CORE_BIT], others[SHARE_BIT], 1 - side
        own_rows, width = tok.shape
        half = width // 2
        rows = 2 * own_rows
        query_width = attended_in.shape[1]
        key_width = (projected_in.shape[1] - query_width) // 2
        tile = 2 * key_width
        block = width // dp_size

        partners = {k: {"dp": me + (1 - 2 * bits[k]) * 2**k} for k in all_bits}
        partners[None] = {"tensor": side_other}

        barrier = pltpu.get_barrier_semaphore()
        for k in all_bits + (None,):
            pl.semaphore_signal(barrier, inc=1, device_id=partners[k], device_id_type=MESH)
        pl.semaphore_wait(barrier, bit_count + 1)

        counter, local_counter = [0], [0]
        unsent = []

        class Push:
            def __init__(self, ends, k):
                self.ends, self.k, self.i = ends, k, counter[0]
                counter[0] += 1
                self.copy().start()
                unsent.append(self)

            def copy(self):
                src, dst = self.ends()
                return pltpu.make_async_remote_copy(
                    src_ref=src,
                    dst_ref=dst,
                    send_sem=send_sem.at[self.i],
                    recv_sem=recv_sem.at[self.i],
                    device_id=partners[self.k],
                    device_id_type=MESH,
                )

            def wait_recv(self):
                self.copy().wait_recv()

        def sent(push):
            push.copy().wait_send()
            unsent[:] = [other for other in unsent if other is not push]

        def keep(src, dst):
            i = local_counter[0]
            local_counter[0] += 1
            copy = pltpu.make_async_copy(src, dst, local_sem.at[i])
            copy.start()
            return copy

        def cells(lead):
            return [tuple((i >> (lead - 1 - j)) & 1 for j in range(lead)) for i in range(2**lead)]

        def strips(count, size, work):
            def step(r, _):
                work(pl.ds(pl.multiple_of(r * size, size), size))
                return 0

            lax.fori_loop(0, count // size, step, 0)

        def half_grad(left, right, which, give):
            lead = bit_count - 1
            kept = 0
            while block * 2**kept < 256 and kept < lead:
                kept += 1
            for i in range(2 ** (lead - kept)):
                parts = []
                for j in range(2**kept):
                    pair = (i * 2**kept + j) * 2 * block
                    if block % 128 == 0:
                        at = pl.multiple_of(pair + which * block, 128)
                        parts.append(left[:, pl.ds(at, block)])
                    else:
                        low = left[:, pair : pair + block].astype(f32)
                        high = left[:, pair + block : pair + 2 * block].astype(f32)
                        parts.append(jnp.where(which == 0, low, high).astype(bf16))
                columns = jnp.concatenate(parts, axis=1)
                product = dot(columns, right[...], ((0,), (0,)))
                index = tuple((i >> (lead - kept - 1 - j)) & 1 for j in range(lead - kept))
                give(index, product.reshape((2,) * kept + (block, product.shape[-1])))

        class Product:
            def __init__(self, ref, lead):
                self.ref, self.lead, self.copy = ref, lead, None

            def away(self, left, right, slot):
                def give(index, value):
                    slot[index] = value.astype(bf16)

                half_grad(left, right, core_other, give)
                self.slot = slot

            def start(self):
                slot, ref, lead = self.slot, self.ref, self.lead
                self.copy = Push(lambda: (slot, ref.at[lead] if lead else ref), CORE_BIT)

            def near(self, left, right):

                def give(index, value):
                    at = self.lead + index
                    self.ref[at] = (value + self.ref[at].astype(f32)).astype(bf16)

                half_grad(left, right, core, give)

        class Fold:
            def __init__(self, ref, lead, start, size, steps, order, staged):
                self.ref, self.lead = ref, lead
                self.start, self.size = start, size
                self.steps = dict(zip(order, steps))
                self.order = list(order)
                self.staged = staged
                self.settled = {}
                self.copy = self.bit = None

            def place(self, cell):
                rest = iter(cell)
                return self.lead + tuple(
                    self.settled[k] if k in self.settled else next(rest) for k in folded
                )

            def open(self):
                return len(folded) - len(self.settled)

            def rows(self):
                return (pl.ds(self.start, self.size),)

            def send(self):
                self.bit = self.order.pop(0)
                self.settled[self.bit] = others[self.bit]
                twice = (pl.ds(0, 2),) * self.open()
                place = self.place(twice) + self.rows()
                target, there = self.steps[self.bit], twice + self.rows()
                self.copy = Push(lambda: (self.ref.at[place], target.at[there]), self.bit)
                self.settled[self.bit] = bits[self.bit]

            def add(self, last=None, loaded=None):
                self.copy.wait_recv()
                arrived, lead = self.steps[self.bit], ()
                if self.staged:
                    there = (pl.ds(0, 2),) * self.open() + self.rows()
                    lead = (0,) * (len(folded) - 1 - self.open())
                    keep(arrived.at[there], recv_stage.at[lead + there]).wait()
                    arrived = recv_stage
                if loaded is not None:
                    loaded.wait()
                for cell in cells(self.open()):
                    place = self.place(cell)

                    def work(r, _, cell=cell, place=place):
                        at = pl.ds(pl.multiple_of(self.start + r * 16, 16), 16)
                        new, old = arrived[lead + cell + (at,)], self.ref[place + (at,)]
                        if last is None:
                            self.ref[place + (at,)] = new + old
                        else:
                            last(cell, at, new.astype(f32) + old.astype(f32))
                        return 0

                    lax.fori_loop(0, self.size // 16, work, 0)

            def step(self):
                self.add()
                self.send()

        class Walk:
            def __init__(self, *actions):
                self.actions = list(actions)
                self.taken = 0

            def step(self):
                if self.actions:
                    self.taken += 1
                    self.actions.pop(0)()

            def finish(self):
                while self.actions:
                    self.step()

        steps, works, done, pushes = {}, {}, set(), {}

        def do(name):
            if name not in done:
                done.add(name)
                works[name]()

        def once(name, ends, k, after):
            def start():
                do(after)
                pushes[name] = Push(ends, k)

            steps[name] = Walk(start, lambda: pushes[name].wait_recv())

        near_loads = {}

        def load_near(slot, p):
            n = local_counter[0]
            local_counter[0] += 1

            def copy():
                if p == 0:
                    view = grad_part.at[share, :, :, pl.ds(0, half)]
                else:
                    view = grad_part.at[:, side, :, pl.ds(half, half)]
                return pltpu.make_async_copy(view, quad_near.at[p], local_sem.at[n])

            copy().start()
            near_loads[slot, p] = copy

        def quad_half(name, slot, p):
            source = (grad_part, out_part)[slot]
            first_bit, second_bit = ((SHARE_BIT, None), (None, SHARE_BIT))[p]
            there = (side_other, share_other)[p]

            def first():
                if slot == 1:
                    do("O")

                def ends():
                    if p == 0:
                        view = source.at[share_other, :, :, pl.ds(0, half)]
                    else:
                        view = source.at[:, side_other, :, pl.ds(half, half)]
                    return view, quad_in.at[slot, p]

                pushes[name] = Push(ends, first_bit)

            def second():
                pushes[name].wait_recv()
                if slot == 0:
                    near_loads[slot, p]().wait()
                for q in range(2):

                    def work(at, q=q):
                        if slot == 0:
                            near = quad_near[p, q, at, :]
                        elif p == 0:
                            near = out_part[share, q, at, :half]
                        else:
                            near = out_part[q, side, at, half:]
                        quad_in[slot, p, q, at, :] = quad_in[slot, p, q, at, :] + near

                    strips(own_rows, 16, work)
                pushes[name] = Push(
                    lambda: (quad_in.at[slot, p, there], quad_step.at[slot, p]), second_bit
                )

            steps[name] = Walk(first, second, lambda: pushes[name].wait_recv())

        def quad_value(slot, at):
            halves = []
            for p, here in ((0, side), (1, share)):
                halves.append(
                    quad_in[slot, p, here, at, :].astype(f32) + quad_step[slot, p, at, :].astype(f32)
                )
            return jnp.concatenate(halves, axis=-1)

        quad_half("el", 0, 0)
        quad_half("er", 0, 1)
        quad_half("ol", 1, 0)
        quad_half("or", 1, 1)
        load_near(0, 0)
        load_near(0, 1)
        middle_load = keep(middle_in, middle)

        part = block // 2
        mlp_products = [Product(mlp_core, (m,)) for m in range(3)]
        mlp_folds = [
            Fold(mlp_core, (m,), p * part, part, mlp_steps[m], low_order, True)
            for m in range(3)
            for p in range(2)
        ]
        qkv_product = Product(qkv_core, ())
        out_product = Product(out_core, ())
        qkv_folds = [Fold(qkv_core, (), p * part, part, qkv_steps, qkv_order, False) for p in range(2)]
        out_folds = [Fold(out_core, (), p * part, part, out_steps[p], out_orders[p], False) for p in range(2)]
        mlp_copies = [None] * 6
        stage_copies = [None, None]
        stage_count = [0]

        def to_output(fill, dst):
            i = stage_count[0] % 2
            stage_count[0] += 1
            if stage_copies[i] is not None:
                stage_copies[i]().wait()
            fill(i)
            n = local_counter[0]
            local_counter[0] += 1

            def copy():
                return pltpu.make_async_copy(stage.at[i], dst(), local_sem.at[n])

            copy().start()
            stage_copies[i] = copy

        hidden_width = hid.shape[-1]
        own_half = pl.multiple_of(share * hidden_width, 128)
        other_half = pl.multiple_of(share_other * hidden_width, 128)
        gain_sums[1] = jnp.zeros_like(gain_sums[1])
        spread_gains(gains, gain_columns)

        def weight_rows(m, rows_of, start):
            columns = pl.ds(start, hidden_width)
            return keep(w_gateup.at[m - 1, rows_of, columns], weight_stage.at[rows_of])

        def give_rows(m, i, at, total):
            if m == 0:
                down_held[i, at, :] = total
                return
            local = pl.ds(pl.multiple_of(at.start % part, 16), 16)
            stage[i, local, :] = total * gain_columns[1, at, :][:, :1]
            weighted = total * weight_stage[at, :].astype(f32)
            gain_sums[1, at, :] += jnp.sum(weighted, axis=-1, keepdims=True)

        def mlp_share(u):
            m, fold = u // 2, mlp_folds[u]
            rows_of = pl.ds(fold.start, fold.size)
            loaded = weight_rows(m, rows_of, own_half) if m > 0 else None

            def fill(i):
                def last(cell, at, total):
                    is_own = share == cell[0]

                    @pl.when(is_own)
                    def _():
                        give_rows(m, i, at, total)

                    @pl.when(jnp.logical_not(is_own))
                    def _():
                        mlp_last[m, 0, at, :] = total.astype(bf16)

                fold.add(last, loaded)

            if m == 0:
                fill(0)
            else:
                columns = pl.ds(own_half, hidden_width)
                to_output(fill, lambda: gateup_grad.at[m - 1, rows_of, columns])
            mlp_copies[u] = Push(
                lambda: (mlp_last.at[m, 0, rows_of], mlp_last.at[m, 1, rows_of]), SHARE_BIT
            )

        def mlp_finish(u):
            m, fold = u // 2, mlp_folds[u]
            rows_of = pl.ds(fold.start, fold.size)
            loaded = weight_rows(m, rows_of, other_half) if m > 0 else None
            mlp_copies[u].wait_recv()
            if loaded is not None:
                loaded.wait()

            def fill(i):
                def work(r, _):
                    at = pl.ds(pl.multiple_of(fold.start + r * 16, 16), 16)
                    give_rows(m, i, at, mlp_last[m, 1, at, :].astype(f32))
                    return 0

                lax.fori_loop(0, fold.size // 16, work, 0)

            if m == 0:
                fill(1)
            else:
                columns = pl.ds(other_half, hidden_width)
                to_output(fill, lambda: gateup_grad.at[m - 1, rows_of, columns])

        def out_rows(cell, at, total):
            out_sum[at, :] = total

        def qkv_rows(cell, at, total):
            gain = gain_columns[0, at, :][:, :1]
            parts = [total[:, :key_width], total[:, key_width:tile], total[:, tile:]]
            weights = [key_value[0, at, :], key_value[1, at, :], w_query[at, :]]
            row_sum = sum(
                jnp.sum(p * w.astype(f32), axis=-1, keepdims=True) for p, w in zip(parts, weights)
            )
            gain_sums[0, at, :] = jnp.broadcast_to(row_sum, (16, 128))
            keyval_grad[0, at, :] = parts[0] * gain
            keyval_grad[1, at, :] = parts[1] * gain
            query_grad[at, :] = parts[2] * gain

        def walk_fold(name, fold, after, *ends):
            def start():
                do(after)
                fold.send()

            steps[name] = Walk(start, *([fold.step] * (len(fold.order) - 1)), *ends)

        for u in range(6):
            walk_fold(
                f"f{u}",
                mlp_folds[u],
                f"B{u // 2}",
                functools.partial(mlp_share, u),
                functools.partial(mlp_finish, u),
            )
        for p in range(2):
            for name, fold, after, last in (
                (f"p{p}", out_folds[p], "OB", out_rows),
                (f"q{p}", qkv_folds[p], "QB", qkv_rows),
            ):
                walk_fold(name, fold, after, functools.partial(fold.add, last))

        def walk_core(name, product, after):
            def start():
                do(after)
                product.start()

            steps[name] = Walk(start, lambda: product.copy.wait_recv())

        for m in range(3):
            walk_core(f"K{m}", mlp_products[m], f"W{m}")
        walk_core("KO", out_product, "OA")
        walk_core("KQ", qkv_product, "QA")
        once("D", lambda: (grad_branch.at[side], grad_branch.at[side]), None, "MR")
        once("N", lambda: (norm_away, norm_in), None, "NA")

        def follow(order):
            for name in order:
                if name in works:
                    do(name)
                else:
                    steps[name].step()

        def first_phase(held_rows, held_cot, held_hid, held_down):
            loads = [
                keep(cot_all, held_cot),
                keep(hid.at[0], held_hid.at[0]),
                keep(normed_two, held_rows),
                keep(hid.at[1], held_hid.at[1]),
            ]
            waited = set()

            def ready(*numbers):
                for n in numbers:
                    if n not in waited:
                        waited.add(n)
                        loads[n].wait()

            sources = [
                (held_cot, held_hid.at[0], away_slots.at[0], (0, 1)),
                (held_rows, held_hid.at[1], away_slots.at[1], (2, 3)),
                (held_rows, held_hid.at[1], away_slots.at[0], (2, 4)),
            ]

            def away_work(m):
                def run():
                    left, right, slot, numbers = sources[m]
                    if m == 2:
                        do("B1")
                        loads.append(keep(hid.at[2], held_hid.at[1]))
                        sent(mlp_products[0].copy)
                    ready(*numbers)
                    mlp_products[m].away(left, right, slot)

                return run

            def near_work(m):
                def run():
                    steps[f"K{m}"].finish()
                    mlp_products[m].near(*sources[m][:2])

                return run

            for m in range(3):
                works[f"W{m}"] = away_work(m)
                works[f"B{m}"] = near_work(m)
            down_tiles = spread(down_full, bit_count, 512)

            def down_load(i):
                return keep(down_full.at[down_tiles[i][0]], held_down.at[i % 2])

            down_first = down_load(0)

            def out_product_rows():
                ready(1)
                load = down_first
                for i, (index, count) in enumerate(down_tiles):
                    load.wait()
                    if i + 1 < len(down_tiles):
                        load = down_load(i + 1)
                    to = slice(i * count, (i + 1) * count)
                    weights = held_down[i % 2].reshape(count, hidden_width)
                    for zone in range(2):
                        at = slice(zone * rows, (zone + 1) * rows)
                        value = dot(held_hid[0, at, :], weights, ((1,), (1,))).astype(bf16)
                        out_part[zone, :, :, to] = value.reshape(2, own_rows, count)

            works["O"] = out_product_rows
            follow(BACKWARD_ORDER[:phase_at])
            for name in ("B0", "B1", "B2", "O"):
                do(name)
            for m in (1, 2):
                sent(mlp_products[m].copy)

        phase_at = BACKWARD_ORDER.index("MR")
        tile_shape = down_full.shape[len(spread(down_full, bit_count, 512)[0][0]) :]
        pl.run_scoped(
            first_phase,
            pltpu.VMEM(normed_two.shape, bf16),
            pltpu.VMEM(cot_all.shape, bf16),
            pltpu.VMEM((2,) + hid.shape[1:], bf16),
            pltpu.VMEM((2,) + tile_shape, bf16),
        )

        def second_phase(
            weights, held_probs, projected, attended, grad_att, grad_qkv, acc, turned
        ):
            qkv_width = query_width + tile
            lead_all = (slice(None),) * (bit_count + 1)
            loads = {
                "out": keep(out_full, weights.at[lead_all + (pl.ds(0, query_width),)]),
                "probs": keep(probs.at[pl.ds(0, HEADS_PER_KV)], held_probs),
                "projected": keep(projected_in, projected),
                "attended": keep(attended_in, attended),
            }

            def ready(*names):
                for name in names:
                    if name in loads:
                        loads.pop(name).wait()

            def middle_work():
                middle_load.wait()
                steps["el"].finish()
                steps["er"].finish()

                def middle_rows(at):
                    x = middle[at, :]
                    total = cot[at, :].astype(f32) + rms_grad(x, rms(x), quad_value(0, at))
                    grad_middle[at, :] = total
                    grad_branch[side, at, :] = total.astype(bf16)

                strips(own_rows, 16, middle_rows)

            works["MR"] = middle_work
            branch_flat = BranchView()
            slots = [
                away_slots.at[(i,) + (slice(None),) * bit_count + (pl.ds(0, columns),)]
                for i, columns in ((0, qkv_width), (1, query_width))
            ]

            def attended_grad():
                steps["D"].finish()
                ready("out")
                branch_all = grad_branch[...].reshape(rows, width)
                for low in range(0, query_width, 256):
                    block_of = weights[lead_all + (slice(low, low + 256),)].reshape(width, 256)
                    grad_att[:, low : low + 256] = jnp.dot(
                        branch_all, block_of, preferred_element_type=f32
                    ).astype(bf16)
                loads["qkv"] = keep(qkv_full, weights)

            works["DA"] = attended_grad

            def out_away():
                steps["D"].finish()
                ready("attended")
                out_product.away(branch_flat, attended, slots[1])

            def out_near():
                steps["KO"].finish()
                out_product.near(branch_flat, attended)
                sent(pushes["D"])
                loads["normed"] = keep(normed, grad_branch)

            works["OA"] = out_away
            works["OB"] = out_near

            pair_lanes = lax.broadcasted_iota(jnp.int32, (rows, 2 * HEAD_SIZE), 1)
            lanes = lax.broadcasted_iota(jnp.int32, (rows, key_width), 1)
            first_half = lanes % HEAD_SIZE < HEAD_SIZE // 2

            def padded(a, head, place):
                moved = a if head == place else pltpu.roll(a, HEAD_SIZE, 1)
                inside = pair_lanes < HEAD_SIZE if place == 0 else pair_lanes >= HEAD_SIZE
                return jnp.where(inside, moved, 0.0).astype(bf16)

            def unrotate(a):
                forward = pltpu.roll(a, key_width - HEAD_SIZE // 2, 1)
                back = pltpu.roll(a, HEAD_SIZE // 2, 1)
                return a * cosines[...] - jnp.where(first_half, forward, back) * sines[...]

            heads = key_width // HEAD_SIZE
            pairs = HEADS_PER_KV // 2
            tile_rows = 128
            lane_tile = lax.broadcasted_iota(jnp.int32, (tile_rows, 2 * HEAD_SIZE), 1)
            totals = []
            heads_at = {}

            def head_pair(n):
                def run():
                    head, i = n // pairs, n % pairs
                    if i == 0:
                        do("DA")
                        ready("probs", "projected")
                        if head > 0:
                            first = head * HEADS_PER_KV
                            keep(probs.at[pl.ds(first, HEADS_PER_KV)], held_probs).wait()
                        keys32 = projected[:, :key_width].astype(f32)
                        values32 = projected[:, key_width:tile].astype(f32)
                        heads_at["keys"] = [padded(keys32, head, p) for p in range(2)]
                        heads_at["values"] = [padded(values32, head, p) for p in range(2)]
                        acc[...] = jnp.zeros_like(acc)
                    keys_at, values_at = heads_at["keys"], heads_at["values"]
                    columns = slice(n * 128, (n + 1) * 128)
                    query_columns = slice(tile + n * 128, tile + (n + 1) * 128)
                    places = [
                        (low, low + tile_rows, p)
                        for low in range(0, rows, tile_rows)
                        for p in range(2)
                    ]
                    insides = [lane_tile < HEAD_SIZE, lane_tile >= HEAD_SIZE]
                    prob = [
                        held_probs[2 * i + p, low:high, :high] for low, high, p in places
                    ]
                    grad_prob = [
                        dot(grad_att[low:high, columns], values_at[p][:high], ((1,), (1,)))
                        for low, high, p in places
                    ]
                    prob32 = [a.astype(f32) for a in prob]
                    weighted = [a * b for a, b in zip(prob32, grad_prob)]
                    centre = [jnp.sum(a, axis=-1, keepdims=True) for a in weighted]
                    grad_score = [
                        (a - b * c).astype(bf16) for a, b, c in zip(weighted, prob32, centre)
                    ]
                    grad_query = [
                        jnp.dot(a, keys_at[p][:high], preferred_element_type=f32)
                        for a, (low, high, p) in zip(grad_score, places)
                    ]
                    for j, (low, high, p) in enumerate(places):
                        query = projected[low:high, query_columns].astype(f32)
                        only_query = jnp.where(insides[p], query, 0.0).astype(bf16)
                        out32 = grad_att[low:high, columns].astype(f32)
                        only_grad = jnp.where(insides[p], out32, 0.0).astype(bf16)
                        acc[0, :high, :] += dot(grad_score[j], only_query, ((0,), (0,)))
                        acc[1, :high, :] += dot(prob[j], only_grad, ((0,), (0,)))
                        if p == 1:
                            total = grad_query[j - 1] + grad_query[j]
                            acc[2, low:high, :] = total * HEAD_SIZE**-0.5
                    grad_qkv[:, query_columns] = unrotate(acc[2]).astype(bf16)
                    if i == pairs - 1:
                        totals.append([acc[j] + pltpu.roll(acc[j], HEAD_SIZE, 1) for j in range(2)])

                return run

            for n in range(query_width // 128):
                works[f"T{n}"] = head_pair(n)

            def qkv_away():
                lower = pair_lanes < HEAD_SIZE
                grad_keys = unrotate(jnp.where(lower, totals[0][0], totals[1][0]))
                grad_qkv[:, :key_width] = grad_keys.astype(bf16)
                grad_values = jnp.where(lower, totals[0][1], totals[1][1])
                grad_qkv[:, key_width:tile] = grad_values.astype(bf16)
                ready("normed")
                qkv_product.away(branch_flat, grad_qkv, slots[0])

            def qkv_near():
                steps["KQ"].finish()
                qkv_product.near(branch_flat, grad_qkv)

            works["QA"] = qkv_away
            works["QB"] = qkv_near
            tiles = spread(weights, bit_count, 512)

            def norm_part(which, give):
                ready("qkv")
                at = pl.ds(pl.multiple_of(which * own_rows, 64), own_rows)
                chosen = grad_qkv[at, :]
                for i, (index, count) in enumerate(tiles):
                    block_of = weights[index].reshape(count, qkv_width)
                    give(slice(i * count, (i + 1) * count), dot(chosen, block_of, ((1,), (1,))))

            def give_away(to, value):
                norm_away[:, to] = value.astype(bf16)

            def give_near(to, value):
                middle[:, to] = value

            works["NA"] = lambda: norm_part(side_other, give_away)

            def result_work():
                steps["ol"].finish()
                steps["or"].finish()

                def result_rows(at):
                    result[at, :] = (middle[at, :] + quad_value(1, at)).astype(bf16)

                strips(own_rows, 16, result_rows)

            works["RR"] = result_work

            def near_rows():
                do("RR")
                norm_part(side, give_near)

            works["NB"] = near_rows

            def input_work():
                do("NB")
                steps["N"].finish()

                def input_rows(at):
                    x = tok[at, :].astype(f32)
                    scaled = middle[at, :] + norm_in[at, :].astype(f32)
                    total = grad_middle[at, :] + rms_grad(x, rms(x), scaled)
                    input_grad[at, :] = total.astype(bf16)

                strips(own_rows, 16, input_rows)

            works["IR"] = input_work

            def turn_down():
                steps["f0"].finish()
                steps["f1"].finish()
                for h, start in ((0, own_half), (1, other_half)):
                    if h == 1:
                        turn_copies.pop().wait()
                    turned[...] = down_held[h].T
                    turn_copies.append(keep(turned, down_grad.at[pl.ds(start, hidden_width)]))

            def turn_out():
                steps["p0"].finish()
                steps["p1"].finish()
                out_grad[...] = out_sum[...].T

            turn_copies = []
            works["TD"] = turn_down
            works["TO"] = turn_out
            follow(BACKWARD_ORDER[phase_at:])
            for name in works:
                do(name)
            for product in (out_product, qkv_product):
                sent(product.copy)
            for copy in turn_copies:
                copy.wait()

        class BranchView:
            def __getitem__(self, index):
                return grad_branch[(slice(None), slice(None), index[1])].reshape(rows, -1)

        pl.run_scoped(
            second_phase,
            pltpu.VMEM(qkv_full.shape, bf16),
            pltpu.VMEM((HEADS_PER_KV,) + probs.shape[1:], bf16),
            pltpu.VMEM(projected_in.shape, bf16),
            pltpu.VMEM(attended_in.shape, bf16),
            pltpu.VMEM(attended_in.shape, bf16),
            pltpu.VMEM(projected_in.shape, bf16),
            pltpu.VMEM((3, rows, 2 * HEAD_SIZE), f32),
            pltpu.VMEM((hid.shape[-1], block), f32),
        )

        for name in steps:
            steps[name].finish()
        quarter = block // 2
        there = pl.ds(pl.multiple_of(side_other * quarter, 16), quarter)
        here = pl.ds(pl.multiple_of(side * quarter, 16), quarter)
        exchange = Push(lambda: (gain_sums.at[:, there], gain_in), None)
        exchange.wait_recv()
        gain_grads[...] = gain_sums[:, here, :] + gain_in[...]
        for copy in stage_copies:
            copy().wait()
        for copy in list(unsent):
            sent(copy)

    def call(
        normed_two,
        cot_all,
        hid,
        grad_part,
        down_full,
        middle,
        tok,
        cot,
        out_full,
        qkv_full,
        normed,
        projected,
        probs,
        attended,
        cosines,
        sines,
        w_query,
        key_value,
        w_gateup,
        gains,
    ):
        bf16, f32 = jnp.bfloat16, jnp.float32
        own_rows, width = tok.shape
        half = width // 2
        block, qkv_width = qkv_full.shape[-2:]
        query_width = out_full.shape[-1]
        mlp_width = hid.shape[-1]
        shape = jax.ShapeDtypeStruct
        whole = pl.BlockSpec(memory_space=pltpu.VMEM)
        away = pl.BlockSpec(memory_space=pl.ANY)

        def twos(count):
            return (2,) * count

        slots = [
            shape(twos(bit_count - 2 - i) + (block, mlp_width), bf16) for i in range(step_count)
        ] * 3

        def steps_of(order, columns):
            return [
                pltpu.VMEM(twos(bit_count - 2 - i) + (block, columns), bf16)
                for i in range(len(order))
            ]

        def at_core(columns):
            return twos(bit_count - 1) + (block, columns)

        count = 6 * (step_count + 2) + 6 * bit_count + 24
        outs = pl.pallas_call(
            kernel,
            out_shape=[
                shape((own_rows, width), bf16),
                shape((own_rows, width), bf16),
                shape((block, query_width), f32),
                shape(key_value.shape, f32),
                shape((query_width, block), f32),
                shape(w_gateup.shape, f32),
                shape((2 * mlp_width, block), f32),
                shape((2, block // 2, 128), f32),
            ]
            + slots,
            in_specs=[away] * 6 + [whole] * 2 + [away] * 6 + [whole] * 4 + [away, whole],
            out_specs=[whole] * 5 + [away] * 2 + [whole] + [away] * len(slots),
            scratch_shapes=[
                pltpu.VMEM(twos(bit_count - 2) + (block, mlp_width), bf16),
                pltpu.VMEM((2, 2, own_rows, width), bf16),
                pltpu.VMEM((2,) + at_core(mlp_width), bf16),
                pltpu.VMEM((3,) + at_core(mlp_width), bf16),
                pltpu.VMEM((3, 2, block, mlp_width), bf16),
                pltpu.VMEM(at_core(qkv_width), bf16),
                pltpu.VMEM(at_core(query_width), bf16),
                pltpu.VMEM((2, 2, 2, own_rows, half), bf16),
                pltpu.VMEM((2, 2, own_rows, half), bf16),
                pltpu.VMEM((2, 2, own_rows, half), bf16),
                pltpu.VMEM((own_rows, width), f32),
                pltpu.VMEM((own_rows, width), f32),
                pltpu.VMEM((2, own_rows, width), bf16),
                pltpu.VMEM((own_rows, width), bf16),
                pltpu.VMEM((own_rows, width), bf16),
                pltpu.VMEM((2, block // 2, mlp_width), f32),
                pltpu.VMEM((2, block, mlp_width), f32),
                pltpu.VMEM((block, query_width), f32),
                pltpu.VMEM((block, mlp_width), bf16),
                pltpu.VMEM((2, block, 128), f32),
                pltpu.VMEM((2, block // 2, 128), f32),
                pltpu.VMEM((2, block, 128), f32),
                pltpu.SemaphoreType.DMA((count,)),
                pltpu.SemaphoreType.DMA((count,)),
                pltpu.SemaphoreType.DMA((6 * step_count + 64,)),
            ]
            + steps_of(qkv_order, qkv_width)
            + steps_of(qkv_order, query_width),
            compiler_params=pltpu.CompilerParams(
                collective_id=2, has_side_effects=True, vmem_limit_bytes=63 * 1024 * 1024
            ),
            name="backward",
        )(
            normed_two,
            cot_all,
            hid,
            grad_part,
            down_full,
            middle,
            tok,
            cot,
            out_full,
            qkv_full,
            normed,
            projected,
            probs,
            attended,
            cosines,
            sines,
            w_query,
            key_value,
            w_gateup,
            gains,
        )
        return outs[:8]

    return call


def make_body(dp_size):
    bit_count = dp_size.bit_length() - 1
    high_bits = tuple(range(bit_count - 1, SHARE_BIT, -1))

    def body(
        tokens,
        attn_gain,
        w_query,
        keyvalue_weight,
        w_out,
        mlp_gain,
        w_gateup,
        w_down,
        segment_ids,
        positions,
        cotangent,
    ):
        f32 = jnp.float32
        own_rows, width = tokens.shape

        gains = jnp.stack([attn_gain, mlp_gain]).astype(f32)
        order = jnp.arange(segment_ids.shape[0])
        allowed = (segment_ids[:, None] == segment_ids[None, :]) & (
            order[:, None] >= order[None, :]
        )
        bias = jnp.where(allowed, 0.0, -1e30).astype(f32)

        cosine_table, sine_table = rotary_tables(positions, HEAD_SIZE)
        sine_table = jnp.where(jnp.arange(HEAD_SIZE) < HEAD_SIZE // 2, -sine_table, sine_table)
        cosine_table = jnp.concatenate([cosine_table, cosine_table], axis=1)
        sine_table = jnp.concatenate([sine_table, sine_table], axis=1)
        (
            qkv_full,
            out_full,
            probs,
            normed,
            projected,
            attended,
            middle,
            normed_two,
            grad_all,
            hid,
            grad_part,
            down_full,
        ) = make_forward(dp_size, high_bits)(
            tokens,
            cotangent,
            w_query,
            keyvalue_weight,
            w_out,
            w_gateup,
            w_down,
            gains,
            cosine_table,
            sine_table,
            bias,
        )
        normed_two = normed_two.reshape(4 * own_rows, width)
        grad_all = grad_all.reshape(4 * own_rows, width)

        quad_shape = (2, 2, own_rows, width)
        (
            result,
            input_grad,
            query_grad,
            keyval_grad,
            out_grad,
            gateup_grad,
            down_grad,
            gain_grads,
        ) = make_backward(dp_size, high_bits)(
            normed_two,
            grad_all,
            hid,
            grad_part.reshape(quad_shape),
            down_full,
            middle,
            tokens,
            cotangent,
            out_full,
            qkv_full,
            normed.reshape(2, own_rows, width),
            projected,
            probs,
            attended,
            cosine_table,
            sine_table,
            w_query,
            keyvalue_weight,
            w_gateup,
            gains,
        )
        return (
            result,
            input_grad,
            gain_grads[0, :, 0],
            query_grad,
            keyval_grad,
            out_grad,
            gain_grads[1, :, 0],
            gateup_grad,
            down_grad,
        )

    return body


def solution(mesh):
    return jax.shard_map(
        make_body(mesh.shape["dp"]),
        mesh=mesh,
        in_specs=(
            P(("dp", "tensor"), None),
            P("dp"),
            P("dp", "tensor"),
            P(None, "dp", "tensor"),
            P("tensor", "dp"),
            P("dp"),
            P(None, "dp", "tensor"),
            P("tensor", "dp"),
            P("dp"),
            P("dp"),
            P(("dp", "tensor"), None),
        ),
        out_specs=(
            P(("dp", "tensor"), None),
            P(("dp", "tensor"), None),
            P(("dp", "tensor")),
            P("dp", "tensor"),
            P(None, "dp", "tensor"),
            P("tensor", "dp"),
            P(("dp", "tensor")),
            P(None, "dp", "tensor"),
            P("tensor", "dp"),
        ),
        check_vma=False,
    )
```

```python
import functools
import math

import jax
import jax.numpy as jnp
from jax import lax
from jax.experimental import pallas as pl
from jax.experimental.pallas import tpu as pltpu
from jax.sharding import PartitionSpec as P

MESH = pl.DeviceIdType.MESH

QUERY_HEAD_COUNT = 32
KEYVALUE_HEADS = 4
HEAD_SIZE = 64
HEADS_PER_KV = QUERY_HEAD_COUNT // KEYVALUE_HEADS
norm_eps = 1e-05

CORE_BIT = 0
SHARE_BIT = 2


FORWARD_ORDER = (
    "q1", "u1", "t", "q0", "W", "o", "q1", "q0", "t", "N", "q1", "o", "c", "q0", "q0", "q1", "u2",
    "o", "q0", "u3", "q1", "u0", "u1", "c", "u2", "K", "u1", "Q0", "Q1", "o", "A0", "Q2", "u5",
    "Q3", "A1", "o", "A2", "A3", "u0", "A4", "A5", "u2", "A6", "A7", "OA", "u3", "b", "u0", "u5",
    "ON", "u4", "b", "M", "nr", "u3", "nl", "u2", "u1", "nl", "u4", "u0", "nr", "u5", "u3", "u1",
    "u3", "c", "u0", "DHb", "u4", "DHa", "u5", "u5", "nr", "u2", "nl", "Gb", "Ub", "Eb", "u4", "Ga",
    "u4", "Ua", "Ea",
)

BACKWARD_ORDER = (
    "er", "el", "W0", "K0", "W1", "K1", "K1", "B1", "f2", "er", "K0", "el", "f3", "O", "ol", "or",
    "W2", "K2", "er", "f2", "el", "B0", "K2", "f1", "B2", "MR", "D", "f3", "f0", "f2", "ol", "or",
    "D", "DA", "f1", "f3", "OA", "KO", "KO", "OB", "T0", "T1", "f4", "T2", "T3", "p0", "T4", "f0",
    "p1", "f4", "T5", "f5", "T6", "T7", "ol", "QA", "f1", "p1", "NA", "p0", "KQ", "KQ", "QB", "N",
    "q0", "q1", "f1", "f5", "f4", "or", "p0", "f0", "f3", "f4", "N", "RR", "q0", "p0", "q1", "f5",
    "NB", "IR", "q0", "p1", "f0", "q1", "q0", "p1", "TD", "f2", "TO", "f5", "q1", "X", "X",
)


def rotary_tables(places, width):
    freqs = jnp.exp(jnp.arange(0, width, 2).astype(jnp.float32) * (-math.log(10000.0) / width))
    turned = places.astype(jnp.float32)[:, None] * freqs[None, :]
    turned = jnp.concatenate([turned, turned], axis=-1)
    return (jnp.cos(turned), jnp.sin(turned))


def dot(left, right, contract):
    return lax.dot_general(left, right, (contract, ((), ())), preferred_element_type=jnp.float32)


def rms(rows):
    return lax.rsqrt(jnp.mean(rows * rows, axis=-1, keepdims=True) + norm_eps)


def rms_grad(rows, inverse, grad_scaled):
    inner = jnp.mean(grad_scaled * rows, axis=-1, keepdims=True)
    return inverse * grad_scaled - rows * (inverse * inverse * inverse) * inner


def spread(ref, lead, row_tile):
    sizes = ref.shape
    block = sizes[-2]
    kept = 0
    while block * 2**kept < row_tile and kept < lead:
        kept += 1
    out = []
    for i in range(2 ** (lead - kept)):
        index = tuple((i >> (lead - kept - 1 - j)) & 1 for j in range(lead - kept))
        out.append((index, (block * 2**kept)))
    return out


def spread_gains(gains, columns):
    block = gains.shape[1]
    order = [lax.broadcasted_iota(jnp.int32, (block, block), axis) for axis in range(2)]
    for i in range(gains.shape[0]):
        only = jnp.where(order[0] == order[1], gains[i : i + 1, :], 0.0)
        columns[i] = jnp.broadcast_to(jnp.sum(only, axis=1, keepdims=True), columns.shape[1:])


def make_forward(dp_size, high_bits):
    bit_count = dp_size.bit_length() - 1
    all_bits = tuple(range(bit_count))

    def kernel(
        tok,
        cot,
        w_query,
        key_value,
        w_out,
        w_gateup,
        w_down,
        gains,
        cosines,
        sines,
        bias,
        qkv_full,
        out_full,
        probs,
        normed_to,
        projected_to,
        attended_to,
        middle_to,
        normed_two_to,
        cot_all_to,
        hid_to,
        grad_part_to,
        down_full,
        normed,
        projected,
        attended,
        middle,
        normed_two,
        cot_all,
        hid,
        grad_part,
        qkv_held,
        out_held,
        mlp_held,
        tok_all,
        branch_away,
        branch_in,
        prob_stage,
        mlp_other,
        gain_columns,
        send_sem,
        recv_sem,
        local_sem,
    ):
        f32, bf16 = jnp.float32, jnp.bfloat16
        me = lax.axis_index("dp")
        side = lax.axis_index("tensor")
        bits = [(me // 2**k) % 2 for k in all_bits]
        share = bits[SHARE_BIT]
        own_rows, width = tok.shape
        half = width // 2
        group_rows = 2 * own_rows
        query_width = attended.shape[1]
        key_width = (projected.shape[1] - query_width) // 2
        tile = 2 * key_width
        hidden_width = hid.shape[-1]

        def partner(k):
            if k is None:
                return {"tensor": 1 - side}
            return {"dp": me + (1 - 2 * bits[k]) * 2**k}

        barrier = pltpu.get_barrier_semaphore()
        for k in all_bits + (None,):
            pl.semaphore_signal(barrier, inc=1, device_id=partner(k), device_id_type=MESH)

        own = tuple(bits[k] for k in reversed(all_bits))
        everything = (slice(None), slice(None))
        halves = [pl.multiple_of(h * hidden_width, 128) for h in (share, 1 - share)]
        raw = {}
        for m in range(2):
            for h in range(2):
                block_at = hid.at[m, pl.ds(h * w_query.shape[0], w_query.shape[0])]
                columns = pl.ds(halves[h], hidden_width)
                raw[m, h] = pltpu.make_async_copy(
                    w_gateup.at[m, :, columns], block_at, local_sem.at[2 * m + h]
                )
                raw[m, h].start()

        spread_gains(gains, gain_columns)

        def scaled(a, gain):
            return (a.astype(f32) * gain_columns[gain][:, :1]).astype(bf16)

        qkv_held[own + (slice(None), slice(0, key_width))] = scaled(key_value[0], 0)
        qkv_held[own + (slice(None), slice(key_width, tile))] = scaled(key_value[1], 0)
        qkv_held[own + (slice(None), slice(tile, tile + query_width))] = scaled(
            w_query[...], 0
        )
        out_held[own + everything] = w_out[...].T

        pl.semaphore_wait(barrier, bit_count + 1)

        counter, local_counter = [0], [4]
        started = []

        def push(src, dst, k):
            i = counter[0]
            counter[0] += 1
            copy = pltpu.make_async_remote_copy(
                src_ref=src,
                dst_ref=dst,
                send_sem=send_sem.at[i],
                recv_sem=recv_sem.at[i],
                device_id=partner(k),
                device_id_type=MESH,
            )
            copy.start()
            started.append(copy)
            return copy

        def keep(src, dst):
            i = local_counter[0]
            local_counter[0] += 1
            copy = pltpu.make_async_copy(src, dst, local_sem.at[i])
            copy.start()
            return copy

        def held(ref, lead, gathered, columns):
            index = tuple(
                pl.ds(0, 2) if k in gathered else bits[k] for k in reversed(all_bits)
            )
            return ref.at[lead + index + (slice(None), columns)]

        class Chain:
            def __init__(self, src, ref, lead, order, columns):
                self.src, self.ref, self.lead, self.columns = src, ref, lead, columns
                self.order = list(order)
                self.gathered = set()
                self.copy = self.bit = None
                self.done = False

            def step(self):
                if self.done:
                    return
                if self.copy is None:
                    self.bit = self.order.pop(0)
                    place = held(self.ref, self.lead, (), self.columns)
                    view = place
                    if self.src is not None:
                        self.src[0]()
                        view = self.src[1].at[:, self.columns]
                    self.copy = push(view, place, self.bit)
                    return
                self.copy.wait_recv()
                self.gathered.add(self.bit)
                if not self.order:
                    self.done = True
                    return
                self.bit = self.order.pop(0)
                view = held(self.ref, self.lead, self.gathered, self.columns)
                self.copy = push(view, view, self.bit)

            def finish(self):
                while not self.done:
                    self.step()

        class Shift:
            def __init__(self, *ends):
                self.ends = list(ends)
                self.copy = None
                self.done = False

            def step(self):
                if self.copy is not None:
                    self.copy.wait_recv()
                    self.copy = None
                if self.ends:
                    self.copy = push(*self.ends.pop(0)())
                else:
                    self.done = True

            def finish(self):
                while not self.done:
                    self.step()

        cut = (hidden_width // 2 + 127) // 128 * 128
        pieces = [pl.ds(0, cut), pl.ds(cut, hidden_width - cut)]
        early = tile + query_width // 2
        full_order = high_bits + (SHARE_BIT, 1, 0)
        steps = {}
        prepared = set()

        def prepare(m):
            if m in prepared:
                return
            prepared.add(m)
            for h in range(2):
                if m == 0:
                    value = w_down[pl.ds(pl.multiple_of(halves[h], 128), hidden_width), :].T
                else:
                    raw[m - 1, h].wait()
                    rows = slice(h * w_query.shape[0], (h + 1) * w_query.shape[0])
                    value = scaled(hid[m - 1, rows, :], 1)
                if h == 0:
                    mlp_held[(m,) + own + everything] = value
                else:
                    mlp_other[m] = value

        steps["q0"] = Chain(None, qkv_held, (), full_order, pl.ds(0, early))
        steps["q1"] = Chain(
            None, qkv_held, (), full_order, pl.ds(early, query_width + tile - early)
        )
        steps["o"] = Chain(None, out_held, (), full_order, pl.ds(0, query_width))
        for m in range(3):
            for p in range(2):
                steps[f"u{2 * m + p}"] = Chain(
                    (functools.partial(prepare, m), mlp_other.at[m]),
                    mlp_held,
                    (m,),
                    (SHARE_BIT,) + high_bits + (1, 0),
                    pieces[p],
                )
        first = pl.ds(0, half)
        far = pl.ds(half, half)
        steps["t"] = Shift(lambda: (tok, tok_all.at[side], None))
        steps["c"] = Shift(
            lambda: (cot, cot_all.at[share, side], SHARE_BIT),
            lambda: (cot_all.at[:, side], cot_all.at[:, side], None),
        )
        steps["b"] = Shift(lambda: (branch_away, branch_in, None))
        two = normed_two
        steps["nr"] = Shift(
            lambda: (two.at[share, side, :, far], two.at[share, side, :, far], SHARE_BIT),
            lambda: (two.at[:, side, :, far], two.at[:, side, :, far], None),
        )
        steps["nl"] = Shift(
            lambda: (two.at[share, side, :, first], two.at[share, side, :, first], None),
            lambda: (two.at[share, :, :, first], two.at[share, :, :, first], SHARE_BIT),
        )

        own_cot = keep(cot, cot_all.at[share, side])
        own_tok = keep(tok, tok_all.at[side])
        out_copies = []
        works = {}

        def start_all():
            for copy in (own_tok, own_cot):
                copy.wait()

        works["W"] = start_all

        def norm():
            steps["t"].finish()

            def norm_rows(r, _):
                rows = pl.ds(pl.multiple_of(r * 16, 16), 16)
                for s in range(2):
                    x = tok_all[s, rows, :].astype(f32)
                    scaled = x * lax.rsqrt(jnp.mean(x * x, axis=-1, keepdims=True) + norm_eps)
                    normed[pl.ds(s * own_rows + r * 16, 16), :] = scaled.astype(bf16)
                return 0

            lax.fori_loop(0, own_rows // 16, norm_rows, 0)

        works["N"] = norm

        lanes = lax.broadcasted_iota(jnp.int32, (group_rows, tile), 1)
        first_half = lanes % HEAD_SIZE < HEAD_SIZE // 2
        lead = (slice(None),) * bit_count + (slice(None),)
        values = {}

        def rotate(a):
            cos2 = jnp.concatenate([cosines[...], cosines[...]], axis=1)
            sin2 = jnp.concatenate([sines[...], sines[...]], axis=1)
            forward = pltpu.roll(a, tile - HEAD_SIZE // 2, 1)
            back = pltpu.roll(a, HEAD_SIZE // 2, 1)
            return a * cos2 + jnp.where(first_half, forward, back) * sin2

        def project(columns):
            weights = qkv_held[lead + (columns,)].reshape(width, tile)
            return jnp.dot(normed[...], weights, preferred_element_type=f32)

        def keys_values():
            steps["q0"].finish()
            first = project(slice(0, tile))
            values["keys"] = rotate(first)[:, :key_width].astype(bf16)
            values["values"] = first[:, key_width:].astype(bf16)
            projected[:, :key_width] = values["keys"]
            projected[:, key_width:tile] = values["values"]

        def queries(i):
            def run():
                if i >= query_width // tile // 2:
                    steps["q1"].finish()
                    if not out_copies:
                        out_copies.append(keep(qkv_held, qkv_full))
                columns = slice(tile + i * tile, tile + (i + 1) * tile)
                rotated = rotate(project(columns)).astype(bf16)
                projected[:, columns] = rotated * jnp.asarray(HEAD_SIZE**-0.5, bf16)

            return run

        works["K"] = keys_values
        for i in range(query_width // tile):
            works[f"Q{i}"] = queries(i)

        rows_tile = 128
        pair_lanes = lax.broadcasted_iota(jnp.int32, (group_rows, 2 * HEAD_SIZE), 1)
        pairs = HEADS_PER_KV // 2
        prob_copies = {}

        def padded(a, head, place):
            moved = a if head == place else pltpu.roll(a, HEAD_SIZE, 1)
            inside = pair_lanes < HEAD_SIZE if place == 0 else pair_lanes >= HEAD_SIZE
            return jnp.where(inside, moved, 0.0).astype(bf16)

        def head_pair(n):
            def run():
                head = n // pairs
                if n % pairs == 0:
                    keys32 = values["keys"].astype(f32)
                    values32 = values["values"].astype(f32)
                    values["at"] = (
                        [padded(keys32, head, p) for p in range(2)],
                        [padded(values32, head, p) for p in range(2)],
                    )
                keys_at, values_at = values["at"]
                slot = n % 2
                if slot in prob_copies:
                    prob_copies[slot].wait()
                columns = slice(tile + n * 128, tile + (n + 1) * 128)
                places = [
                    (low, low + rows_tile, p)
                    for low in range(0, group_rows, rows_tile)
                    for p in range(2)
                ]
                scores = [
                    dot(projected[low:high, columns], keys_at[p][:high], ((1,), (1,)))
                    + bias[low:high, :high]
                    for low, high, p in places
                ]
                peaks = [jnp.max(a, axis=-1, keepdims=True) for a in scores]
                raised = [jnp.exp(a - b) for a, b in zip(scores, peaks)]
                inverses = [1.0 / jnp.sum(a, axis=-1, keepdims=True) for a in raised]
                shares = [(a * b).astype(bf16) for a, b in zip(raised, inverses)]
                for (low, high, p), a in zip(places, shares):
                    prob_stage[slot, p, low:high, :high] = a
                prob_copies[slot] = keep(prob_stage.at[slot], probs.at[pl.ds(2 * n, 2)])
                parts = [
                    jnp.dot(a, values_at[p][:high], preferred_element_type=f32)
                    for (low, high, p), a in zip(places, shares)
                ]
                for j in range(0, len(places), 2):
                    low, high, _ = places[j]
                    mixed = (parts[j] + parts[j + 1]).astype(bf16)
                    attended[low:high, n * 128 : (n + 1) * 128] = mixed

            return run

        for n in range(query_width // 128):
            works[f"A{n}"] = head_pair(n)

        tiles = spread(out_held, bit_count, 512)

        def branch_rows(which, give):
            rows = attended[pl.ds(pl.multiple_of(which * own_rows, 64), own_rows), :]
            for i, (index, count) in enumerate(tiles):
                weights = out_held[index].reshape(count, query_width)
                give(slice(i * count, (i + 1) * count), dot(rows, weights, ((1,), (1,))))

        def give_away(to, value):
            branch_away[:, to] = value.astype(bf16)

        def give_near(to, value):
            middle[:, to] = value

        def branch_first():
            steps["o"].finish()
            out_copies.extend(
                [
                    keep(normed, normed_to),
                    keep(projected, projected_to),
                    keep(attended, attended_to),
                ]
            )
            out_copies.append(keep(out_held, out_full))
            branch_rows(1 - side, give_away)

        works["OA"] = branch_first
        works["ON"] = lambda: branch_rows(side, give_near)

        def middle_all():
            steps["b"].finish()

            def middle_rows(r, _):
                rows = pl.ds(pl.multiple_of(r * 16, 16), 16)
                x = tok[rows, :].astype(f32) + middle[rows, :] + branch_in[rows, :].astype(f32)
                middle[rows, :] = x
                scaled = x * lax.rsqrt(jnp.mean(x * x, axis=-1, keepdims=True) + norm_eps)
                normed_two[share, side, rows, :] = scaled.astype(bf16)
                return 0

            lax.fori_loop(0, own_rows // 16, middle_rows, 0)
            out_copies.append(keep(middle, middle_to))

        works["M"] = middle_all

        bounds = [(0, cut), (cut, hidden_width)]

        def spans(p):
            start, end = bounds[p]
            return [(low, min(low + 512, end)) for low in range(start, end, 512)]

        mlp_lead = (slice(None),) * (bit_count + 1)

        def mlp_product(m, rows_ref, quarter, low, high):
            weights = mlp_held[(m,) + mlp_lead + (slice(low, high),)].reshape(width, high - low)
            return jnp.dot(
                rows_ref[quarter].reshape(group_rows, width), weights, preferred_element_type=f32
            )

        def rows_of(quarter):
            return slice(quarter * group_rows, (quarter + 1) * group_rows)

        prepared_out = set()

        def store_product(m, p, slot, rows_ref, *needed):
            def run():
                for name in (f"u{2 * m + p}",) + needed:
                    steps[name].finish()
                if m == 0:
                    columns = (slice(None),) * (bit_count + 1) + (pieces[p],)
                    out_copies.append(keep(mlp_held.at[(0,) + columns], down_full.at[columns]))
                if slot not in prepared_out:
                    prepared_out.add(slot)
                    target = cot_all_to if m == 0 else normed_two_to
                    out_copies.append(keep(rows_ref, target))
                for low, high in spans(p):
                    for quarter in range(2):
                        value = mlp_product(m, rows_ref, quarter, low, high)
                        hid[slot, rows_of(quarter), low:high] = value.astype(bf16)

            return run

        def up_product(p):
            def run():
                steps[f"u{4 + p}"].finish()
                for low, high in spans(p):
                    for quarter in range(2):
                        up = mlp_product(2, normed_two, quarter, low, high)
                        at = rows_of(quarter)
                        gate = hid[0, at, low:high].astype(f32)
                        grad_hidden = hid[2, at, low:high].astype(f32)
                        sig = jax.nn.sigmoid(gate)
                        silu = gate * sig
                        slope = sig + silu * (1.0 - sig)
                        hid[0, at, low:high] = (silu * up).astype(bf16)
                        hid[1, at, low:high] = (grad_hidden * up * slope).astype(bf16)
                        hid[2, at, low:high] = (grad_hidden * silu).astype(bf16)
                columns = (slice(None), slice(None), pieces[p])
                out_copies.append(keep(hid.at[columns], hid_to.at[columns]))

            return run

        mlp_tiles = spread(mlp_held.at[0], bit_count, 512)
        tall = 2 * own_rows
        opened = set()

        def mlp_back(p, parts, target):
            columns = slice(*bounds[p])
            count_of = bounds[p][1] - bounds[p][0]

            def run():
                again = id(target) in opened
                opened.add(id(target))
                for i, (index, count) in enumerate(mlp_tiles):
                    to = slice(i * count, (i + 1) * count)
                    inner = (slice(None),) * (bit_count + 1 - len(index)) + (columns,)
                    for r in range(2):
                        at = slice(r * tall, (r + 1) * tall)
                        total = target[at, to].astype(f32) if again else None
                        for m, slot in parts:
                            weights = mlp_held[(m,) + index + inner].reshape(count, count_of)
                            term = dot(hid[slot, at, columns], weights, ((1,), (1,)))
                            total = term if total is None else total + term
                        target[at, to] = total.astype(bf16)
                    if again:
                        full = (slice(None), pl.ds(i * count, count))
                        out_copies.append(keep(target.at[full], grad_part_to.at[full]))

            return run

        for p, suffix in enumerate("ab"):
            works["DH" + suffix] = store_product(0, p, 2, cot_all, "c")
            works["G" + suffix] = store_product(1, p, 0, normed_two, "nl", "nr")
            works["U" + suffix] = up_product(p)
            works["E" + suffix] = mlp_back(p, ((1, 1), (2, 2)), grad_part)

        for name in FORWARD_ORDER:
            if name in works:
                works[name]()
            else:
                steps[name].step()
        for name in steps:
            steps[name].finish()
        for copy in out_copies + list(prob_copies.values()):
            copy.wait()
        for copy in started:
            copy.wait_send()

    def call(
        tok,
        cot,
        w_query,
        key_value,
        w_out,
        w_gateup,
        w_down,
        gains,
        cosines,
        sines,
        bias,
    ):
        bf16, f32 = jnp.bfloat16, jnp.float32
        own_rows, width = tok.shape
        block, query_width = w_query.shape
        qkv_width = query_width + 2 * key_value.shape[2]
        mlp_width = w_gateup.shape[2] // 2
        rows = 2 * own_rows
        twos = (2,) * bit_count
        heads = query_width // HEAD_SIZE
        whole = pl.BlockSpec(memory_space=pltpu.VMEM)
        away = pl.BlockSpec(memory_space=pl.ANY)
        count = 10 * (bit_count + 1) + 16
        shape = jax.ShapeDtypeStruct
        return pl.pallas_call(
            kernel,
            out_shape=[
                shape(twos + (block, qkv_width), bf16),
                shape(twos + (block, query_width), bf16),
                shape((heads, rows, rows), bf16),
                shape((rows, width), bf16),
                shape((rows, qkv_width), bf16),
                shape((rows, query_width), bf16),
                shape((own_rows, width), f32),
                shape((2, 2, own_rows, width), bf16),
                shape((2, 2, own_rows, width), bf16),
                shape((3, 2 * rows, mlp_width), bf16),
                shape((2 * rows, width), bf16),
                shape(twos + (block, mlp_width), bf16),
            ],
            in_specs=[whole, away, whole, whole, whole, away] + [whole] * 5,
            out_specs=[away] * 12,
            scratch_shapes=[
                pltpu.VMEM((rows, width), bf16),
                pltpu.VMEM((rows, qkv_width), bf16),
                pltpu.VMEM((rows, query_width), bf16),
                pltpu.VMEM((own_rows, width), f32),
                pltpu.VMEM((2, 2, own_rows, width), bf16),
                pltpu.VMEM((2, 2, own_rows, width), bf16),
                pltpu.VMEM((3, 2 * rows, mlp_width), bf16),
                pltpu.VMEM((2 * rows, width), bf16),
                pltpu.VMEM(twos + (block, qkv_width), bf16),
                pltpu.VMEM(twos + (block, query_width), bf16),
                pltpu.VMEM((3,) + twos + (block, mlp_width), bf16),
                pltpu.VMEM((2, own_rows, width), bf16),
                pltpu.VMEM((own_rows, width), bf16),
                pltpu.VMEM((own_rows, width), bf16),
                pltpu.VMEM((2, 2, rows, rows), bf16),
                pltpu.VMEM((3, block, mlp_width), bf16),
                pltpu.VMEM((2, block, 128), f32),
                pltpu.SemaphoreType.DMA((count,)),
                pltpu.SemaphoreType.DMA((count,)),
                pltpu.SemaphoreType.DMA((40 + heads,)),
            ],
            compiler_params=pltpu.CompilerParams(
                collective_id=1, has_side_effects=True, vmem_limit_bytes=63 * 1024 * 1024
            ),
            name="forward",
        )(
            tok,
            cot,
            w_query,
            key_value,
            w_out,
            w_gateup,
            w_down,
            gains,
            cosines,
            sines,
            bias,
        )

    return call


def make_backward(dp_size, high_bits):
    bit_count = dp_size.bit_length() - 1
    all_bits = tuple(range(bit_count))
    folded = tuple(k for k in reversed(all_bits) if k != CORE_BIT)
    low_order = tuple(range(1, SHARE_BIT)) + high_bits[::-1]
    qkv_order = (1, SHARE_BIT) + high_bits[::-1]
    out_orders = ((1, SHARE_BIT) + high_bits[::-1], (SHARE_BIT,) + high_bits[::-1] + (1,))
    step_count = len(low_order)

    def kernel(
        normed_two,
        cot_all,
        hid,
        grad_part,
        down_full,
        middle_in,
        tok,
        cot,
        out_full,
        qkv_full,
        normed,
        projected_in,
        probs,
        attended_in,
        cosines,
        sines,
        w_query,
        key_value,
        w_gateup,
        gains,
        result,
        input_grad,
        query_grad,
        keyval_grad,
        out_grad,
        gateup_grad,
        down_grad,
        gain_grads,
        *rest,
    ):
        mlp_steps = [list(rest[m * step_count : (m + 1) * step_count]) for m in range(3)]
        (
            recv_stage,
            out_part,
            away_slots,
            mlp_core,
            mlp_last,
            qkv_core,
            out_core,
            quad_in,
            quad_step,
            quad_near,
            middle,
            grad_middle,
            grad_branch,
            norm_away,
            norm_in,
            stage,
            down_held,
            out_sum,
            weight_stage,
            gain_sums,
            gain_in,
            gain_columns,
            send_sem,
            recv_sem,
            local_sem,
        ) = rest[3 * step_count : 3 * step_count + 25]
        steps = list(rest[3 * step_count + 25 :])
        qkv_steps, others_of = steps[: len(qkv_order)], steps[len(qkv_order) :]
        out_steps = (others_of, others_of)
        f32, bf16 = jnp.float32, jnp.bfloat16
        me = lax.axis_index("dp")
        side = lax.axis_index("tensor")
        bits = [(me // 2**k) % 2 for k in all_bits]
        others = [1 - b for b in bits]
        core, share = bits[CORE_BIT], bits[SHARE_BIT]
        core_other, share_other, side_other = others[CORE_BIT], others[SHARE_BIT], 1 - side
        own_rows, width = tok.shape
        half = width // 2
        rows = 2 * own_rows
        query_width = attended_in.shape[1]
        key_width = (projected_in.shape[1] - query_width) // 2
        tile = 2 * key_width
        block = width // dp_size

        partners = {k: {"dp": me + (1 - 2 * bits[k]) * 2**k} for k in all_bits}
        partners[None] = {"tensor": side_other}

        barrier = pltpu.get_barrier_semaphore()
        for k in all_bits + (None,):
            pl.semaphore_signal(barrier, inc=1, device_id=partners[k], device_id_type=MESH)

        counter, local_counter = [0], [0]
        unsent = []

        class Push:
            def __init__(self, ends, k):
                self.ends, self.k, self.i = ends, k, counter[0]
                counter[0] += 1
                self.copy().start()
                unsent.append(self)

            def copy(self):
                src, dst = self.ends()
                return pltpu.make_async_remote_copy(
                    src_ref=src,
                    dst_ref=dst,
                    send_sem=send_sem.at[self.i],
                    recv_sem=recv_sem.at[self.i],
                    device_id=partners[self.k],
                    device_id_type=MESH,
                )

            def wait_recv(self):
                self.copy().wait_recv()

        def sent(push):
            push.copy().wait_send()
            unsent[:] = [other for other in unsent if other is not push]

        def keep(src, dst):
            i = local_counter[0]
            local_counter[0] += 1
            copy = pltpu.make_async_copy(src, dst, local_sem.at[i])
            copy.start()
            return copy

        def cells(lead):
            return [tuple((i >> (lead - 1 - j)) & 1 for j in range(lead)) for i in range(2**lead)]

        def strips(count, size, work):
            def step(r, _):
                work(pl.ds(pl.multiple_of(r * size, size), size))
                return 0

            lax.fori_loop(0, count // size, step, 0)

        def half_grad(left, right, which, give):
            lead = bit_count - 1
            kept = 0
            while block * 2**kept < 256 and kept < lead:
                kept += 1
            for i in range(2 ** (lead - kept)):
                parts = []
                for j in range(2**kept):
                    pair = (i * 2**kept + j) * 2 * block
                    if block % 128 == 0:
                        at = pl.multiple_of(pair + which * block, 128)
                        parts.append(left[:, pl.ds(at, block)])
                    else:
                        low = left[:, pair : pair + block].astype(f32)
                        high = left[:, pair + block : pair + 2 * block].astype(f32)
                        parts.append(jnp.where(which == 0, low, high).astype(bf16))
                columns = jnp.concatenate(parts, axis=1)
                product = dot(columns, right[...], ((0,), (0,)))
                index = tuple((i >> (lead - kept - 1 - j)) & 1 for j in range(lead - kept))
                give(index, product.reshape((2,) * kept + (block, product.shape[-1])))

        class Product:
            def __init__(self, ref, lead):
                self.ref, self.lead, self.copy = ref, lead, None

            def away(self, left, right, slot):
                def give(index, value):
                    slot[index] = value.astype(bf16)

                half_grad(left, right, core_other, give)
                self.slot = slot

            def start(self):
                slot, ref, lead = self.slot, self.ref, self.lead
                self.copy = Push(lambda: (slot, ref.at[lead] if lead else ref), CORE_BIT)

            def near(self, left, right):

                def give(index, value):
                    at = self.lead + index
                    self.ref[at] = (value + self.ref[at].astype(f32)).astype(bf16)

                half_grad(left, right, core, give)

        class Fold:
            def __init__(self, ref, lead, start, size, steps, order, staged):
                self.ref, self.lead = ref, lead
                self.start, self.size = start, size
                self.steps = dict(zip(order, steps))
                self.order = list(order)
                self.staged = staged
                self.settled = {}
                self.copy = self.bit = None

            def place(self, cell):
                rest = iter(cell)
                return self.lead + tuple(
                    self.settled[k] if k in self.settled else next(rest) for k in folded
                )

            def open(self):
                return len(folded) - len(self.settled)

            def rows(self):
                return (pl.ds(self.start, self.size),)

            def send(self):
                self.bit = self.order.pop(0)
                self.settled[self.bit] = others[self.bit]
                twice = (pl.ds(0, 2),) * self.open()
                place = self.place(twice) + self.rows()
                target, there = self.steps[self.bit], twice + self.rows()
                self.copy = Push(lambda: (self.ref.at[place], target.at[there]), self.bit)
                self.settled[self.bit] = bits[self.bit]

            def add(self, last=None, loaded=None):
                self.copy.wait_recv()
                arrived, lead = self.steps[self.bit], ()
                if self.staged:
                    there = (pl.ds(0, 2),) * self.open() + self.rows()
                    lead = (0,) * (len(folded) - 1 - self.open())
                    keep(arrived.at[there], recv_stage.at[lead + there]).wait()
                    arrived = recv_stage
                if loaded is not None:
                    loaded.wait()
                for cell in cells(self.open()):
                    place = self.place(cell)

                    def work(r, _, cell=cell, place=place):
                        at = pl.ds(pl.multiple_of(self.start + r * 16, 16), 16)
                        new, old = arrived[lead + cell + (at,)], self.ref[place + (at,)]
                        if last is None:
                            self.ref[place + (at,)] = new + old
                        else:
                            last(cell, at, new.astype(f32) + old.astype(f32))
                        return 0

                    lax.fori_loop(0, self.size // 16, work, 0)

            def step(self):
                self.add()
                self.send()

        class Walk:
            def __init__(self, *actions):
                self.actions = list(actions)
                self.taken = 0

            def step(self):
                if self.actions:
                    self.taken += 1
                    self.actions.pop(0)()

            def finish(self):
                while self.actions:
                    self.step()

        steps, works, done, pushes = {}, {}, set(), {}

        def do(name):
            if name not in done:
                done.add(name)
                works[name]()

        def once(name, ends, k, after):
            def start():
                do(after)
                pushes[name] = Push(ends, k)

            steps[name] = Walk(start, lambda: pushes[name].wait_recv())

        near_loads = {}

        def load_near(slot, p):
            n = local_counter[0]
            local_counter[0] += 1

            def copy():
                if p == 0:
                    view = grad_part.at[share, :, :, pl.ds(0, half)]
                else:
                    view = grad_part.at[:, side, :, pl.ds(half, half)]
                return pltpu.make_async_copy(view, quad_near.at[p], local_sem.at[n])

            copy().start()
            near_loads[slot, p] = copy

        def quad_half(name, slot, p):
            source = (grad_part, out_part)[slot]
            first_bit, second_bit = ((SHARE_BIT, None), (None, SHARE_BIT))[p]
            there = (side_other, share_other)[p]

            def first():
                if slot == 1:
                    do("O")

                def ends():
                    if p == 0:
                        view = source.at[share_other, :, :, pl.ds(0, half)]
                    else:
                        view = source.at[:, side_other, :, pl.ds(half, half)]
                    return view, quad_in.at[slot, p]

                pushes[name] = Push(ends, first_bit)

            def second():
                pushes[name].wait_recv()
                if slot == 0:
                    near_loads[slot, p]().wait()
                for q in range(2):

                    def work(at, q=q):
                        if slot == 0:
                            near = quad_near[p, q, at, :]
                        elif p == 0:
                            near = out_part[share, q, at, :half]
                        else:
                            near = out_part[q, side, at, half:]
                        quad_in[slot, p, q, at, :] = quad_in[slot, p, q, at, :] + near

                    strips(own_rows, 16, work)
                pushes[name] = Push(
                    lambda: (quad_in.at[slot, p, there], quad_step.at[slot, p]), second_bit
                )

            steps[name] = Walk(first, second, lambda: pushes[name].wait_recv())

        def quad_value(slot, at):
            halves = []
            for p, here in ((0, side), (1, share)):
                halves.append(
                    quad_in[slot, p, here, at, :].astype(f32) + quad_step[slot, p, at, :].astype(f32)
                )
            return jnp.concatenate(halves, axis=-1)

        quad_half("el", 0, 0)
        quad_half("er", 0, 1)
        quad_half("ol", 1, 0)
        quad_half("or", 1, 1)
        load_near(0, 0)
        load_near(0, 1)
        middle_load = keep(middle_in, middle)

        part = block // 2
        mlp_products = [Product(mlp_core, (m,)) for m in range(3)]
        mlp_folds = [
            Fold(mlp_core, (m,), p * part, part, mlp_steps[m], low_order, True)
            for m in range(3)
            for p in range(2)
        ]
        qkv_product = Product(qkv_core, ())
        out_product = Product(out_core, ())
        qkv_folds = [Fold(qkv_core, (), p * part, part, qkv_steps, qkv_order, False) for p in range(2)]
        out_folds = [Fold(out_core, (), p * part, part, out_steps[p], out_orders[p], False) for p in range(2)]
        mlp_copies = [None] * 6
        stage_copies = [None, None]
        stage_count = [0]

        def to_output(fill, dst):
            i = stage_count[0] % 2
            stage_count[0] += 1
            if stage_copies[i] is not None:
                stage_copies[i]().wait()
            fill(i)
            n = local_counter[0]
            local_counter[0] += 1

            def copy():
                return pltpu.make_async_copy(stage.at[i], dst(), local_sem.at[n])

            copy().start()
            stage_copies[i] = copy

        hidden_width = hid.shape[-1]
        own_half = pl.multiple_of(share * hidden_width, 128)
        other_half = pl.multiple_of(share_other * hidden_width, 128)
        gain_sums[1] = jnp.zeros_like(gain_sums[1])
        spread_gains(gains, gain_columns)

        def weight_rows(m, rows_of, start):
            columns = pl.ds(start, hidden_width)
            return keep(w_gateup.at[m - 1, rows_of, columns], weight_stage.at[rows_of])

        def give_rows(m, i, at, total):
            if m == 0:
                down_held[i, at, :] = total
                return
            local = pl.ds(pl.multiple_of(at.start % part, 16), 16)
            stage[i, local, :] = total * gain_columns[1, at, :][:, :1]
            weighted = total * weight_stage[at, :].astype(f32)
            gain_sums[1, at, :] += jnp.sum(weighted, axis=-1, keepdims=True)

        def mlp_share(u):
            m, fold = u // 2, mlp_folds[u]
            rows_of = pl.ds(fold.start, fold.size)
            loaded = weight_rows(m, rows_of, own_half) if m > 0 else None

            def fill(i):
                def last(cell, at, total):
                    is_own = share == cell[0]

                    @pl.when(is_own)
                    def _():
                        give_rows(m, i, at, total)

                    @pl.when(jnp.logical_not(is_own))
                    def _():
                        mlp_last[m, 0, at, :] = total.astype(bf16)

                fold.add(last, loaded)

            if m == 0:
                fill(0)
            else:
                columns = pl.ds(own_half, hidden_width)
                to_output(fill, lambda: gateup_grad.at[m - 1, rows_of, columns])
            mlp_copies[u] = Push(
                lambda: (mlp_last.at[m, 0, rows_of], mlp_last.at[m, 1, rows_of]), SHARE_BIT
            )

        def mlp_finish(u):
            m, fold = u // 2, mlp_folds[u]
            rows_of = pl.ds(fold.start, fold.size)
            loaded = weight_rows(m, rows_of, other_half) if m > 0 else None
            mlp_copies[u].wait_recv()
            if loaded is not None:
                loaded.wait()

            def fill(i):
                def work(r, _):
                    at = pl.ds(pl.multiple_of(fold.start + r * 16, 16), 16)
                    give_rows(m, i, at, mlp_last[m, 1, at, :].astype(f32))
                    return 0

                lax.fori_loop(0, fold.size // 16, work, 0)

            if m == 0:
                fill(1)
            else:
                columns = pl.ds(other_half, hidden_width)
                to_output(fill, lambda: gateup_grad.at[m - 1, rows_of, columns])

        def out_rows(cell, at, total):
            out_sum[at, :] = total

        def qkv_rows(cell, at, total):
            gain = gain_columns[0, at, :][:, :1]
            parts = [total[:, :key_width], total[:, key_width:tile], total[:, tile:]]
            weights = [key_value[0, at, :], key_value[1, at, :], w_query[at, :]]
            row_sum = sum(
                jnp.sum(p * w.astype(f32), axis=-1, keepdims=True) for p, w in zip(parts, weights)
            )
            gain_sums[0, at, :] = jnp.broadcast_to(row_sum, (16, 128))
            keyval_grad[0, at, :] = parts[0] * gain
            keyval_grad[1, at, :] = parts[1] * gain
            query_grad[at, :] = parts[2] * gain

        def walk_fold(name, fold, after, *ends):
            def start():
                do(after)
                fold.send()

            steps[name] = Walk(start, *([fold.step] * (len(fold.order) - 1)), *ends)

        for u in range(6):
            walk_fold(
                f"f{u}",
                mlp_folds[u],
                f"B{u // 2}",
                functools.partial(mlp_share, u),
                functools.partial(mlp_finish, u),
            )
        for p in range(2):
            for name, fold, after, last in (
                (f"p{p}", out_folds[p], "OB", out_rows),
                (f"q{p}", qkv_folds[p], "QB", qkv_rows),
            ):
                walk_fold(name, fold, after, functools.partial(fold.add, last))

        def walk_core(name, product, after):
            def start():
                do(after)
                product.start()

            steps[name] = Walk(start, lambda: product.copy.wait_recv())

        for m in range(3):
            walk_core(f"K{m}", mlp_products[m], f"W{m}")
        walk_core("KO", out_product, "OA")
        walk_core("KQ", qkv_product, "QA")
        once("D", lambda: (grad_branch.at[side], grad_branch.at[side]), None, "MR")
        once("N", lambda: (norm_away, norm_in), None, "NA")

        quarter = block // 2
        there = pl.ds(pl.multiple_of(side_other * quarter, 16), quarter)
        here = pl.ds(pl.multiple_of(side * quarter, 16), quarter)

        def gains_away():
            for name in ("q0", "q1", "f2", "f3", "f4", "f5"):
                steps[name].finish()
            pushes["X"] = Push(lambda: (gain_sums.at[:, there], gain_in), None)

        def gains_near():
            pushes["X"].wait_recv()
            gain_grads[...] = gain_sums[:, here, :] + gain_in[...]

        steps["X"] = Walk(gains_away, gains_near)

        def follow(order):
            for name in order:
                if name in works:
                    do(name)
                else:
                    steps[name].step()

        down_tiles = spread(down_full, bit_count, 512)

        def down_load(i, held_down):
            return keep(down_full.at[down_tiles[i][0]], held_down.at[i % 2])

        def first_phase(held_rows, held_cot, held_hid, held_down):
            loads = [
                keep(cot_all, held_cot),
                keep(hid.at[0], held_hid.at[0]),
                keep(normed_two, held_rows),
                keep(hid.at[1], held_hid.at[1]),
            ]
            down_first = down_load(0, held_down)
            pl.semaphore_wait(barrier, bit_count + 1)
            waited = set()

            def ready(*numbers):
                for n in numbers:
                    if n not in waited:
                        waited.add(n)
                        loads[n].wait()

            sources = [
                (held_cot, held_hid.at[0], away_slots.at[0], (0, 1)),
                (held_rows, held_hid.at[1], away_slots.at[1], (2, 3)),
                (held_rows, held_hid.at[1], away_slots.at[0], (2, 4)),
            ]

            def away_work(m):
                def run():
                    left, right, slot, numbers = sources[m]
                    if m == 2:
                        do("B1")
                        loads.append(keep(hid.at[2], held_hid.at[1]))
                        sent(mlp_products[0].copy)
                    ready(*numbers)
                    mlp_products[m].away(left, right, slot)

                return run

            def near_work(m):
                def run():
                    steps[f"K{m}"].finish()
                    mlp_products[m].near(*sources[m][:2])

                return run

            for m in range(3):
                works[f"W{m}"] = away_work(m)
                works[f"B{m}"] = near_work(m)
            def out_product_rows():
                ready(1)
                load = down_first
                for i, (index, count) in enumerate(down_tiles):
                    load.wait()
                    if i + 1 < len(down_tiles):
                        load = down_load(i + 1, held_down)
                    to = slice(i * count, (i + 1) * count)
                    weights = held_down[i % 2].reshape(count, hidden_width)
                    for zone in range(2):
                        at = slice(zone * rows, (zone + 1) * rows)
                        value = dot(held_hid[0, at, :], weights, ((1,), (1,))).astype(bf16)
                        out_part[zone, :, :, to] = value.reshape(2, own_rows, count)

            works["O"] = out_product_rows
            follow(BACKWARD_ORDER[:phase_at])
            for name in ("B0", "B1", "B2", "O"):
                do(name)
            for m in (1, 2):
                sent(mlp_products[m].copy)

        phase_at = BACKWARD_ORDER.index("MR")
        tile_shape = down_full.shape[len(spread(down_full, bit_count, 512)[0][0]) :]
        pl.run_scoped(
            first_phase,
            pltpu.VMEM(normed_two.shape, bf16),
            pltpu.VMEM(cot_all.shape, bf16),
            pltpu.VMEM((2,) + hid.shape[1:], bf16),
            pltpu.VMEM((2,) + tile_shape, bf16),
        )

        def second_phase(
            weights, held_probs, projected, attended, grad_att, grad_qkv, acc, turned
        ):
            qkv_width = query_width + tile
            lead_all = (slice(None),) * (bit_count + 1)
            loads = {
                "out": keep(out_full, weights.at[lead_all + (pl.ds(0, query_width),)]),
                "probs": keep(probs.at[pl.ds(0, HEADS_PER_KV)], held_probs),
                "projected": keep(projected_in, projected),
                "attended": keep(attended_in, attended),
            }

            def ready(*names):
                for name in names:
                    if name in loads:
                        loads.pop(name).wait()

            def middle_work():
                middle_load.wait()
                steps["el"].finish()
                steps["er"].finish()

                def middle_rows(at):
                    x = middle[at, :]
                    total = cot[at, :].astype(f32) + rms_grad(x, rms(x), quad_value(0, at))
                    grad_middle[at, :] = total
                    grad_branch[side, at, :] = total.astype(bf16)

                strips(own_rows, 16, middle_rows)

            works["MR"] = middle_work
            branch_flat = BranchView()
            slots = [
                away_slots.at[(i,) + (slice(None),) * bit_count + (pl.ds(0, columns),)]
                for i, columns in ((0, qkv_width), (1, query_width))
            ]

            def attended_grad():
                steps["D"].finish()
                ready("out")
                branch_all = grad_branch[...].reshape(rows, width)
                for low in range(0, query_width, 256):
                    block_of = weights[lead_all + (slice(low, low + 256),)].reshape(width, 256)
                    grad_att[:, low : low + 256] = jnp.dot(
                        branch_all, block_of, preferred_element_type=f32
                    ).astype(bf16)
                loads["qkv"] = keep(qkv_full, weights)

            works["DA"] = attended_grad

            def out_away():
                steps["D"].finish()
                ready("attended")
                out_product.away(branch_flat, attended, slots[1])

            def out_near():
                steps["KO"].finish()
                out_product.near(branch_flat, attended)
                sent(pushes["D"])
                loads["normed"] = keep(normed, grad_branch)

            works["OA"] = out_away
            works["OB"] = out_near

            pair_lanes = lax.broadcasted_iota(jnp.int32, (rows, 2 * HEAD_SIZE), 1)
            lanes = lax.broadcasted_iota(jnp.int32, (rows, key_width), 1)
            first_half = lanes % HEAD_SIZE < HEAD_SIZE // 2

            def padded(a, head, place):
                moved = a if head == place else pltpu.roll(a, HEAD_SIZE, 1)
                inside = pair_lanes < HEAD_SIZE if place == 0 else pair_lanes >= HEAD_SIZE
                return jnp.where(inside, moved, 0.0).astype(bf16)

            def unrotate(a):
                forward = pltpu.roll(a, key_width - HEAD_SIZE // 2, 1)
                back = pltpu.roll(a, HEAD_SIZE // 2, 1)
                return a * cosines[...] - jnp.where(first_half, forward, back) * sines[...]

            heads = key_width // HEAD_SIZE
            pairs = HEADS_PER_KV // 2
            tile_rows = 128
            lane_tile = lax.broadcasted_iota(jnp.int32, (tile_rows, 2 * HEAD_SIZE), 1)
            totals = []
            heads_at = {}

            def head_pair(n):
                def run():
                    head, i = n // pairs, n % pairs
                    if i == 0:
                        do("DA")
                        ready("probs", "projected")
                        if head > 0:
                            first = head * HEADS_PER_KV
                            keep(probs.at[pl.ds(first, HEADS_PER_KV)], held_probs).wait()
                        keys32 = projected[:, :key_width].astype(f32)
                        values32 = projected[:, key_width:tile].astype(f32)
                        heads_at["keys"] = [padded(keys32, head, p) for p in range(2)]
                        heads_at["values"] = [padded(values32, head, p) for p in range(2)]
                        acc[...] = jnp.zeros_like(acc)
                    keys_at, values_at = heads_at["keys"], heads_at["values"]
                    columns = slice(n * 128, (n + 1) * 128)
                    query_columns = slice(tile + n * 128, tile + (n + 1) * 128)
                    places = [
                        (low, low + tile_rows, p)
                        for low in range(0, rows, tile_rows)
                        for p in range(2)
                    ]
                    insides = [lane_tile < HEAD_SIZE, lane_tile >= HEAD_SIZE]
                    prob = [
                        held_probs[2 * i + p, low:high, :high] for low, high, p in places
                    ]
                    grad_prob = [
                        dot(grad_att[low:high, columns], values_at[p][:high], ((1,), (1,)))
                        for low, high, p in places
                    ]
                    prob32 = [a.astype(f32) for a in prob]
                    weighted = [a * b for a, b in zip(prob32, grad_prob)]
                    centre = [jnp.sum(a, axis=-1, keepdims=True) for a in weighted]
                    grad_score = [
                        (a - b * c).astype(bf16) for a, b, c in zip(weighted, prob32, centre)
                    ]
                    grad_query = [
                        jnp.dot(a, keys_at[p][:high], preferred_element_type=f32)
                        for a, (low, high, p) in zip(grad_score, places)
                    ]
                    for j, (low, high, p) in enumerate(places):
                        query = projected[low:high, query_columns].astype(f32)
                        only_query = jnp.where(insides[p], query, 0.0).astype(bf16)
                        out32 = grad_att[low:high, columns].astype(f32)
                        only_grad = jnp.where(insides[p], out32, 0.0).astype(bf16)
                        acc[0, :high, :] += dot(grad_score[j], only_query, ((0,), (0,)))
                        acc[1, :high, :] += dot(prob[j], only_grad, ((0,), (0,)))
                        if p == 1:
                            total = grad_query[j - 1] + grad_query[j]
                            acc[2, low:high, :] = total * HEAD_SIZE**-0.5
                    grad_qkv[:, query_columns] = unrotate(acc[2]).astype(bf16)
                    if i == pairs - 1:
                        totals.append([acc[j] + pltpu.roll(acc[j], HEAD_SIZE, 1) for j in range(2)])

                return run

            for n in range(query_width // 128):
                works[f"T{n}"] = head_pair(n)

            def qkv_away():
                lower = pair_lanes < HEAD_SIZE
                grad_keys = unrotate(jnp.where(lower, totals[0][0], totals[1][0]))
                grad_qkv[:, :key_width] = grad_keys.astype(bf16)
                grad_values = jnp.where(lower, totals[0][1], totals[1][1])
                grad_qkv[:, key_width:tile] = grad_values.astype(bf16)
                ready("normed")
                qkv_product.away(branch_flat, grad_qkv, slots[0])

            def qkv_near():
                steps["KQ"].finish()
                qkv_product.near(branch_flat, grad_qkv)

            works["QA"] = qkv_away
            works["QB"] = qkv_near
            tiles = spread(weights, bit_count, 512)

            def norm_part(which, give):
                ready("qkv")
                at = pl.ds(pl.multiple_of(which * own_rows, 64), own_rows)
                chosen = grad_qkv[at, :]
                for i, (index, count) in enumerate(tiles):
                    block_of = weights[index].reshape(count, qkv_width)
                    give(slice(i * count, (i + 1) * count), dot(chosen, block_of, ((1,), (1,))))

            def give_away(to, value):
                norm_away[:, to] = value.astype(bf16)

            def give_near(to, value):
                middle[:, to] = value

            works["NA"] = lambda: norm_part(side_other, give_away)

            def result_work():
                steps["ol"].finish()
                steps["or"].finish()

                def result_rows(at):
                    result[at, :] = (middle[at, :] + quad_value(1, at)).astype(bf16)

                strips(own_rows, 16, result_rows)

            works["RR"] = result_work

            def near_rows():
                do("RR")
                norm_part(side, give_near)

            works["NB"] = near_rows

            def input_work():
                do("NB")
                steps["N"].finish()

                def input_rows(at):
                    x = tok[at, :].astype(f32)
                    scaled = middle[at, :] + norm_in[at, :].astype(f32)
                    total = grad_middle[at, :] + rms_grad(x, rms(x), scaled)
                    input_grad[at, :] = total.astype(bf16)

                strips(own_rows, 16, input_rows)

            works["IR"] = input_work

            def turn_down():
                steps["f0"].finish()
                steps["f1"].finish()
                for h, start in ((0, own_half), (1, other_half)):
                    if h == 1:
                        turn_copies.pop().wait()
                    turned[...] = down_held[h].T
                    turn_copies.append(keep(turned, down_grad.at[pl.ds(start, hidden_width)]))

            def turn_out():
                steps["p0"].finish()
                steps["p1"].finish()
                out_grad[...] = out_sum[...].T

            turn_copies = []
            works["TD"] = turn_down
            works["TO"] = turn_out
            follow(BACKWARD_ORDER[phase_at:])
            for name in works:
                do(name)
            for product in (out_product, qkv_product):
                sent(product.copy)
            for copy in turn_copies:
                copy.wait()

        class BranchView:
            def __getitem__(self, index):
                return grad_branch[(slice(None), slice(None), index[1])].reshape(rows, -1)

        pl.run_scoped(
            second_phase,
            pltpu.VMEM(qkv_full.shape, bf16),
            pltpu.VMEM((HEADS_PER_KV,) + probs.shape[1:], bf16),
            pltpu.VMEM(projected_in.shape, bf16),
            pltpu.VMEM(attended_in.shape, bf16),
            pltpu.VMEM(attended_in.shape, bf16),
            pltpu.VMEM(projected_in.shape, bf16),
            pltpu.VMEM((3, rows, 2 * HEAD_SIZE), f32),
            pltpu.VMEM((hid.shape[-1], block), f32),
        )

        for name in steps:
            steps[name].finish()
        for copy in stage_copies:
            copy().wait()
        for copy in list(unsent):
            sent(copy)

    def call(
        normed_two,
        cot_all,
        hid,
        grad_part,
        down_full,
        middle,
        tok,
        cot,
        out_full,
        qkv_full,
        normed,
        projected,
        probs,
        attended,
        cosines,
        sines,
        w_query,
        key_value,
        w_gateup,
        gains,
    ):
        bf16, f32 = jnp.bfloat16, jnp.float32
        own_rows, width = tok.shape
        half = width // 2
        block, qkv_width = qkv_full.shape[-2:]
        query_width = out_full.shape[-1]
        mlp_width = hid.shape[-1]
        shape = jax.ShapeDtypeStruct
        whole = pl.BlockSpec(memory_space=pltpu.VMEM)
        away = pl.BlockSpec(memory_space=pl.ANY)

        def twos(count):
            return (2,) * count

        slots = [
            shape(twos(bit_count - 2 - i) + (block, mlp_width), bf16) for i in range(step_count)
        ] * 3

        def steps_of(order, columns):
            return [
                pltpu.VMEM(twos(bit_count - 2 - i) + (block, columns), bf16)
                for i in range(len(order))
            ]

        def at_core(columns):
            return twos(bit_count - 1) + (block, columns)

        count = 6 * (step_count + 2) + 6 * bit_count + 24
        outs = pl.pallas_call(
            kernel,
            out_shape=[
                shape((own_rows, width), bf16),
                shape((own_rows, width), bf16),
                shape((block, query_width), f32),
                shape(key_value.shape, f32),
                shape((query_width, block), f32),
                shape(w_gateup.shape, f32),
                shape((2 * mlp_width, block), f32),
                shape((2, block // 2, 128), f32),
            ]
            + slots,
            in_specs=[away] * 6 + [whole] * 2 + [away] * 6 + [whole] * 4 + [away, whole],
            out_specs=[whole] * 5 + [away] * 2 + [whole] + [away] * len(slots),
            scratch_shapes=[
                pltpu.VMEM(twos(bit_count - 2) + (block, mlp_width), bf16),
                pltpu.VMEM((2, 2, own_rows, width), bf16),
                pltpu.VMEM((2,) + at_core(mlp_width), bf16),
                pltpu.VMEM((3,) + at_core(mlp_width), bf16),
                pltpu.VMEM((3, 2, block, mlp_width), bf16),
                pltpu.VMEM(at_core(qkv_width), bf16),
                pltpu.VMEM(at_core(query_width), bf16),
                pltpu.VMEM((2, 2, 2, own_rows, half), bf16),
                pltpu.VMEM((2, 2, own_rows, half), bf16),
                pltpu.VMEM((2, 2, own_rows, half), bf16),
                pltpu.VMEM((own_rows, width), f32),
                pltpu.VMEM((own_rows, width), f32),
                pltpu.VMEM((2, own_rows, width), bf16),
                pltpu.VMEM((own_rows, width), bf16),
                pltpu.VMEM((own_rows, width), bf16),
                pltpu.VMEM((2, block // 2, mlp_width), f32),
                pltpu.VMEM((2, block, mlp_width), f32),
                pltpu.VMEM((block, query_width), f32),
                pltpu.VMEM((block, mlp_width), bf16),
                pltpu.VMEM((2, block, 128), f32),
                pltpu.VMEM((2, block // 2, 128), f32),
                pltpu.VMEM((2, block, 128), f32),
                pltpu.SemaphoreType.DMA((count,)),
                pltpu.SemaphoreType.DMA((count,)),
                pltpu.SemaphoreType.DMA((6 * step_count + 64,)),
            ]
            + steps_of(qkv_order, qkv_width)
            + steps_of(qkv_order, query_width),
            compiler_params=pltpu.CompilerParams(
                collective_id=2, has_side_effects=True, vmem_limit_bytes=63 * 1024 * 1024
            ),
            name="backward",
        )(
            normed_two,
            cot_all,
            hid,
            grad_part,
            down_full,
            middle,
            tok,
            cot,
            out_full,
            qkv_full,
            normed,
            projected,
            probs,
            attended,
            cosines,
            sines,
            w_query,
            key_value,
            w_gateup,
            gains,
        )
        return outs[:8]

    return call


def pass_on(arrays):
    count = len(arrays)

    def kernel(*refs):
        sources, targets = refs[:count], refs[count : 2 * count]
        held, sems = refs[2 * count : 3 * count], refs[3 * count]
        loads = []
        for i in range(count):
            loads.append(pltpu.make_async_copy(sources[i], held[i], sems.at[0, i]))
            loads[i].start()
        stores = []
        for i in range(count):
            loads[i].wait()
            stores.append(pltpu.make_async_copy(held[i], targets[i], sems.at[1, i]))
            stores[i].start()
        for copy in stores:
            copy.wait()

    away = pl.BlockSpec(memory_space=pl.ANY)
    return pl.pallas_call(
        kernel,
        out_shape=[jax.ShapeDtypeStruct(a.shape, a.dtype) for a in arrays],
        in_specs=[away] * count,
        out_specs=[away] * count,
        scratch_shapes=[pltpu.VMEM(a.shape, a.dtype) for a in arrays]
        + [pltpu.SemaphoreType.DMA((2, count))],
        compiler_params=pltpu.CompilerParams(vmem_limit_bytes=62 * 1024 * 1024),
        cost_estimate=pl.CostEstimate(
            flops=0, bytes_accessed=2 * sum(a.size * a.dtype.itemsize for a in arrays), transcendentals=0
        ),
        name="pass_on",
    )(*arrays)


def make_body(dp_size):
    bit_count = dp_size.bit_length() - 1
    high_bits = tuple(range(bit_count - 1, SHARE_BIT, -1))

    def body(
        tokens,
        attn_gain,
        w_query,
        keyvalue_weight,
        w_out,
        mlp_gain,
        w_gateup,
        w_down,
        segment_ids,
        positions,
        cotangent,
    ):
        f32 = jnp.float32
        own_rows, width = tokens.shape

        gains = jnp.stack([attn_gain, mlp_gain]).astype(f32)
        order = jnp.arange(segment_ids.shape[0])
        allowed = (segment_ids[:, None] == segment_ids[None, :]) & (
            order[:, None] >= order[None, :]
        )
        bias = jnp.where(allowed, 0.0, -1e30).astype(f32)

        cosine_table, sine_table = rotary_tables(positions, HEAD_SIZE)
        sine_table = jnp.where(jnp.arange(HEAD_SIZE) < HEAD_SIZE // 2, -sine_table, sine_table)
        cosine_table = jnp.concatenate([cosine_table, cosine_table], axis=1)
        sine_table = jnp.concatenate([sine_table, sine_table], axis=1)
        (
            qkv_full,
            out_full,
            probs,
            normed,
            projected,
            attended,
            middle,
            normed_two,
            grad_all,
            hid,
            grad_part,
            down_full,
        ) = make_forward(dp_size, high_bits)(
            tokens,
            cotangent,
            w_query,
            keyvalue_weight,
            w_out,
            w_gateup,
            w_down,
            gains,
            cosine_table,
            sine_table,
            bias,
        )
        normed_two = normed_two.reshape(4 * own_rows, width)
        grad_all = grad_all.reshape(4 * own_rows, width)

        quad_shape = (2, 2, own_rows, width)
        (
            result,
            input_grad,
            query_grad,
            keyval_grad,
            out_grad,
            gateup_grad,
            down_grad,
            gain_grads,
        ) = make_backward(dp_size, high_bits)(
            normed_two,
            grad_all,
            hid,
            grad_part.reshape(quad_shape),
            down_full,
            middle,
            tokens,
            cotangent,
            out_full,
            qkv_full,
            normed.reshape(2, own_rows, width),
            projected,
            probs,
            attended,
            cosine_table,
            sine_table,
            w_query,
            keyvalue_weight,
            w_gateup,
            gains,
        )
        result, input_grad, query_grad, keyval_grad, out_grad, gateup_grad, down_grad = pass_on(
            [result, input_grad, query_grad, keyval_grad, out_grad, gateup_grad, down_grad]
        )
        return (
            result,
            input_grad,
            gain_grads[0, :, 0],
            query_grad,
            keyval_grad,
            out_grad,
            gain_grads[1, :, 0],
            gateup_grad,
            down_grad,
        )

    return body


def solution(mesh):
    return jax.shard_map(
        make_body(mesh.shape["dp"]),
        mesh=mesh,
        in_specs=(
            P(("dp", "tensor"), None),
            P("dp"),
            P("dp", "tensor"),
            P(None, "dp", "tensor"),
            P("tensor", "dp"),
            P("dp"),
            P(None, "dp", "tensor"),
            P("tensor", "dp"),
            P("dp"),
            P("dp"),
            P(("dp", "tensor"), None),
        ),
        out_specs=(
            P(("dp", "tensor"), None),
            P(("dp", "tensor"), None),
            P(("dp", "tensor")),
            P("dp", "tensor"),
            P(None, "dp", "tensor"),
            P("tensor", "dp"),
            P(("dp", "tensor")),
            P(None, "dp", "tensor"),
            P("tensor", "dp"),
        ),
        check_vma=False,
    )
```

```python
import functools
import math

import jax
import jax.numpy as jnp
from jax import lax
from jax.experimental import pallas as pl
from jax.experimental.pallas import tpu as pltpu
from jax.sharding import PartitionSpec as P

MESH = pl.DeviceIdType.MESH

QUERY_HEAD_COUNT = 32
KEYVALUE_HEADS = 4
HEAD_SIZE = 64
HEADS_PER_KV = QUERY_HEAD_COUNT // KEYVALUE_HEADS
norm_eps = 1e-05

CORE_BIT = 0
SHARE_BIT = 2


FORWARD_ORDER = (
    "q1", "u1", "q0", "o", "W", "q1", "q0", "q1", "o", "c", "t", "q0", "o", "q1", "t", "q1", "q0",
    "N", "u0", "q0", "K", "u1", "c", "Q0", "u3", "u0", "Q1", "A0", "A1", "u1", "Q2", "A2", "A3",
    "Q3", "u5", "A4", "u4", "u3", "o", "A5", "o", "u2", "u0", "A6", "A7", "u1", "OA", "ON", "u4",
    "b", "u3", "b", "M", "nr", "u2", "u1", "c", "u4", "nl", "nl", "DHb", "u2", "nr", "u5", "u0",
    "u0", "u3", "u4", "DHa", "u5", "u2", "nr", "u3", "u2", "u4", "nl", "Ga", "Ua", "Ea", "u5", "Gb",
    "u5", "Ub", "Eb",
)

BACKWARD_ORDER = (
    "er", "el", "W0", "K0", "W1", "K1", "K1", "B1", "f2", "er", "K0", "el", "f3", "O", "ol", "or",
    "W2", "K2", "er", "f2", "el", "B0", "K2", "f1", "B2", "MR", "D", "f3", "f0", "f2", "ol", "or",
    "D", "DA", "f1", "f3", "OA", "KO", "KO", "OB", "T0", "T1", "f4", "T2", "T3", "p0", "T4", "f0",
    "p1", "f4", "T5", "f5", "T6", "T7", "ol", "QA", "f1", "p1", "NA", "p0", "KQ", "KQ", "QB", "N",
    "q0", "q1", "f1", "f5", "f4", "or", "p0", "f0", "f3", "f4", "N", "RR", "q0", "p0", "q1", "f5",
    "NB", "IR", "q0", "p1", "f0", "q1", "q0", "p1", "TD", "f2", "TO", "f5", "q1", "X", "X",
)


def rotary_tables(places, width):
    freqs = jnp.exp(jnp.arange(0, width, 2).astype(jnp.float32) * (-math.log(10000.0) / width))
    turned = places.astype(jnp.float32)[:, None] * freqs[None, :]
    turned = jnp.concatenate([turned, turned], axis=-1)
    return (jnp.cos(turned), jnp.sin(turned))


def dot(left, right, contract):
    return lax.dot_general(left, right, (contract, ((), ())), preferred_element_type=jnp.float32)


def rms(rows):
    return lax.rsqrt(jnp.mean(rows * rows, axis=-1, keepdims=True) + norm_eps)


def rms_grad(rows, inverse, grad_scaled):
    inner = jnp.mean(grad_scaled * rows, axis=-1, keepdims=True)
    return inverse * grad_scaled - rows * (inverse * inverse * inverse) * inner


def spread(ref, lead, row_tile):
    sizes = ref.shape
    block = sizes[-2]
    kept = 0
    while block * 2**kept < row_tile and kept < lead:
        kept += 1
    out = []
    for i in range(2 ** (lead - kept)):
        index = tuple((i >> (lead - kept - 1 - j)) & 1 for j in range(lead - kept))
        out.append((index, (block * 2**kept)))
    return out


def spread_gains(gains, columns):
    block = gains.shape[1]
    order = [lax.broadcasted_iota(jnp.int32, (block, block), axis) for axis in range(2)]
    for i in range(gains.shape[0]):
        only = jnp.where(order[0] == order[1], gains[i : i + 1, :], 0.0)
        columns[i] = jnp.broadcast_to(jnp.sum(only, axis=1, keepdims=True), columns.shape[1:])


def make_forward(dp_size, high_bits):
    bit_count = dp_size.bit_length() - 1
    all_bits = tuple(range(bit_count))

    def kernel(
        tok,
        cot,
        w_query,
        key_value,
        w_out,
        w_gateup,
        w_down,
        gains,
        cosines,
        sines,
        bias,
        qkv_full,
        out_full,
        probs,
        normed_to,
        projected_to,
        attended_to,
        middle_to,
        normed_two_to,
        cot_all_to,
        hid_to,
        grad_part_to,
        down_full,
        normed,
        projected,
        attended,
        middle,
        normed_two,
        cot_all,
        hid,
        grad_part,
        qkv_held,
        out_held,
        mlp_held,
        tok_all,
        branch_away,
        branch_in,
        prob_stage,
        mlp_other,
        gain_columns,
        send_sem,
        recv_sem,
        local_sem,
    ):
        f32, bf16 = jnp.float32, jnp.bfloat16
        me = lax.axis_index("dp")
        side = lax.axis_index("tensor")
        bits = [(me // 2**k) % 2 for k in all_bits]
        share = bits[SHARE_BIT]
        own_rows, width = tok.shape
        half = width // 2
        group_rows = 2 * own_rows
        query_width = attended.shape[1]
        key_width = (projected.shape[1] - query_width) // 2
        tile = 2 * key_width
        hidden_width = hid.shape[-1]

        def partner(k):
            if k is None:
                return {"tensor": 1 - side}
            return {"dp": me + (1 - 2 * bits[k]) * 2**k}

        barrier = pltpu.get_barrier_semaphore()
        for k in all_bits + (None,):
            pl.semaphore_signal(barrier, inc=1, device_id=partner(k), device_id_type=MESH)

        own = tuple(bits[k] for k in reversed(all_bits))
        everything = (slice(None), slice(None))
        halves = [pl.multiple_of(h * hidden_width, 128) for h in (share, 1 - share)]
        raw = {}
        for m in range(2):
            for h in range(2):
                block_at = hid.at[m, pl.ds(h * w_query.shape[0], w_query.shape[0])]
                columns = pl.ds(halves[h], hidden_width)
                raw[m, h] = pltpu.make_async_copy(
                    w_gateup.at[m, :, columns], block_at, local_sem.at[2 * m + h]
                )
                raw[m, h].start()

        spread_gains(gains, gain_columns)

        def scaled(a, gain):
            return (a.astype(f32) * gain_columns[gain][:, :1]).astype(bf16)

        qkv_held[own + (slice(None), slice(0, key_width))] = scaled(key_value[0], 0)
        qkv_held[own + (slice(None), slice(key_width, tile))] = scaled(key_value[1], 0)
        qkv_held[own + (slice(None), slice(tile, tile + query_width))] = scaled(
            w_query[...], 0
        )
        out_held[own + everything] = w_out[...].T

        pl.semaphore_wait(barrier, bit_count + 1)

        counter, local_counter = [0], [4]
        started = []

        def push(src, dst, k):
            i = counter[0]
            counter[0] += 1
            copy = pltpu.make_async_remote_copy(
                src_ref=src,
                dst_ref=dst,
                send_sem=send_sem.at[i],
                recv_sem=recv_sem.at[i],
                device_id=partner(k),
                device_id_type=MESH,
            )
            copy.start()
            started.append(copy)
            return copy

        def keep(src, dst):
            i = local_counter[0]
            local_counter[0] += 1
            copy = pltpu.make_async_copy(src, dst, local_sem.at[i])
            copy.start()
            return copy

        def held(ref, lead, gathered, columns):
            index = tuple(
                pl.ds(0, 2) if k in gathered else bits[k] for k in reversed(all_bits)
            )
            return ref.at[lead + index + (slice(None), columns)]

        class Chain:
            def __init__(self, src, ref, lead, order, columns):
                self.src, self.ref, self.lead, self.columns = src, ref, lead, columns
                self.order = list(order)
                self.gathered = set()
                self.copy = self.bit = None
                self.done = False

            def step(self):
                if self.done:
                    return
                if self.copy is None:
                    self.bit = self.order.pop(0)
                    place = held(self.ref, self.lead, (), self.columns)
                    view = place
                    if self.src is not None:
                        self.src[0]()
                        view = self.src[1].at[:, self.columns]
                    self.copy = push(view, place, self.bit)
                    return
                self.copy.wait_recv()
                self.gathered.add(self.bit)
                if not self.order:
                    self.done = True
                    return
                self.bit = self.order.pop(0)
                view = held(self.ref, self.lead, self.gathered, self.columns)
                self.copy = push(view, view, self.bit)

            def finish(self):
                while not self.done:
                    self.step()

        class Shift:
            def __init__(self, *ends):
                self.ends = list(ends)
                self.copy = None
                self.done = False

            def step(self):
                if self.copy is not None:
                    self.copy.wait_recv()
                    self.copy = None
                if self.ends:
                    self.copy = push(*self.ends.pop(0)())
                else:
                    self.done = True

            def finish(self):
                while not self.done:
                    self.step()

        cut = (hidden_width // 2 + 127) // 128 * 128
        pieces = [pl.ds(0, cut), pl.ds(cut, hidden_width - cut)]
        early = tile + query_width // 2
        full_order = high_bits + (SHARE_BIT, 1, 0)
        steps = {}
        prepared = set()

        def prepare(m):
            if m in prepared:
                return
            prepared.add(m)
            for h in range(2):
                if m == 0:
                    value = w_down[pl.ds(pl.multiple_of(halves[h], 128), hidden_width), :].T
                else:
                    raw[m - 1, h].wait()
                    rows = slice(h * w_query.shape[0], (h + 1) * w_query.shape[0])
                    value = scaled(hid[m - 1, rows, :], 1)
                if h == 0:
                    mlp_held[(m,) + own + everything] = value
                else:
                    mlp_other[m] = value

        steps["q0"] = Chain(None, qkv_held, (), full_order, pl.ds(0, early))
        steps["q1"] = Chain(
            None, qkv_held, (), full_order, pl.ds(early, query_width + tile - early)
        )
        steps["o"] = Chain(None, out_held, (), full_order, pl.ds(0, query_width))
        for m in range(3):
            for p in range(2):
                steps[f"u{2 * m + p}"] = Chain(
                    (functools.partial(prepare, m), mlp_other.at[m]),
                    mlp_held,
                    (m,),
                    (SHARE_BIT,) + high_bits + (1, 0),
                    pieces[p],
                )
        first = pl.ds(0, half)
        far = pl.ds(half, half)
        steps["t"] = Shift(lambda: (tok, tok_all.at[side], None))
        steps["c"] = Shift(
            lambda: (cot, cot_all.at[share, side], SHARE_BIT),
            lambda: (cot_all.at[:, side], cot_all.at[:, side], None),
        )
        steps["b"] = Shift(lambda: (branch_away, branch_in, None))
        two = normed_two
        steps["nr"] = Shift(
            lambda: (two.at[share, side, :, far], two.at[share, side, :, far], SHARE_BIT),
            lambda: (two.at[:, side, :, far], two.at[:, side, :, far], None),
        )
        steps["nl"] = Shift(
            lambda: (two.at[share, side, :, first], two.at[share, side, :, first], None),
            lambda: (two.at[share, :, :, first], two.at[share, :, :, first], SHARE_BIT),
        )

        own_cot = keep(cot, cot_all.at[share, side])
        own_tok = keep(tok, tok_all.at[side])
        out_copies = []
        works = {}

        def start_all():
            for copy in (own_tok, own_cot):
                copy.wait()

        works["W"] = start_all

        def norm():
            steps["t"].finish()

            def norm_rows(r, _):
                rows = pl.ds(pl.multiple_of(r * 16, 16), 16)
                for s in range(2):
                    x = tok_all[s, rows, :].astype(f32)
                    scaled = x * lax.rsqrt(jnp.mean(x * x, axis=-1, keepdims=True) + norm_eps)
                    normed[pl.ds(s * own_rows + r * 16, 16), :] = scaled.astype(bf16)
                return 0

            lax.fori_loop(0, own_rows // 16, norm_rows, 0)

        works["N"] = norm

        lanes = lax.broadcasted_iota(jnp.int32, (group_rows, tile), 1)
        first_half = lanes % HEAD_SIZE < HEAD_SIZE // 2
        lead = (slice(None),) * bit_count + (slice(None),)
        values = {}

        def rotate(a):
            cos2 = jnp.concatenate([cosines[...], cosines[...]], axis=1)
            sin2 = jnp.concatenate([sines[...], sines[...]], axis=1)
            forward = pltpu.roll(a, tile - HEAD_SIZE // 2, 1)
            back = pltpu.roll(a, HEAD_SIZE // 2, 1)
            return a * cos2 + jnp.where(first_half, forward, back) * sin2

        def project(columns):
            weights = qkv_held[lead + (columns,)].reshape(width, tile)
            return jnp.dot(normed[...], weights, preferred_element_type=f32)

        def keys_values():
            steps["q0"].finish()
            first = project(slice(0, tile))
            values["keys"] = rotate(first)[:, :key_width].astype(bf16)
            values["values"] = first[:, key_width:].astype(bf16)
            projected[:, :key_width] = values["keys"]
            projected[:, key_width:tile] = values["values"]

        def queries(i):
            def run():
                if i >= query_width // tile // 2:
                    steps["q1"].finish()
                    if not out_copies:
                        out_copies.append(keep(qkv_held, qkv_full))
                columns = slice(tile + i * tile, tile + (i + 1) * tile)
                rotated = rotate(project(columns)).astype(bf16)
                projected[:, columns] = rotated * jnp.asarray(HEAD_SIZE**-0.5, bf16)

            return run

        works["K"] = keys_values
        for i in range(query_width // tile):
            works[f"Q{i}"] = queries(i)

        rows_tile = 128
        pair_lanes = lax.broadcasted_iota(jnp.int32, (group_rows, 2 * HEAD_SIZE), 1)
        pairs = HEADS_PER_KV // 2
        prob_copies = {}

        def padded(a, head, place):
            moved = a if head == place else pltpu.roll(a, HEAD_SIZE, 1)
            inside = pair_lanes < HEAD_SIZE if place == 0 else pair_lanes >= HEAD_SIZE
            return jnp.where(inside, moved, 0.0).astype(bf16)

        def head_pair(n):
            def run():
                head = n // pairs
                if n % pairs == 0:
                    keys32 = values["keys"].astype(f32)
                    values32 = values["values"].astype(f32)
                    values["at"] = (
                        [padded(keys32, head, p) for p in range(2)],
                        [padded(values32, head, p) for p in range(2)],
                    )
                keys_at, values_at = values["at"]
                slot = n % 2
                if slot in prob_copies:
                    prob_copies[slot].wait()
                columns = slice(tile + n * 128, tile + (n + 1) * 128)
                places = [
                    (low, low + rows_tile, p)
                    for low in range(0, group_rows, rows_tile)
                    for p in range(2)
                ]
                scores = [
                    dot(projected[low:high, columns], keys_at[p][:high], ((1,), (1,)))
                    + bias[low:high, :high]
                    for low, high, p in places
                ]
                peaks = [jnp.max(a, axis=-1, keepdims=True) for a in scores]
                raised = [jnp.exp(a - b) for a, b in zip(scores, peaks)]
                inverses = [1.0 / jnp.sum(a, axis=-1, keepdims=True) for a in raised]
                shares = [(a * b).astype(bf16) for a, b in zip(raised, inverses)]
                for (low, high, p), a in zip(places, shares):
                    prob_stage[slot, p, low:high, :high] = a
                prob_copies[slot] = keep(prob_stage.at[slot], probs.at[pl.ds(2 * n, 2)])
                parts = [
                    jnp.dot(a, values_at[p][:high], preferred_element_type=f32)
                    for (low, high, p), a in zip(places, shares)
                ]
                for j in range(0, len(places), 2):
                    low, high, _ = places[j]
                    mixed = (parts[j] + parts[j + 1]).astype(bf16)
                    attended[low:high, n * 128 : (n + 1) * 128] = mixed

            return run

        for n in range(query_width // 128):
            works[f"A{n}"] = head_pair(n)

        tiles = spread(out_held, bit_count, 512)

        def branch_rows(which, give):
            rows = attended[pl.ds(pl.multiple_of(which * own_rows, 64), own_rows), :]
            for i, (index, count) in enumerate(tiles):
                weights = out_held[index].reshape(count, query_width)
                give(slice(i * count, (i + 1) * count), dot(rows, weights, ((1,), (1,))))

        def give_away(to, value):
            branch_away[:, to] = value.astype(bf16)

        def give_near(to, value):
            middle[:, to] = value

        def branch_first():
            steps["o"].finish()
            out_copies.extend(
                [
                    keep(normed, normed_to),
                    keep(projected, projected_to),
                    keep(attended, attended_to),
                ]
            )
            out_copies.append(keep(out_held, out_full))
            branch_rows(1 - side, give_away)

        works["OA"] = branch_first
        works["ON"] = lambda: branch_rows(side, give_near)

        def middle_all():
            steps["b"].finish()

            def middle_rows(r, _):
                rows = pl.ds(pl.multiple_of(r * 16, 16), 16)
                x = tok[rows, :].astype(f32) + middle[rows, :] + branch_in[rows, :].astype(f32)
                middle[rows, :] = x
                scaled = x * lax.rsqrt(jnp.mean(x * x, axis=-1, keepdims=True) + norm_eps)
                normed_two[share, side, rows, :] = scaled.astype(bf16)
                return 0

            lax.fori_loop(0, own_rows // 16, middle_rows, 0)
            out_copies.append(keep(middle, middle_to))

        works["M"] = middle_all

        bounds = [(0, cut), (cut, hidden_width)]

        def spans(p):
            start, end = bounds[p]
            return [(low, min(low + 512, end)) for low in range(start, end, 512)]

        mlp_lead = (slice(None),) * (bit_count + 1)

        def mlp_product(m, rows_ref, quarter, low, high):
            weights = mlp_held[(m,) + mlp_lead + (slice(low, high),)].reshape(width, high - low)
            return jnp.dot(
                rows_ref[quarter].reshape(group_rows, width), weights, preferred_element_type=f32
            )

        def rows_of(quarter):
            return slice(quarter * group_rows, (quarter + 1) * group_rows)

        prepared_out = set()

        def store_product(m, p, slot, rows_ref, *needed):
            def run():
                for name in (f"u{2 * m + p}",) + needed:
                    steps[name].finish()
                if m == 0:
                    columns = (slice(None),) * (bit_count + 1) + (pieces[p],)
                    out_copies.append(keep(mlp_held.at[(0,) + columns], down_full.at[columns]))
                if slot not in prepared_out:
                    prepared_out.add(slot)
                    target = cot_all_to if m == 0 else normed_two_to
                    out_copies.append(keep(rows_ref, target))
                for low, high in spans(p):
                    for quarter in range(2):
                        value = mlp_product(m, rows_ref, quarter, low, high)
                        hid[slot, rows_of(quarter), low:high] = value.astype(bf16)

            return run

        def up_product(p):
            def run():
                steps[f"u{4 + p}"].finish()
                for low, high in spans(p):
                    for quarter in range(2):
                        up = mlp_product(2, normed_two, quarter, low, high)
                        at = rows_of(quarter)
                        gate = hid[0, at, low:high].astype(f32)
                        grad_hidden = hid[2, at, low:high].astype(f32)
                        sig = jax.nn.sigmoid(gate)
                        silu = gate * sig
                        slope = sig + silu * (1.0 - sig)
                        hid[0, at, low:high] = (silu * up).astype(bf16)
                        hid[1, at, low:high] = (grad_hidden * up * slope).astype(bf16)
                        hid[2, at, low:high] = (grad_hidden * silu).astype(bf16)
                columns = (slice(None), slice(None), pieces[p])
                out_copies.append(keep(hid.at[columns], hid_to.at[columns]))

            return run

        mlp_tiles = spread(mlp_held.at[0], bit_count, 512)
        tall = 2 * own_rows
        opened = set()

        def mlp_back(p, parts, target):
            columns = slice(*bounds[p])
            count_of = bounds[p][1] - bounds[p][0]

            def run():
                again = id(target) in opened
                opened.add(id(target))
                for i, (index, count) in enumerate(mlp_tiles):
                    to = slice(i * count, (i + 1) * count)
                    inner = (slice(None),) * (bit_count + 1 - len(index)) + (columns,)
                    for r in range(2):
                        at = slice(r * tall, (r + 1) * tall)
                        total = target[at, to].astype(f32) if again else None
                        for m, slot in parts:
                            weights = mlp_held[(m,) + index + inner].reshape(count, count_of)
                            term = dot(hid[slot, at, columns], weights, ((1,), (1,)))
                            total = term if total is None else total + term
                        target[at, to] = total.astype(bf16)
                    if again:
                        full = (slice(None), pl.ds(i * count, count))
                        out_copies.append(keep(target.at[full], grad_part_to.at[full]))

            return run

        for p, suffix in enumerate("ab"):
            works["DH" + suffix] = store_product(0, p, 2, cot_all, "c")
            works["G" + suffix] = store_product(1, p, 0, normed_two, "nl", "nr")
            works["U" + suffix] = up_product(p)
            works["E" + suffix] = mlp_back(p, ((1, 1), (2, 2)), grad_part)

        for name in FORWARD_ORDER:
            if name in works:
                works[name]()
            else:
                steps[name].step()
        for name in steps:
            steps[name].finish()
        for copy in out_copies + list(prob_copies.values()):
            copy.wait()
        for copy in started:
            copy.wait_send()

    def call(
        tok,
        cot,
        w_query,
        key_value,
        w_out,
        w_gateup,
        w_down,
        gains,
        cosines,
        sines,
        bias,
    ):
        bf16, f32 = jnp.bfloat16, jnp.float32
        own_rows, width = tok.shape
        block, query_width = w_query.shape
        qkv_width = query_width + 2 * key_value.shape[2]
        mlp_width = w_gateup.shape[2] // 2
        rows = 2 * own_rows
        twos = (2,) * bit_count
        heads = query_width // HEAD_SIZE
        whole = pl.BlockSpec(memory_space=pltpu.VMEM)
        away = pl.BlockSpec(memory_space=pl.ANY)
        count = 10 * (bit_count + 1) + 16
        shape = jax.ShapeDtypeStruct
        return pl.pallas_call(
            kernel,
            out_shape=[
                shape(twos + (block, qkv_width), bf16),
                shape(twos + (block, query_width), bf16),
                shape((heads, rows, rows), bf16),
                shape((rows, width), bf16),
                shape((rows, qkv_width), bf16),
                shape((rows, query_width), bf16),
                shape((own_rows, width), f32),
                shape((2, 2, own_rows, width), bf16),
                shape((2, 2, own_rows, width), bf16),
                shape((3, 2 * rows, mlp_width), bf16),
                shape((2 * rows, width), bf16),
                shape(twos + (block, mlp_width), bf16),
            ],
            in_specs=[whole, away, whole, whole, whole, away] + [whole] * 5,
            out_specs=[away] * 12,
            scratch_shapes=[
                pltpu.VMEM((rows, width), bf16),
                pltpu.VMEM((rows, qkv_width), bf16),
                pltpu.VMEM((rows, query_width), bf16),
                pltpu.VMEM((own_rows, width), f32),
                pltpu.VMEM((2, 2, own_rows, width), bf16),
                pltpu.VMEM((2, 2, own_rows, width), bf16),
                pltpu.VMEM((3, 2 * rows, mlp_width), bf16),
                pltpu.VMEM((2 * rows, width), bf16),
                pltpu.VMEM(twos + (block, qkv_width), bf16),
                pltpu.VMEM(twos + (block, query_width), bf16),
                pltpu.VMEM((3,) + twos + (block, mlp_width), bf16),
                pltpu.VMEM((2, own_rows, width), bf16),
                pltpu.VMEM((own_rows, width), bf16),
                pltpu.VMEM((own_rows, width), bf16),
                pltpu.VMEM((2, 2, rows, rows), bf16),
                pltpu.VMEM((3, block, mlp_width), bf16),
                pltpu.VMEM((2, block, 128), f32),
                pltpu.SemaphoreType.DMA((count,)),
                pltpu.SemaphoreType.DMA((count,)),
                pltpu.SemaphoreType.DMA((40 + heads,)),
            ],
            compiler_params=pltpu.CompilerParams(
                collective_id=1, has_side_effects=True, vmem_limit_bytes=63 * 1024 * 1024
            ),
            name="forward",
        )(
            tok,
            cot,
            w_query,
            key_value,
            w_out,
            w_gateup,
            w_down,
            gains,
            cosines,
            sines,
            bias,
        )

    return call


def make_backward(dp_size, high_bits):
    bit_count = dp_size.bit_length() - 1
    all_bits = tuple(range(bit_count))
    folded = tuple(k for k in reversed(all_bits) if k != CORE_BIT)
    low_order = tuple(range(1, SHARE_BIT)) + high_bits[::-1]
    qkv_order = (1, SHARE_BIT) + high_bits[::-1]
    out_orders = ((1, SHARE_BIT) + high_bits[::-1], (SHARE_BIT,) + high_bits[::-1] + (1,))
    step_count = len(low_order)

    def kernel(
        normed_two,
        cot_all,
        hid,
        grad_part,
        down_full,
        middle_in,
        tok,
        cot,
        out_full,
        qkv_full,
        normed,
        projected_in,
        probs,
        attended_in,
        cosines,
        sines,
        w_query,
        key_value,
        w_gateup,
        gains,
        result,
        input_grad,
        query_grad,
        keyval_grad,
        out_grad,
        gateup_grad,
        down_grad,
        gain_grads,
        *rest,
    ):
        mlp_steps = [list(rest[m * step_count : (m + 1) * step_count]) for m in range(3)]
        (
            recv_stage,
            out_part,
            away_slots,
            mlp_core,
            mlp_last,
            qkv_core,
            out_core,
            quad_in,
            quad_step,
            quad_near,
            middle,
            grad_middle,
            grad_branch,
            norm_away,
            norm_in,
            stage,
            down_held,
            out_sum,
            weight_stage,
            gain_sums,
            gain_in,
            gain_columns,
            send_sem,
            recv_sem,
            local_sem,
        ) = rest[3 * step_count : 3 * step_count + 25]
        steps = list(rest[3 * step_count + 25 :])
        qkv_steps, others_of = steps[: len(qkv_order)], steps[len(qkv_order) :]
        out_steps = (others_of, others_of)
        f32, bf16 = jnp.float32, jnp.bfloat16
        me = lax.axis_index("dp")
        side = lax.axis_index("tensor")
        bits = [(me // 2**k) % 2 for k in all_bits]
        others = [1 - b for b in bits]
        core, share = bits[CORE_BIT], bits[SHARE_BIT]
        core_other, share_other, side_other = others[CORE_BIT], others[SHARE_BIT], 1 - side
        own_rows, width = tok.shape
        half = width // 2
        rows = 2 * own_rows
        query_width = attended_in.shape[1]
        key_width = (projected_in.shape[1] - query_width) // 2
        tile = 2 * key_width
        block = width // dp_size

        partners = {k: {"dp": me + (1 - 2 * bits[k]) * 2**k} for k in all_bits}
        partners[None] = {"tensor": side_other}

        barrier = pltpu.get_barrier_semaphore()
        for k in all_bits + (None,):
            pl.semaphore_signal(barrier, inc=1, device_id=partners[k], device_id_type=MESH)

        counter, local_counter = [0], [0]
        unsent = []

        class Push:
            def __init__(self, ends, k):
                self.ends, self.k, self.i = ends, k, counter[0]
                counter[0] += 1
                self.copy().start()
                unsent.append(self)

            def copy(self):
                src, dst = self.ends()
                return pltpu.make_async_remote_copy(
                    src_ref=src,
                    dst_ref=dst,
                    send_sem=send_sem.at[self.i],
                    recv_sem=recv_sem.at[self.i],
                    device_id=partners[self.k],
                    device_id_type=MESH,
                )

            def wait_recv(self):
                self.copy().wait_recv()

        def sent(push):
            push.copy().wait_send()
            unsent[:] = [other for other in unsent if other is not push]

        def keep(src, dst):
            i = local_counter[0]
            local_counter[0] += 1
            copy = pltpu.make_async_copy(src, dst, local_sem.at[i])
            copy.start()
            return copy

        def cells(lead):
            return [tuple((i >> (lead - 1 - j)) & 1 for j in range(lead)) for i in range(2**lead)]

        def strips(count, size, work):
            def step(r, _):
                work(pl.ds(pl.multiple_of(r * size, size), size))
                return 0

            lax.fori_loop(0, count // size, step, 0)

        def half_grad(left, right, which, give):
            lead = bit_count - 1
            kept = 0
            while block * 2**kept < 256 and kept < lead:
                kept += 1
            for i in range(2 ** (lead - kept)):
                parts = []
                for j in range(2**kept):
                    pair = (i * 2**kept + j) * 2 * block
                    if block % 128 == 0:
                        at = pl.multiple_of(pair + which * block, 128)
                        parts.append(left[:, pl.ds(at, block)])
                    else:
                        low = left[:, pair : pair + block].astype(f32)
                        high = left[:, pair + block : pair + 2 * block].astype(f32)
                        parts.append(jnp.where(which == 0, low, high).astype(bf16))
                columns = jnp.concatenate(parts, axis=1)
                product = dot(columns, right[...], ((0,), (0,)))
                index = tuple((i >> (lead - kept - 1 - j)) & 1 for j in range(lead - kept))
                give(index, product.reshape((2,) * kept + (block, product.shape[-1])))

        class Product:
            def __init__(self, ref, lead):
                self.ref, self.lead, self.copy = ref, lead, None

            def away(self, left, right, slot):
                def give(index, value):
                    slot[index] = value.astype(bf16)

                half_grad(left, right, core_other, give)
                self.slot = slot

            def start(self):
                slot, ref, lead = self.slot, self.ref, self.lead
                self.copy = Push(lambda: (slot, ref.at[lead] if lead else ref), CORE_BIT)

            def near(self, left, right):

                def give(index, value):
                    at = self.lead + index
                    self.ref[at] = (value + self.ref[at].astype(f32)).astype(bf16)

                half_grad(left, right, core, give)

        class Fold:
            def __init__(self, ref, lead, start, size, steps, order, staged):
                self.ref, self.lead = ref, lead
                self.start, self.size = start, size
                self.steps = dict(zip(order, steps))
                self.order = list(order)
                self.staged = staged
                self.settled = {}
                self.copy = self.bit = None

            def place(self, cell):
                rest = iter(cell)
                return self.lead + tuple(
                    self.settled[k] if k in self.settled else next(rest) for k in folded
                )

            def open(self):
                return len(folded) - len(self.settled)

            def rows(self):
                return (pl.ds(self.start, self.size),)

            def send(self):
                self.bit = self.order.pop(0)
                self.settled[self.bit] = others[self.bit]
                twice = (pl.ds(0, 2),) * self.open()
                place = self.place(twice) + self.rows()
                target, there = self.steps[self.bit], twice + self.rows()
                self.copy = Push(lambda: (self.ref.at[place], target.at[there]), self.bit)
                self.settled[self.bit] = bits[self.bit]

            def add(self, last=None, loaded=None):
                self.copy.wait_recv()
                arrived, lead = self.steps[self.bit], ()
                if self.staged:
                    there = (pl.ds(0, 2),) * self.open() + self.rows()
                    lead = (0,) * (len(folded) - 1 - self.open())
                    keep(arrived.at[there], recv_stage.at[lead + there]).wait()
                    arrived = recv_stage
                if loaded is not None:
                    loaded.wait()
                for cell in cells(self.open()):
                    place = self.place(cell)

                    def work(r, _, cell=cell, place=place):
                        at = pl.ds(pl.multiple_of(self.start + r * 16, 16), 16)
                        new, old = arrived[lead + cell + (at,)], self.ref[place + (at,)]
                        if last is None:
                            self.ref[place + (at,)] = new + old
                        else:
                            last(cell, at, new.astype(f32) + old.astype(f32))
                        return 0

                    lax.fori_loop(0, self.size // 16, work, 0)

            def step(self):
                self.add()
                self.send()

        class Walk:
            def __init__(self, *actions):
                self.actions = list(actions)
                self.taken = 0

            def step(self):
                if self.actions:
                    self.taken += 1
                    self.actions.pop(0)()

            def finish(self):
                while self.actions:
                    self.step()

        steps, works, done, pushes = {}, {}, set(), {}

        def do(name):
            if name not in done:
                done.add(name)
                works[name]()

        def once(name, ends, k, after):
            def start():
                do(after)
                pushes[name] = Push(ends, k)

            steps[name] = Walk(start, lambda: pushes[name].wait_recv())

        near_loads = {}

        def load_near(slot, p):
            n = local_counter[0]
            local_counter[0] += 1

            def copy():
                if p == 0:
                    view = grad_part.at[share, :, :, pl.ds(0, half)]
                else:
                    view = grad_part.at[:, side, :, pl.ds(half, half)]
                return pltpu.make_async_copy(view, quad_near.at[p], local_sem.at[n])

            copy().start()
            near_loads[slot, p] = copy

        def quad_half(name, slot, p):
            source = (grad_part, out_part)[slot]
            first_bit, second_bit = ((SHARE_BIT, None), (None, SHARE_BIT))[p]
            there = (side_other, share_other)[p]

            def first():
                if slot == 1:
                    do("O")

                def ends():
                    if p == 0:
                        view = source.at[share_other, :, :, pl.ds(0, half)]
                    else:
                        view = source.at[:, side_other, :, pl.ds(half, half)]
                    return view, quad_in.at[slot, p]

                pushes[name] = Push(ends, first_bit)

            def second():
                pushes[name].wait_recv()
                if slot == 0:
                    near_loads[slot, p]().wait()
                for q in range(2):

                    def work(at, q=q):
                        if slot == 0:
                            near = quad_near[p, q, at, :]
                        elif p == 0:
                            near = out_part[share, q, at, :half]
                        else:
                            near = out_part[q, side, at, half:]
                        quad_in[slot, p, q, at, :] = quad_in[slot, p, q, at, :] + near

                    strips(own_rows, 16, work)
                pushes[name] = Push(
                    lambda: (quad_in.at[slot, p, there], quad_step.at[slot, p]), second_bit
                )

            steps[name] = Walk(first, second, lambda: pushes[name].wait_recv())

        def quad_value(slot, at):
            halves = []
            for p, here in ((0, side), (1, share)):
                halves.append(
                    quad_in[slot, p, here, at, :].astype(f32) + quad_step[slot, p, at, :].astype(f32)
                )
            return jnp.concatenate(halves, axis=-1)

        quad_half("el", 0, 0)
        quad_half("er", 0, 1)
        quad_half("ol", 1, 0)
        quad_half("or", 1, 1)
        load_near(0, 0)
        load_near(0, 1)
        middle_load = keep(middle_in, middle)

        part = block // 2
        mlp_products = [Product(mlp_core, (m,)) for m in range(3)]
        mlp_folds = [
            Fold(mlp_core, (m,), p * part, part, mlp_steps[m], low_order, True)
            for m in range(3)
            for p in range(2)
        ]
        qkv_product = Product(qkv_core, ())
        out_product = Product(out_core, ())
        qkv_folds = [Fold(qkv_core, (), p * part, part, qkv_steps, qkv_order, False) for p in range(2)]
        out_folds = [Fold(out_core, (), p * part, part, out_steps[p], out_orders[p], False) for p in range(2)]
        mlp_copies = [None] * 6
        stage_copies = [None, None]
        stage_count = [0]

        def to_output(fill, dst):
            i = stage_count[0] % 2
            stage_count[0] += 1
            if stage_copies[i] is not None:
                stage_copies[i]().wait()
            fill(i)
            n = local_counter[0]
            local_counter[0] += 1

            def copy():
                return pltpu.make_async_copy(stage.at[i], dst(), local_sem.at[n])

            copy().start()
            stage_copies[i] = copy

        hidden_width = hid.shape[-1]
        own_half = pl.multiple_of(share * hidden_width, 128)
        other_half = pl.multiple_of(share_other * hidden_width, 128)
        gain_sums[1] = jnp.zeros_like(gain_sums[1])
        spread_gains(gains, gain_columns)

        def weight_rows(m, rows_of, start):
            columns = pl.ds(start, hidden_width)
            return keep(w_gateup.at[m - 1, rows_of, columns], weight_stage.at[rows_of])

        def give_rows(m, i, at, total):
            if m == 0:
                down_held[i, at, :] = total
                return
            local = pl.ds(pl.multiple_of(at.start % part, 16), 16)
            stage[i, local, :] = total * gain_columns[1, at, :][:, :1]
            weighted = total * weight_stage[at, :].astype(f32)
            gain_sums[1, at, :] += jnp.sum(weighted, axis=-1, keepdims=True)

        def mlp_share(u):
            m, fold = u // 2, mlp_folds[u]
            rows_of = pl.ds(fold.start, fold.size)
            loaded = weight_rows(m, rows_of, own_half) if m > 0 else None

            def fill(i):
                def last(cell, at, total):
                    is_own = share == cell[0]

                    @pl.when(is_own)
                    def _():
                        give_rows(m, i, at, total)

                    @pl.when(jnp.logical_not(is_own))
                    def _():
                        mlp_last[m, 0, at, :] = total.astype(bf16)

                fold.add(last, loaded)

            if m == 0:
                fill(0)
            else:
                columns = pl.ds(own_half, hidden_width)
                to_output(fill, lambda: gateup_grad.at[m - 1, rows_of, columns])
            mlp_copies[u] = Push(
                lambda: (mlp_last.at[m, 0, rows_of], mlp_last.at[m, 1, rows_of]), SHARE_BIT
            )

        def mlp_finish(u):
            m, fold = u // 2, mlp_folds[u]
            rows_of = pl.ds(fold.start, fold.size)
            loaded = weight_rows(m, rows_of, other_half) if m > 0 else None
            mlp_copies[u].wait_recv()
            if loaded is not None:
                loaded.wait()

            def fill(i):
                def work(r, _):
                    at = pl.ds(pl.multiple_of(fold.start + r * 16, 16), 16)
                    give_rows(m, i, at, mlp_last[m, 1, at, :].astype(f32))
                    return 0

                lax.fori_loop(0, fold.size // 16, work, 0)

            if m == 0:
                fill(1)
            else:
                columns = pl.ds(other_half, hidden_width)
                to_output(fill, lambda: gateup_grad.at[m - 1, rows_of, columns])

        def out_rows(cell, at, total):
            out_sum[at, :] = total

        def qkv_rows(cell, at, total):
            gain = gain_columns[0, at, :][:, :1]
            parts = [total[:, :key_width], total[:, key_width:tile], total[:, tile:]]
            weights = [key_value[0, at, :], key_value[1, at, :], w_query[at, :]]
            row_sum = sum(
                jnp.sum(p * w.astype(f32), axis=-1, keepdims=True) for p, w in zip(parts, weights)
            )
            gain_sums[0, at, :] = jnp.broadcast_to(row_sum, (16, 128))
            keyval_grad[0, at, :] = parts[0] * gain
            keyval_grad[1, at, :] = parts[1] * gain
            query_grad[at, :] = parts[2] * gain

        def walk_fold(name, fold, after, *ends):
            def start():
                do(after)
                fold.send()

            steps[name] = Walk(start, *([fold.step] * (len(fold.order) - 1)), *ends)

        for u in range(6):
            walk_fold(
                f"f{u}",
                mlp_folds[u],
                f"B{u // 2}",
                functools.partial(mlp_share, u),
                functools.partial(mlp_finish, u),
            )
        for p in range(2):
            for name, fold, after, last in (
                (f"p{p}", out_folds[p], "OB", out_rows),
                (f"q{p}", qkv_folds[p], "QB", qkv_rows),
            ):
                walk_fold(name, fold, after, functools.partial(fold.add, last))

        def walk_core(name, product, after):
            def start():
                do(after)
                product.start()

            steps[name] = Walk(start, lambda: product.copy.wait_recv())

        for m in range(3):
            walk_core(f"K{m}", mlp_products[m], f"W{m}")
        walk_core("KO", out_product, "OA")
        walk_core("KQ", qkv_product, "QA")
        once("D", lambda: (grad_branch.at[side], grad_branch.at[side]), None, "MR")
        once("N", lambda: (norm_away, norm_in), None, "NA")

        quarter = block // 2
        there = pl.ds(pl.multiple_of(side_other * quarter, 16), quarter)
        here = pl.ds(pl.multiple_of(side * quarter, 16), quarter)

        def gains_away():
            for name in ("q0", "q1", "f2", "f3", "f4", "f5"):
                steps[name].finish()
            pushes["X"] = Push(lambda: (gain_sums.at[:, there], gain_in), None)

        def gains_near():
            pushes["X"].wait_recv()
            gain_grads[...] = gain_sums[:, here, :] + gain_in[...]

        steps["X"] = Walk(gains_away, gains_near)

        def follow(order):
            for name in order:
                if name in works:
                    do(name)
                else:
                    steps[name].step()

        down_tiles = spread(down_full, bit_count, 512)

        def down_load(i, held_down):
            return keep(down_full.at[down_tiles[i][0]], held_down.at[i % 2])

        def first_phase(held_rows, held_cot, held_hid, held_down):
            loads = [
                keep(cot_all, held_cot),
                keep(hid.at[0], held_hid.at[0]),
                keep(normed_two, held_rows),
                keep(hid.at[1], held_hid.at[1]),
            ]
            down_first = down_load(0, held_down)
            pl.semaphore_wait(barrier, bit_count + 1)
            waited = set()

            def ready(*numbers):
                for n in numbers:
                    if n not in waited:
                        waited.add(n)
                        loads[n].wait()

            sources = [
                (held_cot, held_hid.at[0], away_slots.at[0], (0, 1)),
                (held_rows, held_hid.at[1], away_slots.at[1], (2, 3)),
                (held_rows, held_hid.at[1], away_slots.at[0], (2, 4)),
            ]

            def away_work(m):
                def run():
                    left, right, slot, numbers = sources[m]
                    if m == 2:
                        do("B1")
                        loads.append(keep(hid.at[2], held_hid.at[1]))
                        sent(mlp_products[0].copy)
                    ready(*numbers)
                    mlp_products[m].away(left, right, slot)

                return run

            def near_work(m):
                def run():
                    steps[f"K{m}"].finish()
                    mlp_products[m].near(*sources[m][:2])

                return run

            for m in range(3):
                works[f"W{m}"] = away_work(m)
                works[f"B{m}"] = near_work(m)
            def out_product_rows():
                ready(1)
                load = down_first
                for i, (index, count) in enumerate(down_tiles):
                    load.wait()
                    if i + 1 < len(down_tiles):
                        load = down_load(i + 1, held_down)
                    to = slice(i * count, (i + 1) * count)
                    weights = held_down[i % 2].reshape(count, hidden_width)
                    for zone in range(2):
                        at = slice(zone * rows, (zone + 1) * rows)
                        value = dot(held_hid[0, at, :], weights, ((1,), (1,))).astype(bf16)
                        out_part[zone, :, :, to] = value.reshape(2, own_rows, count)

            works["O"] = out_product_rows
            follow(BACKWARD_ORDER[:phase_at])
            for name in ("B0", "B1", "B2", "O"):
                do(name)
            for m in (1, 2):
                sent(mlp_products[m].copy)

        phase_at = BACKWARD_ORDER.index("MR")
        tile_shape = down_full.shape[len(spread(down_full, bit_count, 512)[0][0]) :]
        pl.run_scoped(
            first_phase,
            pltpu.VMEM(normed_two.shape, bf16),
            pltpu.VMEM(cot_all.shape, bf16),
            pltpu.VMEM((2,) + hid.shape[1:], bf16),
            pltpu.VMEM((2,) + tile_shape, bf16),
        )

        def second_phase(
            weights, held_probs, projected, attended, grad_att, grad_qkv, acc, turned
        ):
            qkv_width = query_width + tile
            lead_all = (slice(None),) * (bit_count + 1)
            loads = {
                "out": keep(out_full, weights.at[lead_all + (pl.ds(0, query_width),)]),
                "probs": keep(probs.at[pl.ds(0, HEADS_PER_KV)], held_probs),
                "projected": keep(projected_in, projected),
                "attended": keep(attended_in, attended),
            }

            def ready(*names):
                for name in names:
                    if name in loads:
                        loads.pop(name).wait()

            def middle_work():
                middle_load.wait()
                steps["el"].finish()
                steps["er"].finish()

                def middle_rows(at):
                    x = middle[at, :]
                    total = cot[at, :].astype(f32) + rms_grad(x, rms(x), quad_value(0, at))
                    grad_middle[at, :] = total
                    grad_branch[side, at, :] = total.astype(bf16)

                strips(own_rows, 16, middle_rows)

            works["MR"] = middle_work
            branch_flat = BranchView()
            slots = [
                away_slots.at[(i,) + (slice(None),) * bit_count + (pl.ds(0, columns),)]
                for i, columns in ((0, qkv_width), (1, query_width))
            ]

            def attended_grad():
                steps["D"].finish()
                ready("out")
                branch_all = grad_branch[...].reshape(rows, width)
                for low in range(0, query_width, 256):
                    block_of = weights[lead_all + (slice(low, low + 256),)].reshape(width, 256)
                    grad_att[:, low : low + 256] = jnp.dot(
                        branch_all, block_of, preferred_element_type=f32
                    ).astype(bf16)
                loads["qkv"] = keep(qkv_full, weights)

            works["DA"] = attended_grad

            def out_away():
                steps["D"].finish()
                ready("attended")
                out_product.away(branch_flat, attended, slots[1])

            def out_near():
                steps["KO"].finish()
                out_product.near(branch_flat, attended)
                sent(pushes["D"])
                loads["normed"] = keep(normed, grad_branch)

            works["OA"] = out_away
            works["OB"] = out_near

            pair_lanes = lax.broadcasted_iota(jnp.int32, (rows, 2 * HEAD_SIZE), 1)
            lanes = lax.broadcasted_iota(jnp.int32, (rows, key_width), 1)
            first_half = lanes % HEAD_SIZE < HEAD_SIZE // 2

            def padded(a, head, place):
                moved = a if head == place else pltpu.roll(a, HEAD_SIZE, 1)
                inside = pair_lanes < HEAD_SIZE if place == 0 else pair_lanes >= HEAD_SIZE
                return jnp.where(inside, moved, 0.0).astype(bf16)

            def unrotate(a):
                forward = pltpu.roll(a, key_width - HEAD_SIZE // 2, 1)
                back = pltpu.roll(a, HEAD_SIZE // 2, 1)
                return a * cosines[...] - jnp.where(first_half, forward, back) * sines[...]

            heads = key_width // HEAD_SIZE
            pairs = HEADS_PER_KV // 2
            tile_rows = 128
            lane_tile = lax.broadcasted_iota(jnp.int32, (tile_rows, 2 * HEAD_SIZE), 1)
            totals = []
            heads_at = {}

            def head_pair(n):
                def run():
                    head, i = n // pairs, n % pairs
                    if i == 0:
                        do("DA")
                        ready("probs", "projected")
                        if head > 0:
                            first = head * HEADS_PER_KV
                            keep(probs.at[pl.ds(first, HEADS_PER_KV)], held_probs).wait()
                        keys32 = projected[:, :key_width].astype(f32)
                        values32 = projected[:, key_width:tile].astype(f32)
                        heads_at["keys"] = [padded(keys32, head, p) for p in range(2)]
                        heads_at["values"] = [padded(values32, head, p) for p in range(2)]
                        acc[...] = jnp.zeros_like(acc)
                    keys_at, values_at = heads_at["keys"], heads_at["values"]
                    columns = slice(n * 128, (n + 1) * 128)
                    query_columns = slice(tile + n * 128, tile + (n + 1) * 128)
                    places = [
                        (low, low + tile_rows, p)
                        for low in range(0, rows, tile_rows)
                        for p in range(2)
                    ]
                    insides = [lane_tile < HEAD_SIZE, lane_tile >= HEAD_SIZE]
                    prob = [
                        held_probs[2 * i + p, low:high, :high] for low, high, p in places
                    ]
                    grad_prob = [
                        dot(grad_att[low:high, columns], values_at[p][:high], ((1,), (1,)))
                        for low, high, p in places
                    ]
                    prob32 = [a.astype(f32) for a in prob]
                    weighted = [a * b for a, b in zip(prob32, grad_prob)]
                    centre = [jnp.sum(a, axis=-1, keepdims=True) for a in weighted]
                    grad_score = [
                        (a - b * c).astype(bf16) for a, b, c in zip(weighted, prob32, centre)
                    ]
                    grad_query = [
                        jnp.dot(a, keys_at[p][:high], preferred_element_type=f32)
                        for a, (low, high, p) in zip(grad_score, places)
                    ]
                    for j, (low, high, p) in enumerate(places):
                        query = projected[low:high, query_columns].astype(f32)
                        only_query = jnp.where(insides[p], query, 0.0).astype(bf16)
                        out32 = grad_att[low:high, columns].astype(f32)
                        only_grad = jnp.where(insides[p], out32, 0.0).astype(bf16)
                        acc[0, :high, :] += dot(grad_score[j], only_query, ((0,), (0,)))
                        acc[1, :high, :] += dot(prob[j], only_grad, ((0,), (0,)))
                        if p == 1:
                            total = grad_query[j - 1] + grad_query[j]
                            acc[2, low:high, :] = total * HEAD_SIZE**-0.5
                    grad_qkv[:, query_columns] = unrotate(acc[2]).astype(bf16)
                    if i == pairs - 1:
                        totals.append([acc[j] + pltpu.roll(acc[j], HEAD_SIZE, 1) for j in range(2)])

                return run

            for n in range(query_width // 128):
                works[f"T{n}"] = head_pair(n)

            def qkv_away():
                lower = pair_lanes < HEAD_SIZE
                grad_keys = unrotate(jnp.where(lower, totals[0][0], totals[1][0]))
                grad_qkv[:, :key_width] = grad_keys.astype(bf16)
                grad_values = jnp.where(lower, totals[0][1], totals[1][1])
                grad_qkv[:, key_width:tile] = grad_values.astype(bf16)
                ready("normed")
                qkv_product.away(branch_flat, grad_qkv, slots[0])

            def qkv_near():
                steps["KQ"].finish()
                qkv_product.near(branch_flat, grad_qkv)

            works["QA"] = qkv_away
            works["QB"] = qkv_near
            tiles = spread(weights, bit_count, 512)

            def norm_part(which, give):
                ready("qkv")
                at = pl.ds(pl.multiple_of(which * own_rows, 64), own_rows)
                chosen = grad_qkv[at, :]
                for i, (index, count) in enumerate(tiles):
                    block_of = weights[index].reshape(count, qkv_width)
                    give(slice(i * count, (i + 1) * count), dot(chosen, block_of, ((1,), (1,))))

            def give_away(to, value):
                norm_away[:, to] = value.astype(bf16)

            def give_near(to, value):
                middle[:, to] = value

            works["NA"] = lambda: norm_part(side_other, give_away)

            def result_work():
                steps["ol"].finish()
                steps["or"].finish()

                def result_rows(at):
                    result[at, :] = (middle[at, :] + quad_value(1, at)).astype(bf16)

                strips(own_rows, 16, result_rows)

            works["RR"] = result_work

            def near_rows():
                do("RR")
                norm_part(side, give_near)

            works["NB"] = near_rows

            def input_work():
                do("NB")
                steps["N"].finish()

                def input_rows(at):
                    x = tok[at, :].astype(f32)
                    scaled = middle[at, :] + norm_in[at, :].astype(f32)
                    total = grad_middle[at, :] + rms_grad(x, rms(x), scaled)
                    input_grad[at, :] = total.astype(bf16)

                strips(own_rows, 16, input_rows)

            works["IR"] = input_work

            def turn_down():
                steps["f0"].finish()
                steps["f1"].finish()
                for h, start in ((0, own_half), (1, other_half)):
                    if h == 1:
                        turn_copies.pop().wait()
                    turned[...] = down_held[h].T
                    turn_copies.append(keep(turned, down_grad.at[pl.ds(start, hidden_width)]))

            def turn_out():
                steps["p0"].finish()
                steps["p1"].finish()
                out_grad[...] = out_sum[...].T

            turn_copies = []
            works["TD"] = turn_down
            works["TO"] = turn_out
            follow(BACKWARD_ORDER[phase_at:])
            for name in works:
                do(name)
            for product in (out_product, qkv_product):
                sent(product.copy)
            for copy in turn_copies:
                copy.wait()

        class BranchView:
            def __getitem__(self, index):
                return grad_branch[(slice(None), slice(None), index[1])].reshape(rows, -1)

        pl.run_scoped(
            second_phase,
            pltpu.VMEM(qkv_full.shape, bf16),
            pltpu.VMEM((HEADS_PER_KV,) + probs.shape[1:], bf16),
            pltpu.VMEM(projected_in.shape, bf16),
            pltpu.VMEM(attended_in.shape, bf16),
            pltpu.VMEM(attended_in.shape, bf16),
            pltpu.VMEM(projected_in.shape, bf16),
            pltpu.VMEM((3, rows, 2 * HEAD_SIZE), f32),
            pltpu.VMEM((hid.shape[-1], block), f32),
        )

        for name in steps:
            steps[name].finish()
        for copy in stage_copies:
            copy().wait()
        for copy in list(unsent):
            sent(copy)

    def call(
        normed_two,
        cot_all,
        hid,
        grad_part,
        down_full,
        middle,
        tok,
        cot,
        out_full,
        qkv_full,
        normed,
        projected,
        probs,
        attended,
        cosines,
        sines,
        w_query,
        key_value,
        w_gateup,
        gains,
    ):
        bf16, f32 = jnp.bfloat16, jnp.float32
        own_rows, width = tok.shape
        half = width // 2
        block, qkv_width = qkv_full.shape[-2:]
        query_width = out_full.shape[-1]
        mlp_width = hid.shape[-1]
        shape = jax.ShapeDtypeStruct
        whole = pl.BlockSpec(memory_space=pltpu.VMEM)
        away = pl.BlockSpec(memory_space=pl.ANY)

        def twos(count):
            return (2,) * count

        slots = [
            shape(twos(bit_count - 2 - i) + (block, mlp_width), bf16) for i in range(step_count)
        ] * 3

        def steps_of(order, columns):
            return [
                pltpu.VMEM(twos(bit_count - 2 - i) + (block, columns), bf16)
                for i in range(len(order))
            ]

        def at_core(columns):
            return twos(bit_count - 1) + (block, columns)

        count = 6 * (step_count + 2) + 6 * bit_count + 24
        outs = pl.pallas_call(
            kernel,
            out_shape=[
                shape((own_rows, width), bf16),
                shape((own_rows, width), bf16),
                shape((block, query_width), f32),
                shape(key_value.shape, f32),
                shape((query_width, block), f32),
                shape(w_gateup.shape, f32),
                shape((2 * mlp_width, block), f32),
                shape((2, block // 2, 128), f32),
            ]
            + slots,
            in_specs=[away] * 6 + [whole] * 2 + [away] * 6 + [whole] * 4 + [away, whole],
            out_specs=[whole] * 5 + [away] * 2 + [whole] + [away] * len(slots),
            scratch_shapes=[
                pltpu.VMEM(twos(bit_count - 2) + (block, mlp_width), bf16),
                pltpu.VMEM((2, 2, own_rows, width), bf16),
                pltpu.VMEM((2,) + at_core(mlp_width), bf16),
                pltpu.VMEM((3,) + at_core(mlp_width), bf16),
                pltpu.VMEM((3, 2, block, mlp_width), bf16),
                pltpu.VMEM(at_core(qkv_width), bf16),
                pltpu.VMEM(at_core(query_width), bf16),
                pltpu.VMEM((2, 2, 2, own_rows, half), bf16),
                pltpu.VMEM((2, 2, own_rows, half), bf16),
                pltpu.VMEM((2, 2, own_rows, half), bf16),
                pltpu.VMEM((own_rows, width), f32),
                pltpu.VMEM((own_rows, width), f32),
                pltpu.VMEM((2, own_rows, width), bf16),
                pltpu.VMEM((own_rows, width), bf16),
                pltpu.VMEM((own_rows, width), bf16),
                pltpu.VMEM((2, block // 2, mlp_width), f32),
                pltpu.VMEM((2, block, mlp_width), f32),
                pltpu.VMEM((block, query_width), f32),
                pltpu.VMEM((block, mlp_width), bf16),
                pltpu.VMEM((2, block, 128), f32),
                pltpu.VMEM((2, block // 2, 128), f32),
                pltpu.VMEM((2, block, 128), f32),
                pltpu.SemaphoreType.DMA((count,)),
                pltpu.SemaphoreType.DMA((count,)),
                pltpu.SemaphoreType.DMA((6 * step_count + 64,)),
            ]
            + steps_of(qkv_order, qkv_width)
            + steps_of(qkv_order, query_width),
            compiler_params=pltpu.CompilerParams(
                collective_id=2, has_side_effects=True, vmem_limit_bytes=63 * 1024 * 1024
            ),
            name="backward",
        )(
            normed_two,
            cot_all,
            hid,
            grad_part,
            down_full,
            middle,
            tok,
            cot,
            out_full,
            qkv_full,
            normed,
            projected,
            probs,
            attended,
            cosines,
            sines,
            w_query,
            key_value,
            w_gateup,
            gains,
        )
        return outs[:8]

    return call


def pass_on(arrays):
    count = len(arrays)

    def kernel(*refs):
        sources, targets = refs[:count], refs[count : 2 * count]
        held, sems = refs[2 * count : 3 * count], refs[3 * count]
        loads = []
        for i in range(count):
            loads.append(pltpu.make_async_copy(sources[i], held[i], sems.at[0, i]))
            loads[i].start()
        stores = []
        for i in range(count):
            loads[i].wait()
            stores.append(pltpu.make_async_copy(held[i], targets[i], sems.at[1, i]))
            stores[i].start()
        for copy in stores:
            copy.wait()

    away = pl.BlockSpec(memory_space=pl.ANY)
    return pl.pallas_call(
        kernel,
        out_shape=[jax.ShapeDtypeStruct(a.shape, a.dtype) for a in arrays],
        in_specs=[away] * count,
        out_specs=[away] * count,
        scratch_shapes=[pltpu.VMEM(a.shape, a.dtype) for a in arrays]
        + [pltpu.SemaphoreType.DMA((2, count))],
        compiler_params=pltpu.CompilerParams(vmem_limit_bytes=62 * 1024 * 1024),
        cost_estimate=pl.CostEstimate(
            flops=0, bytes_accessed=2 * sum(a.size * a.dtype.itemsize for a in arrays), transcendentals=0
        ),
        name="pass_on",
    )(*arrays)


def make_body(dp_size):
    bit_count = dp_size.bit_length() - 1
    high_bits = tuple(range(bit_count - 1, SHARE_BIT, -1))

    def body(
        tokens,
        attn_gain,
        w_query,
        keyvalue_weight,
        w_out,
        mlp_gain,
        w_gateup,
        w_down,
        segment_ids,
        positions,
        cotangent,
    ):
        f32 = jnp.float32
        own_rows, width = tokens.shape

        gains = jnp.stack([attn_gain, mlp_gain]).astype(f32)
        order = jnp.arange(segment_ids.shape[0])
        allowed = (segment_ids[:, None] == segment_ids[None, :]) & (
            order[:, None] >= order[None, :]
        )
        bias = jnp.where(allowed, 0.0, -1e30).astype(f32)

        cosine_table, sine_table = rotary_tables(positions, HEAD_SIZE)
        sine_table = jnp.where(jnp.arange(HEAD_SIZE) < HEAD_SIZE // 2, -sine_table, sine_table)
        cosine_table = jnp.concatenate([cosine_table, cosine_table], axis=1)
        sine_table = jnp.concatenate([sine_table, sine_table], axis=1)
        (
            qkv_full,
            out_full,
            probs,
            normed,
            projected,
            attended,
            middle,
            normed_two,
            grad_all,
            hid,
            grad_part,
            down_full,
        ) = make_forward(dp_size, high_bits)(
            tokens,
            cotangent,
            w_query,
            keyvalue_weight,
            w_out,
            w_gateup,
            w_down,
            gains,
            cosine_table,
            sine_table,
            bias,
        )
        normed_two = normed_two.reshape(4 * own_rows, width)
        grad_all = grad_all.reshape(4 * own_rows, width)

        quad_shape = (2, 2, own_rows, width)
        (
            result,
            input_grad,
            query_grad,
            keyval_grad,
            out_grad,
            gateup_grad,
            down_grad,
            gain_grads,
        ) = make_backward(dp_size, high_bits)(
            normed_two,
            grad_all,
            hid,
            grad_part.reshape(quad_shape),
            down_full,
            middle,
            tokens,
            cotangent,
            out_full,
            qkv_full,
            normed.reshape(2, own_rows, width),
            projected,
            probs,
            attended,
            cosine_table,
            sine_table,
            w_query,
            keyvalue_weight,
            w_gateup,
            gains,
        )
        result, input_grad, query_grad, keyval_grad, out_grad, gateup_grad, down_grad = pass_on(
            [result, input_grad, query_grad, keyval_grad, out_grad, gateup_grad, down_grad]
        )
        return (
            result,
            input_grad,
            gain_grads[0, :, 0],
            query_grad,
            keyval_grad,
            out_grad,
            gain_grads[1, :, 0],
            gateup_grad,
            down_grad,
        )

    return body


def solution(mesh):
    return jax.shard_map(
        make_body(mesh.shape["dp"]),
        mesh=mesh,
        in_specs=(
            P(("dp", "tensor"), None),
            P("dp"),
            P("dp", "tensor"),
            P(None, "dp", "tensor"),
            P("tensor", "dp"),
            P("dp"),
            P(None, "dp", "tensor"),
            P("tensor", "dp"),
            P("dp"),
            P("dp"),
            P(("dp", "tensor"), None),
        ),
        out_specs=(
            P(("dp", "tensor"), None),
            P(("dp", "tensor"), None),
            P(("dp", "tensor")),
            P("dp", "tensor"),
            P(None, "dp", "tensor"),
            P("tensor", "dp"),
            P(("dp", "tensor")),
            P(None, "dp", "tensor"),
            P("tensor", "dp"),
        ),
        check_vma=False,
    )
```

```python
import functools
import math

import jax
import jax.numpy as jnp
from jax import lax
from jax.experimental import pallas as pl
from jax.experimental.pallas import tpu as pltpu
from jax.sharding import PartitionSpec as P

MESH = pl.DeviceIdType.MESH

QUERY_HEAD_COUNT = 32
KEYVALUE_HEADS = 4
HEAD_SIZE = 64
HEADS_PER_KV = QUERY_HEAD_COUNT // KEYVALUE_HEADS
norm_eps = 1e-05

CORE_BIT = 0
SHARE_BIT = 2


FORWARD_ORDER = (
    "q1", "u1", "q0", "o", "W", "q1", "q0", "q1", "o", "c", "t", "q0", "o", "q1", "t", "q1", "q0",
    "N", "u0", "q0", "K", "u1", "c", "Q0", "u3", "u0", "Q1", "A0", "A1", "u1", "Q2", "A2", "A3",
    "Q3", "u5", "A4", "u4", "u3", "o", "A5", "o", "u2", "u0", "A6", "A7", "u1", "OA", "ON", "u4",
    "b", "u3", "b", "M", "nr", "u2", "u1", "c", "u4", "nl", "nl", "DHb", "u2", "nr", "u5", "u0",
    "u0", "u3", "u4", "DHa", "u5", "u2", "nr", "u3", "u2", "u4", "nl", "Ga", "Ua", "Ea", "u5", "Gb",
    "u5", "Ub", "Eb",
)

BACKWARD_ORDER = (
    "er", "el", "W0", "K0", "W1", "K1", "K1", "B1", "f2", "er", "K0", "el", "f3", "O", "ol", "or",
    "W2", "K2", "er", "f2", "el", "B0", "K2", "f1", "B2", "MR", "D", "f3", "f0", "f2", "ol", "or",
    "D", "DA", "f1", "f3", "OA", "KO", "KO", "OB", "T0", "T1", "f4", "T2", "T3", "p0", "T4", "f0",
    "p1", "f4", "T5", "f5", "T6", "T7", "ol", "QA", "f1", "p1", "NA", "p0", "KQ", "KQ", "QB", "N",
    "q0", "q1", "f1", "f5", "f4", "or", "p0", "f0", "f3", "f4", "N", "RR", "q0", "p0", "q1", "f5",
    "NB", "IR", "q0", "p1", "f0", "q1", "q0", "p1", "TD", "f2", "TO", "f5", "q1", "X", "X",
)


def rotary_tables(places, lanes):
    lane = jnp.arange(lanes)
    freqs = jnp.exp((lane % (HEAD_SIZE // 2)).astype(jnp.float32) * (-2 * math.log(10000.0) / HEAD_SIZE))
    turned = places.astype(jnp.float32)[:, None] * freqs[None, :]
    sign = jnp.where(lane % HEAD_SIZE < HEAD_SIZE // 2, -1.0, 1.0)
    return (jnp.cos(turned), jnp.sin(turned) * sign[None, :])


def dot(left, right, contract):
    return lax.dot_general(left, right, (contract, ((), ())), preferred_element_type=jnp.float32)


def rms(rows):
    return lax.rsqrt(jnp.mean(rows * rows, axis=-1, keepdims=True) + norm_eps)


def rms_grad(rows, inverse, grad_scaled):
    inner = jnp.mean(grad_scaled * rows, axis=-1, keepdims=True)
    return inverse * grad_scaled - rows * (inverse * inverse * inverse) * inner


def spread(ref, lead, row_tile):
    sizes = ref.shape
    block = sizes[-2]
    kept = 0
    while block * 2**kept < row_tile and kept < lead:
        kept += 1
    out = []
    for i in range(2 ** (lead - kept)):
        index = tuple((i >> (lead - kept - 1 - j)) & 1 for j in range(lead - kept))
        out.append((index, (block * 2**kept)))
    return out


def spread_gains(gains, columns):
    block = gains.shape[1]
    order = [lax.broadcasted_iota(jnp.int32, (block, block), axis) for axis in range(2)]
    for i in range(gains.shape[0]):
        only = jnp.where(order[0] == order[1], gains[i : i + 1, :], 0.0)
        columns[i] = jnp.broadcast_to(jnp.sum(only, axis=1, keepdims=True), columns.shape[1:])


def make_forward(dp_size, high_bits):
    bit_count = dp_size.bit_length() - 1
    all_bits = tuple(range(bit_count))

    def kernel(
        tok,
        cot,
        w_query,
        key_value,
        w_out,
        w_gateup,
        w_down,
        gains,
        cosines,
        sines,
        bias,
        qkv_full,
        out_full,
        probs,
        normed_to,
        projected_to,
        attended_to,
        middle_to,
        normed_two_to,
        cot_all_to,
        hid_to,
        grad_part_to,
        down_full,
        normed,
        projected,
        attended,
        middle,
        normed_two,
        cot_all,
        hid,
        grad_part,
        qkv_held,
        out_held,
        mlp_held,
        tok_all,
        branch_away,
        branch_in,
        prob_stage,
        mlp_other,
        gain_columns,
        send_sem,
        recv_sem,
        local_sem,
    ):
        f32, bf16 = jnp.float32, jnp.bfloat16
        me = lax.axis_index("dp")
        side = lax.axis_index("tensor")
        bits = [(me // 2**k) % 2 for k in all_bits]
        share = bits[SHARE_BIT]
        own_rows, width = tok.shape
        half = width // 2
        group_rows = 2 * own_rows
        query_width = attended.shape[1]
        key_width = (projected.shape[1] - query_width) // 2
        tile = 2 * key_width
        hidden_width = hid.shape[-1]

        def partner(k):
            if k is None:
                return {"tensor": 1 - side}
            return {"dp": me + (1 - 2 * bits[k]) * 2**k}

        barrier = pltpu.get_barrier_semaphore()
        for k in all_bits + (None,):
            pl.semaphore_signal(barrier, inc=1, device_id=partner(k), device_id_type=MESH)

        own = tuple(bits[k] for k in reversed(all_bits))
        everything = (slice(None), slice(None))
        halves = [pl.multiple_of(h * hidden_width, 128) for h in (share, 1 - share)]
        raw = {}
        for m in range(2):
            for h in range(2):
                block_at = hid.at[m, pl.ds(h * w_query.shape[0], w_query.shape[0])]
                columns = pl.ds(halves[h], hidden_width)
                raw[m, h] = pltpu.make_async_copy(
                    w_gateup.at[m, :, columns], block_at, local_sem.at[2 * m + h]
                )
                raw[m, h].start()

        spread_gains(gains, gain_columns)

        def scaled(a, gain):
            return (a.astype(f32) * gain_columns[gain][:, :1]).astype(bf16)

        qkv_held[own + (slice(None), slice(0, key_width))] = scaled(key_value[0], 0)
        qkv_held[own + (slice(None), slice(key_width, tile))] = scaled(key_value[1], 0)
        qkv_held[own + (slice(None), slice(tile, tile + query_width))] = scaled(
            w_query[...], 0
        )
        out_held[own + everything] = w_out[...].T

        pl.semaphore_wait(barrier, bit_count + 1)

        counter, local_counter = [0], [4]
        started = []

        def push(src, dst, k):
            i = counter[0]
            counter[0] += 1
            copy = pltpu.make_async_remote_copy(
                src_ref=src,
                dst_ref=dst,
                send_sem=send_sem.at[i],
                recv_sem=recv_sem.at[i],
                device_id=partner(k),
                device_id_type=MESH,
            )
            copy.start()
            started.append(copy)
            return copy

        def keep(src, dst):
            i = local_counter[0]
            local_counter[0] += 1
            copy = pltpu.make_async_copy(src, dst, local_sem.at[i])
            copy.start()
            return copy

        def held(ref, lead, gathered, columns):
            index = tuple(
                pl.ds(0, 2) if k in gathered else bits[k] for k in reversed(all_bits)
            )
            return ref.at[lead + index + (slice(None), columns)]

        class Chain:
            def __init__(self, src, ref, lead, order, columns):
                self.src, self.ref, self.lead, self.columns = src, ref, lead, columns
                self.order = list(order)
                self.gathered = set()
                self.copy = self.bit = None
                self.done = False

            def step(self):
                if self.done:
                    return
                if self.copy is None:
                    self.bit = self.order.pop(0)
                    place = held(self.ref, self.lead, (), self.columns)
                    view = place
                    if self.src is not None:
                        self.src[0]()
                        view = self.src[1].at[:, self.columns]
                    self.copy = push(view, place, self.bit)
                    return
                self.copy.wait_recv()
                self.gathered.add(self.bit)
                if not self.order:
                    self.done = True
                    return
                self.bit = self.order.pop(0)
                view = held(self.ref, self.lead, self.gathered, self.columns)
                self.copy = push(view, view, self.bit)

            def finish(self):
                while not self.done:
                    self.step()

        class Shift:
            def __init__(self, *ends):
                self.ends = list(ends)
                self.copy = None
                self.done = False

            def step(self):
                if self.copy is not None:
                    self.copy.wait_recv()
                    self.copy = None
                if self.ends:
                    self.copy = push(*self.ends.pop(0)())
                else:
                    self.done = True

            def finish(self):
                while not self.done:
                    self.step()

        cut = (hidden_width // 2 + 127) // 128 * 128
        pieces = [pl.ds(0, cut), pl.ds(cut, hidden_width - cut)]
        early = tile + query_width // 2
        full_order = high_bits + (SHARE_BIT, 1, 0)
        steps = {}
        prepared = set()

        def prepare(m):
            if m in prepared:
                return
            prepared.add(m)
            for h in range(2):
                if m == 0:
                    value = w_down[pl.ds(pl.multiple_of(halves[h], 128), hidden_width), :].T
                else:
                    raw[m - 1, h].wait()
                    rows = slice(h * w_query.shape[0], (h + 1) * w_query.shape[0])
                    value = scaled(hid[m - 1, rows, :], 1)
                if h == 0:
                    mlp_held[(m,) + own + everything] = value
                else:
                    mlp_other[m] = value

        steps["q0"] = Chain(None, qkv_held, (), full_order, pl.ds(0, early))
        steps["q1"] = Chain(
            None, qkv_held, (), full_order, pl.ds(early, query_width + tile - early)
        )
        steps["o"] = Chain(None, out_held, (), full_order, pl.ds(0, query_width))
        for m in range(3):
            for p in range(2):
                steps[f"u{2 * m + p}"] = Chain(
                    (functools.partial(prepare, m), mlp_other.at[m]),
                    mlp_held,
                    (m,),
                    (SHARE_BIT,) + high_bits + (1, 0),
                    pieces[p],
                )
        first = pl.ds(0, half)
        far = pl.ds(half, half)
        steps["t"] = Shift(lambda: (tok, tok_all.at[side], None))
        steps["c"] = Shift(
            lambda: (cot, cot_all.at[share, side], SHARE_BIT),
            lambda: (cot_all.at[:, side], cot_all.at[:, side], None),
        )
        steps["b"] = Shift(lambda: (branch_away, branch_in, None))
        two = normed_two
        steps["nr"] = Shift(
            lambda: (two.at[share, side, :, far], two.at[share, side, :, far], SHARE_BIT),
            lambda: (two.at[:, side, :, far], two.at[:, side, :, far], None),
        )
        steps["nl"] = Shift(
            lambda: (two.at[share, side, :, first], two.at[share, side, :, first], None),
            lambda: (two.at[share, :, :, first], two.at[share, :, :, first], SHARE_BIT),
        )

        own_cot = keep(cot, cot_all.at[share, side])
        own_tok = keep(tok, tok_all.at[side])
        out_copies = []
        works = {}

        def start_all():
            for copy in (own_tok, own_cot):
                copy.wait()

        works["W"] = start_all

        def norm():
            steps["t"].finish()

            def norm_rows(r, _):
                rows = pl.ds(pl.multiple_of(r * 16, 16), 16)
                for s in range(2):
                    x = tok_all[s, rows, :].astype(f32)
                    scaled = x * lax.rsqrt(jnp.mean(x * x, axis=-1, keepdims=True) + norm_eps)
                    normed[pl.ds(s * own_rows + r * 16, 16), :] = scaled.astype(bf16)
                return 0

            lax.fori_loop(0, own_rows // 16, norm_rows, 0)

        works["N"] = norm

        lanes = lax.broadcasted_iota(jnp.int32, (group_rows, tile), 1)
        first_half = lanes % HEAD_SIZE < HEAD_SIZE // 2
        lead = (slice(None),) * bit_count + (slice(None),)
        values = {}

        def rotate(a):
            cos2 = jnp.concatenate([cosines[...], cosines[...]], axis=1)
            sin2 = jnp.concatenate([sines[...], sines[...]], axis=1)
            forward = pltpu.roll(a, tile - HEAD_SIZE // 2, 1)
            back = pltpu.roll(a, HEAD_SIZE // 2, 1)
            return a * cos2 + jnp.where(first_half, forward, back) * sin2

        def project(columns):
            weights = qkv_held[lead + (columns,)].reshape(width, tile)
            return jnp.dot(normed[...], weights, preferred_element_type=f32)

        def keys_values():
            steps["q0"].finish()
            first = project(slice(0, tile))
            values["keys"] = rotate(first)[:, :key_width].astype(bf16)
            values["values"] = first[:, key_width:].astype(bf16)
            projected[:, :key_width] = values["keys"]
            projected[:, key_width:tile] = values["values"]

        def queries(i):
            def run():
                if i >= query_width // tile // 2:
                    steps["q1"].finish()
                    if not out_copies:
                        out_copies.append(keep(qkv_held, qkv_full))
                columns = slice(tile + i * tile, tile + (i + 1) * tile)
                rotated = rotate(project(columns)).astype(bf16)
                projected[:, columns] = rotated * jnp.asarray(HEAD_SIZE**-0.5, bf16)

            return run

        works["K"] = keys_values
        for i in range(query_width // tile):
            works[f"Q{i}"] = queries(i)

        rows_tile = 128
        pair_lanes = lax.broadcasted_iota(jnp.int32, (group_rows, 2 * HEAD_SIZE), 1)
        pairs = HEADS_PER_KV // 2
        prob_copies = {}

        def padded(a, head, place):
            moved = a if head == place else pltpu.roll(a, HEAD_SIZE, 1)
            inside = pair_lanes < HEAD_SIZE if place == 0 else pair_lanes >= HEAD_SIZE
            return jnp.where(inside, moved, 0.0).astype(bf16)

        def head_pair(n):
            def run():
                head = n // pairs
                if n % pairs == 0:
                    keys32 = values["keys"].astype(f32)
                    values32 = values["values"].astype(f32)
                    values["at"] = (
                        [padded(keys32, head, p) for p in range(2)],
                        [padded(values32, head, p) for p in range(2)],
                    )
                keys_at, values_at = values["at"]
                slot = n % 2
                if slot in prob_copies:
                    prob_copies[slot].wait()
                columns = slice(tile + n * 128, tile + (n + 1) * 128)
                places = [
                    (low, low + rows_tile, p)
                    for low in range(0, group_rows, rows_tile)
                    for p in range(2)
                ]
                scores = [
                    dot(projected[low:high, columns], keys_at[p][:high], ((1,), (1,)))
                    + bias[low:high, :high]
                    for low, high, p in places
                ]
                peaks = [jnp.max(a, axis=-1, keepdims=True) for a in scores]
                raised = [jnp.exp(a - b) for a, b in zip(scores, peaks)]
                inverses = [1.0 / jnp.sum(a, axis=-1, keepdims=True) for a in raised]
                shares = [(a * b).astype(bf16) for a, b in zip(raised, inverses)]
                for (low, high, p), a in zip(places, shares):
                    prob_stage[slot, p, low:high, :high] = a
                prob_copies[slot] = keep(prob_stage.at[slot], probs.at[pl.ds(2 * n, 2)])
                parts = [
                    jnp.dot(a, values_at[p][:high], preferred_element_type=f32)
                    for (low, high, p), a in zip(places, shares)
                ]
                for j in range(0, len(places), 2):
                    low, high, _ = places[j]
                    mixed = (parts[j] + parts[j + 1]).astype(bf16)
                    attended[low:high, n * 128 : (n + 1) * 128] = mixed

            return run

        for n in range(query_width // 128):
            works[f"A{n}"] = head_pair(n)

        tiles = spread(out_held, bit_count, 512)

        def branch_rows(which, give):
            rows = attended[pl.ds(pl.multiple_of(which * own_rows, 64), own_rows), :]
            for i, (index, count) in enumerate(tiles):
                weights = out_held[index].reshape(count, query_width)
                give(slice(i * count, (i + 1) * count), dot(rows, weights, ((1,), (1,))))

        def give_away(to, value):
            branch_away[:, to] = value.astype(bf16)

        def give_near(to, value):
            middle[:, to] = value

        def branch_first():
            steps["o"].finish()
            out_copies.extend(
                [
                    keep(normed, normed_to),
                    keep(projected, projected_to),
                    keep(attended, attended_to),
                ]
            )
            out_copies.append(keep(out_held, out_full))
            branch_rows(1 - side, give_away)

        works["OA"] = branch_first
        works["ON"] = lambda: branch_rows(side, give_near)

        def middle_all():
            steps["b"].finish()

            def middle_rows(r, _):
                rows = pl.ds(pl.multiple_of(r * 16, 16), 16)
                x = tok[rows, :].astype(f32) + middle[rows, :] + branch_in[rows, :].astype(f32)
                middle[rows, :] = x
                scaled = x * lax.rsqrt(jnp.mean(x * x, axis=-1, keepdims=True) + norm_eps)
                normed_two[share, side, rows, :] = scaled.astype(bf16)
                return 0

            lax.fori_loop(0, own_rows // 16, middle_rows, 0)
            out_copies.append(keep(middle, middle_to))

        works["M"] = middle_all

        bounds = [(0, cut), (cut, hidden_width)]

        def spans(p):
            start, end = bounds[p]
            return [(low, min(low + 512, end)) for low in range(start, end, 512)]

        mlp_lead = (slice(None),) * (bit_count + 1)

        def mlp_product(m, rows_ref, quarter, low, high):
            weights = mlp_held[(m,) + mlp_lead + (slice(low, high),)].reshape(width, high - low)
            return jnp.dot(
                rows_ref[quarter].reshape(group_rows, width), weights, preferred_element_type=f32
            )

        def rows_of(quarter):
            return slice(quarter * group_rows, (quarter + 1) * group_rows)

        prepared_out = set()

        def store_product(m, p, slot, rows_ref, *needed):
            def run():
                for name in (f"u{2 * m + p}",) + needed:
                    steps[name].finish()
                if m == 0:
                    columns = (slice(None),) * (bit_count + 1) + (pieces[p],)
                    out_copies.append(keep(mlp_held.at[(0,) + columns], down_full.at[columns]))
                if slot not in prepared_out:
                    prepared_out.add(slot)
                    target = cot_all_to if m == 0 else normed_two_to
                    out_copies.append(keep(rows_ref, target))
                for low, high in spans(p):
                    for quarter in range(2):
                        value = mlp_product(m, rows_ref, quarter, low, high)
                        hid[slot, rows_of(quarter), low:high] = value.astype(bf16)

            return run

        def up_product(p):
            def run():
                steps[f"u{4 + p}"].finish()
                for low, high in spans(p):
                    for quarter in range(2):
                        up = mlp_product(2, normed_two, quarter, low, high)
                        at = rows_of(quarter)
                        gate = hid[0, at, low:high].astype(f32)
                        grad_hidden = hid[2, at, low:high].astype(f32)
                        sig = jax.nn.sigmoid(gate)
                        silu = gate * sig
                        slope = sig + silu * (1.0 - sig)
                        hid[0, at, low:high] = (silu * up).astype(bf16)
                        hid[1, at, low:high] = (grad_hidden * up * slope).astype(bf16)
                        hid[2, at, low:high] = (grad_hidden * silu).astype(bf16)
                columns = (slice(None), slice(None), pieces[p])
                out_copies.append(keep(hid.at[columns], hid_to.at[columns]))

            return run

        mlp_tiles = spread(mlp_held.at[0], bit_count, 512)
        tall = 2 * own_rows
        opened = set()

        def mlp_back(p, parts, target):
            columns = slice(*bounds[p])
            count_of = bounds[p][1] - bounds[p][0]

            def run():
                again = id(target) in opened
                opened.add(id(target))
                for i, (index, count) in enumerate(mlp_tiles):
                    to = slice(i * count, (i + 1) * count)
                    inner = (slice(None),) * (bit_count + 1 - len(index)) + (columns,)
                    for r in range(2):
                        at = slice(r * tall, (r + 1) * tall)
                        total = target[at, to].astype(f32) if again else None
                        for m, slot in parts:
                            weights = mlp_held[(m,) + index + inner].reshape(count, count_of)
                            term = dot(hid[slot, at, columns], weights, ((1,), (1,)))
                            total = term if total is None else total + term
                        target[at, to] = total.astype(bf16)
                    if again:
                        full = (slice(None), pl.ds(i * count, count))
                        out_copies.append(keep(target.at[full], grad_part_to.at[full]))

            return run

        for p, suffix in enumerate("ab"):
            works["DH" + suffix] = store_product(0, p, 2, cot_all, "c")
            works["G" + suffix] = store_product(1, p, 0, normed_two, "nl", "nr")
            works["U" + suffix] = up_product(p)
            works["E" + suffix] = mlp_back(p, ((1, 1), (2, 2)), grad_part)

        for name in FORWARD_ORDER:
            if name in works:
                works[name]()
            else:
                steps[name].step()
        for name in steps:
            steps[name].finish()
        for copy in out_copies + list(prob_copies.values()):
            copy.wait()
        for copy in started:
            copy.wait_send()

    def call(
        tok,
        cot,
        w_query,
        key_value,
        w_out,
        w_gateup,
        w_down,
        gains,
        cosines,
        sines,
        bias,
    ):
        bf16, f32 = jnp.bfloat16, jnp.float32
        own_rows, width = tok.shape
        block, query_width = w_query.shape
        qkv_width = query_width + 2 * key_value.shape[2]
        mlp_width = w_gateup.shape[2] // 2
        rows = 2 * own_rows
        twos = (2,) * bit_count
        heads = query_width // HEAD_SIZE
        whole = pl.BlockSpec(memory_space=pltpu.VMEM)
        away = pl.BlockSpec(memory_space=pl.ANY)
        count = 10 * (bit_count + 1) + 16
        shape = jax.ShapeDtypeStruct
        return pl.pallas_call(
            kernel,
            out_shape=[
                shape(twos + (block, qkv_width), bf16),
                shape(twos + (block, query_width), bf16),
                shape((heads, rows, rows), bf16),
                shape((rows, width), bf16),
                shape((rows, qkv_width), bf16),
                shape((rows, query_width), bf16),
                shape((own_rows, width), f32),
                shape((2, 2, own_rows, width), bf16),
                shape((2, 2, own_rows, width), bf16),
                shape((3, 2 * rows, mlp_width), bf16),
                shape((2 * rows, width), bf16),
                shape(twos + (block, mlp_width), bf16),
            ],
            in_specs=[whole, away, whole, whole, whole, away] + [whole] * 5,
            out_specs=[away] * 12,
            scratch_shapes=[
                pltpu.VMEM((rows, width), bf16),
                pltpu.VMEM((rows, qkv_width), bf16),
                pltpu.VMEM((rows, query_width), bf16),
                pltpu.VMEM((own_rows, width), f32),
                pltpu.VMEM((2, 2, own_rows, width), bf16),
                pltpu.VMEM((2, 2, own_rows, width), bf16),
                pltpu.VMEM((3, 2 * rows, mlp_width), bf16),
                pltpu.VMEM((2 * rows, width), bf16),
                pltpu.VMEM(twos + (block, qkv_width), bf16),
                pltpu.VMEM(twos + (block, query_width), bf16),
                pltpu.VMEM((3,) + twos + (block, mlp_width), bf16),
                pltpu.VMEM((2, own_rows, width), bf16),
                pltpu.VMEM((own_rows, width), bf16),
                pltpu.VMEM((own_rows, width), bf16),
                pltpu.VMEM((2, 2, rows, rows), bf16),
                pltpu.VMEM((3, block, mlp_width), bf16),
                pltpu.VMEM((2, block, 128), f32),
                pltpu.SemaphoreType.DMA((count,)),
                pltpu.SemaphoreType.DMA((count,)),
                pltpu.SemaphoreType.DMA((40 + heads,)),
            ],
            compiler_params=pltpu.CompilerParams(
                collective_id=1, has_side_effects=True, vmem_limit_bytes=63 * 1024 * 1024
            ),
            name="forward",
        )(
            tok,
            cot,
            w_query,
            key_value,
            w_out,
            w_gateup,
            w_down,
            gains,
            cosines,
            sines,
            bias,
        )

    return call


def make_backward(dp_size, high_bits):
    bit_count = dp_size.bit_length() - 1
    all_bits = tuple(range(bit_count))
    folded = tuple(k for k in reversed(all_bits) if k != CORE_BIT)
    low_order = tuple(range(1, SHARE_BIT)) + high_bits[::-1]
    qkv_order = (1, SHARE_BIT) + high_bits[::-1]
    out_orders = ((1, SHARE_BIT) + high_bits[::-1], (SHARE_BIT,) + high_bits[::-1] + (1,))
    step_count = len(low_order)

    def kernel(
        normed_two,
        cot_all,
        hid,
        grad_part,
        down_full,
        middle_in,
        tok,
        cot,
        out_full,
        qkv_full,
        normed,
        projected_in,
        probs,
        attended_in,
        cosines,
        sines,
        w_query,
        key_value,
        w_gateup,
        gains,
        result,
        input_grad,
        query_grad,
        keyval_grad,
        out_grad,
        gateup_grad,
        down_grad,
        gain_grads,
        *rest,
    ):
        mlp_steps = [list(rest[m * step_count : (m + 1) * step_count]) for m in range(3)]
        (
            recv_stage,
            out_part,
            away_slots,
            mlp_core,
            mlp_last,
            qkv_core,
            out_core,
            quad_in,
            quad_step,
            quad_near,
            middle,
            grad_middle,
            grad_branch,
            norm_away,
            norm_in,
            stage,
            down_held,
            out_sum,
            weight_stage,
            gain_sums,
            gain_in,
            gain_columns,
            send_sem,
            recv_sem,
            local_sem,
        ) = rest[3 * step_count : 3 * step_count + 25]
        steps = list(rest[3 * step_count + 25 :])
        qkv_steps, others_of = steps[: len(qkv_order)], steps[len(qkv_order) :]
        out_steps = (others_of, others_of)
        f32, bf16 = jnp.float32, jnp.bfloat16
        me = lax.axis_index("dp")
        side = lax.axis_index("tensor")
        bits = [(me // 2**k) % 2 for k in all_bits]
        others = [1 - b for b in bits]
        core, share = bits[CORE_BIT], bits[SHARE_BIT]
        core_other, share_other, side_other = others[CORE_BIT], others[SHARE_BIT], 1 - side
        own_rows, width = tok.shape
        half = width // 2
        rows = 2 * own_rows
        query_width = attended_in.shape[1]
        key_width = (projected_in.shape[1] - query_width) // 2
        tile = 2 * key_width
        block = width // dp_size

        partners = {k: {"dp": me + (1 - 2 * bits[k]) * 2**k} for k in all_bits}
        partners[None] = {"tensor": side_other}

        barrier = pltpu.get_barrier_semaphore()
        for k in all_bits + (None,):
            pl.semaphore_signal(barrier, inc=1, device_id=partners[k], device_id_type=MESH)

        counter, local_counter = [0], [0]
        unsent = []

        class Push:
            def __init__(self, ends, k):
                self.ends, self.k, self.i = ends, k, counter[0]
                counter[0] += 1
                self.copy().start()
                unsent.append(self)

            def copy(self):
                src, dst = self.ends()
                return pltpu.make_async_remote_copy(
                    src_ref=src,
                    dst_ref=dst,
                    send_sem=send_sem.at[self.i],
                    recv_sem=recv_sem.at[self.i],
                    device_id=partners[self.k],
                    device_id_type=MESH,
                )

            def wait_recv(self):
                self.copy().wait_recv()

        def sent(push):
            push.copy().wait_send()
            unsent[:] = [other for other in unsent if other is not push]

        def keep(src, dst):
            i = local_counter[0]
            local_counter[0] += 1
            copy = pltpu.make_async_copy(src, dst, local_sem.at[i])
            copy.start()
            return copy

        def cells(lead):
            return [tuple((i >> (lead - 1 - j)) & 1 for j in range(lead)) for i in range(2**lead)]

        def strips(count, size, work):
            def step(r, _):
                work(pl.ds(pl.multiple_of(r * size, size), size))
                return 0

            lax.fori_loop(0, count // size, step, 0)

        def half_grad(left, right, which, give):
            lead = bit_count - 1
            kept = 0
            while block * 2**kept < 256 and kept < lead:
                kept += 1
            for i in range(2 ** (lead - kept)):
                parts = []
                for j in range(2**kept):
                    pair = (i * 2**kept + j) * 2 * block
                    if block % 128 == 0:
                        at = pl.multiple_of(pair + which * block, 128)
                        parts.append(left[:, pl.ds(at, block)])
                    else:
                        low = left[:, pair : pair + block].astype(f32)
                        high = left[:, pair + block : pair + 2 * block].astype(f32)
                        parts.append(jnp.where(which == 0, low, high).astype(bf16))
                columns = jnp.concatenate(parts, axis=1)
                product = dot(columns, right[...], ((0,), (0,)))
                index = tuple((i >> (lead - kept - 1 - j)) & 1 for j in range(lead - kept))
                give(index, product.reshape((2,) * kept + (block, product.shape[-1])))

        class Product:
            def __init__(self, ref, lead):
                self.ref, self.lead, self.copy = ref, lead, None

            def away(self, left, right, slot):
                def give(index, value):
                    slot[index] = value.astype(bf16)

                half_grad(left, right, core_other, give)
                self.slot = slot

            def start(self):
                slot, ref, lead = self.slot, self.ref, self.lead
                self.copy = Push(lambda: (slot, ref.at[lead] if lead else ref), CORE_BIT)

            def near(self, left, right):

                def give(index, value):
                    at = self.lead + index
                    self.ref[at] = (value + self.ref[at].astype(f32)).astype(bf16)

                half_grad(left, right, core, give)

        class Fold:
            def __init__(self, ref, lead, start, size, steps, order, staged):
                self.ref, self.lead = ref, lead
                self.start, self.size = start, size
                self.steps = dict(zip(order, steps))
                self.order = list(order)
                self.staged = staged
                self.settled = {}
                self.copy = self.bit = None

            def place(self, cell):
                rest = iter(cell)
                return self.lead + tuple(
                    self.settled[k] if k in self.settled else next(rest) for k in folded
                )

            def open(self):
                return len(folded) - len(self.settled)

            def rows(self):
                return (pl.ds(self.start, self.size),)

            def send(self):
                self.bit = self.order.pop(0)
                self.settled[self.bit] = others[self.bit]
                twice = (pl.ds(0, 2),) * self.open()
                place = self.place(twice) + self.rows()
                target, there = self.steps[self.bit], twice + self.rows()
                self.copy = Push(lambda: (self.ref.at[place], target.at[there]), self.bit)
                self.settled[self.bit] = bits[self.bit]

            def add(self, last=None, loaded=None):
                self.copy.wait_recv()
                arrived, lead = self.steps[self.bit], ()
                if self.staged:
                    there = (pl.ds(0, 2),) * self.open() + self.rows()
                    lead = (0,) * (len(folded) - 1 - self.open())
                    keep(arrived.at[there], recv_stage.at[lead + there]).wait()
                    arrived = recv_stage
                if loaded is not None:
                    loaded.wait()
                rows_at_once = 32 if last is None and self.size % 32 == 0 else 16
                for cell in cells(self.open()):
                    place = self.place(cell)

                    def work(r, _, cell=cell, place=place):
                        at = pl.ds(pl.multiple_of(self.start + r * rows_at_once, 16), rows_at_once)
                        new, old = arrived[lead + cell + (at,)], self.ref[place + (at,)]
                        if last is None:
                            self.ref[place + (at,)] = new + old
                        else:
                            last(cell, at, new.astype(f32) + old.astype(f32))
                        return 0

                    lax.fori_loop(0, self.size // rows_at_once, work, 0)

            def step(self):
                self.add()
                self.send()

        class Walk:
            def __init__(self, *actions):
                self.actions = list(actions)
                self.taken = 0

            def step(self):
                if self.actions:
                    self.taken += 1
                    self.actions.pop(0)()

            def finish(self):
                while self.actions:
                    self.step()

        steps, works, done, pushes = {}, {}, set(), {}

        def do(name):
            if name not in done:
                done.add(name)
                works[name]()

        def once(name, ends, k, after):
            def start():
                do(after)
                pushes[name] = Push(ends, k)

            steps[name] = Walk(start, lambda: pushes[name].wait_recv())

        near_loads = {}

        def load_near(slot, p):
            n = local_counter[0]
            local_counter[0] += 1

            def copy():
                if p == 0:
                    view = grad_part.at[share, :, :, pl.ds(0, half)]
                else:
                    view = grad_part.at[:, side, :, pl.ds(half, half)]
                return pltpu.make_async_copy(view, quad_near.at[p], local_sem.at[n])

            copy().start()
            near_loads[slot, p] = copy

        def quad_half(name, slot, p):
            source = (grad_part, out_part)[slot]
            first_bit, second_bit = ((SHARE_BIT, None), (None, SHARE_BIT))[p]
            there = (side_other, share_other)[p]

            def first():
                if slot == 1:
                    do("O")

                def ends():
                    if p == 0:
                        view = source.at[share_other, :, :, pl.ds(0, half)]
                    else:
                        view = source.at[:, side_other, :, pl.ds(half, half)]
                    return view, quad_in.at[slot, p]

                pushes[name] = Push(ends, first_bit)

            def second():
                pushes[name].wait_recv()
                if slot == 0:
                    near_loads[slot, p]().wait()
                for q in range(2):

                    def work(at, q=q):
                        if slot == 0:
                            near = quad_near[p, q, at, :]
                        elif p == 0:
                            near = out_part[share, q, at, :half]
                        else:
                            near = out_part[q, side, at, half:]
                        quad_in[slot, p, q, at, :] = quad_in[slot, p, q, at, :] + near

                    strips(own_rows, 16, work)
                pushes[name] = Push(
                    lambda: (quad_in.at[slot, p, there], quad_step.at[slot, p]), second_bit
                )

            steps[name] = Walk(first, second, lambda: pushes[name].wait_recv())

        def quad_value(slot, at):
            halves = []
            for p, here in ((0, side), (1, share)):
                halves.append(
                    quad_in[slot, p, here, at, :].astype(f32) + quad_step[slot, p, at, :].astype(f32)
                )
            return jnp.concatenate(halves, axis=-1)

        quad_half("el", 0, 0)
        quad_half("er", 0, 1)
        quad_half("ol", 1, 0)
        quad_half("or", 1, 1)
        load_near(0, 0)
        load_near(0, 1)
        middle_load = keep(middle_in, middle)

        part = block // 2
        mlp_products = [Product(mlp_core, (m,)) for m in range(3)]
        mlp_folds = [
            Fold(mlp_core, (m,), p * part, part, mlp_steps[m], low_order, True)
            for m in range(3)
            for p in range(2)
        ]
        qkv_product = Product(qkv_core, ())
        out_product = Product(out_core, ())
        qkv_folds = [Fold(qkv_core, (), p * part, part, qkv_steps, qkv_order, False) for p in range(2)]
        out_folds = [Fold(out_core, (), p * part, part, out_steps[p], out_orders[p], False) for p in range(2)]
        mlp_copies = [None] * 6
        stage_copies = [None, None]
        stage_count = [0]

        def to_output(fill, dst):
            i = stage_count[0] % 2
            stage_count[0] += 1
            if stage_copies[i] is not None:
                stage_copies[i]().wait()
            fill(i)
            n = local_counter[0]
            local_counter[0] += 1

            def copy():
                return pltpu.make_async_copy(stage.at[i], dst(), local_sem.at[n])

            copy().start()
            stage_copies[i] = copy

        hidden_width = hid.shape[-1]
        own_half = pl.multiple_of(share * hidden_width, 128)
        other_half = pl.multiple_of(share_other * hidden_width, 128)
        gain_sums[1] = jnp.zeros_like(gain_sums[1])
        spread_gains(gains, gain_columns)

        def weight_rows(m, rows_of, start):
            columns = pl.ds(start, hidden_width)
            return keep(w_gateup.at[m - 1, rows_of, columns], weight_stage.at[rows_of])

        def give_rows(m, i, at, total):
            if m == 0:
                down_held[i, at, :] = total
                return
            local = pl.ds(pl.multiple_of(at.start % part, 16), 16)
            stage[i, local, :] = total * gain_columns[1, at, :][:, :1]
            weighted = total * weight_stage[at, :].astype(f32)
            gain_sums[1, at, :] += jnp.sum(weighted, axis=-1, keepdims=True)

        def mlp_share(u):
            m, fold = u // 2, mlp_folds[u]
            rows_of = pl.ds(fold.start, fold.size)
            loaded = weight_rows(m, rows_of, own_half) if m > 0 else None

            def fill(i):
                def last(cell, at, total):
                    is_own = share == cell[0]

                    @pl.when(is_own)
                    def _():
                        give_rows(m, i, at, total)

                    @pl.when(jnp.logical_not(is_own))
                    def _():
                        mlp_last[m, 0, at, :] = total.astype(bf16)

                fold.add(last, loaded)

            if m == 0:
                fill(0)
            else:
                columns = pl.ds(own_half, hidden_width)
                to_output(fill, lambda: gateup_grad.at[m - 1, rows_of, columns])
            mlp_copies[u] = Push(
                lambda: (mlp_last.at[m, 0, rows_of], mlp_last.at[m, 1, rows_of]), SHARE_BIT
            )

        def mlp_finish(u):
            m, fold = u // 2, mlp_folds[u]
            rows_of = pl.ds(fold.start, fold.size)
            loaded = weight_rows(m, rows_of, other_half) if m > 0 else None
            mlp_copies[u].wait_recv()
            if loaded is not None:
                loaded.wait()

            def fill(i):
                def work(r, _):
                    at = pl.ds(pl.multiple_of(fold.start + r * 16, 16), 16)
                    give_rows(m, i, at, mlp_last[m, 1, at, :].astype(f32))
                    return 0

                lax.fori_loop(0, fold.size // 16, work, 0)

            if m == 0:
                fill(1)
            else:
                columns = pl.ds(other_half, hidden_width)
                to_output(fill, lambda: gateup_grad.at[m - 1, rows_of, columns])

        def out_rows(cell, at, total):
            out_sum[at, :] = total

        def qkv_rows(cell, at, total):
            gain = gain_columns[0, at, :][:, :1]
            parts = [total[:, :key_width], total[:, key_width:tile], total[:, tile:]]
            weights = [key_value[0, at, :], key_value[1, at, :], w_query[at, :]]
            row_sum = sum(
                jnp.sum(p * w.astype(f32), axis=-1, keepdims=True) for p, w in zip(parts, weights)
            )
            gain_sums[0, at, :] = jnp.broadcast_to(row_sum, (16, 128))
            keyval_grad[0, at, :] = parts[0] * gain
            keyval_grad[1, at, :] = parts[1] * gain
            query_grad[at, :] = parts[2] * gain

        def walk_fold(name, fold, after, *ends):
            def start():
                do(after)
                fold.send()

            steps[name] = Walk(start, *([fold.step] * (len(fold.order) - 1)), *ends)

        for u in range(6):
            walk_fold(
                f"f{u}",
                mlp_folds[u],
                f"B{u // 2}",
                functools.partial(mlp_share, u),
                functools.partial(mlp_finish, u),
            )
        for p in range(2):
            for name, fold, after, last in (
                (f"p{p}", out_folds[p], "OB", out_rows),
                (f"q{p}", qkv_folds[p], "QB", qkv_rows),
            ):
                walk_fold(name, fold, after, functools.partial(fold.add, last))

        def walk_core(name, product, after):
            def start():
                do(after)
                product.start()

            steps[name] = Walk(start, lambda: product.copy.wait_recv())

        for m in range(3):
            walk_core(f"K{m}", mlp_products[m], f"W{m}")
        walk_core("KO", out_product, "OA")
        walk_core("KQ", qkv_product, "QA")
        once("D", lambda: (grad_branch.at[side], grad_branch.at[side]), None, "MR")
        once("N", lambda: (norm_away, norm_in), None, "NA")

        quarter = block // 2
        there = pl.ds(pl.multiple_of(side_other * quarter, 16), quarter)
        here = pl.ds(pl.multiple_of(side * quarter, 16), quarter)

        def gains_away():
            for name in ("q0", "q1", "f2", "f3", "f4", "f5"):
                steps[name].finish()
            pushes["X"] = Push(lambda: (gain_sums.at[:, there], gain_in), None)

        def gains_near():
            pushes["X"].wait_recv()
            gain_grads[...] = gain_sums[:, here, :] + gain_in[...]

        steps["X"] = Walk(gains_away, gains_near)

        def follow(order):
            for name in order:
                if name in works:
                    do(name)
                else:
                    steps[name].step()

        down_tiles = spread(down_full, bit_count, 512)

        def down_load(i, held_down):
            return keep(down_full.at[down_tiles[i][0]], held_down.at[i % 2])

        def first_phase(held_rows, held_cot, held_hid, held_down):
            loads = [
                keep(cot_all, held_cot),
                keep(hid.at[0], held_hid.at[0]),
                keep(normed_two, held_rows),
                keep(hid.at[1], held_hid.at[1]),
            ]
            down_first = down_load(0, held_down)
            pl.semaphore_wait(barrier, bit_count + 1)
            waited = set()

            def ready(*numbers):
                for n in numbers:
                    if n not in waited:
                        waited.add(n)
                        loads[n].wait()

            sources = [
                (held_cot, held_hid.at[0], away_slots.at[0], (0, 1)),
                (held_rows, held_hid.at[1], away_slots.at[1], (2, 3)),
                (held_rows, held_hid.at[1], away_slots.at[0], (2, 4)),
            ]

            def away_work(m):
                def run():
                    left, right, slot, numbers = sources[m]
                    if m == 2:
                        do("B1")
                        loads.append(keep(hid.at[2], held_hid.at[1]))
                        sent(mlp_products[0].copy)
                    ready(*numbers)
                    mlp_products[m].away(left, right, slot)

                return run

            def near_work(m):
                def run():
                    steps[f"K{m}"].finish()
                    mlp_products[m].near(*sources[m][:2])

                return run

            for m in range(3):
                works[f"W{m}"] = away_work(m)
                works[f"B{m}"] = near_work(m)
            def out_product_rows():
                ready(1)
                load = down_first
                for i, (index, count) in enumerate(down_tiles):
                    load.wait()
                    if i + 1 < len(down_tiles):
                        load = down_load(i + 1, held_down)
                    to = slice(i * count, (i + 1) * count)
                    weights = held_down[i % 2].reshape(count, hidden_width)
                    for zone in range(2):
                        at = slice(zone * rows, (zone + 1) * rows)
                        value = dot(held_hid[0, at, :], weights, ((1,), (1,))).astype(bf16)
                        out_part[zone, :, :, to] = value.reshape(2, own_rows, count)

            works["O"] = out_product_rows
            follow(BACKWARD_ORDER[:phase_at])
            for name in ("B0", "B1", "B2", "O"):
                do(name)
            for m in (1, 2):
                sent(mlp_products[m].copy)

        phase_at = BACKWARD_ORDER.index("MR")
        tile_shape = down_full.shape[len(spread(down_full, bit_count, 512)[0][0]) :]
        pl.run_scoped(
            first_phase,
            pltpu.VMEM(normed_two.shape, bf16),
            pltpu.VMEM(cot_all.shape, bf16),
            pltpu.VMEM((2,) + hid.shape[1:], bf16),
            pltpu.VMEM((2,) + tile_shape, bf16),
        )

        def second_phase(
            weights, held_probs, projected, attended, grad_att, grad_qkv, acc, turned
        ):
            qkv_width = query_width + tile
            lead_all = (slice(None),) * (bit_count + 1)
            loads = {
                "out": keep(out_full, weights.at[lead_all + (pl.ds(0, query_width),)]),
                "probs": keep(probs.at[pl.ds(0, HEADS_PER_KV)], held_probs),
                "projected": keep(projected_in, projected),
                "attended": keep(attended_in, attended),
            }

            def ready(*names):
                for name in names:
                    if name in loads:
                        loads.pop(name).wait()

            def middle_work():
                middle_load.wait()
                steps["el"].finish()
                steps["er"].finish()

                def middle_rows(at):
                    x = middle[at, :]
                    total = cot[at, :].astype(f32) + rms_grad(x, rms(x), quad_value(0, at))
                    grad_middle[at, :] = total
                    grad_branch[side, at, :] = total.astype(bf16)

                strips(own_rows, 16, middle_rows)

            works["MR"] = middle_work
            branch_flat = BranchView()
            slots = [
                away_slots.at[(i,) + (slice(None),) * bit_count + (pl.ds(0, columns),)]
                for i, columns in ((0, qkv_width), (1, query_width))
            ]

            def attended_grad():
                steps["D"].finish()
                ready("out")
                branch_all = grad_branch[...].reshape(rows, width)
                for low in range(0, query_width, 256):
                    block_of = weights[lead_all + (slice(low, low + 256),)].reshape(width, 256)
                    grad_att[:, low : low + 256] = jnp.dot(
                        branch_all, block_of, preferred_element_type=f32
                    ).astype(bf16)
                loads["qkv"] = keep(qkv_full, weights)

            works["DA"] = attended_grad

            def out_away():
                steps["D"].finish()
                ready("attended")
                out_product.away(branch_flat, attended, slots[1])

            def out_near():
                steps["KO"].finish()
                out_product.near(branch_flat, attended)
                sent(pushes["D"])
                loads["normed"] = keep(normed, grad_branch)

            works["OA"] = out_away
            works["OB"] = out_near

            pair_lanes = lax.broadcasted_iota(jnp.int32, (rows, 2 * HEAD_SIZE), 1)
            lanes = lax.broadcasted_iota(jnp.int32, (rows, key_width), 1)
            first_half = lanes % HEAD_SIZE < HEAD_SIZE // 2

            def padded(a, head, place):
                moved = a if head == place else pltpu.roll(a, HEAD_SIZE, 1)
                inside = pair_lanes < HEAD_SIZE if place == 0 else pair_lanes >= HEAD_SIZE
                return jnp.where(inside, moved, 0.0).astype(bf16)

            def unrotate(a):
                forward = pltpu.roll(a, key_width - HEAD_SIZE // 2, 1)
                back = pltpu.roll(a, HEAD_SIZE // 2, 1)
                return a * cosines[...] - jnp.where(first_half, forward, back) * sines[...]

            heads = key_width // HEAD_SIZE
            pairs = HEADS_PER_KV // 2
            tile_rows = 128
            lane_tile = lax.broadcasted_iota(jnp.int32, (tile_rows, 2 * HEAD_SIZE), 1)
            totals = []
            heads_at = {}

            def head_pair(n):
                def run():
                    head, i = n // pairs, n % pairs
                    if i == 0:
                        do("DA")
                        ready("probs", "projected")
                        if head > 0:
                            first = head * HEADS_PER_KV
                            keep(probs.at[pl.ds(first, HEADS_PER_KV)], held_probs).wait()
                        keys32 = projected[:, :key_width].astype(f32)
                        values32 = projected[:, key_width:tile].astype(f32)
                        heads_at["keys"] = [padded(keys32, head, p) for p in range(2)]
                        heads_at["values"] = [padded(values32, head, p) for p in range(2)]
                        acc[...] = jnp.zeros_like(acc)
                    keys_at, values_at = heads_at["keys"], heads_at["values"]
                    columns = slice(n * 128, (n + 1) * 128)
                    query_columns = slice(tile + n * 128, tile + (n + 1) * 128)
                    places = [
                        (low, low + tile_rows, p)
                        for low in range(0, rows, tile_rows)
                        for p in range(2)
                    ]
                    insides = [lane_tile < HEAD_SIZE, lane_tile >= HEAD_SIZE]
                    prob = [
                        held_probs[2 * i + p, low:high, :high] for low, high, p in places
                    ]
                    grad_prob = [
                        dot(grad_att[low:high, columns], values_at[p][:high], ((1,), (1,)))
                        for low, high, p in places
                    ]
                    prob32 = [a.astype(f32) for a in prob]
                    weighted = [a * b for a, b in zip(prob32, grad_prob)]
                    centre = [jnp.sum(a, axis=-1, keepdims=True) for a in weighted]
                    grad_score = [
                        (a - b * c).astype(bf16) for a, b, c in zip(weighted, prob32, centre)
                    ]
                    grad_query = [
                        jnp.dot(a, keys_at[p][:high], preferred_element_type=f32)
                        for a, (low, high, p) in zip(grad_score, places)
                    ]
                    for j, (low, high, p) in enumerate(places):
                        query = projected[low:high, query_columns].astype(f32)
                        only_query = jnp.where(insides[p], query, 0.0).astype(bf16)
                        out32 = grad_att[low:high, columns].astype(f32)
                        only_grad = jnp.where(insides[p], out32, 0.0).astype(bf16)
                        acc[0, :high, :] += dot(grad_score[j], only_query, ((0,), (0,)))
                        acc[1, :high, :] += dot(prob[j], only_grad, ((0,), (0,)))
                        if p == 1:
                            total = grad_query[j - 1] + grad_query[j]
                            acc[2, low:high, :] = total * HEAD_SIZE**-0.5
                    grad_qkv[:, query_columns] = unrotate(acc[2]).astype(bf16)
                    if i == pairs - 1:
                        totals.append([acc[j] + pltpu.roll(acc[j], HEAD_SIZE, 1) for j in range(2)])

                return run

            for n in range(query_width // 128):
                works[f"T{n}"] = head_pair(n)

            def qkv_away():
                lower = pair_lanes < HEAD_SIZE
                grad_keys = unrotate(jnp.where(lower, totals[0][0], totals[1][0]))
                grad_qkv[:, :key_width] = grad_keys.astype(bf16)
                grad_values = jnp.where(lower, totals[0][1], totals[1][1])
                grad_qkv[:, key_width:tile] = grad_values.astype(bf16)
                ready("normed")
                qkv_product.away(branch_flat, grad_qkv, slots[0])

            def qkv_near():
                steps["KQ"].finish()
                qkv_product.near(branch_flat, grad_qkv)

            works["QA"] = qkv_away
            works["QB"] = qkv_near
            tiles = spread(weights, bit_count, 512)

            def norm_part(which, give):
                ready("qkv")
                at = pl.ds(pl.multiple_of(which * own_rows, 64), own_rows)
                chosen = grad_qkv[at, :]
                for i, (index, count) in enumerate(tiles):
                    block_of = weights[index].reshape(count, qkv_width)
                    give(slice(i * count, (i + 1) * count), dot(chosen, block_of, ((1,), (1,))))

            def give_away(to, value):
                norm_away[:, to] = value.astype(bf16)

            def give_near(to, value):
                middle[:, to] = value

            works["NA"] = lambda: norm_part(side_other, give_away)

            def result_work():
                steps["ol"].finish()
                steps["or"].finish()

                def result_rows(at):
                    result[at, :] = (middle[at, :] + quad_value(1, at)).astype(bf16)

                strips(own_rows, 16, result_rows)

            works["RR"] = result_work

            def near_rows():
                do("RR")
                norm_part(side, give_near)

            works["NB"] = near_rows

            def input_work():
                do("NB")
                steps["N"].finish()

                def input_rows(at):
                    x = tok[at, :].astype(f32)
                    scaled = middle[at, :] + norm_in[at, :].astype(f32)
                    total = grad_middle[at, :] + rms_grad(x, rms(x), scaled)
                    input_grad[at, :] = total.astype(bf16)

                strips(own_rows, 16, input_rows)

            works["IR"] = input_work

            def turn_down():
                steps["f0"].finish()
                steps["f1"].finish()
                for h, start in ((0, own_half), (1, other_half)):
                    if h == 1:
                        turn_copies.pop().wait()
                    turned[...] = down_held[h].T
                    turn_copies.append(keep(turned, down_grad.at[pl.ds(start, hidden_width)]))

            def turn_out():
                steps["p0"].finish()
                steps["p1"].finish()
                out_grad[...] = out_sum[...].T

            turn_copies = []
            works["TD"] = turn_down
            works["TO"] = turn_out
            follow(BACKWARD_ORDER[phase_at:])
            for name in works:
                do(name)
            for product in (out_product, qkv_product):
                sent(product.copy)
            for copy in turn_copies:
                copy.wait()

        class BranchView:
            def __getitem__(self, index):
                return grad_branch[(slice(None), slice(None), index[1])].reshape(rows, -1)

        pl.run_scoped(
            second_phase,
            pltpu.VMEM(qkv_full.shape, bf16),
            pltpu.VMEM((HEADS_PER_KV,) + probs.shape[1:], bf16),
            pltpu.VMEM(projected_in.shape, bf16),
            pltpu.VMEM(attended_in.shape, bf16),
            pltpu.VMEM(attended_in.shape, bf16),
            pltpu.VMEM(projected_in.shape, bf16),
            pltpu.VMEM((3, rows, 2 * HEAD_SIZE), f32),
            pltpu.VMEM((hid.shape[-1], block), f32),
        )

        for name in steps:
            steps[name].finish()
        for copy in stage_copies:
            copy().wait()
        for copy in list(unsent):
            sent(copy)

    def call(
        normed_two,
        cot_all,
        hid,
        grad_part,
        down_full,
        middle,
        tok,
        cot,
        out_full,
        qkv_full,
        normed,
        projected,
        probs,
        attended,
        cosines,
        sines,
        w_query,
        key_value,
        w_gateup,
        gains,
    ):
        bf16, f32 = jnp.bfloat16, jnp.float32
        own_rows, width = tok.shape
        half = width // 2
        block, qkv_width = qkv_full.shape[-2:]
        query_width = out_full.shape[-1]
        mlp_width = hid.shape[-1]
        shape = jax.ShapeDtypeStruct
        whole = pl.BlockSpec(memory_space=pltpu.VMEM)
        away = pl.BlockSpec(memory_space=pl.ANY)

        def twos(count):
            return (2,) * count

        slots = [
            shape(twos(bit_count - 2 - i) + (block, mlp_width), bf16) for i in range(step_count)
        ] * 3

        def steps_of(order, columns):
            return [
                pltpu.VMEM(twos(bit_count - 2 - i) + (block, columns), bf16)
                for i in range(len(order))
            ]

        def at_core(columns):
            return twos(bit_count - 1) + (block, columns)

        count = 6 * (step_count + 2) + 6 * bit_count + 24
        outs = pl.pallas_call(
            kernel,
            out_shape=[
                shape((own_rows, width), bf16),
                shape((own_rows, width), bf16),
                shape((block, query_width), f32),
                shape(key_value.shape, f32),
                shape((query_width, block), f32),
                shape(w_gateup.shape, f32),
                shape((2 * mlp_width, block), f32),
                shape((2, block // 2, 128), f32),
            ]
            + slots,
            in_specs=[away] * 6 + [whole] * 2 + [away] * 6 + [whole] * 4 + [away, whole],
            out_specs=[whole] * 5 + [away] * 2 + [whole] + [away] * len(slots),
            scratch_shapes=[
                pltpu.VMEM(twos(bit_count - 2) + (block, mlp_width), bf16),
                pltpu.VMEM((2, 2, own_rows, width), bf16),
                pltpu.VMEM((2,) + at_core(mlp_width), bf16),
                pltpu.VMEM((3,) + at_core(mlp_width), bf16),
                pltpu.VMEM((3, 2, block, mlp_width), bf16),
                pltpu.VMEM(at_core(qkv_width), bf16),
                pltpu.VMEM(at_core(query_width), bf16),
                pltpu.VMEM((2, 2, 2, own_rows, half), bf16),
                pltpu.VMEM((2, 2, own_rows, half), bf16),
                pltpu.VMEM((2, 2, own_rows, half), bf16),
                pltpu.VMEM((own_rows, width), f32),
                pltpu.VMEM((own_rows, width), f32),
                pltpu.VMEM((2, own_rows, width), bf16),
                pltpu.VMEM((own_rows, width), bf16),
                pltpu.VMEM((own_rows, width), bf16),
                pltpu.VMEM((2, block // 2, mlp_width), f32),
                pltpu.VMEM((2, block, mlp_width), f32),
                pltpu.VMEM((block, query_width), f32),
                pltpu.VMEM((block, mlp_width), bf16),
                pltpu.VMEM((2, block, 128), f32),
                pltpu.VMEM((2, block // 2, 128), f32),
                pltpu.VMEM((2, block, 128), f32),
                pltpu.SemaphoreType.DMA((count,)),
                pltpu.SemaphoreType.DMA((count,)),
                pltpu.SemaphoreType.DMA((6 * step_count + 64,)),
            ]
            + steps_of(qkv_order, qkv_width)
            + steps_of(qkv_order, query_width),
            compiler_params=pltpu.CompilerParams(
                collective_id=2, has_side_effects=True, vmem_limit_bytes=63 * 1024 * 1024
            ),
            name="backward",
        )(
            normed_two,
            cot_all,
            hid,
            grad_part,
            down_full,
            middle,
            tok,
            cot,
            out_full,
            qkv_full,
            normed,
            projected,
            probs,
            attended,
            cosines,
            sines,
            w_query,
            key_value,
            w_gateup,
            gains,
        )
        return outs[:8]

    return call


def pass_on(arrays):
    count = len(arrays)

    def kernel(*refs):
        sources, targets = refs[:count], refs[count : 2 * count]
        held, sems = refs[2 * count : 3 * count], refs[3 * count]
        loads = []
        for i in range(count):
            loads.append(pltpu.make_async_copy(sources[i], held[i], sems.at[0, i]))
            loads[i].start()
        stores = []
        for i in range(count):
            loads[i].wait()
            stores.append(pltpu.make_async_copy(held[i], targets[i], sems.at[1, i]))
            stores[i].start()
        for copy in stores:
            copy.wait()

    away = pl.BlockSpec(memory_space=pl.ANY)
    return pl.pallas_call(
        kernel,
        out_shape=[jax.ShapeDtypeStruct(a.shape, a.dtype) for a in arrays],
        in_specs=[away] * count,
        out_specs=[away] * count,
        scratch_shapes=[pltpu.VMEM(a.shape, a.dtype) for a in arrays]
        + [pltpu.SemaphoreType.DMA((2, count))],
        compiler_params=pltpu.CompilerParams(vmem_limit_bytes=62 * 1024 * 1024),
        cost_estimate=pl.CostEstimate(
            flops=0, bytes_accessed=2 * sum(a.size * a.dtype.itemsize for a in arrays), transcendentals=0
        ),
        name="pass_on",
    )(*arrays)


def make_body(dp_size):
    bit_count = dp_size.bit_length() - 1
    high_bits = tuple(range(bit_count - 1, SHARE_BIT, -1))

    def body(
        tokens,
        attn_gain,
        w_query,
        keyvalue_weight,
        w_out,
        mlp_gain,
        w_gateup,
        w_down,
        segment_ids,
        positions,
        cotangent,
    ):
        f32 = jnp.float32
        own_rows, width = tokens.shape

        gains = jnp.stack([attn_gain, mlp_gain]).astype(f32)
        order = jnp.arange(segment_ids.shape[0])
        allowed = (segment_ids[:, None] == segment_ids[None, :]) & (
            order[:, None] >= order[None, :]
        )
        bias = jnp.where(allowed, 0.0, -1e30).astype(f32)

        cosine_table, sine_table = rotary_tables(positions, 2 * HEAD_SIZE)
        (
            qkv_full,
            out_full,
            probs,
            normed,
            projected,
            attended,
            middle,
            normed_two,
            grad_all,
            hid,
            grad_part,
            down_full,
        ) = make_forward(dp_size, high_bits)(
            tokens,
            cotangent,
            w_query,
            keyvalue_weight,
            w_out,
            w_gateup,
            w_down,
            gains,
            cosine_table,
            sine_table,
            bias,
        )
        normed_two = normed_two.reshape(4 * own_rows, width)
        grad_all = grad_all.reshape(4 * own_rows, width)

        quad_shape = (2, 2, own_rows, width)
        (
            result,
            input_grad,
            query_grad,
            keyval_grad,
            out_grad,
            gateup_grad,
            down_grad,
            gain_grads,
        ) = make_backward(dp_size, high_bits)(
            normed_two,
            grad_all,
            hid,
            grad_part.reshape(quad_shape),
            down_full,
            middle,
            tokens,
            cotangent,
            out_full,
            qkv_full,
            normed.reshape(2, own_rows, width),
            projected,
            probs,
            attended,
            cosine_table,
            sine_table,
            w_query,
            keyvalue_weight,
            w_gateup,
            gains,
        )
        result, input_grad, query_grad, keyval_grad, out_grad, gateup_grad, down_grad = pass_on(
            [result, input_grad, query_grad, keyval_grad, out_grad, gateup_grad, down_grad]
        )
        return (
            result,
            input_grad,
            gain_grads[0, :, 0],
            query_grad,
            keyval_grad,
            out_grad,
            gain_grads[1, :, 0],
            gateup_grad,
            down_grad,
        )

    return body


def solution(mesh):
    return jax.shard_map(
        make_body(mesh.shape["dp"]),
        mesh=mesh,
        in_specs=(
            P(("dp", "tensor"), None),
            P("dp"),
            P("dp", "tensor"),
            P(None, "dp", "tensor"),
            P("tensor", "dp"),
            P("dp"),
            P(None, "dp", "tensor"),
            P("tensor", "dp"),
            P("dp"),
            P("dp"),
            P(("dp", "tensor"), None),
        ),
        out_specs=(
            P(("dp", "tensor"), None),
            P(("dp", "tensor"), None),
            P(("dp", "tensor")),
            P("dp", "tensor"),
            P(None, "dp", "tensor"),
            P("tensor", "dp"),
            P(("dp", "tensor")),
            P(None, "dp", "tensor"),
            P("tensor", "dp"),
        ),
        check_vma=False,
    )
```
